32 devices in a mesh: dp: 8 (over z, core), tensor: 4 (over y, x).
Axes of the slice: x: 2, y: 2, z: 4, core: 2. Of those that a mesh axis runs over, the one named last changes fastest.
Arguments:
- latents: bfloat16 [8192, 1536], P(('dp', 'tensor')), may hold values from -6 to 6
- conditioning: bfloat16 [8, 130, 768], P('dp'), may hold values from -6 to 6
- gain_attn: float32 [1536], replicated, may hold values from 0.1 to 1.9
- w_qkv: float32 [1536, 4608], P('dp', 'tensor'), may hold values from -0.15625 to 0.15625
- w_attn_out: float32 [1536, 1536], P('tensor', 'dp'), may hold values from -3 to 3
- gain_cross: float32 [1536], replicated, may hold values from 0.1 to 1.9
- w_cross_q: float32 [1536, 1536], P('dp', 'tensor'), may hold values from -0.15625 to 0.15625
- w_cross_kv: float32 [768, 3072], P('dp', 'tensor'), may hold values from -0.21875 to 0.21875
- w_cross_out: float32 [1536, 1536], P('tensor', 'dp'), may hold values from -1 to 1
- gain_mlp: float32 [1536], replicated, may hold values from 0.1 to 1.9
- w_gate: float32 [1536, 6144], P('dp', 'tensor'), may hold values from -0.15625 to 0.15625
- w_up: float32 [1536, 6144], P('dp', 'tensor'), may hold values from -0.15625 to 0.15625
- w_down: float32 [6144, 1536], P('tensor', 'dp'), may hold values from -0.078125 to 0.078125
- cotangent: bfloat16 [8192, 1536], P(('dp', 'tensor')), may hold values from -6 to 6
Outputs:
- block_out: float32 [8192, 1536], P(('dp', 'tensor'))
- grad_latents: float32 [8192, 1536], P(('dp', 'tensor'))
- grad_conditioning: float32 [8, 130, 768], P('dp')
- grad_gain_attn: float32 [1536], replicated
- grad_w_qkv: float32 [1536, 4608], P('dp', 'tensor')
- grad_w_attn_out: float32 [1536, 1536], P('tensor', 'dp')
- grad_gain_cross: float32 [1536], replicated
- grad_w_cross_q: float32 [1536, 1536], P('dp', 'tensor')
- grad_w_cross_kv: float32 [768, 3072], P('dp', 'tensor')
- grad_w_cross_out: float32 [1536, 1536], P('tensor', 'dp')
- grad_gain_mlp: float32 [1536], replicated
- grad_w_gate: float32 [1536, 6144], P('dp', 'tensor')
- grad_w_up: float32 [1536, 6144], P('dp', 'tensor')
- grad_w_down: float32 [6144, 1536], P('tensor', 'dp')
The draws below stay inside these ranges and needn't reach their ends.
All inputs are finite; a program needn't handle non-finite values.
Results may differ from the reference program's by a relative error of at most 0.025.
Values may be sent and summed in bfloat16 or wider, within the bound.
A program may use at most 192 MiB of HBM per device.

```python
import jax
import jax.numpy as jnp
from jax import lax

D = 1536
HEADS = 24
DH = 64
FF = 6144
DC = 768
CTX = 130
LENGTH = 1024
SEQS = 8
TOKENS = 8192


def raised(drawn, rng, source, target, parts, factor):
    def block_of(axis_at):
        return (jnp.arange(drawn.shape[axis_at]) // (drawn.shape[axis_at] // parts)).reshape((-1,) + (1,) * (drawn.ndim - 1 - axis_at))

    first = jax.random.permutation(rng, parts)[block_of(target)]
    second = (block_of(target) + parts // 2) % parts
    return jnp.where((block_of(source) == first) | (block_of(source) == second), factor * drawn, drawn)


def levels(stream_key, dims, pieces, low, top_value):
    gain, own = 1.0, jax.random.fold_in(stream_key, 6)
    for position, shards_of in pieces:
        draws = jnp.exp(jax.random.uniform(jax.random.fold_in(own, position), (shards_of,), jnp.float32, low / len(pieces), top_value / len(pieces)))
        gain = gain * jnp.repeat(draws, dims[position] // shards_of).reshape([-1 if axis == position else 1 for axis in range(len(dims))])
    return gain


def scatter_about(key, extent, width, most, split=(), kind=jnp.bfloat16):
    values = jax.random.normal(key, extent, jnp.float32) * width
    if len(split) > 0:
        values = levels(key, extent, split, -0.22, 0.18) * values
    return jnp.clip(values, min=-most, max=most).astype(kind)


def noise_with(key, dims, scale, limit, shards, heavy, kind=jnp.bfloat16):
    array = scale * jax.random.normal(key, dims, jnp.float32)
    if shards:
        array = array * levels(key, dims, shards, -0.22, 0.18)
    return jnp.clip(raised(array, jax.random.fold_in(key, 3), *heavy), -limit, limit).astype(kind)


def setup_inputs(seed: int = 0) -> dict:
    streams_of = jax.random.split(jax.random.key(seed), 15)
    latents = scatter_about(streams_of[0], (TOKENS, D), 1.0, 6.0, ((0, 32),))
    conditioning = scatter_about(streams_of[1], (SEQS, CTX, DC), 1.0, 6.0, ((0, 8),))
    gain_attn = jnp.clip(1.0 + 0.18 * jax.random.normal(streams_of[2], (D,), jnp.float32), 0.1, 1.9)
    w_qkv = scatter_about(streams_of[3], (D, 3 * D), D ** -0.5, 0.15625, ((0, 8), (1, 4)), jnp.float32)
    w_attn_out = scatter_about(streams_of[4], (D, D), (max(1, 8 * D // (3 * LENGTH))) ** -0.5, 3.0, ((0, 4), (1, 8)), jnp.float32)
    gain_cross = jnp.clip(1.0 + 0.18 * jax.random.normal(streams_of[5], (D,), jnp.float32), 0.1, 1.9)
    w_cross_q = scatter_about(streams_of[6], (D, D), D ** -0.5, 0.15625, ((0, 8), (1, 4)), jnp.float32)
    w_cross_kv = scatter_about(streams_of[7], (DC, 2 * D), DC ** -0.5, 0.21875, ((0, 8), (1, 4)), jnp.float32)
    w_cross_out = scatter_about(streams_of[8], (D, D), (max(1, 8 * D // (3 * CTX))) ** -0.5, 1.0, ((0, 4), (1, 8)), jnp.float32)
    gain_mlp = jnp.clip(1.0 + 0.18 * jax.random.normal(streams_of[9], (D,), jnp.float32), 0.1, 1.9)
    w_gate = scatter_about(streams_of[10], (D, FF), D ** -0.5, 0.15625, ((0, 8), (1, 4)), jnp.float32)
    w_up = scatter_about(streams_of[11], (D, FF), D ** -0.5, 0.15625, ((0, 8), (1, 4)), jnp.float32)
    w_down = scatter_about(streams_of[12], (FF, D), FF ** -0.5, 0.078125, ((0, 4), (1, 8)), jnp.float32)
    cotangent = noise_with(streams_of[13], (TOKENS, D), 1.0, 6.0, ((0, 32),), (0, 1, 32, 2.75))
    return dict(latents=latents, conditioning=conditioning, gain_attn=gain_attn, w_qkv=w_qkv, w_attn_out=w_attn_out, gain_cross=gain_cross, w_cross_q=w_cross_q, w_cross_kv=w_cross_kv, w_cross_out=w_cross_out, gain_mlp=gain_mlp, w_gate=w_gate, w_up=w_up, w_down=w_down, cotangent=cotangent)


norm_eps = 1e-05
rope_base = 10000.0

@jax.custom_vjp
def low(v):
    return lax.optimization_barrier(v.astype(jnp.bfloat16)).astype(jnp.float32)

@jax.custom_vjp
def low_back(v):
    return v

def low_keep(v):
    return (low(v), None)

def low_pass(kept, grad):
    return (grad,)

def back_keep(v):
    return (v, None)

def back_low(kept, grad):
    return (low(grad),)
low.defvjp(low_keep, low_pass)
low_back.defvjp(back_keep, back_low)

def highest_dot(left_op, right_op):
    return jnp.dot(left_op, right_op, precision=lax.Precision.HIGHEST, preferred_element_type=jnp.float32)

def layer_norm(values, gain_vec):
    center = values - lax.optimization_barrier(jnp.mean(values, axis=-1, keepdims=True))
    spread = lax.optimization_barrier(jnp.mean(center * center, axis=-1, keepdims=True))
    return center * lax.rsqrt(spread + norm_eps) * gain_vec

def rotary_tables(positions):
    quarter = DH // 4
    frequency = jnp.exp(-jnp.log(rope_base) * jnp.arange(quarter).astype(jnp.float32) / quarter)
    angles = positions.astype(jnp.float32)[:, None] * frequency[None, :]
    return (jnp.cos(angles)[:, None, :], jnp.sin(angles)[:, None, :])

def rotate_heads(values, cosine_table, sine_table):
    quarter = DH // 4
    first_half = values[..., :quarter]
    second_half = values[..., quarter:2 * quarter]
    return jnp.concatenate([first_half * cosine_table - second_half * sine_table, second_half * cosine_table + first_half * sine_table, values[..., 2 * quarter:]], axis=-1)

def softmax_rows(scores):
    shifted = jnp.exp(scores - lax.optimization_barrier(jnp.max(scores, axis=-1, keepdims=True)))
    return shifted / lax.optimization_barrier(jnp.sum(shifted, axis=-1, keepdims=True))

def self_attend(queries, keys_rot, values_in):
    block_rows = min(512, LENGTH)
    scaling = DH ** (-0.5)
    blocks = queries.reshape(LENGTH // block_rows, block_rows, HEADS, DH)

    @jax.checkpoint
    def one_block(query_block):
        scores = low_back(jnp.einsum('qhd,khd->hqk', query_block, keys_rot, precision=lax.Precision.HIGHEST) * scaling)
        probabilities = softmax_rows(scores)
        return jnp.einsum('hqk,khd->qhd', low(probabilities), values_in, precision=lax.Precision.HIGHEST)
    return lax.map(one_block, blocks).reshape(LENGTH, D)

def cross_attend(queries, keys_in, values_in):
    scores = low_back(jnp.einsum('qhd,khd->hqk', queries, keys_in, precision=lax.Precision.HIGHEST) * DH ** (-0.5))
    probabilities = softmax_rows(scores)
    return jnp.einsum('hqk,khd->qhd', low(probabilities), values_in, precision=lax.Precision.HIGHEST).reshape(LENGTH, D)

def layer_forward(params, tokens, context):
    gain_attn, w_qkv, w_attn_out, gain_cross, w_cross_q, w_cross_kv, w_cross_out, gain_mlp, w_gate, w_up, w_down = params
    cosine_table, sine_table = rotary_tables(jnp.arange(LENGTH))
    normed = low(layer_norm(tokens, gain_attn))
    packed = low_back(highest_dot(normed, low(w_qkv))).reshape(LENGTH, HEADS, 3, DH)
    queries = low(rotate_heads(packed[:, :, 0], cosine_table, sine_table))
    keys_rot = low(rotate_heads(packed[:, :, 1], cosine_table, sine_table))
    values_in = low(packed[:, :, 2])
    attended = low(low_back(self_attend(queries, keys_rot, values_in)))
    first_sum = tokens + low_back(highest_dot(attended, low(w_attn_out)))
    normed = low(layer_norm(first_sum, gain_cross))
    cross_query = low(low_back(highest_dot(normed, low(w_cross_q)))).reshape(LENGTH, HEADS, DH)
    cross_pack = low(low_back(highest_dot(context, low(w_cross_kv)))).reshape(CTX, HEADS, 2, DH)
    crossed = low(low_back(cross_attend(cross_query, cross_pack[:, :, 0], cross_pack[:, :, 1])))
    second_sum = first_sum + low_back(highest_dot(crossed, low(w_cross_out)))
    normed = low(layer_norm(second_sum, gain_mlp))
    gate_pre = low_back(highest_dot(normed, low(w_gate)))
    up_pre = low_back(highest_dot(normed, low(w_up)))
    hidden = low(jax.nn.silu(gate_pre) * up_pre)
    return second_sum + low_back(highest_dot(hidden, low(w_down)))

def reference(latents, conditioning, gain_attn, w_qkv, w_attn_out, gain_cross, w_cross_q, w_cross_kv, w_cross_out, gain_mlp, w_gate, w_up, w_down, cotangent):
    params = (gain_attn, w_qkv, w_attn_out, gain_cross, w_cross_q, w_cross_kv, w_cross_out, gain_mlp, w_gate, w_up, w_down)
    params = tuple((member.astype(jnp.float32) for member in params))
    tokens = latents.astype(jnp.float32).reshape(SEQS, LENGTH, D)
    context = conditioning.astype(jnp.float32)
    cotangents = cotangent.astype(jnp.float32).reshape(SEQS, LENGTH, D)
    zeroed = tuple((jnp.zeros_like(member) for member in params))

    def one_sequence(totals, inputs):
        seq_tokens, seq_context, seq_grad = inputs
        result, pullback = jax.vjp(layer_forward, params, seq_tokens, seq_context)
        grad_params, grad_tokens, grad_context = pullback(seq_grad)
        totals = tuple((earlier + addend for earlier, addend in zip(totals, grad_params)))
        return (totals, (result, grad_tokens, grad_context))
    totals, (outputs, grad_tokens, grad_context) = lax.scan(one_sequence, zeroed, (tokens, context, cotangents))
    return (outputs.reshape(TOKENS, D), grad_tokens.reshape(TOKENS, D), grad_context, totals[0], totals[1], totals[2], totals[3], totals[4], totals[5], totals[6], totals[7], totals[8], totals[9], totals[10])
```

```python
from functools import reduce

import jax
import jax.numpy as jnp
from jax import lax
from jax.experimental import pallas as pl
from jax.experimental.pallas import tpu as pltpu
from jax.sharding import PartitionSpec as P

DH = 64
CTX = 130
LENGTH = 1024
PAIR = 2 * DH
ROWS = 256
VMEM_BYTES = 48 * 2**20

norm_eps = 1e-05
rope_base = 10000.0


def head_turn(values, cosine, minus_sine, plus_sine):
    quarter = DH // 4
    ahead = pltpu.roll(values, PAIR - quarter, 1)
    behind = pltpu.roll(values, quarter, 1)
    return values * cosine + ahead * minus_sine + behind * plus_sine


def half_mask(shape, axis, which):
    place = lax.broadcasted_iota(jnp.int32, shape, axis)
    return (place >= DH) if which else (place < DH)


def attend_kernel(q_ref, k_ref, v_ref, cos_ref, msin_ref, psin_ref, out_ref, rot_ref, log_ref, kt_ref, vm_ref):
    pairs = pl.num_programs(0)
    pair = pl.program_id(0)
    turn = (cos_ref[...], msin_ref[...], psin_ref[...])
    query = head_turn(q_ref[...], *turn).astype(jnp.bfloat16)
    key = head_turn(k_ref[...], *turn).astype(jnp.bfloat16)
    value = v_ref[...].astype(jnp.bfloat16)
    for part, array in enumerate((query, key, value)):
        start = pl.multiple_of((part * pairs + pair) * PAIR, PAIR)
        rot_ref[:, pl.ds(start, PAIR)] = array
    key_t = key.astype(jnp.float32).T
    for which in range(2):
        kt_ref[which] = jnp.where(half_mask(key_t.shape, 0, which), key_t, 0.0).astype(jnp.bfloat16)
        vm_ref[which] = jnp.where(half_mask(value.shape, 1, which), value.astype(jnp.float32), 0.0).astype(jnp.bfloat16)
    q_start = pl.multiple_of(pair * PAIR, PAIR)

    def one_block(step, carry):
        rows = pl.ds(pl.multiple_of(step * ROWS, ROWS), ROWS)
        block = rot_ref[rows, pl.ds(q_start, PAIR)] * jnp.bfloat16(DH**-0.5)
        outs, logs = [], []
        for which in range(2):
            scores = jnp.dot(block, kt_ref[which], preferred_element_type=jnp.float32)
            peak = jnp.max(scores, axis=1, keepdims=True)
            shifted = jnp.exp(scores - peak)
            total = jnp.sum(shifted, axis=1, keepdims=True)
            product = jnp.dot(shifted.astype(jnp.bfloat16), vm_ref[which], preferred_element_type=jnp.float32)
            outs.append(product * (1.0 / total))
            logs.append(peak + jnp.log(total))
        out_ref[rows, :] = (outs[0] + outs[1]).astype(jnp.bfloat16)
        low = half_mask((ROWS, PAIR), 1, 0)
        log_ref[rows, :] = jnp.where(low, logs[0], logs[1])
        return carry

    lax.fori_loop(0, LENGTH // ROWS, one_block, 0)


def attend_back_kernel(
    q_ref, k_ref, v_ref, grad_ref, log_ref, cos_ref, msin_ref, psin_ref, out_ref,
    kt_ref, vt_ref, km_ref, qt_ref, gt_ref, dq_ref, dk_ref, dv_ref,
):
    pairs = pl.num_programs(0)
    pair = pl.program_id(0)
    key_t = k_ref[...].astype(jnp.float32).T
    value_t = v_ref[...].astype(jnp.float32).T
    for which in range(2):
        keep = half_mask(key_t.shape, 0, which)
        kt_ref[which] = jnp.where(keep, key_t, 0.0).astype(jnp.bfloat16)
        vt_ref[which] = jnp.where(keep, value_t, 0.0).astype(jnp.bfloat16)
        key = k_ref[...].astype(jnp.float32)
        km_ref[which] = jnp.where(half_mask(key.shape, 1, which), key, 0.0).astype(jnp.bfloat16)
    qt_ref[...] = (q_ref[...].astype(jnp.float32) * DH**-0.5).T.astype(jnp.bfloat16)
    gt_ref[...] = grad_ref[...].astype(jnp.float32).T.astype(jnp.bfloat16)
    dk_ref[...] = jnp.zeros_like(dk_ref)
    dv_ref[...] = jnp.zeros_like(dv_ref)

    def one_block(step, carry):
        rows = pl.ds(pl.multiple_of(step * ROWS, ROWS), ROWS)
        block = q_ref[rows, :] * jnp.bfloat16(DH**-0.5)
        grads = grad_ref[rows, :]
        d_query = jnp.zeros((ROWS, PAIR), jnp.float32)
        for which in range(2):
            half = slice(which * DH, (which + 1) * DH)
            scores = jnp.dot(block, kt_ref[which], preferred_element_type=jnp.float32)
            probs = jnp.exp(scores - log_ref[rows, which * DH : which * DH + 1])
            d_prob = jnp.dot(grads, vt_ref[which], preferred_element_type=jnp.float32)
            center = jnp.sum(probs * d_prob, axis=1, keepdims=True)
            d_score = (probs * (d_prob - center)).astype(jnp.bfloat16)
            d_query += jnp.dot(d_score, km_ref[which], preferred_element_type=jnp.float32)
            dk_ref[half, :] += jnp.dot(qt_ref[half, rows], d_score, preferred_element_type=jnp.float32)
            dv_ref[half, :] += jnp.dot(
                gt_ref[half, rows], probs.astype(jnp.bfloat16), preferred_element_type=jnp.float32
            )
        dq_ref[rows, :] = d_query * DH**-0.5
        return carry

    lax.fori_loop(0, LENGTH // ROWS, one_block, 0)
    turn = (cos_ref[...], -msin_ref[...], -psin_ref[...])
    results = (head_turn(dq_ref[...], *turn), head_turn(dk_ref[...].T, *turn), dv_ref[...].T)
    for part, array in enumerate(results):
        start = pl.multiple_of((part * pairs + pair) * PAIR, PAIR)
        out_ref[:, pl.ds(start, PAIR)] = array.astype(jnp.bfloat16)


def column_block(offset):
    return pl.BlockSpec((LENGTH, PAIR), lambda pair: (0, pair + offset))


def whole_block(columns):
    return pl.BlockSpec((LENGTH, columns), lambda pair: (0, 0))


def attend(packed, tables):
    columns = packed.shape[1]
    pairs = columns // (3 * PAIR)
    return pl.pallas_call(
        attend_kernel,
        grid=(pairs,),
        in_specs=[column_block(part * pairs) for part in range(3)] + [whole_block(PAIR)] * 3,
        out_specs=[column_block(0), whole_block(columns), column_block(0)],
        out_shape=[
            jax.ShapeDtypeStruct((LENGTH, pairs * PAIR), jnp.bfloat16),
            jax.ShapeDtypeStruct((LENGTH, columns), jnp.bfloat16),
            jax.ShapeDtypeStruct((LENGTH, pairs * PAIR), jnp.float32),
        ],
        scratch_shapes=[pltpu.VMEM((2, PAIR, LENGTH), jnp.bfloat16), pltpu.VMEM((2, LENGTH, PAIR), jnp.bfloat16)],
        compiler_params=pltpu.CompilerParams(vmem_limit_bytes=VMEM_BYTES),
        cost_estimate=pl.CostEstimate(flops=pairs * 2**32, bytes_accessed=2**24, transcendentals=pairs * 2**21),
    )(packed, packed, packed, *tables)


def attend_back(rotated, d_attended, logs, tables):
    columns = rotated.shape[1]
    pairs = columns // (3 * PAIR)
    tall = pltpu.VMEM((PAIR, LENGTH), jnp.bfloat16)
    return pl.pallas_call(
        attend_back_kernel,
        grid=(pairs,),
        in_specs=[column_block(part * pairs) for part in range(3)]
        + [column_block(0), column_block(0)]
        + [whole_block(PAIR)] * 3,
        out_specs=whole_block(columns),
        out_shape=jax.ShapeDtypeStruct((LENGTH, columns), jnp.bfloat16),
        scratch_shapes=[
            pltpu.VMEM((2, PAIR, LENGTH), jnp.bfloat16),
            pltpu.VMEM((2, PAIR, LENGTH), jnp.bfloat16),
            pltpu.VMEM((2, LENGTH, PAIR), jnp.bfloat16),
            tall,
            tall,
            pltpu.VMEM((LENGTH, PAIR), jnp.float32),
            pltpu.VMEM((PAIR, LENGTH), jnp.float32),
            pltpu.VMEM((PAIR, LENGTH), jnp.float32),
        ],
        compiler_params=pltpu.CompilerParams(vmem_limit_bytes=VMEM_BYTES),
        cost_estimate=pl.CostEstimate(flops=pairs * 2**33, bytes_accessed=2**24, transcendentals=pairs * 2**21),
    )(rotated, rotated, rotated, d_attended, logs, *tables)


def turn_tables(positions):
    quarter = DH // 4
    frequency = jnp.exp(-jnp.log(rope_base) * jnp.arange(quarter).astype(jnp.float32) / quarter)
    angles = positions.astype(jnp.float32)[:, None] * frequency[None, :]
    cosine, sine = jnp.cos(angles), jnp.sin(angles)
    zeros, ones = jnp.zeros_like(sine), jnp.ones_like(sine)
    rows = (
        jnp.concatenate([cosine, cosine, ones, ones], axis=1),
        jnp.concatenate([-sine, zeros, zeros, zeros], axis=1),
        jnp.concatenate([zeros, sine, zeros, zeros], axis=1),
    )
    return tuple(jnp.concatenate([row, row], axis=1) for row in rows)


def dot_plain(left_op, right_op):
    return jnp.dot(left_op, right_op, preferred_element_type=jnp.float32)


def dot_rows(left_op, right_op):
    return lax.dot_general(
        left_op, right_op, (((0,), (0,)), ((), ())), preferred_element_type=jnp.float32
    )


def dot_cols(left_op, right_op):
    return lax.dot_general(
        left_op, right_op, (((1,), (1,)), ((), ())), preferred_element_type=jnp.float32
    )


def layer_norm(values, gain_vec):
    center = values - jnp.mean(values, axis=-1, keepdims=True)
    spread = jnp.mean(center * center, axis=-1, keepdims=True)
    inverse = lax.rsqrt(spread + norm_eps)
    scaled = center * inverse
    return (scaled * gain_vec, scaled, inverse)


def norm_backward(upstream, scaled, inverse, gain_vec):
    weighted = upstream * gain_vec
    inner = jnp.mean(weighted, axis=-1, keepdims=True) + scaled * jnp.mean(
        weighted * scaled, axis=-1, keepdims=True
    )
    return (inverse * (weighted - inner), jnp.sum(upstream * scaled, axis=0))


def swap(values, bit):
    return lax.ppermute(values, "tensor", [(member, member ^ bit) for member in range(4)])


def spread_rows(values):
    if lax.axis_size("tensor") != 4:
        return lax.all_gather(values, "tensor", axis=0, tiled=True)
    half = values.shape[0] // 2
    near, far = swap(values, 1), swap(values, 2)
    return jnp.concatenate([values, near, far, swap(near[:half], 2), swap(far[half:], 1)], axis=0)


def sum_rows(partial):
    if lax.axis_size("tensor") != 4:
        return lax.psum_scatter(
            partial.astype(jnp.bfloat16), "tensor", scatter_dimension=0, tiled=True
        ).astype(jnp.float32)
    size = partial.shape[0] // 4
    half = size // 2
    own, near, far, last = (partial[part * size : (part + 1) * size] for part in range(4))
    first = swap(last[:half].astype(jnp.bfloat16), 1)
    second = swap(last[half:].astype(jnp.bfloat16), 2)
    far = jnp.concatenate([far[:half] + first.astype(jnp.float32), far[half:]], axis=0)
    near = jnp.concatenate([near[:half], near[half:] + second.astype(jnp.float32)], axis=0)
    return (
        own
        + swap(near.astype(jnp.bfloat16), 1).astype(jnp.float32)
        + swap(far.astype(jnp.bfloat16), 2).astype(jnp.float32)
    )


def group_positions(rows):
    group = lax.axis_size("tensor")
    blocks = jnp.arange(group)
    if group == 4:
        blocks = blocks ^ lax.axis_index("tensor")
    return (blocks[:, None] * rows + jnp.arange(rows)[None, :]).reshape(-1)


def cross_forward(queries, keys_in, values_in):
    scores = jnp.einsum("qhd,khd->hqk", queries, keys_in, preferred_element_type=jnp.float32) * DH ** (-0.5)
    peak_score = jnp.max(scores, axis=-1, keepdims=True)
    shifted = jnp.exp(scores - peak_score)
    totals = jnp.sum(shifted, axis=-1, keepdims=True)
    probabilities = (shifted / totals).astype(jnp.bfloat16)
    output = jnp.einsum("hqk,khd->qhd", probabilities, values_in, preferred_element_type=jnp.float32)
    return (output, peak_score + jnp.log(totals))


def cross_backward(queries, keys_in, values_in, d_output, log_totals):
    scaling = DH ** (-0.5)
    scores = jnp.einsum("qhd,khd->hqk", queries, keys_in, preferred_element_type=jnp.float32) * scaling
    probabilities = jnp.exp(scores - log_totals)
    d_prob = jnp.einsum("qhd,khd->hqk", d_output, values_in, preferred_element_type=jnp.float32)
    center = jnp.sum(probabilities * d_prob, axis=-1, keepdims=True)
    d_score = (probabilities * (d_prob - center)).astype(jnp.bfloat16)
    d_query = jnp.einsum("hqk,khd->qhd", d_score, keys_in, preferred_element_type=jnp.float32) * scaling
    d_key = jnp.einsum("hqk,qhd->khd", d_score, queries, preferred_element_type=jnp.float32) * scaling
    d_value = jnp.einsum(
        "hqk,qhd->khd", probabilities.astype(jnp.bfloat16), d_output, preferred_element_type=jnp.float32
    )
    return (d_query, d_key, d_value)


def by_part(columns, parts):
    rows = columns.shape[0]
    return columns.reshape(rows, -1, parts, DH).swapaxes(1, 2).reshape(rows, -1)


def by_head(columns, parts):
    rows = columns.shape[0]
    return columns.reshape(rows, parts, -1, DH).swapaxes(1, 2).reshape(rows, -1)


def pad_heads(columns, parts):
    rows, width = columns.shape
    each = width // parts
    if each % PAIR == 0:
        return columns
    return jnp.pad(columns.reshape(rows, parts, each), ((0, 0), (0, 0), (0, -each % PAIR))).reshape(rows, -1)


def drop_heads(columns, parts, width):
    rows = columns.shape[0]
    return columns.reshape(rows, parts, -1)[:, :, : width // parts].reshape(rows, width)


def dp_sum(grads):
    return lax.psum_scatter(grads.astype(jnp.bfloat16), "dp", scatter_dimension=0, tiled=True)


def after(value, earlier):
    return lax.optimization_barrier((value, earlier))[0]


def per_device(
    latents,
    conditioning,
    gain_attn,
    w_qkv,
    w_attn_out,
    gain_cross,
    w_cross_q,
    w_cross_kv,
    w_cross_out,
    gain_mlp,
    w_gate,
    w_up,
    w_down,
    cotangent,
):
    low = jnp.bfloat16
    heads_wide = w_cross_q.shape[1]
    hidden_wide = w_gate.shape[1]
    resid_in = latents.astype(jnp.float32)
    normed_one, scaled_one, inverse_one = layer_norm(resid_in, gain_attn)
    rows_one = spread_rows(normed_one.astype(low))
    own_qkv = by_part(w_qkv.astype(low), 3)
    qkv_all = lax.all_gather(own_qkv, "dp", axis=0, tiled=True)
    own_kv = by_part(w_cross_kv.astype(low), 2)
    own_kv = jnp.concatenate([own_kv[:, :heads_wide], own_kv[:, heads_wide:]], axis=0)
    own_mid = jnp.concatenate(
        [w_attn_out.astype(low).T, w_cross_q.astype(low), w_cross_out.astype(low).T, own_kv], axis=1
    )
    mid_all = lax.all_gather(after(own_mid, qkv_all), "dp", axis=0, tiled=True)
    own_mlp = jnp.concatenate([w_gate.astype(low), w_up.astype(low)], axis=1)
    mlp_all = lax.all_gather(after(own_mlp, mid_all), "dp", axis=0, tiled=True)
    down_all = lax.all_gather(after(w_down.astype(low).T, mlp_all), "dp", axis=0, tiled=True)
    attn_out_t, cross_q, cross_out_t = (mid_all[:, part * heads_wide : (part + 1) * heads_wide] for part in range(3))
    model = mid_all.shape[0]
    cross_kv = (
        mid_all[:, 3 * heads_wide :]
        .reshape(lax.axis_size("dp"), 2, -1, heads_wide)
        .transpose(0, 2, 1, 3)
        .reshape(model // 2, 2 * heads_wide)
    )

    tables = turn_tables(group_positions(latents.shape[0]))
    packed = dot_plain(rows_one, qkv_all)
    attended, rotated, logs = attend(pad_heads(packed, 3), tables)
    attended = attended[:, :heads_wide]
    resid_one = resid_in + sum_rows(dot_cols(attended, attn_out_t))
    normed_two, scaled_two, inverse_two = layer_norm(resid_one, gain_cross)
    rows_two = spread_rows(normed_two.astype(low))
    head_shape = (-1, heads_wide // DH, DH)
    cross_query = dot_plain(rows_two, cross_q).astype(low).reshape(head_shape)
    context = conditioning.reshape(CTX, conditioning.shape[2])
    cross_pack = dot_plain(context, cross_kv).astype(low)
    cross_key = cross_pack[:, :heads_wide].reshape(head_shape)
    cross_value = cross_pack[:, heads_wide:].reshape(head_shape)
    crossed, cross_logs = cross_forward(cross_query, cross_key, cross_value)
    crossed = crossed.reshape(-1, heads_wide).astype(low)
    resid_two = resid_one + sum_rows(dot_cols(crossed, cross_out_t))
    normed_three, scaled_three, inverse_three = layer_norm(resid_two, gain_mlp)
    rows_three = spread_rows(normed_three.astype(low))
    mlp_seed = spread_rows(cotangent)
    both = dot_plain(rows_three, mlp_all)
    gate_pre, up_pre = both[:, :hidden_wide], both[:, hidden_wide:]
    sigma_gate = jax.nn.sigmoid(gate_pre)
    swish = gate_pre * sigma_gate
    hidden = (swish * up_pre).astype(low)
    sum_down = dp_sum(dot_rows(mlp_seed, hidden))
    d_hidden = dot_plain(mlp_seed, down_all)
    d_gate = (d_hidden * up_pre * sigma_gate * (1.0 + gate_pre * (1.0 - sigma_gate))).astype(low)
    d_up = (d_hidden * swish).astype(low)
    d_both = jnp.concatenate([d_gate, d_up], axis=1)
    sum_mlp = dp_sum(after(dot_rows(rows_three, d_both), sum_down))
    d_normed = sum_rows(dot_cols(d_both, mlp_all))
    d_part, gain_grad_three = norm_backward(d_normed, scaled_three, inverse_three, gain_mlp)
    d_resid = cotangent.astype(jnp.float32) + d_part
    block_out = resid_two + sum_rows(dot_cols(hidden, down_all))
    cross_seed = spread_rows(d_resid.astype(low))
    grad_cross_out = dot_rows(cross_seed, crossed)
    d_crossed = dot_plain(cross_seed, cross_out_t).astype(low).reshape(head_shape)
    d_query, d_key, d_value = cross_backward(cross_query, cross_key, cross_value, d_crossed, cross_logs)
    d_query = d_query.reshape(-1, heads_wide).astype(low)
    d_keyval = jnp.concatenate([d_key.reshape(CTX, -1), d_value.reshape(CTX, -1)], axis=1).astype(low)
    grad_cross_q = dot_rows(rows_two, d_query)
    grad_cross_kv = dot_rows(context, d_keyval)
    context_part = dot_cols(d_keyval, cross_kv)
    d_normed = sum_rows(dot_cols(d_query, cross_q))
    d_part, gain_grad_two = norm_backward(d_normed, scaled_two, inverse_two, gain_cross)
    d_resid = d_resid + d_part
    self_seed = spread_rows(d_resid.astype(low))
    grad_attn_out = dot_rows(self_seed, attended)
    grad_kv = (
        grad_cross_kv.astype(low)
        .reshape(lax.axis_size("dp"), -1, 2, heads_wide)
        .transpose(0, 2, 1, 3)
        .reshape(model, heads_wide)
    )
    grad_mid = jnp.concatenate([grad_attn_out.astype(low), grad_cross_q.astype(low), grad_cross_out.astype(low), grad_kv], axis=1)
    sum_mid = dp_sum(after(grad_mid, sum_mlp))
    d_attended = dot_plain(self_seed, attn_out_t).astype(low)
    d_packed = drop_heads(attend_back(rotated, pad_heads(d_attended, 1), logs, tables), 3, packed.shape[1])
    sum_qkv = dp_sum(after(dot_rows(rows_one, d_packed), sum_mid))
    d_normed = sum_rows(dot_cols(d_packed, qkv_all))
    d_part, gain_grad_one = norm_backward(d_normed, scaled_one, inverse_one, gain_attn)
    grad_latents = d_resid + d_part
    grad_context = (
        lax.psum(context_part.astype(low), "tensor").astype(jnp.float32).reshape(conditioning.shape)
    )
    gains = lax.psum(jnp.stack([gain_grad_one, gain_grad_two, gain_grad_three]), ("dp", "tensor"))
    sums = [sum_mid[:, part * heads_wide : (part + 1) * heads_wide].astype(jnp.float32) for part in range(4)]
    half = sums[3].shape[0] // 2
    sum_kv = jnp.concatenate([sums[3][:half], sums[3][half:]], axis=1)
    return (
        block_out,
        grad_latents,
        grad_context,
        gains[0],
        by_head(sum_qkv, 3).astype(jnp.float32),
        sums[0].T,
        gains[1],
        sums[1],
        by_head(sum_kv, 2),
        sums[2].T,
        gains[2],
        sum_mlp[:, :hidden_wide].astype(jnp.float32),
        sum_mlp[:, hidden_wide:].astype(jnp.float32),
        sum_down.astype(jnp.float32).T,
    )


def solution(mesh):
    in_specs = (
        P(("dp", "tensor"), None),
        P("dp", None, None),
        P(),
        P("dp", "tensor"),
        P("tensor", "dp"),
        P(),
        P("dp", "tensor"),
        P("dp", "tensor"),
        P("tensor", "dp"),
        P(),
        P("dp", "tensor"),
        P("dp", "tensor"),
        P("tensor", "dp"),
        P(("dp", "tensor"), None),
    )
    out_specs = (
        P(("dp", "tensor"), None),
        P(("dp", "tensor"), None),
        P("dp", None, None),
        P(),
        P("dp", "tensor"),
        P("tensor", "dp"),
        P(),
        P("dp", "tensor"),
        P("dp", "tensor"),
        P("tensor", "dp"),
        P(),
        P("dp", "tensor"),
        P("dp", "tensor"),
        P("tensor", "dp"),
    )
    return jax.shard_map(
        per_device, mesh=mesh, in_specs=in_specs, out_specs=out_specs, check_vma=False
    )
```

```python
import math
from functools import reduce

import jax
import jax.numpy as jnp
from jax import lax
from jax.experimental import pallas as pl
from jax.experimental.pallas import tpu as pltpu
from jax.sharding import PartitionSpec as P

DH = 64
CTX = 130
LENGTH = 1024
PAIR = 2 * DH
ROWS = 256
VMEM_BYTES = 58 * 2**20

norm_eps = 1e-05
rope_base = 10000.0


def head_turn(values, cosine, minus_sine, plus_sine):
    quarter = DH // 4
    ahead = pltpu.roll(values, PAIR - quarter, 1)
    behind = pltpu.roll(values, quarter, 1)
    return values * cosine + ahead * minus_sine + behind * plus_sine


def half_mask(shape, axis, which):
    place = lax.broadcasted_iota(jnp.int32, shape, axis)
    return (place >= DH) if which else (place < DH)


def attend_kernel(q_ref, k_ref, v_ref, cos_ref, msin_ref, psin_ref, out_ref, rot_ref, log_ref, kt_ref, vm_ref):
    pairs = pl.num_programs(0)
    pair = pl.program_id(0)
    turn = (cos_ref[...], msin_ref[...], psin_ref[...])
    query = head_turn(q_ref[...], *turn).astype(jnp.bfloat16)
    key = head_turn(k_ref[...], *turn).astype(jnp.bfloat16)
    value = v_ref[...].astype(jnp.bfloat16)
    for part, array in enumerate((query, key, value)):
        start = pl.multiple_of((part * pairs + pair) * PAIR, PAIR)
        rot_ref[:, pl.ds(start, PAIR)] = array
    key_t = key.astype(jnp.float32).T
    for which in range(2):
        kt_ref[which] = jnp.where(half_mask(key_t.shape, 0, which), key_t, 0.0).astype(jnp.bfloat16)
        vm_ref[which] = jnp.where(half_mask(value.shape, 1, which), value.astype(jnp.float32), 0.0).astype(jnp.bfloat16)
    q_start = pl.multiple_of(pair * PAIR, PAIR)

    def one_block(step, carry):
        rows = pl.ds(pl.multiple_of(step * ROWS, ROWS), ROWS)
        block = rot_ref[rows, pl.ds(q_start, PAIR)] * jnp.bfloat16(DH**-0.5)
        outs, logs = [], []
        for which in range(2):
            scores = jnp.dot(block, kt_ref[which], preferred_element_type=jnp.float32)
            peak = jnp.max(scores, axis=1, keepdims=True)
            shifted = jnp.exp(scores - peak)
            total = jnp.sum(shifted, axis=1, keepdims=True)
            product = jnp.dot(shifted.astype(jnp.bfloat16), vm_ref[which], preferred_element_type=jnp.float32)
            outs.append(product * (1.0 / total))
            logs.append(peak + jnp.log(total))
        out_ref[rows, :] = (outs[0] + outs[1]).astype(jnp.bfloat16)
        low = half_mask((ROWS, PAIR), 1, 0)
        log_ref[rows, :] = jnp.where(low, logs[0], logs[1])
        return carry

    lax.fori_loop(0, LENGTH // ROWS, one_block, 0)


def attend_back_kernel(
    q_ref, k_ref, v_ref, grad_ref, log_ref, cos_ref, msin_ref, psin_ref, out_ref,
    kt_ref, vt_ref, km_ref, qt_ref, gt_ref, dq_ref, dk_ref, dv_ref,
):
    pairs = pl.num_programs(0)
    pair = pl.program_id(0)
    key_t = k_ref[...].astype(jnp.float32).T
    value_t = v_ref[...].astype(jnp.float32).T
    for which in range(2):
        keep = half_mask(key_t.shape, 0, which)
        kt_ref[which] = jnp.where(keep, key_t, 0.0).astype(jnp.bfloat16)
        vt_ref[which] = jnp.where(keep, value_t, 0.0).astype(jnp.bfloat16)
        key = k_ref[...].astype(jnp.float32)
        km_ref[which] = jnp.where(half_mask(key.shape, 1, which), key, 0.0).astype(jnp.bfloat16)
    qt_ref[...] = (q_ref[...].astype(jnp.float32) * DH**-0.5).T.astype(jnp.bfloat16)
    gt_ref[...] = grad_ref[...].astype(jnp.float32).T.astype(jnp.bfloat16)
    dk_ref[...] = jnp.zeros_like(dk_ref)
    dv_ref[...] = jnp.zeros_like(dv_ref)

    def one_block(step, carry):
        rows = pl.ds(pl.multiple_of(step * ROWS, ROWS), ROWS)
        block = q_ref[rows, :] * jnp.bfloat16(DH**-0.5)
        grads = grad_ref[rows, :]
        d_query = jnp.zeros((ROWS, PAIR), jnp.float32)
        for which in range(2):
            half = slice(which * DH, (which + 1) * DH)
            scores = jnp.dot(block, kt_ref[which], preferred_element_type=jnp.float32)
            probs = jnp.exp(scores - log_ref[rows, which * DH : which * DH + 1])
            d_prob = jnp.dot(grads, vt_ref[which], preferred_element_type=jnp.float32)
            center = jnp.sum(probs * d_prob, axis=1, keepdims=True)
            d_score = (probs * (d_prob - center)).astype(jnp.bfloat16)
            d_query += jnp.dot(d_score, km_ref[which], preferred_element_type=jnp.float32)
            dk_ref[half, :] += jnp.dot(qt_ref[half, rows], d_score, preferred_element_type=jnp.float32)
            dv_ref[half, :] += jnp.dot(
                gt_ref[half, rows], probs.astype(jnp.bfloat16), preferred_element_type=jnp.float32
            )
        dq_ref[rows, :] = d_query * DH**-0.5
        return carry

    lax.fori_loop(0, LENGTH // ROWS, one_block, 0)
    turn = (cos_ref[...], -msin_ref[...], -psin_ref[...])
    results = (head_turn(dq_ref[...], *turn), head_turn(dk_ref[...].T, *turn), dv_ref[...].T)
    for part, array in enumerate(results):
        start = pl.multiple_of((part * pairs + pair) * PAIR, PAIR)
        out_ref[:, pl.ds(start, PAIR)] = array.astype(jnp.bfloat16)


def column_block(offset):
    return pl.BlockSpec((LENGTH, PAIR), lambda pair: (0, pair + offset))


def whole_block(columns):
    return pl.BlockSpec((LENGTH, columns), lambda pair: (0, 0))


def attend(packed, tables):
    columns = packed.shape[1]
    pairs = columns // (3 * PAIR)
    return pl.pallas_call(
        attend_kernel,
        grid=(pairs,),
        in_specs=[column_block(part * pairs) for part in range(3)] + [whole_block(PAIR)] * 3,
        out_specs=[column_block(0), whole_block(columns), column_block(0)],
        out_shape=[
            jax.ShapeDtypeStruct((LENGTH, pairs * PAIR), jnp.bfloat16),
            jax.ShapeDtypeStruct((LENGTH, columns), jnp.bfloat16),
            jax.ShapeDtypeStruct((LENGTH, pairs * PAIR), jnp.float32),
        ],
        scratch_shapes=[pltpu.VMEM((2, PAIR, LENGTH), jnp.bfloat16), pltpu.VMEM((2, LENGTH, PAIR), jnp.bfloat16)],
        compiler_params=pltpu.CompilerParams(vmem_limit_bytes=VMEM_BYTES),
        cost_estimate=pl.CostEstimate(flops=pairs * 2**32, bytes_accessed=2**24, transcendentals=pairs * 2**21),
    )(packed, packed, packed, *tables)


def attend_back(rotated, d_attended, logs, tables):
    columns = rotated.shape[1]
    pairs = columns // (3 * PAIR)
    tall = pltpu.VMEM((PAIR, LENGTH), jnp.bfloat16)
    return pl.pallas_call(
        attend_back_kernel,
        grid=(pairs,),
        in_specs=[column_block(part * pairs) for part in range(3)]
        + [column_block(0), column_block(0)]
        + [whole_block(PAIR)] * 3,
        out_specs=whole_block(columns),
        out_shape=jax.ShapeDtypeStruct((LENGTH, columns), jnp.bfloat16),
        scratch_shapes=[
            pltpu.VMEM((2, PAIR, LENGTH), jnp.bfloat16),
            pltpu.VMEM((2, PAIR, LENGTH), jnp.bfloat16),
            pltpu.VMEM((2, LENGTH, PAIR), jnp.bfloat16),
            tall,
            tall,
            pltpu.VMEM((LENGTH, PAIR), jnp.float32),
            pltpu.VMEM((PAIR, LENGTH), jnp.float32),
            pltpu.VMEM((PAIR, LENGTH), jnp.float32),
        ],
        compiler_params=pltpu.CompilerParams(vmem_limit_bytes=VMEM_BYTES),
        cost_estimate=pl.CostEstimate(flops=pairs * 2**33, bytes_accessed=2**24, transcendentals=pairs * 2**21),
    )(rotated, rotated, rotated, d_attended, logs, *tables)


def turn_tables(positions):
    quarter = DH // 4
    frequency = jnp.exp(-jnp.log(rope_base) * jnp.arange(quarter).astype(jnp.float32) / quarter)
    angles = positions.astype(jnp.float32)[:, None] * frequency[None, :]
    cosine, sine = jnp.cos(angles), jnp.sin(angles)
    zeros, ones = jnp.zeros_like(sine), jnp.ones_like(sine)
    rows = (
        jnp.concatenate([cosine, cosine, ones, ones], axis=1),
        jnp.concatenate([-sine, zeros, zeros, zeros], axis=1),
        jnp.concatenate([zeros, sine, zeros, zeros], axis=1),
    )
    return tuple(jnp.concatenate([row, row], axis=1) for row in rows)


def dot_plain(left_op, right_op):
    return jnp.dot(left_op, right_op, preferred_element_type=jnp.float32)


def dot_rows(left_op, right_op):
    return lax.dot_general(
        left_op, right_op, (((0,), (0,)), ((), ())), preferred_element_type=jnp.float32
    )


def dot_cols(left_op, right_op):
    return lax.dot_general(
        left_op, right_op, (((1,), (1,)), ((), ())), preferred_element_type=jnp.float32
    )


def layer_norm(values, gain_vec):
    center = values - jnp.mean(values, axis=-1, keepdims=True)
    spread = jnp.mean(center * center, axis=-1, keepdims=True)
    inverse = lax.rsqrt(spread + norm_eps)
    scaled = center * inverse
    return (scaled * gain_vec, scaled, inverse)


def norm_backward(upstream, scaled, inverse, gain_vec):
    weighted = upstream * gain_vec
    inner = jnp.mean(weighted, axis=-1, keepdims=True) + scaled * jnp.mean(
        weighted * scaled, axis=-1, keepdims=True
    )
    return (inverse * (weighted - inner), jnp.sum(upstream * scaled, axis=0))


def swap(values, bit):
    return lax.ppermute(values, "tensor", [(member, member ^ bit) for member in range(4)])


def spread_rows(values):
    if lax.axis_size("tensor") != 4:
        return lax.all_gather(values, "tensor", axis=0, tiled=True)
    half = values.shape[0] // 2
    near, far = swap(values, 1), swap(values, 2)
    return jnp.concatenate([values, near, far, swap(near[:half], 2), swap(far[half:], 1)], axis=0)


def sum_rows(partial):
    if lax.axis_size("tensor") != 4:
        return lax.psum_scatter(
            partial.astype(jnp.bfloat16), "tensor", scatter_dimension=0, tiled=True
        ).astype(jnp.float32)
    size = partial.shape[0] // 4
    half = size // 2
    own, near, far, last = (partial[part * size : (part + 1) * size] for part in range(4))
    first = swap(last[:half].astype(jnp.bfloat16), 1)
    second = swap(last[half:].astype(jnp.bfloat16), 2)
    far = jnp.concatenate([far[:half] + first.astype(jnp.float32), far[half:]], axis=0)
    near = jnp.concatenate([near[:half], near[half:] + second.astype(jnp.float32)], axis=0)
    return (
        own
        + swap(near.astype(jnp.bfloat16), 1).astype(jnp.float32)
        + swap(far.astype(jnp.bfloat16), 2).astype(jnp.float32)
    )


def group_positions(rows):
    group = lax.axis_size("tensor")
    blocks = jnp.arange(group)
    if group == 4:
        blocks = blocks ^ lax.axis_index("tensor")
    return (blocks[:, None] * rows + jnp.arange(rows)[None, :]).reshape(-1)


def cross_forward(queries, keys_in, values_in):
    scores = jnp.einsum("qhd,khd->hqk", queries, keys_in, preferred_element_type=jnp.float32) * DH ** (-0.5)
    peak_score = jnp.max(scores, axis=-1, keepdims=True)
    shifted = jnp.exp(scores - peak_score)
    totals = jnp.sum(shifted, axis=-1, keepdims=True)
    probabilities = (shifted / totals).astype(jnp.bfloat16)
    output = jnp.einsum("hqk,khd->qhd", probabilities, values_in, preferred_element_type=jnp.float32)
    return (output, peak_score + jnp.log(totals))


def cross_backward(queries, keys_in, values_in, d_output, log_totals):
    scaling = DH ** (-0.5)
    scores = jnp.einsum("qhd,khd->hqk", queries, keys_in, preferred_element_type=jnp.float32) * scaling
    probabilities = jnp.exp(scores - log_totals)
    d_prob = jnp.einsum("qhd,khd->hqk", d_output, values_in, preferred_element_type=jnp.float32)
    center = jnp.sum(probabilities * d_prob, axis=-1, keepdims=True)
    d_score = (probabilities * (d_prob - center)).astype(jnp.bfloat16)
    d_query = jnp.einsum("hqk,khd->qhd", d_score, keys_in, preferred_element_type=jnp.float32) * scaling
    d_key = jnp.einsum("hqk,qhd->khd", d_score, queries, preferred_element_type=jnp.float32) * scaling
    d_value = jnp.einsum(
        "hqk,qhd->khd", probabilities.astype(jnp.bfloat16), d_output, preferred_element_type=jnp.float32
    )
    return (d_query, d_key, d_value)


def by_part(columns, parts):
    rows = columns.shape[0]
    return columns.reshape(rows, -1, parts, DH).swapaxes(1, 2).reshape(rows, -1)


def by_head(columns, parts):
    rows = columns.shape[0]
    return columns.reshape(rows, parts, -1, DH).swapaxes(1, 2).reshape(rows, -1)


def pad_heads(columns, parts):
    rows, width = columns.shape
    each = width // parts
    if each % PAIR == 0:
        return columns
    return jnp.pad(columns.reshape(rows, parts, each), ((0, 0), (0, 0), (0, -each % PAIR))).reshape(rows, -1)


def drop_heads(columns, parts, width):
    rows = columns.shape[0]
    return columns.reshape(rows, parts, -1)[:, :, : width // parts].reshape(rows, width)


def dp_sum(grads):
    return lax.psum_scatter(grads.astype(jnp.bfloat16), "dp", scatter_dimension=0, tiled=True)


def after(value, earlier):
    return lax.optimization_barrier((value, earlier))[0]


MESH = pl.DeviceIdType.MESH
BLOCK = LENGTH // 4
HALF = BLOCK // 2
FULL = 256


class Links:
    def __init__(self, send, recv, local):
        self.send, self.recv, self.local = send, recv, local
        self.used = self.used_local = 0
        self.pending, self.pending_local = [], []
        self.dp, self.tensor = lax.axis_index("dp"), lax.axis_index("tensor")

    def remote(self, src, dst, dp_bit, tensor_bit):
        at = self.used
        self.used += 1
        return pltpu.make_async_remote_copy(
            src_ref=src,
            dst_ref=dst,
            send_sem=self.send.at[at],
            recv_sem=self.recv.at[at],
            device_id=(self.dp ^ dp_bit, self.tensor ^ tensor_bit),
            device_id_type=MESH,
        )

    def go(self, src, dst, dp_bit, tensor_bit):
        copy = self.remote(src, dst, dp_bit, tensor_bit)
        copy.start()
        self.pending.append(copy)
        return copy

    def store(self, src, dst):
        copy = pltpu.make_async_copy(src, dst, self.local.at[self.used_local])
        self.used_local += 1
        copy.start()
        self.pending_local.append(copy)
        return copy

    def settle(self, copy):
        copy.wait()
        self.pending_local = [other for other in self.pending_local if other is not copy]

    def greet(self, partners):
        barrier = pltpu.get_barrier_semaphore()
        for dp_bit, tensor_bit in partners:
            pl.semaphore_signal(
                barrier, inc=1, device_id=(self.dp ^ dp_bit, self.tensor ^ tensor_bit), device_id_type=MESH
            )
        pl.semaphore_wait(barrier, len(partners))

    def finish(self):
        for copy in self.pending:
            copy.wait_send()
        for copy in self.pending_local:
            copy.wait()


class Spread:
    def __init__(self, links, rows):
        self.links, self.rows = links, rows
        self.near = links.go(rows.at[0], rows.at[1], 0, 1)
        self.far = links.go(rows.at[0], rows.at[2], 0, 2)
        self.stage = 0

    def wait(self, block):
        rows, links = self.rows, self.links
        if block >= 1 and self.stage == 0:
            self.near.wait_recv()
            low = pl.ds(0, HALF)
            self.last_low = links.go(rows.at[1, low], rows.at[3, low], 0, 2)
            self.stage = 1
        if block >= 2 and self.stage == 1:
            self.far.wait_recv()
            high = pl.ds(HALF, HALF)
            self.last_high = links.go(rows.at[2, high], rows.at[3, high], 0, 1)
            self.stage = 2
        if block >= 3 and self.stage == 2:
            self.last_low.wait_recv()
            self.last_high.wait_recv()
            self.stage = 3


class Gather:
    def __init__(self, links, shard, whole):
        self.links, self.whole = links, whole
        self.size = shard.shape[0]
        self.place = links.dp // 2
        self.middle = (self.place == 1) | (self.place == 2)
        own = self.rows(0)
        self.own = links.store(shard, own)
        self.core = [links.go(shard, own, 1, 0)]
        self.beside = links.go(shard, own, 2, 0)
        self.skip = links.go(shard, own, 4, 0)
        self.third_at = links.used
        self.third = links.remote(shard, own, 6, 0)

        @pl.when(self.middle)
        def _():
            self.third.start()

    def rows(self, step):
        start = pl.multiple_of((self.links.dp ^ (2 * step)) * self.size, self.size)
        return self.whole.at[pl.ds(start, self.size)]

    def forward(self):
        links = self.links
        block = self.rows(2)
        self.skip.wait_recv()
        self.onward = pltpu.make_async_remote_copy(
            src_ref=block,
            dst_ref=block,
            send_sem=links.send.at[links.used],
            recv_sem=links.recv.at[self.third_at],
            device_id=(links.dp ^ 2, links.tensor),
            device_id_type=MESH,
        )
        links.used += 1

        @pl.when(self.middle)
        def _():
            self.onward.start()

        self.core.append(links.go(block, block, 1, 0))

    def arrive(self):
        links = self.links
        self.beside.wait_recv()
        block = self.rows(1)
        self.core.append(links.go(block, block, 1, 0))
        self.third.wait_recv()
        block = self.rows(3)
        self.core.append(links.go(block, block, 1, 0))
        links.settle(self.own)
        for copy in self.core:
            copy.wait_recv()

    def finish(self):
        @pl.when(self.middle)
        def _():
            self.third.wait_send()
            self.onward.wait_send()


class Sums:
    def __init__(self, links, parts, half_near, half_far, near, far):
        self.links, self.parts = links, parts
        self.half_near, self.half_far, self.near, self.far = half_near, half_far, near, far
        self.low, self.high = pl.ds(0, HALF), pl.ds(HALF, HALF)

    def ready(self, block):
        links, parts, low, high = self.links, self.parts, self.low, self.high
        if block == 3:
            self.first = links.go(parts.at[3, low], self.half_near, 0, 1)
            self.second = links.go(parts.at[3, high], self.half_far, 0, 2)
        if block == 1:
            self.near_low = links.go(parts.at[1, low], self.near.at[low], 0, 1)
        if block == 2:
            self.far_high = links.go(parts.at[2, high], self.far.at[high], 0, 2)

    def add(self):
        links, parts, low, high = self.links, self.parts, self.low, self.high
        self.first.wait_recv()
        parts[2, low] = (parts[2, low].astype(jnp.float32) + self.half_near[...].astype(jnp.float32)).astype(
            jnp.bfloat16
        )
        self.far_low = links.go(parts.at[2, low], self.far.at[low], 0, 2)
        self.second.wait_recv()
        parts[1, high] = (parts[1, high].astype(jnp.float32) + self.half_far[...].astype(jnp.float32)).astype(
            jnp.bfloat16
        )
        self.near_high = links.go(parts.at[1, high], self.near.at[high], 0, 1)

    def arrive(self):
        for copy in (self.near_low, self.far_high, self.far_low, self.near_high):
            copy.wait_recv()

    def sent(self):
        links = self.links
        mine = (self.first, self.second, self.near_low, self.far_high, self.far_low, self.near_high)
        for copy in mine:
            copy.wait_send()
        links.pending = [copy for copy in links.pending if all(copy is not other for other in mine)]

    def total(self, rows):
        return self.near[rows].astype(jnp.float32) + self.far[rows].astype(jnp.float32)
def columns(total, width, body):
    def step(index, carry):
        body(pl.ds(pl.multiple_of(index * width, width), width))
        return carry

    lax.fori_loop(0, total // width, step, 0)


def split_heads(array, at, axis):
    wide = array.astype(jnp.float32)
    for which in range(2):
        at[which] = jnp.where(half_mask(array.shape, axis, which), wide, 0.0).astype(jnp.bfloat16)


def attend_rows(block, keys_t, values, limit):
    outs, logs = [], []
    for which in range(2):
        scores = jnp.dot(block, keys_t[which], preferred_element_type=jnp.float32)
        if limit is not None:
            scores = jnp.where(lax.broadcasted_iota(jnp.int32, scores.shape, 1) < limit, scores, -jnp.inf)
        peak = jnp.max(scores, axis=1, keepdims=True)
        shifted = jnp.exp(scores - peak)
        total = jnp.sum(shifted, axis=1, keepdims=True)
        product = jnp.dot(shifted.astype(jnp.bfloat16), values[which], preferred_element_type=jnp.float32)
        outs.append(product * (1.0 / total))
        logs.append(peak + jnp.log(total))
    low = half_mask(block.shape, 1, 0)
    return outs[0] + outs[1], jnp.where(low, logs[0], logs[1])


def block_rows(block):
    return pl.ds(block * BLOCK, BLOCK)


def two_heads(weights, part, parts, pair):
    starts = [((2 * pair + which) * parts + part) * DH for which in range(2)]
    return jnp.concatenate([weights[:, start : start + DH] for start in starts], axis=1).astype(jnp.bfloat16)


def fill_tables(cosine, minus_sine, plus_sine, member):
    quarter = DH // 4
    shape = (BLOCK, PAIR)
    lane = lax.broadcasted_iota(jnp.int32, shape, 1) % DH
    frequency = jnp.exp((lane % quarter).astype(jnp.float32) * (-math.log(rope_base) / quarter))
    for block in range(4):
        place = (member ^ block) * BLOCK + lax.broadcasted_iota(jnp.int32, shape, 0)
        angle = place.astype(jnp.float32) * frequency
        turned, sine = jnp.cos(angle), jnp.sin(angle)
        rows = block_rows(block)
        cosine[rows] = jnp.where(lane < 2 * quarter, turned, 1.0)
        minus_sine[rows] = jnp.where(lane < quarter, -sine, 0.0)
        plus_sine[rows] = jnp.where((lane >= quarter) & (lane < 2 * quarter), sine, 0.0)


def forward_kernel(
    latents, gains, conditioning, f32_qkv,
    f32_attn_out, f32_cross_q, f32_cross_kv, f32_cross_out, f32_gate, f32_up, f32_down, cotangent,
    rows_one_out, rows_two_out, rows_three_out, seeds_out, qkv_out, attn_out_out, cross_out, keyval_w_out, mlp_out,
    down_out, rotated_out, attended_out, logs_out,
    query_out, keyval_out, crossed_out, cross_logs_out, resid_one_out, resid_two_out, tables_out,
    rows_one, rows_two, rows_three, w_qkv, w_attn_out, w_cross, w_keyval, rotated, attended, logs, query, keyval,
    crossed, cross_logs, keys_t, values, cross_keys_t, cross_values, parts, got_one, got_two, resid_one, resid_two,
    packed, tables, context, raw_attn_out, raw_cross_q, raw_cross_kv, raw_cross_out, raw_gate, raw_up, raw_down,
    own_qkv, own_attn_out, own_cross, own_keyval, own_mlp, own_down, send, recv, local,
):
    low = jnp.bfloat16
    pairs = attended.shape[1] // PAIR
    width = pairs * PAIR
    links = Links(send, recv, local)
    loads = [
        links.store(source, target)
        for source, target in (
            (f32_attn_out, raw_attn_out), (f32_cross_q, raw_cross_q), (f32_cross_kv, raw_cross_kv),
            (f32_cross_out, raw_cross_out), (f32_gate, raw_gate), (f32_up, raw_up), (f32_down, raw_down),
        )
    ]
    seed_own = links.store(cotangent, seeds_out.at[0])
    for part in range(3):
        for pair in range(pairs):
            at = part * width + pair * PAIR
            own_qkv[:, at : at + PAIR] = two_heads(f32_qkv, part, 3, pair)
    links.greet([(1, 0), (2, 0), (4, 0), (6, 0), (0, 1), (0, 2)])
    gather_qkv = Gather(links, own_qkv, w_qkv)
    resid = latents[...].astype(jnp.float32)
    rows_one[0] = layer_norm(resid, gains[0:1])[0].astype(low)
    spread_one = Spread(links, rows_one)
    cosine, minus_sine, plus_sine = (tables.at[part] for part in range(3))
    fill_tables(cosine, minus_sine, plus_sine, links.tensor)
    links.store(tables, tables_out)
    for load in loads:
        links.settle(load)
    own_attn_out[...] = raw_attn_out[...].T.astype(low)
    own_cross[:, :width] = raw_cross_q[...].astype(low)
    own_cross[:, width:] = raw_cross_out[...].T.astype(low)
    for part in range(2):
        for pair in range(pairs):
            at = part * width + pair * PAIR
            own_keyval[:, at : at + PAIR] = two_heads(raw_cross_kv, part, 2, pair)
    hidden = raw_gate.shape[1]
    own_mlp[:, :hidden] = raw_gate[...].astype(low)
    own_mlp[:, hidden:] = raw_up[...].astype(low)
    own_down[...] = raw_down[...].T.astype(low)
    context[...] = jnp.zeros_like(context)
    context[:CTX] = conditioning[0]
    spread_one.wait(1)
    gather_qkv.forward()
    gather_attn_out = Gather(links, own_attn_out, w_attn_out)
    gather_cross = Gather(links, own_cross, w_cross)
    gather_keyval = Gather(links, own_keyval, w_keyval)
    spread_one.wait(2)
    gather_qkv.arrive()
    links.store(w_qkv, qkv_out)

    for block in range(4):
        spread_one.wait(block)
        rows = block_rows(block)
        turn = (cosine[rows], minus_sine[rows], plus_sine[rows])

        def project(cols):
            packed[:, cols] = dot_plain(rows_one[block], w_qkv[:, cols])

        columns(3 * width, width, project)
        for part in range(3):
            for pair in range(pairs):
                at = slice(part * width + pair * PAIR, part * width + (pair + 1) * PAIR)
                value = packed[:, at]
                rotated[rows, at] = (value if part == 2 else head_turn(value, *turn)).astype(low)
    links.store(rows_one, rows_one_out)
    links.store(rotated, rotated_out)
    for pair in range(pairs):
        key = rotated[:, width + pair * PAIR : width + (pair + 1) * PAIR]
        split_heads(key.astype(jnp.float32).T, keys_t.at[pair], 0)
        split_heads(rotated[:, 2 * width + pair * PAIR : 2 * width + (pair + 1) * PAIR], values.at[pair], 1)

    def out_project(source, block, weight, sums):
        def project(cols):
            parts[block, :, cols] = dot_cols(source[block_rows(block)], weight(cols)).astype(low)

        columns(parts.shape[2], 512, project)
        sums.ready(block)

    sums_one = Sums(links, parts, *got_one)
    for block in (3, 1, 2, 0):
        rows = block_rows(block)

        def one_pair(pair, carry):
            at = pl.ds(pl.multiple_of(pair * PAIR, PAIR), PAIR)
            out, log = attend_rows(rotated[rows, at] * low(DH**-0.5), keys_t.at[pair], values.at[pair], None)
            attended[rows, at] = out.astype(low)
            logs[rows, at] = log
            return carry

        lax.fori_loop(0, pairs, one_pair, 0)
        if block == 3:
            gather_attn_out.forward()
            gather_attn_out.arrive()
            links.store(w_attn_out, attn_out_out)
        out_project(attended, block, lambda cols: w_attn_out[cols, :], sums_one)
        if block == 1:
            gather_cross.forward()
            gather_keyval.forward()
            gather_mlp = Gather(links, own_mlp, mlp_out)
        if block == 2:
            sums_one.add()
    links.store(attended, attended_out)
    links.store(logs, logs_out)
    sums_one.arrive()
    resid_one[...] = resid + parts[0].astype(jnp.float32) + sums_one.total(slice(None))
    links.store(resid_one, resid_one_out)
    rows_two[0] = layer_norm(resid_one[...], gains[1:2])[0].astype(low)
    spread_two = Spread(links, rows_two)
    gather_keyval.arrive()
    links.store(w_keyval, keyval_w_out)
    for part in range(2):
        keyval[part] = dot_plain(context[...], w_keyval[:, part * width : (part + 1) * width]).astype(low)
    for pair in range(pairs):
        at = slice(pair * PAIR, (pair + 1) * PAIR)
        split_heads(keyval[0, :, at].astype(jnp.float32).T, cross_keys_t.at[pair], 0)
        split_heads(keyval[1, :, at], cross_values.at[pair], 1)
    links.store(keyval, keyval_out)
    gather_cross.arrive()
    links.store(w_cross, cross_out)
    sums_one.sent()
    sums_two = Sums(links, parts, *got_two)
    for block in range(4):
        spread_two.wait(block)
        rows = block_rows(block)
        query[rows] = dot_plain(rows_two[block], w_cross[:, :width]).astype(low)
        for pair in range(pairs):
            at = slice(pair * PAIR, (pair + 1) * PAIR)
            out, log = attend_rows(query[rows, at] * low(DH**-0.5), cross_keys_t.at[pair], cross_values.at[pair], CTX)
            crossed[rows, at] = out.astype(low)
            cross_logs[rows, at] = log
        out_project(crossed, block, lambda cols: w_cross[cols, width:], sums_two)
    sums_two.add()
    links.store(rows_two, rows_two_out)
    links.store(query, query_out)
    links.store(crossed, crossed_out)
    links.store(cross_logs, cross_logs_out)
    links.settle(seed_own)
    spread_seed = Spread(links, seeds_out)
    gather_mlp.forward()
    gather_down = Gather(links, own_down, down_out)
    sums_two.arrive()
    resid_two[...] = resid_one[...] + parts[0].astype(jnp.float32) + sums_two.total(slice(None))
    links.store(resid_two, resid_two_out)
    rows_three[0] = layer_norm(resid_two[...], gains[2:3])[0].astype(low)
    spread_three = Spread(links, rows_three)
    spread_seed.wait(2)
    spread_three.wait(2)
    gather_down.forward()
    gather_mlp.arrive()
    spread_seed.wait(3)
    spread_three.wait(3)
    links.store(rows_three, rows_three_out)
    gather_down.arrive()
    links.finish()
    for gather in (gather_qkv, gather_attn_out, gather_cross, gather_keyval, gather_mlp, gather_down):
        gather.finish()


def whole_vmem():
    return pl.BlockSpec(memory_space=pltpu.VMEM)


def anywhere():
    return pl.BlockSpec(memory_space=pl.ANY)


def sum_buffers(model):
    return [
        pltpu.VMEM((HALF, model), jnp.bfloat16),
        pltpu.VMEM((HALF, model), jnp.bfloat16),
        pltpu.VMEM((BLOCK, model), jnp.bfloat16),
        pltpu.VMEM((BLOCK, model), jnp.bfloat16),
    ]


def forward_part(latents, gains, conditioning, weights, cotangent):
    w_qkv, w_attn_out, w_cross_q, w_cross_kv, w_cross_out, w_gate, w_up, w_down = weights
    model = latents.shape[1]
    depth = conditioning.shape[2]
    wide = w_qkv.shape[1]
    width = wide // 3
    hidden = w_gate.shape[1]
    pairs = width // PAIR
    low, high = jnp.bfloat16, jnp.float32
    share = w_qkv.shape[0]
    outs = [
        ((4, BLOCK, model), low),
        ((4, BLOCK, model), low),
        ((4, BLOCK, model), low),
        ((4, BLOCK, model), low),
        ((model, wide), low),
        ((model, width), low),
        ((model, 2 * width), low),
        ((depth, 2 * width), low),
        ((model, 2 * hidden), low),
        ((model, hidden), low),
        ((LENGTH, wide), low),
        ((LENGTH, width), low),
        ((LENGTH, width), high),
        ((LENGTH, width), low),
        ((2, FULL, width), low),
        ((LENGTH, width), low),
        ((LENGTH, width), high),
        ((BLOCK, model), high),
        ((BLOCK, model), high),
        ((3, LENGTH, PAIR), high),
    ]
    work = [
        ((4, BLOCK, model), low),
        ((4, BLOCK, model), low),
        ((4, BLOCK, model), low),
        ((model, wide), low),
        ((model, width), low),
        ((model, 2 * width), low),
        ((depth, 2 * width), low),
        ((LENGTH, wide), low),
        ((LENGTH, width), low),
        ((LENGTH, width), high),
        ((LENGTH, width), low),
        ((2, FULL, width), low),
        ((LENGTH, width), low),
        ((LENGTH, width), high),
        ((pairs, 2, PAIR, LENGTH), low),
        ((pairs, 2, LENGTH, PAIR), low),
        ((pairs, 2, PAIR, FULL), low),
        ((pairs, 2, FULL, PAIR), low),
        ((4, BLOCK, model), low),
    ]
    more = [
        ((BLOCK, model), high),
        ((BLOCK, model), high),
        ((BLOCK, wide), high),
        ((3, LENGTH, PAIR), high),
        ((FULL, depth), low),
        (w_attn_out.shape, high),
        (w_cross_q.shape, high),
        (w_cross_kv.shape, high),
        (w_cross_out.shape, high),
        (w_gate.shape, high),
        (w_up.shape, high),
        (w_down.shape, high),
        ((share, wide), low),
        ((share, width), low),
        ((share, 2 * width), low),
        (w_cross_kv.shape, low),
        ((share, 2 * hidden), low),
        ((share, hidden), low),
    ]
    scratch = [pltpu.VMEM(*buffer) for buffer in work] + [sum_buffers(model), sum_buffers(model)]
    scratch += [pltpu.VMEM(*buffer) for buffer in more]
    scratch += [pltpu.SemaphoreType.DMA((96,)), pltpu.SemaphoreType.DMA((96,)), pltpu.SemaphoreType.DMA((40,))]
    return pl.pallas_call(
        forward_kernel,
        out_shape=[jax.ShapeDtypeStruct(*out) for out in outs],
        in_specs=[whole_vmem()] * 4 + [anywhere()] * 8,
        out_specs=[anywhere()] * len(outs),
        scratch_shapes=scratch,
        compiler_params=pltpu.CompilerParams(collective_id=1, has_side_effects=True, vmem_limit_bytes=VMEM_BYTES),
        cost_estimate=pl.CostEstimate(flops=2**37, bytes_accessed=2**26, transcendentals=2**23),
    )(latents, gains, conditioning, *weights, cotangent)


def per_device(
    latents,
    conditioning,
    gain_attn,
    w_qkv,
    w_attn_out,
    gain_cross,
    w_cross_q,
    w_cross_kv,
    w_cross_out,
    gain_mlp,
    w_gate,
    w_up,
    w_down,
    cotangent,
):
    low = jnp.bfloat16
    heads_wide = w_cross_q.shape[1]
    hidden_wide = w_gate.shape[1]
    members = lax.axis_size("dp")
    context = conditioning[0]
    (
        rows_one, rows_two, rows_three, mlp_seed, qkv_all, attn_out_t, cross_all, cross_kv, mlp_all, down_all,
        rotated, attended, logs, cross_query, keyval, crossed, cross_logs, resid_one, resid_two, tables,
    ) = forward_part(
        latents,
        jnp.stack([gain_attn, gain_cross, gain_mlp]),
        conditioning,
        (w_qkv, w_attn_out, w_cross_q, w_cross_kv, w_cross_out, w_gate, w_up, w_down),
        cotangent,
    )
    rows_one, rows_two, rows_three, mlp_seed = (
        array.reshape(LENGTH, -1) for array in (rows_one, rows_two, rows_three, mlp_seed)
    )
    cross_q, cross_out_t = cross_all[:, :heads_wide], cross_all[:, heads_wide:]
    head_shape = (-1, heads_wide // DH, DH)
    both = dot_plain(rows_three, mlp_all)
    gate_pre, up_pre = both[:, :hidden_wide], both[:, hidden_wide:]
    sigma_gate = jax.nn.sigmoid(gate_pre)
    swish = gate_pre * sigma_gate
    hidden = (swish * up_pre).astype(low)
    sum_down = dp_sum(dot_rows(mlp_seed, hidden))
    d_hidden = dot_plain(mlp_seed, down_all)
    d_gate = (d_hidden * up_pre * sigma_gate * (1.0 + gate_pre * (1.0 - sigma_gate))).astype(low)
    d_up = (d_hidden * swish).astype(low)
    d_both = jnp.concatenate([d_gate, d_up], axis=1)
    sum_mlp = dp_sum(after(dot_rows(rows_three, d_both), sum_down))
    d_normed = sum_rows(dot_cols(d_both, mlp_all))
    _, scaled_three, inverse_three = layer_norm(resid_two, gain_mlp)
    d_part, gain_grad_three = norm_backward(d_normed, scaled_three, inverse_three, gain_mlp)
    d_resid = cotangent.astype(jnp.float32) + d_part
    block_out = resid_two + sum_rows(dot_cols(hidden, down_all))
    cross_seed = spread_rows(d_resid.astype(low))
    grad_cross_out = dot_rows(cross_seed, crossed)
    d_crossed = dot_plain(cross_seed, cross_out_t).astype(low).reshape(head_shape)
    cross_log_heads = cross_logs.reshape(LENGTH, -1, DH)[:, :, 0].T[:, :, None]
    d_query, d_key, d_value = cross_backward(
        cross_query.reshape(head_shape),
        keyval[0, :CTX].reshape(head_shape),
        keyval[1, :CTX].reshape(head_shape),
        d_crossed,
        cross_log_heads,
    )
    d_query = d_query.reshape(-1, heads_wide).astype(low)
    d_key, d_value = (array.reshape(CTX, -1).astype(low) for array in (d_key, d_value))
    grad_cross_q = dot_rows(rows_two, d_query)
    d_keyval = jnp.concatenate([d_key, d_value], axis=1)
    grad_kv = dot_rows(context, d_keyval).astype(low)
    grad_kv = jnp.concatenate([grad_kv.reshape(members, -1, 2, heads_wide)[:, :, part] for part in range(2)], axis=1)
    context_part = dot_cols(d_keyval, cross_kv)
    d_normed = sum_rows(dot_cols(d_query, cross_q))
    _, scaled_two, inverse_two = layer_norm(resid_one, gain_cross)
    d_part, gain_grad_two = norm_backward(d_normed, scaled_two, inverse_two, gain_cross)
    d_resid = d_resid + d_part
    self_seed = spread_rows(d_resid.astype(low))
    grad_attn_out = dot_rows(self_seed, attended)
    grad_mid = jnp.concatenate([grad.astype(low) for grad in (grad_attn_out, grad_cross_q, grad_cross_out, grad_kv.reshape(-1, heads_wide))], axis=1)
    sum_mid = dp_sum(after(grad_mid, sum_mlp))
    d_attended = dot_plain(self_seed, attn_out_t).astype(low)
    d_packed = attend_back(rotated, d_attended, logs, tables)
    sum_qkv = dp_sum(after(dot_rows(rows_one, d_packed), sum_mid))
    d_normed = sum_rows(dot_cols(d_packed, qkv_all))
    _, scaled_one, inverse_one = layer_norm(latents.astype(jnp.float32), gain_attn)
    d_part, gain_grad_one = norm_backward(d_normed, scaled_one, inverse_one, gain_attn)
    grad_latents = d_resid + d_part
    grad_context = lax.psum(context_part.astype(low), "tensor").astype(jnp.float32)[None]
    gains = lax.psum(jnp.stack([gain_grad_one, gain_grad_two, gain_grad_three]), ("dp", "tensor"))
    sums = [sum_mid[:, part * heads_wide : (part + 1) * heads_wide].astype(jnp.float32) for part in range(4)]
    half = sums[3].shape[0] // 2
    sum_kv = jnp.concatenate([sums[3][:half], sums[3][half:]], axis=1)
    return (
        block_out,
        grad_latents,
        grad_context,
        gains[0],
        by_head(sum_qkv, 3).astype(jnp.float32),
        sums[0].T,
        gains[1],
        sums[1],
        by_head(sum_kv, 2),
        sums[2].T,
        gains[2],
        sum_mlp[:, :hidden_wide].astype(jnp.float32),
        sum_mlp[:, hidden_wide:].astype(jnp.float32),
        sum_down.astype(jnp.float32).T,
    )


def per_device_general(
    latents,
    conditioning,
    gain_attn,
    w_qkv,
    w_attn_out,
    gain_cross,
    w_cross_q,
    w_cross_kv,
    w_cross_out,
    gain_mlp,
    w_gate,
    w_up,
    w_down,
    cotangent,
):
    low = jnp.bfloat16
    heads_wide = w_cross_q.shape[1]
    hidden_wide = w_gate.shape[1]
    resid_in = latents.astype(jnp.float32)
    normed_one, scaled_one, inverse_one = layer_norm(resid_in, gain_attn)
    rows_one = spread_rows(normed_one.astype(low))
    own_qkv = by_part(w_qkv.astype(low), 3)
    qkv_all = lax.all_gather(own_qkv, "dp", axis=0, tiled=True)
    own_kv = by_part(w_cross_kv.astype(low), 2)
    own_kv = jnp.concatenate([own_kv[:, :heads_wide], own_kv[:, heads_wide:]], axis=0)
    own_mid = jnp.concatenate(
        [w_attn_out.astype(low).T, w_cross_q.astype(low), w_cross_out.astype(low).T, own_kv], axis=1
    )
    mid_all = lax.all_gather(after(own_mid, qkv_all), "dp", axis=0, tiled=True)
    own_mlp = jnp.concatenate([w_gate.astype(low), w_up.astype(low)], axis=1)
    mlp_all = lax.all_gather(after(own_mlp, mid_all), "dp", axis=0, tiled=True)
    down_all = lax.all_gather(after(w_down.astype(low).T, mlp_all), "dp", axis=0, tiled=True)
    attn_out_t, cross_q, cross_out_t = (mid_all[:, part * heads_wide : (part + 1) * heads_wide] for part in range(3))
    model = mid_all.shape[0]
    cross_kv = (
        mid_all[:, 3 * heads_wide :]
        .reshape(lax.axis_size("dp"), 2, -1, heads_wide)
        .transpose(0, 2, 1, 3)
        .reshape(model // 2, 2 * heads_wide)
    )

    tables = turn_tables(group_positions(latents.shape[0]))
    packed = dot_plain(rows_one, qkv_all)
    attended, rotated, logs = attend(pad_heads(packed, 3), tables)
    attended = attended[:, :heads_wide]
    resid_one = resid_in + sum_rows(dot_cols(attended, attn_out_t))
    normed_two, scaled_two, inverse_two = layer_norm(resid_one, gain_cross)
    rows_two = spread_rows(normed_two.astype(low))
    head_shape = (-1, heads_wide // DH, DH)
    cross_query = dot_plain(rows_two, cross_q).astype(low).reshape(head_shape)
    context = conditioning.reshape(CTX, conditioning.shape[2])
    cross_pack = dot_plain(context, cross_kv).astype(low)
    cross_key = cross_pack[:, :heads_wide].reshape(head_shape)
    cross_value = cross_pack[:, heads_wide:].reshape(head_shape)
    crossed, cross_logs = cross_forward(cross_query, cross_key, cross_value)
    crossed = crossed.reshape(-1, heads_wide).astype(low)
    resid_two = resid_one + sum_rows(dot_cols(crossed, cross_out_t))
    normed_three, scaled_three, inverse_three = layer_norm(resid_two, gain_mlp)
    rows_three = spread_rows(normed_three.astype(low))
    mlp_seed = spread_rows(cotangent)
    both = dot_plain(rows_three, mlp_all)
    gate_pre, up_pre = both[:, :hidden_wide], both[:, hidden_wide:]
    sigma_gate = jax.nn.sigmoid(gate_pre)
    swish = gate_pre * sigma_gate
    hidden = (swish * up_pre).astype(low)
    sum_down = dp_sum(dot_rows(mlp_seed, hidden))
    d_hidden = dot_plain(mlp_seed, down_all)
    d_gate = (d_hidden * up_pre * sigma_gate * (1.0 + gate_pre * (1.0 - sigma_gate))).astype(low)
    d_up = (d_hidden * swish).astype(low)
    d_both = jnp.concatenate([d_gate, d_up], axis=1)
    sum_mlp = dp_sum(after(dot_rows(rows_three, d_both), sum_down))
    d_normed = sum_rows(dot_cols(d_both, mlp_all))
    d_part, gain_grad_three = norm_backward(d_normed, scaled_three, inverse_three, gain_mlp)
    d_resid = cotangent.astype(jnp.float32) + d_part
    block_out = resid_two + sum_rows(dot_cols(hidden, down_all))
    cross_seed = spread_rows(d_resid.astype(low))
    grad_cross_out = dot_rows(cross_seed, crossed)
    d_crossed = dot_plain(cross_seed, cross_out_t).astype(low).reshape(head_shape)
    d_query, d_key, d_value = cross_backward(cross_query, cross_key, cross_value, d_crossed, cross_logs)
    d_query = d_query.reshape(-1, heads_wide).astype(low)
    d_keyval = jnp.concatenate([d_key.reshape(CTX, -1), d_value.reshape(CTX, -1)], axis=1).astype(low)
    grad_cross_q = dot_rows(rows_two, d_query)
    grad_cross_kv = dot_rows(context, d_keyval)
    context_part = dot_cols(d_keyval, cross_kv)
    d_normed = sum_rows(dot_cols(d_query, cross_q))
    d_part, gain_grad_two = norm_backward(d_normed, scaled_two, inverse_two, gain_cross)
    d_resid = d_resid + d_part
    self_seed = spread_rows(d_resid.astype(low))
    grad_attn_out = dot_rows(self_seed, attended)
    grad_kv = (
        grad_cross_kv.astype(low)
        .reshape(lax.axis_size("dp"), -1, 2, heads_wide)
        .transpose(0, 2, 1, 3)
        .reshape(model, heads_wide)
    )
    grad_mid = jnp.concatenate([grad_attn_out.astype(low), grad_cross_q.astype(low), grad_cross_out.astype(low), grad_kv], axis=1)
    sum_mid = dp_sum(after(grad_mid, sum_mlp))
    d_attended = dot_plain(self_seed, attn_out_t).astype(low)
    d_packed = drop_heads(attend_back(rotated, pad_heads(d_attended, 1), logs, tables), 3, packed.shape[1])
    sum_qkv = dp_sum(after(dot_rows(rows_one, d_packed), sum_mid))
    d_normed = sum_rows(dot_cols(d_packed, qkv_all))
    d_part, gain_grad_one = norm_backward(d_normed, scaled_one, inverse_one, gain_attn)
    grad_latents = d_resid + d_part
    grad_context = (
        lax.psum(context_part.astype(low), "tensor").astype(jnp.float32).reshape(conditioning.shape)
    )
    gains = lax.psum(jnp.stack([gain_grad_one, gain_grad_two, gain_grad_three]), ("dp", "tensor"))
    sums = [sum_mid[:, part * heads_wide : (part + 1) * heads_wide].astype(jnp.float32) for part in range(4)]
    half = sums[3].shape[0] // 2
    sum_kv = jnp.concatenate([sums[3][:half], sums[3][half:]], axis=1)
    return (
        block_out,
        grad_latents,
        grad_context,
        gains[0],
        by_head(sum_qkv, 3).astype(jnp.float32),
        sums[0].T,
        gains[1],
        sums[1],
        by_head(sum_kv, 2),
        sums[2].T,
        gains[2],
        sum_mlp[:, :hidden_wide].astype(jnp.float32),
        sum_mlp[:, hidden_wide:].astype(jnp.float32),
        sum_down.astype(jnp.float32).T,
    )


def solution(mesh):
    in_specs = (
        P(("dp", "tensor"), None),
        P("dp", None, None),
        P(),
        P("dp", "tensor"),
        P("tensor", "dp"),
        P(),
        P("dp", "tensor"),
        P("dp", "tensor"),
        P("tensor", "dp"),
        P(),
        P("dp", "tensor"),
        P("dp", "tensor"),
        P("tensor", "dp"),
        P(("dp", "tensor"), None),
    )
    out_specs = (
        P(("dp", "tensor"), None),
        P(("dp", "tensor"), None),
        P("dp", None, None),
        P(),
        P("dp", "tensor"),
        P("tensor", "dp"),
        P(),
        P("dp", "tensor"),
        P("dp", "tensor"),
        P("tensor", "dp"),
        P(),
        P("dp", "tensor"),
        P("dp", "tensor"),
        P("tensor", "dp"),
    )
    special = dict(mesh.shape) == {"dp": 8, "tensor": 4}
    return jax.shard_map(
        per_device if special else per_device_general, mesh=mesh, in_specs=in_specs, out_specs=out_specs, check_vma=False
    )
```

```python
import math
from functools import reduce

import jax
import jax.numpy as jnp
from jax import lax
from jax.experimental import pallas as pl
from jax.experimental.pallas import tpu as pltpu
from jax.sharding import PartitionSpec as P

DH = 64
CTX = 130
LENGTH = 1024
PAIR = 2 * DH
ROWS = 256
VMEM_BYTES = 62 * 2**20

norm_eps = 1e-05
rope_base = 10000.0


def head_turn(values, cosine, sine):
    quarter = DH // 4
    ahead = pltpu.roll(values, PAIR - quarter, 1)
    behind = pltpu.roll(values, quarter, 1)
    lane = lax.broadcasted_iota(jnp.int32, values.shape, 1) % DH
    return values * cosine + jnp.where(lane < quarter, -ahead, behind) * sine


def half_mask(shape, axis, which):
    place = lax.broadcasted_iota(jnp.int32, shape, axis)
    return (place >= DH) if which else (place < DH)


def attend_kernel(q_ref, k_ref, v_ref, cos_ref, sin_ref, out_ref, rot_ref, log_ref, kt_ref, vm_ref):
    pairs = pl.num_programs(0)
    pair = pl.program_id(0)
    turn = (cos_ref[...], sin_ref[...])
    query = head_turn(q_ref[...], *turn).astype(jnp.bfloat16)
    key = head_turn(k_ref[...], *turn).astype(jnp.bfloat16)
    value = v_ref[...].astype(jnp.bfloat16)
    for part, array in enumerate((query, key, value)):
        start = pl.multiple_of((part * pairs + pair) * PAIR, PAIR)
        rot_ref[:, pl.ds(start, PAIR)] = array
    key_t = key.astype(jnp.float32).T
    for which in range(2):
        kt_ref[which] = jnp.where(half_mask(key_t.shape, 0, which), key_t, 0.0).astype(jnp.bfloat16)
        vm_ref[which] = jnp.where(half_mask(value.shape, 1, which), value.astype(jnp.float32), 0.0).astype(jnp.bfloat16)
    q_start = pl.multiple_of(pair * PAIR, PAIR)

    def one_block(step, carry):
        rows = pl.ds(pl.multiple_of(step * ROWS, ROWS), ROWS)
        block = rot_ref[rows, pl.ds(q_start, PAIR)] * jnp.bfloat16(DH**-0.5)
        outs, logs = [], []
        for which in range(2):
            scores = jnp.dot(block, kt_ref[which], preferred_element_type=jnp.float32)
            peak = jnp.max(scores, axis=1, keepdims=True)
            shifted = jnp.exp(scores - peak)
            total = jnp.sum(shifted, axis=1, keepdims=True)
            product = jnp.dot(shifted.astype(jnp.bfloat16), vm_ref[which], preferred_element_type=jnp.float32)
            outs.append(product * (1.0 / total))
            logs.append(peak + jnp.log(total))
        out_ref[rows, :] = (outs[0] + outs[1]).astype(jnp.bfloat16)
        low = half_mask((ROWS, PAIR), 1, 0)
        log_ref[rows, :] = jnp.where(low, logs[0], logs[1])
        return carry

    lax.fori_loop(0, LENGTH // ROWS, one_block, 0)


def attend_back_kernel(
    q_ref, k_ref, v_ref, grad_ref, log_ref, cos_ref, sin_ref, out_ref,
    kt_ref, vt_ref, km_ref, qt_ref, gt_ref, dq_ref, dk_ref, dv_ref,
):
    pairs = pl.num_programs(0)
    pair = pl.program_id(0)
    key_t = k_ref[...].astype(jnp.float32).T
    value_t = v_ref[...].astype(jnp.float32).T
    for which in range(2):
        keep = half_mask(key_t.shape, 0, which)
        kt_ref[which] = jnp.where(keep, key_t, 0.0).astype(jnp.bfloat16)
        vt_ref[which] = jnp.where(keep, value_t, 0.0).astype(jnp.bfloat16)
        key = k_ref[...].astype(jnp.float32)
        km_ref[which] = jnp.where(half_mask(key.shape, 1, which), key, 0.0).astype(jnp.bfloat16)
    qt_ref[...] = (q_ref[...].astype(jnp.float32) * DH**-0.5).T.astype(jnp.bfloat16)
    gt_ref[...] = grad_ref[...].astype(jnp.float32).T.astype(jnp.bfloat16)
    dk_ref[...] = jnp.zeros_like(dk_ref)
    dv_ref[...] = jnp.zeros_like(dv_ref)

    def one_block(step, carry):
        rows = pl.ds(pl.multiple_of(step * ROWS, ROWS), ROWS)
        block = q_ref[rows, :] * jnp.bfloat16(DH**-0.5)
        grads = grad_ref[rows, :]
        d_query = jnp.zeros((ROWS, PAIR), jnp.float32)
        for which in range(2):
            half = slice(which * DH, (which + 1) * DH)
            scores = jnp.dot(block, kt_ref[which], preferred_element_type=jnp.float32)
            probs = jnp.exp(scores - log_ref[rows, which * DH : which * DH + 1])
            d_prob = jnp.dot(grads, vt_ref[which], preferred_element_type=jnp.float32)
            center = jnp.sum(probs * d_prob, axis=1, keepdims=True)
            d_score = (probs * (d_prob - center)).astype(jnp.bfloat16)
            d_query += jnp.dot(d_score, km_ref[which], preferred_element_type=jnp.float32)
            dk_ref[half, :] += jnp.dot(qt_ref[half, rows], d_score, preferred_element_type=jnp.float32)
            dv_ref[half, :] += jnp.dot(
                gt_ref[half, rows], probs.astype(jnp.bfloat16), preferred_element_type=jnp.float32
            )
        dq_ref[rows, :] = d_query * DH**-0.5
        return carry

    lax.fori_loop(0, LENGTH // ROWS, one_block, 0)
    turn = (cos_ref[...], -sin_ref[...])
    results = (head_turn(dq_ref[...], *turn), head_turn(dk_ref[...].T, *turn), dv_ref[...].T)
    for part, array in enumerate(results):
        start = pl.multiple_of((part * pairs + pair) * PAIR, PAIR)
        out_ref[:, pl.ds(start, PAIR)] = array.astype(jnp.bfloat16)


def column_block(offset):
    return pl.BlockSpec((LENGTH, PAIR), lambda pair: (0, pair + offset))


def whole_block(columns):
    return pl.BlockSpec((LENGTH, columns), lambda pair: (0, 0))


def attend(packed, tables):
    columns = packed.shape[1]
    pairs = columns // (3 * PAIR)
    return pl.pallas_call(
        attend_kernel,
        grid=(pairs,),
        in_specs=[column_block(part * pairs) for part in range(3)] + [whole_block(PAIR)] * 2,
        out_specs=[column_block(0), whole_block(columns), column_block(0)],
        out_shape=[
            jax.ShapeDtypeStruct((LENGTH, pairs * PAIR), jnp.bfloat16),
            jax.ShapeDtypeStruct((LENGTH, columns), jnp.bfloat16),
            jax.ShapeDtypeStruct((LENGTH, pairs * PAIR), jnp.float32),
        ],
        scratch_shapes=[pltpu.VMEM((2, PAIR, LENGTH), jnp.bfloat16), pltpu.VMEM((2, LENGTH, PAIR), jnp.bfloat16)],
        compiler_params=pltpu.CompilerParams(vmem_limit_bytes=VMEM_BYTES),
        cost_estimate=pl.CostEstimate(flops=pairs * 2**32, bytes_accessed=2**24, transcendentals=pairs * 2**21),
    )(packed, packed, packed, *tables)


def attend_back(rotated, d_attended, logs, tables):
    columns = rotated.shape[1]
    pairs = columns // (3 * PAIR)
    tall = pltpu.VMEM((PAIR, LENGTH), jnp.bfloat16)
    return pl.pallas_call(
        attend_back_kernel,
        grid=(pairs,),
        in_specs=[column_block(part * pairs) for part in range(3)]
        + [column_block(0), column_block(0)]
        + [whole_block(PAIR)] * 2,
        out_specs=whole_block(columns),
        out_shape=jax.ShapeDtypeStruct((LENGTH, columns), jnp.bfloat16),
        scratch_shapes=[
            pltpu.VMEM((2, PAIR, LENGTH), jnp.bfloat16),
            pltpu.VMEM((2, PAIR, LENGTH), jnp.bfloat16),
            pltpu.VMEM((2, LENGTH, PAIR), jnp.bfloat16),
            tall,
            tall,
            pltpu.VMEM((LENGTH, PAIR), jnp.float32),
            pltpu.VMEM((PAIR, LENGTH), jnp.float32),
            pltpu.VMEM((PAIR, LENGTH), jnp.float32),
        ],
        compiler_params=pltpu.CompilerParams(vmem_limit_bytes=VMEM_BYTES),
        cost_estimate=pl.CostEstimate(flops=pairs * 2**33, bytes_accessed=2**24, transcendentals=pairs * 2**21),
    )(rotated, rotated, rotated, d_attended, logs, *tables)


def turn_tables(positions):
    quarter = DH // 4
    frequency = jnp.exp(-jnp.log(rope_base) * jnp.arange(quarter).astype(jnp.float32) / quarter)
    angles = positions.astype(jnp.float32)[:, None] * frequency[None, :]
    cosine, sine = jnp.cos(angles), jnp.sin(angles)
    zeros, ones = jnp.zeros_like(sine), jnp.ones_like(sine)
    rows = (
        jnp.concatenate([cosine, cosine, ones, ones], axis=1),
        jnp.concatenate([sine, sine, zeros, zeros], axis=1),
    )
    return tuple(jnp.concatenate([row, row], axis=1) for row in rows)


def dot_plain(left_op, right_op):
    return jnp.dot(left_op, right_op, preferred_element_type=jnp.float32)


def dot_rows(left_op, right_op):
    return lax.dot_general(
        left_op, right_op, (((0,), (0,)), ((), ())), preferred_element_type=jnp.float32
    )


def dot_cols(left_op, right_op):
    return lax.dot_general(
        left_op, right_op, (((1,), (1,)), ((), ())), preferred_element_type=jnp.float32
    )


def layer_norm(values, gain_vec):
    center = values - jnp.mean(values, axis=-1, keepdims=True)
    spread = jnp.mean(center * center, axis=-1, keepdims=True)
    inverse = lax.rsqrt(spread + norm_eps)
    scaled = center * inverse
    return (scaled * gain_vec, scaled, inverse)


def norm_backward(upstream, scaled, inverse, gain_vec):
    weighted = upstream * gain_vec
    inner = jnp.mean(weighted, axis=-1, keepdims=True) + scaled * jnp.mean(
        weighted * scaled, axis=-1, keepdims=True
    )
    return (inverse * (weighted - inner), jnp.sum(upstream * scaled, axis=0))


def swap(values, bit):
    return lax.ppermute(values, "tensor", [(member, member ^ bit) for member in range(4)])


def spread_rows(values):
    if lax.axis_size("tensor") != 4:
        return lax.all_gather(values, "tensor", axis=0, tiled=True)
    half = values.shape[0] // 2
    near, far = swap(values, 1), swap(values, 2)
    return jnp.concatenate([values, near, far, swap(near[:half], 2), swap(far[half:], 1)], axis=0)


def sum_rows(partial):
    if lax.axis_size("tensor") != 4:
        return lax.psum_scatter(
            partial.astype(jnp.bfloat16), "tensor", scatter_dimension=0, tiled=True
        ).astype(jnp.float32)
    size = partial.shape[0] // 4
    half = size // 2
    own, near, far, last = (partial[part * size : (part + 1) * size] for part in range(4))
    first = swap(last[:half].astype(jnp.bfloat16), 1)
    second = swap(last[half:].astype(jnp.bfloat16), 2)
    far = jnp.concatenate([far[:half] + first.astype(jnp.float32), far[half:]], axis=0)
    near = jnp.concatenate([near[:half], near[half:] + second.astype(jnp.float32)], axis=0)
    return (
        own
        + swap(near.astype(jnp.bfloat16), 1).astype(jnp.float32)
        + swap(far.astype(jnp.bfloat16), 2).astype(jnp.float32)
    )


def group_positions(rows):
    group = lax.axis_size("tensor")
    blocks = jnp.arange(group)
    if group == 4:
        blocks = blocks ^ lax.axis_index("tensor")
    return (blocks[:, None] * rows + jnp.arange(rows)[None, :]).reshape(-1)


def cross_forward(queries, keys_in, values_in):
    scores = jnp.einsum("qhd,khd->hqk", queries, keys_in, preferred_element_type=jnp.float32) * DH ** (-0.5)
    peak_score = jnp.max(scores, axis=-1, keepdims=True)
    shifted = jnp.exp(scores - peak_score)
    totals = jnp.sum(shifted, axis=-1, keepdims=True)
    probabilities = (shifted / totals).astype(jnp.bfloat16)
    output = jnp.einsum("hqk,khd->qhd", probabilities, values_in, preferred_element_type=jnp.float32)
    return (output, peak_score + jnp.log(totals))


def cross_backward(queries, keys_in, values_in, d_output, log_totals):
    scaling = DH ** (-0.5)
    scores = jnp.einsum("qhd,khd->hqk", queries, keys_in, preferred_element_type=jnp.float32) * scaling
    probabilities = jnp.exp(scores - log_totals)
    d_prob = jnp.einsum("qhd,khd->hqk", d_output, values_in, preferred_element_type=jnp.float32)
    center = jnp.sum(probabilities * d_prob, axis=-1, keepdims=True)
    d_score = (probabilities * (d_prob - center)).astype(jnp.bfloat16)
    d_query = jnp.einsum("hqk,khd->qhd", d_score, keys_in, preferred_element_type=jnp.float32) * scaling
    d_key = jnp.einsum("hqk,qhd->khd", d_score, queries, preferred_element_type=jnp.float32) * scaling
    d_value = jnp.einsum(
        "hqk,qhd->khd", probabilities.astype(jnp.bfloat16), d_output, preferred_element_type=jnp.float32
    )
    return (d_query, d_key, d_value)


def by_part(columns, parts):
    rows = columns.shape[0]
    return columns.reshape(rows, -1, parts, DH).swapaxes(1, 2).reshape(rows, -1)


def by_head(columns, parts):
    rows = columns.shape[0]
    return columns.reshape(rows, parts, -1, DH).swapaxes(1, 2).reshape(rows, -1)


def pad_heads(columns, parts):
    rows, width = columns.shape
    each = width // parts
    if each % PAIR == 0:
        return columns
    return jnp.pad(columns.reshape(rows, parts, each), ((0, 0), (0, 0), (0, -each % PAIR))).reshape(rows, -1)


def drop_heads(columns, parts, width):
    rows = columns.shape[0]
    return columns.reshape(rows, parts, -1)[:, :, : width // parts].reshape(rows, width)


def dp_sum(grads):
    return lax.psum_scatter(grads.astype(jnp.bfloat16), "dp", scatter_dimension=0, tiled=True)


def after(value, earlier):
    return lax.optimization_barrier((value, earlier))[0]


MESH = pl.DeviceIdType.MESH
BLOCK = LENGTH // 4
HALF = BLOCK // 2
FULL = 256


class Links:
    def __init__(self, send, recv, local):
        self.send, self.recv, self.local = send, recv, local
        self.used = self.used_local = 0
        self.pending, self.pending_local = [], []
        self.dp, self.tensor = lax.axis_index("dp"), lax.axis_index("tensor")

    def remote(self, src, dst, dp_bit, tensor_bit):
        at = self.used
        self.used += 1
        return pltpu.make_async_remote_copy(
            src_ref=src,
            dst_ref=dst,
            send_sem=self.send.at[at],
            recv_sem=self.recv.at[at],
            device_id=(self.dp ^ dp_bit, self.tensor ^ tensor_bit),
            device_id_type=MESH,
        )

    def go(self, src, dst, dp_bit, tensor_bit):
        copy = self.remote(src, dst, dp_bit, tensor_bit)
        copy.start()
        self.pending.append(copy)
        return copy

    def store(self, src, dst):
        copy = pltpu.make_async_copy(src, dst, self.local.at[self.used_local])
        self.used_local += 1
        copy.start()
        self.pending_local.append(copy)
        return copy

    def settle(self, copy):
        copy.wait()
        self.pending_local = [other for other in self.pending_local if other is not copy]

    def settle_sends(self, copies):
        for copy in copies:
            copy.wait_send()
        self.pending = [copy for copy in self.pending if all(copy is not other for other in copies)]

    def greet(self, partners):
        barrier = pltpu.get_barrier_semaphore()
        for dp_bit, tensor_bit in partners:
            pl.semaphore_signal(
                barrier, inc=1, device_id=(self.dp ^ dp_bit, self.tensor ^ tensor_bit), device_id_type=MESH
            )
        pl.semaphore_wait(barrier, len(partners))

    def finish(self):
        for copy in self.pending:
            copy.wait_send()
        for copy in self.pending_local:
            copy.wait()


class Spread:
    def __init__(self, links, rows):
        self.links, self.rows = links, rows
        self.near = links.go(rows.at[0], rows.at[1], 0, 1)
        self.far = links.go(rows.at[0], rows.at[2], 0, 2)
        self.stage = 0

    def wait(self, block):
        rows, links = self.rows, self.links
        if block >= 1 and self.stage == 0:
            self.near.wait_recv()
            low = pl.ds(0, HALF)
            self.last_low = links.go(rows.at[1, low], rows.at[3, low], 0, 2)
            self.stage = 1
        if block >= 2 and self.stage == 1:
            self.far.wait_recv()
            high = pl.ds(HALF, HALF)
            self.last_high = links.go(rows.at[2, high], rows.at[3, high], 0, 1)
            self.stage = 2
        if block >= 3 and self.stage == 2:
            self.last_low.wait_recv()
            self.last_high.wait_recv()
            self.stage = 3

    def sent(self):
        self.links.settle_sends((self.near, self.far, self.last_low, self.last_high))


class Gather:
    def __init__(self, links, shard, whole):
        self.links, self.whole = links, whole
        self.size = shard.shape[0]
        self.place = links.dp // 2
        self.middle = (self.place == 1) | (self.place == 2)
        own = self.rows(0)
        self.own = links.store(shard, own)
        self.core = [links.go(shard, own, 1, 0)]
        self.beside = links.go(shard, own, 2, 0)
        self.skip = links.go(shard, own, 4, 0)
        self.third_at = links.used
        self.third = links.remote(shard, own, 6, 0)

        @pl.when(self.middle)
        def _():
            self.third.start()

    def rows(self, step):
        start = pl.multiple_of((self.links.dp ^ (2 * step)) * self.size, self.size)
        return self.whole.at[pl.ds(start, self.size)]

    def forward(self):
        links = self.links
        block = self.rows(2)
        self.skip.wait_recv()
        self.onward = pltpu.make_async_remote_copy(
            src_ref=block,
            dst_ref=block,
            send_sem=links.send.at[links.used],
            recv_sem=links.recv.at[self.third_at],
            device_id=(links.dp ^ 2, links.tensor),
            device_id_type=MESH,
        )
        links.used += 1

        @pl.when(self.middle)
        def _():
            self.onward.start()

        self.core.append(links.go(block, block, 1, 0))

    def arrive(self):
        links = self.links
        self.beside.wait_recv()
        block = self.rows(1)
        self.core.append(links.go(block, block, 1, 0))
        self.third.wait_recv()
        block = self.rows(3)
        self.core.append(links.go(block, block, 1, 0))
        links.settle(self.own)
        for copy in self.core:
            copy.wait_recv()

    def finish(self):
        @pl.when(self.middle)
        def _():
            self.third.wait_send()
            self.onward.wait_send()


class Sums:
    def __init__(self, links, parts, half_near, half_far, near, far):
        self.links, self.parts = links, parts
        self.half_near, self.half_far, self.near, self.far = half_near, half_far, near, far
        self.low, self.high = pl.ds(0, HALF), pl.ds(HALF, HALF)

    def ready(self, block):
        links, parts, low, high = self.links, self.parts, self.low, self.high
        if block == 3:
            self.first = links.go(parts.at[3, low], self.half_near, 0, 1)
            self.second = links.go(parts.at[3, high], self.half_far, 0, 2)
        if block == 1:
            self.near_low = links.go(parts.at[1, low], self.near.at[low], 0, 1)
        if block == 2:
            self.far_high = links.go(parts.at[2, high], self.far.at[high], 0, 2)

    def add(self):
        links, parts, low, high = self.links, self.parts, self.low, self.high
        self.first.wait_recv()
        parts[2, low] = (parts[2, low].astype(jnp.float32) + self.half_near[...].astype(jnp.float32)).astype(
            jnp.bfloat16
        )
        self.far_low = links.go(parts.at[2, low], self.far.at[low], 0, 2)
        self.second.wait_recv()
        parts[1, high] = (parts[1, high].astype(jnp.float32) + self.half_far[...].astype(jnp.float32)).astype(
            jnp.bfloat16
        )
        self.near_high = links.go(parts.at[1, high], self.near.at[high], 0, 1)

    def arrive(self):
        for copy in (self.near_low, self.far_high, self.far_low, self.near_high):
            copy.wait_recv()

    def sent(self):
        self.links.settle_sends(
            (self.first, self.second, self.near_low, self.far_high, self.far_low, self.near_high)
        )

    def total(self, rows):
        return self.near[rows].astype(jnp.float32) + self.far[rows].astype(jnp.float32)
def columns(total, width, body):
    def step(index, carry):
        body(pl.ds(pl.multiple_of(index * width, width), width))
        return carry

    lax.fori_loop(0, total // width, step, 0)


def attend_rows(block, keys_t, values, limit):
    outs, logs = [], []
    for which in range(2):
        part = jnp.where(half_mask(block.shape, 1, which), block, jnp.zeros_like(block))
        scores = jnp.dot(part, keys_t, preferred_element_type=jnp.float32)
        if limit is not None:
            scores = jnp.where(lax.broadcasted_iota(jnp.int32, scores.shape, 1) < limit, scores, -jnp.inf)
        peak = jnp.max(scores, axis=1, keepdims=True)
        shifted = jnp.exp(scores - peak)
        total = jnp.sum(shifted, axis=1, keepdims=True)
        product = jnp.dot(shifted.astype(jnp.bfloat16), values, preferred_element_type=jnp.float32)
        outs.append(product * (1.0 / total))
        logs.append(peak + jnp.log(total))
    low = half_mask(block.shape, 1, 0)
    return jnp.where(low, outs[0], outs[1]), jnp.where(low, logs[0], logs[1])


def row_steps(total, body):
    def step(index, carry):
        body(pl.ds(pl.multiple_of(index * 32, 32), 32))
        return carry

    lax.fori_loop(0, total // 32, step, 0)


def block_rows(block):
    return pl.ds(block * BLOCK, BLOCK)


def two_heads(weights, part, parts, pair):
    starts = [((2 * pair + which) * parts + part) * DH for which in range(2)]
    return jnp.concatenate([weights[:, start : start + DH] for start in starts], axis=1).astype(jnp.bfloat16)


def fill_tables(cosine, sine, member):
    quarter = DH // 4
    shape = (BLOCK, PAIR)
    lane = lax.broadcasted_iota(jnp.int32, shape, 1) % DH
    frequency = jnp.exp((lane % quarter).astype(jnp.float32) * (-math.log(rope_base) / quarter))
    for block in range(4):
        place = (member ^ block) * BLOCK + lax.broadcasted_iota(jnp.int32, shape, 0)
        angle = place.astype(jnp.float32) * frequency
        rows = block_rows(block)
        cosine[rows] = jnp.where(lane < 2 * quarter, jnp.cos(angle), 1.0)
        sine[rows] = jnp.where(lane < 2 * quarter, jnp.sin(angle), 0.0)


def forward_kernel(
    latents, gains, conditioning, f32_qkv,
    f32_attn_out, f32_cross_q, f32_cross_kv, f32_cross_out, f32_gate, f32_up, f32_down, cotangent,
    rows_one_out, rows_two_out, rows_three_out, seeds_out, qkv_out, attn_out_out, cross_out, keyval_w_out, mlp_out,
    down_out, rotated_out, attended_out, logs_out,
    query_out, keyval_out, crossed_out, cross_logs_out, resid_one_out, resid_two_out, tables_out,
    rows_one, rows_two, rows_three, w_qkv, w_attn_out, w_cross, w_keyval, rotated, attended, logs, query, keyval,
    crossed, cross_logs, keys_t, cross_keys_t, parts, got_one, got_two, resid_one, resid_two,
    packed, tables, context, raw_attn_out, raw_cross_q, raw_cross_kv, raw_cross_out, raw_gate, raw_up, raw_down,
    own_qkv, own_attn_out, own_cross, own_keyval, own_mlp, own_down, send, recv, local,
):
    low = jnp.bfloat16
    pairs = attended.shape[1] // PAIR
    width = pairs * PAIR
    links = Links(send, recv, local)
    loads = [
        links.store(source, target)
        for source, target in (
            (f32_attn_out, raw_attn_out), (f32_cross_q, raw_cross_q), (f32_cross_kv, raw_cross_kv),
            (f32_cross_out, raw_cross_out), (f32_gate, raw_gate), (f32_up, raw_up), (f32_down, raw_down),
        )
    ]
    seed_own = links.store(cotangent, seeds_out.at[0])
    for part in range(3):
        for pair in range(pairs):
            at = part * width + pair * PAIR
            own_qkv[:, at : at + PAIR] = two_heads(f32_qkv, part, 3, pair)
    links.greet([(1, 0), (2, 0), (4, 0), (6, 0), (0, 1), (0, 2)])
    gather_qkv = Gather(links, own_qkv, w_qkv)

    def norm_one(rows):
        rows_one[0, rows] = layer_norm(latents[rows].astype(jnp.float32), gains[0:1])[0].astype(low)

    row_steps(BLOCK, norm_one)
    spread_one = Spread(links, rows_one)
    cosine, sine = (tables.at[part] for part in range(2))
    fill_tables(cosine, sine, links.tensor)
    links.store(tables, tables_out)
    for load in loads:
        links.settle(load)
    own_attn_out[...] = raw_attn_out[...].astype(low)
    own_cross[:, :width] = raw_cross_q[...].astype(low)
    own_cross[:, width:] = raw_cross_out[...].astype(low)
    for part in range(2):
        for pair in range(pairs):
            at = part * width + pair * PAIR
            own_keyval[:, at : at + PAIR] = two_heads(raw_cross_kv, part, 2, pair)
    hidden = raw_gate.shape[1]
    own_mlp[:, :hidden] = raw_gate[...].astype(low)
    own_mlp[:, hidden:] = raw_up[...].astype(low)
    own_down[...] = raw_down[...].astype(low)
    context[...] = jnp.zeros_like(context)
    context[:CTX] = conditioning[0]
    spread_one.wait(1)
    gather_qkv.forward()
    gather_attn_out = Gather(links, own_attn_out, w_attn_out)
    gather_cross = Gather(links, own_cross, w_cross)
    gather_keyval = Gather(links, own_keyval, w_keyval)
    spread_one.wait(2)
    gather_qkv.arrive()
    links.store(w_qkv, qkv_out)

    for block in range(4):
        spread_one.wait(block)
        rows = block_rows(block)
        turn = (cosine[rows], sine[rows])

        def project(cols):
            packed[:, cols] = dot_plain(rows_one[block], w_qkv[:, cols])

        columns(3 * width, width, project)
        for part in range(3):
            for pair in range(pairs):
                at = slice(part * width + pair * PAIR, part * width + (pair + 1) * PAIR)
                value = packed[:, at]
                rotated[rows, at] = (value if part == 2 else head_turn(value, *turn)).astype(low)
    links.store(rows_one, rows_one_out)
    links.store(rotated, rotated_out)
    for pair in range(pairs):
        key = rotated[:, width + pair * PAIR : width + (pair + 1) * PAIR]
        keys_t[pair] = key.astype(jnp.float32).T.astype(low)

    def out_project(source, block, weight, sums):
        def project(cols):
            parts[block, :, cols] = dot_cols(source[block_rows(block)], weight(cols)).astype(low)

        columns(parts.shape[2], 512, project)
        sums.ready(block)

    sums_one = Sums(links, parts, *got_one)
    for block in (3, 1, 2, 0):
        rows = block_rows(block)

        def one_pair(pair, carry):
            at = pl.ds(pl.multiple_of(pair * PAIR, PAIR), PAIR)
            values_at = pl.ds(pl.multiple_of(2 * width + pair * PAIR, PAIR), PAIR)
            out, log = attend_rows(rotated[rows, at] * low(DH**-0.5), keys_t[pair], rotated[:, values_at], None)
            attended[rows, at] = out.astype(low)
            logs[rows, at] = log
            return carry

        lax.fori_loop(0, pairs, one_pair, 0)
        if block == 3:
            gather_attn_out.forward()
            gather_attn_out.arrive()
            links.store(w_attn_out, attn_out_out)
        out_project(attended, block, lambda cols: w_attn_out[cols, :], sums_one)
        if block == 1:
            gather_cross.forward()
            gather_keyval.forward()
            gather_mlp = Gather(links, own_mlp, mlp_out)
        if block == 2:
            sums_one.add()
    links.store(attended, attended_out)
    links.store(logs, logs_out)
    sums_one.arrive()

    def norm_two(rows):
        value = latents[rows].astype(jnp.float32) + parts[0, rows].astype(jnp.float32) + sums_one.total(rows)
        resid_one[rows] = value
        rows_two[0, rows] = layer_norm(value, gains[1:2])[0].astype(low)

    row_steps(BLOCK, norm_two)
    spread_two = Spread(links, rows_two)
    links.store(resid_one, resid_one_out)
    gather_keyval.arrive()
    links.store(w_keyval, keyval_w_out)
    for part in range(2):
        keyval[part] = dot_plain(context[...], w_keyval[:, part * width : (part + 1) * width]).astype(low)
    for pair in range(pairs):
        at = slice(pair * PAIR, (pair + 1) * PAIR)
        cross_keys_t[pair] = keyval[0, :, at].astype(jnp.float32).T.astype(low)
    links.store(keyval, keyval_out)
    gather_cross.arrive()
    links.store(w_cross, cross_out)
    sums_one.sent()
    sums_two = Sums(links, parts, *got_two)
    for block in range(4):
        spread_two.wait(block)
        rows = block_rows(block)
        query[rows] = dot_plain(rows_two[block], w_cross[:, :width]).astype(low)
        for pair in range(pairs):
            at = slice(pair * PAIR, (pair + 1) * PAIR)
            out, log = attend_rows(query[rows, at] * low(DH**-0.5), cross_keys_t[pair], keyval[1, :, at], CTX)
            crossed[rows, at] = out.astype(low)
            cross_logs[rows, at] = log
        out_project(crossed, block, lambda cols: w_cross[cols, width:], sums_two)
    sums_two.add()
    links.store(rows_two, rows_two_out)
    links.store(query, query_out)
    links.store(crossed, crossed_out)
    links.store(cross_logs, cross_logs_out)
    links.settle(seed_own)
    spread_seed = Spread(links, seeds_out)
    gather_mlp.forward()
    gather_down = Gather(links, own_down, down_out)
    sums_two.arrive()

    def norm_three(rows):
        value = resid_one[rows] + parts[0, rows].astype(jnp.float32) + sums_two.total(rows)
        resid_two[rows] = value
        rows_three[0, rows] = layer_norm(value, gains[2:3])[0].astype(low)

    row_steps(BLOCK, norm_three)
    spread_three = Spread(links, rows_three)
    links.store(resid_two, resid_two_out)
    spread_seed.wait(2)
    spread_three.wait(2)
    gather_down.forward()
    gather_mlp.arrive()
    spread_seed.wait(3)
    spread_three.wait(3)
    links.store(rows_three, rows_three_out)
    gather_down.arrive()
    links.finish()
    for gather in (gather_qkv, gather_attn_out, gather_cross, gather_keyval, gather_mlp, gather_down):
        gather.finish()


def whole_vmem():
    return pl.BlockSpec(memory_space=pltpu.VMEM)


def anywhere():
    return pl.BlockSpec(memory_space=pl.ANY)


def sum_buffers(model):
    return [
        pltpu.VMEM((HALF, model), jnp.bfloat16),
        pltpu.VMEM((HALF, model), jnp.bfloat16),
        pltpu.VMEM((BLOCK, model), jnp.bfloat16),
        pltpu.VMEM((BLOCK, model), jnp.bfloat16),
    ]


def forward_part(latents, gains, conditioning, weights, cotangent):
    w_qkv, w_attn_out, w_cross_q, w_cross_kv, w_cross_out, w_gate, w_up, w_down = weights
    model = latents.shape[1]
    depth = conditioning.shape[2]
    wide = w_qkv.shape[1]
    width = wide // 3
    hidden = w_gate.shape[1]
    pairs = width // PAIR
    low, high = jnp.bfloat16, jnp.float32
    share = w_qkv.shape[0]
    outs = [
        ((4, BLOCK, model), low),
        ((4, BLOCK, model), low),
        ((4, BLOCK, model), low),
        ((4, BLOCK, model), low),
        ((model, wide), low),
        ((model, width), low),
        ((model, 2 * width), low),
        ((depth, 2 * width), low),
        ((model, 2 * hidden), low),
        ((model, hidden), low),
        ((LENGTH, wide), low),
        ((LENGTH, width), low),
        ((LENGTH, width), high),
        ((LENGTH, width), low),
        ((2, FULL, width), low),
        ((LENGTH, width), low),
        ((LENGTH, width), high),
        ((BLOCK, model), high),
        ((BLOCK, model), high),
        ((2, LENGTH, PAIR), high),
    ]
    work = [
        ((4, BLOCK, model), low),
        ((4, BLOCK, model), low),
        ((4, BLOCK, model), low),
        ((model, wide), low),
        ((model, width), low),
        ((model, 2 * width), low),
        ((depth, 2 * width), low),
        ((LENGTH, wide), low),
        ((LENGTH, width), low),
        ((LENGTH, width), high),
        ((LENGTH, width), low),
        ((2, FULL, width), low),
        ((LENGTH, width), low),
        ((LENGTH, width), high),
        ((pairs, PAIR, LENGTH), low),
        ((pairs, PAIR, FULL), low),
        ((4, BLOCK, model), low),
    ]
    more = [
        ((BLOCK, model), high),
        ((BLOCK, model), high),
        ((BLOCK, wide), high),
        ((2, LENGTH, PAIR), high),
        ((FULL, depth), low),
        (w_attn_out.shape, high),
        (w_cross_q.shape, high),
        (w_cross_kv.shape, high),
        (w_cross_out.shape, high),
        (w_gate.shape, high),
        (w_up.shape, high),
        (w_down.shape, high),
        ((share, wide), low),
        ((share, width), low),
        ((share, 2 * width), low),
        (w_cross_kv.shape, low),
        ((share, 2 * hidden), low),
        ((share, hidden), low),
    ]
    scratch = [pltpu.VMEM(*buffer) for buffer in work] + [sum_buffers(model), sum_buffers(model)]
    scratch += [pltpu.VMEM(*buffer) for buffer in more]
    scratch += [pltpu.SemaphoreType.DMA((96,)), pltpu.SemaphoreType.DMA((96,)), pltpu.SemaphoreType.DMA((40,))]
    return pl.pallas_call(
        forward_kernel,
        out_shape=[jax.ShapeDtypeStruct(*out) for out in outs],
        in_specs=[whole_vmem()] * 4 + [anywhere()] * 8,
        out_specs=[anywhere()] * len(outs),
        scratch_shapes=scratch,
        compiler_params=pltpu.CompilerParams(collective_id=1, has_side_effects=True, vmem_limit_bytes=VMEM_BYTES),
        cost_estimate=pl.CostEstimate(flops=2**37, bytes_accessed=2**26, transcendentals=2**23),
    )(latents, gains, conditioning, *weights, cotangent)


class Scatter:
    def __init__(self, links, grads, got_core, extra, got, core_bit):
        self.links, self.grads, self.got_core, self.extra, self.got = links, grads, got_core, extra, got
        self.size = got.shape[1]
        self.place, self.which = links.dp // 2, links.dp % 2
        self.middle = (self.place == 1) | (self.place == 2)

    def rows(self, place, which):
        start = pl.multiple_of((2 * place + which) * self.size, self.size)
        return pl.ds(start, self.size)

    def pair_up(self):
        self.core = [
            self.links.go(self.grads.at[self.rows(place, 1 - self.which)], self.got_core.at[place], 1, 0)
            for place in range(4)
        ]

    def combine(self):
        links, grads = self.links, self.grads
        for copy in self.core:
            copy.wait_recv()

        def add(place, carry):
            rows = self.rows(place, self.which)
            grads[rows] = (grads[rows].astype(jnp.float32) + self.got_core[place].astype(jnp.float32)).astype(
                jnp.bfloat16
            )
            return carry

        lax.fori_loop(0, 4, add, 0)
        block = [grads.at[self.rows(self.place ^ step, self.which)] for step in range(4)]
        self.to_extra = links.remote(block[3], self.extra, 2, 0)
        self.to_third = links.remote(block[3], self.got.at[2], 6, 0)
        self.to_skip = links.remote(block[2], self.got.at[1], 4, 0)

        @pl.when(self.middle)
        def _():
            self.to_third.start()

        @pl.when(jnp.logical_not(self.middle))
        def _():
            self.to_extra.start()
            self.to_skip.start()

        self.beside = links.go(block[1], self.got.at[0], 2, 0)

    def relay(self):
        @pl.when(self.middle)
        def _():
            self.to_extra.wait_recv()
            rows = self.rows(self.place ^ 2, self.which)
            self.grads[rows] = (
                self.grads[rows].astype(jnp.float32) + self.extra[...].astype(jnp.float32)
            ).astype(jnp.bfloat16)
            self.to_skip.start()

    def arrive(self):
        self.beside.wait_recv()
        self.to_skip.wait_recv()

        @pl.when(self.middle)
        def _():
            self.to_third.wait_recv()

    def total(self, out, cols):
        mine = self.grads[self.rows(self.place, self.which), cols].astype(jnp.float32)
        out[...] = mine + self.got[0, :, cols].astype(jnp.float32) + self.got[1, :, cols].astype(jnp.float32)

        @pl.when(self.middle)
        def _():
            out[...] += self.got[2, :, cols].astype(jnp.float32)

    def finish(self):
        self.to_skip.wait_send()

        @pl.when(self.middle)
        def _():
            self.to_third.wait_send()

        @pl.when(jnp.logical_not(self.middle))
        def _():
            self.to_extra.wait_send()


def attend_rows_back(block, grads, log, keys_t, values_t, keys, d_keys_t, d_values_t, limit):
    block_t = block.astype(jnp.float32).T.astype(jnp.bfloat16)
    grads_t = grads.astype(jnp.float32).T.astype(jnp.bfloat16)
    outs = []
    for which in range(2):
        half = slice(which * DH, (which + 1) * DH)
        keep = half_mask(block.shape, 1, which)
        scores = jnp.dot(jnp.where(keep, block, jnp.zeros_like(block)), keys_t, preferred_element_type=jnp.float32)
        probs = jnp.exp(scores - log[:, which * DH : which * DH + 1])
        if limit is not None:
            probs = jnp.where(lax.broadcasted_iota(jnp.int32, probs.shape, 1) < limit, probs, 0.0)
        d_prob = jnp.dot(jnp.where(keep, grads, jnp.zeros_like(grads)), values_t, preferred_element_type=jnp.float32)
        center = jnp.sum(probs * d_prob, axis=1, keepdims=True)
        d_score = (probs * (d_prob - center)).astype(jnp.bfloat16)
        outs.append(jnp.dot(d_score, keys, preferred_element_type=jnp.float32))
        d_keys_t[half, :] += jnp.dot(block_t[half], d_score, preferred_element_type=jnp.float32)
        d_values_t[half, :] += jnp.dot(grads_t[half], probs.astype(jnp.bfloat16), preferred_element_type=jnp.float32)
    return jnp.where(half_mask(block.shape, 1, 0), outs[0], outs[1]) * DH**-0.5


def backward_kernel(
    latents, gains, conditioning, cotangent,
    in_parts, in_last, in_resid_one, in_resid_two, in_qkv, in_attn_out, in_cross, in_keyval_w, in_rows_one, in_rows_two,
    in_rotated, in_attended, in_logs, in_query, in_keyval, in_crossed, in_cross_logs, in_tables,
    block_out, grad_latents, grad_context, grad_gains, grad_qkv, grad_attn_out, grad_cross_q, grad_keyval,
    grad_cross_out,
    parts, rows_two, seed_one, seed_two, w_qkv, w_attn_out, w_cross, w_keyval, rotated, attended, crossed, query,
    d_attended, logs, keys_t, values_t, d_keys_t, d_values_t, cross_keys_t, cross_values_t, d_cross_keys_t,
    d_cross_values_t, keyval, d_keyval, context, context_sum, context_got, resid, d_resid, tables,
    gain_rows, gain_got, got_one, got_two, core_qkv, core_attn_out, core_cross, core_keyval,
    extra_qkv, extra_attn_out, extra_cross, extra_keyval, far_qkv, far_attn_out, far_cross, far_keyval,
    sum_keyval, sum_last, out_qkv, out_keyval,
    send, recv, local,
):
    low = jnp.bfloat16
    width = attended.shape[1]
    pairs = width // PAIR
    model = latents.shape[1]
    links = Links(send, recv, local)
    load_parts = [links.store(in_parts.at[block], parts.at[block]) for block in (3, 1, 2, 0)]
    load_resid = links.store(in_resid_two, resid)
    load_cross = [
        links.store(source, target)
        for source, target in (
            (in_cross, w_cross), (in_keyval, keyval), (in_query, query), (in_crossed, crossed), (in_cross_logs, logs),
        )
    ]
    load_mid = [links.store(in_rows_two, rows_two), links.store(in_keyval_w, w_keyval)]
    load_self = [
        links.store(source, target)
        for source, target in (
            (in_attn_out, w_attn_out), (in_rotated, rotated), (in_attended, attended), (in_tables, tables),
            (in_qkv, w_qkv),
        )
    ]
    links.greet([(1, 0), (2, 0), (4, 0), (6, 0), (0, 1), (0, 2)])
    sums_one = Sums(links, parts, *got_one)
    for load, block in zip(load_parts, (3, 1, 2, 0)):
        links.settle(load)
        sums_one.ready(block)
    gain_rows[...] = jnp.zeros_like(gain_rows)
    context[...] = jnp.zeros_like(context)
    context[:CTX] = conditioning[0]
    links.settle(load_resid)
    for load in load_cross:
        links.settle(load)
    for pair in range(pairs):
        at = slice(pair * PAIR, (pair + 1) * PAIR)
        cross_keys_t[pair] = keyval[0, :, at].astype(jnp.float32).T.astype(low)
        cross_values_t[pair] = keyval[1, :, at].astype(jnp.float32).T.astype(low)
    d_cross_keys_t[...] = jnp.zeros_like(d_cross_keys_t)
    d_cross_values_t[...] = jnp.zeros_like(d_cross_values_t)
    d_keys_t[...] = jnp.zeros_like(d_keys_t)
    d_values_t[...] = jnp.zeros_like(d_values_t)
    sums_one.add()
    sums_one.arrive()

    def norm_back(which, values, sums):
        def step(rows):
            gain = gains[which : which + 1]
            _, scaled, inverse = layer_norm(values[rows].astype(jnp.float32), gain)
            d_normed = parts[0, rows].astype(jnp.float32) + sums.total(rows)
            d_part, gain_grad = norm_backward(d_normed, scaled, inverse, gain)
            gain_rows[which : which + 1] += gain_grad[None]
            earlier = cotangent[rows].astype(jnp.float32) if which == 2 else d_resid[rows]
            d_resid[rows] = earlier + d_part
            if which > 0:
                (seed_one if which == 2 else seed_two)[0, rows] = d_resid[rows].astype(low)

        row_steps(BLOCK, step)

    norm_back(2, resid, sums_one)
    spread_one = Spread(links, seed_one)
    load_resid = links.store(in_resid_one, resid)
    sums_one.sent()

    def back_project(source, weight, block, sums):
        def project(cols):
            parts[block, :, cols] = dot_cols(source, weight(cols)).astype(low)

        columns(model, 512, project)
        sums.ready(block)

    sums_two = Sums(links, parts, *got_two)
    for block in range(4):
        spread_one.wait(block)
        rows = block_rows(block)
        d_crossed = dot_plain(seed_one[block], w_cross[:, width:]).astype(low)
        for pair in range(pairs):
            at = slice(pair * PAIR, (pair + 1) * PAIR)
            out = attend_rows_back(
                query[rows, at] * low(DH**-0.5), d_crossed[:, at], logs[rows, at], cross_keys_t[pair],
                cross_values_t[pair], keyval[0, :, at], d_cross_keys_t.at[pair], d_cross_values_t.at[pair], CTX,
            )
            query[rows, at] = out.astype(low)
        back_project(query[rows], lambda cols: w_cross[cols, :width], block, sums_two)
    sums_two.add()
    load_logs = links.store(in_logs, logs)
    for load in load_mid:
        links.settle(load)

    def whole(rows, cols):
        return rows[:, :, cols].reshape(LENGTH, -1)

    def grads_into(target, rows, cols, right):
        def product(part):
            target[part, cols] = dot_rows(whole(rows, part), right).astype(low)

        columns(model, 384, product)

    for pair in range(pairs):
        at = slice(pair * PAIR, (pair + 1) * PAIR)
        d_keyval[:, at] = d_cross_keys_t[pair].T.astype(low)
        d_keyval[:, width + pair * PAIR : width + (pair + 1) * PAIR] = d_cross_values_t[pair].T.astype(low)
    context_sum[...] = dot_cols(d_keyval[...], w_keyval[...]).astype(low)
    context_near = links.go(context_sum, context_got.at[0], 0, 1)
    w_keyval[...] = dot_rows(context[...], d_keyval[...]).astype(low)
    scatter_keyval = Scatter(links, w_keyval, core_keyval, extra_keyval, far_keyval, 1)
    scatter_keyval.pair_up()
    grads_into(w_cross, rows_two, slice(0, width), query[...])
    grads_into(w_cross, seed_one, slice(width, 2 * width), crossed[...])
    scatter_cross = Scatter(links, w_cross, core_cross, extra_cross, far_cross, 1)
    scatter_cross.pair_up()
    links.settle(load_resid)
    context_near.wait_recv()
    links.settle_sends((context_near,))
    context_sum[...] = (context_sum[...].astype(jnp.float32) + context_got[0].astype(jnp.float32)).astype(low)
    scatter_keyval.combine()
    scatter_cross.combine()
    load_last = links.store(in_last, rows_two)
    sums_two.arrive()
    norm_back(1, resid, sums_two)
    spread_two = Spread(links, seed_two)
    sums_two.sent()
    spread_one.sent()
    load_rows = links.store(in_rows_one, seed_one)
    context_far = links.go(context_sum, context_got.at[1], 0, 2)
    for load in load_self:
        links.settle(load)
    links.settle(load_logs)
    for pair in range(pairs):
        key = rotated[:, width + pair * PAIR : width + (pair + 1) * PAIR]
        value = rotated[:, 2 * width + pair * PAIR : 2 * width + (pair + 1) * PAIR]
        keys_t[pair] = key.astype(jnp.float32).T.astype(low)
        values_t[pair] = value.astype(jnp.float32).T.astype(low)
    cosine, sine = (tables.at[part] for part in range(2))
    sums_last = Sums(links, rows_two, *got_one)

    for block in range(4):
        spread_two.wait(block)
        rows = block_rows(block)
        d_attended[rows] = dot_plain(seed_two[block], w_attn_out[...]).astype(low)
        turn = (cosine[rows], -sine[rows])

        def one_pair(pair, carry):
            at = pl.ds(pl.multiple_of(pair * PAIR, PAIR), PAIR)
            keys_at = pl.ds(pl.multiple_of(width + pair * PAIR, PAIR), PAIR)
            out = attend_rows_back(
                rotated[rows, at] * low(DH**-0.5), d_attended[rows, at], logs[rows, at], keys_t[pair],
                values_t[pair], rotated[:, keys_at], d_keys_t.at[pair], d_values_t.at[pair], None,
            )
            rotated[rows, at] = head_turn(out, *turn).astype(low)
            return carry

        lax.fori_loop(0, pairs, one_pair, 0)
        if block == 0:
            scatter_keyval.relay()
        if block == 1:
            scatter_cross.relay()
        if block == 2:
            links.settle(load_last)
            for last in (3, 1, 2):
                sums_last.ready(last)
    grads_into(w_attn_out, seed_two, slice(None), attended[...])
    scatter_attn_out = Scatter(links, w_attn_out, core_attn_out, extra_attn_out, far_attn_out, 1)
    scatter_attn_out.pair_up()
    for pair in range(pairs):
        for block in range(4):
            rows = block_rows(block)
            turn = (cosine[rows], -sine[rows])
            at = slice(width + pair * PAIR, width + (pair + 1) * PAIR)
            rotated[rows, at] = head_turn(d_keys_t[pair, :, rows].T, *turn).astype(low)
            at = slice(2 * width + pair * PAIR, 2 * width + (pair + 1) * PAIR)
            rotated[rows, at] = d_values_t[pair, :, rows].T.astype(low)
    sums_last.add()
    sums_three = Sums(links, parts, *got_two)
    for block in (3, 1, 2, 0):
        back_project(rotated[block_rows(block)], lambda cols: w_qkv[cols, :], block, sums_three)
    links.settle(load_rows)
    scatter_attn_out.combine()
    grads_into(w_qkv, seed_one, slice(None), rotated[...])
    scatter_qkv = Scatter(links, w_qkv, core_qkv, extra_qkv, far_qkv, 1)
    scatter_qkv.pair_up()
    sums_three.add()
    scatter_qkv.combine()
    load_resid = links.store(in_resid_two, resid)
    sums_last.arrive()
    links.settle(load_resid)

    def add_last(rows):
        resid[rows] += rows_two[0, rows].astype(jnp.float32) + sums_last.total(rows)

    row_steps(BLOCK, add_last)
    links.store(resid, block_out)
    context_far.wait_recv()
    context_total = context_sum[...].astype(jnp.float32) + context_got[1].astype(jnp.float32)
    grad_context[0] = context_total[:CTX]
    scatter_attn_out.relay()
    scatter_keyval.arrive()
    scatter_keyval.total(sum_keyval, slice(None))
    heads = width // DH
    for head in range(heads):
        pieces = [sum_keyval[:, start + head * DH : start + (head + 1) * DH] for start in (0, width)]
        out_keyval[:, 2 * head * DH : 2 * (head + 1) * DH] = jnp.concatenate(pieces, axis=1)
    links.store(out_keyval, grad_keyval)
    scatter_cross.arrive()
    share = out_qkv.shape[0]
    spot = [logs.at[pl.ds(step * share, share)] for step in range(5)]
    qkv_spot = spot[3:5] + [sum_last]
    scatter_cross.total(spot[0], slice(0, width))
    links.store(spot[0], grad_cross_q)
    scatter_cross.total(spot[1], slice(width, 2 * width))
    links.store(spot[1], grad_cross_out)
    sums_three.arrive()
    norm_back(0, latents, sums_three)
    links.store(d_resid, grad_latents)
    for step, (dp_bit, tensor_bit) in enumerate(((1, 0), (0, 1), (0, 2), (2, 0), (4, 0))):
        trade = links.remote(gain_rows, gain_got.at[step], dp_bit, tensor_bit)
        trade.start()
        if step == 2:
            scatter_qkv.relay()
        trade.wait()
        gain_rows[...] += gain_got[step]
    grad_gains[...] = gain_rows[...]
    scatter_attn_out.arrive()
    scatter_attn_out.total(spot[2], slice(None))
    links.store(spot[2], grad_attn_out)
    scatter_qkv.arrive()
    for part in range(3):
        scatter_qkv.total(qkv_spot[part], slice(part * width, (part + 1) * width))
    for pair in range(pairs):
        heads_of = [qkv_spot[part][:, (2 * pair + which) * DH : (2 * pair + which + 1) * DH] for which in range(2) for part in range(3)]
        for step in range(3):
            start = (3 * pair + step) * PAIR
            out_qkv[:, start : start + PAIR] = jnp.concatenate(heads_of[2 * step : 2 * step + 2], axis=1)
    links.store(out_qkv, grad_qkv)
    links.finish()
    for scatter in (scatter_keyval, scatter_cross, scatter_attn_out, scatter_qkv):
        scatter.finish()


def backward_part(latents, gains, conditioning, cotangent, parts, last, kept):
    (
        resid_one, resid_two, w_qkv, w_attn_out, w_cross, w_keyval, rows_one, rows_two, rotated, attended, logs, query,
        keyval, crossed, cross_logs, tables,
    ) = kept
    model = latents.shape[1]
    depth = conditioning.shape[2]
    wide = w_qkv.shape[1]
    width = wide // 3
    pairs = width // PAIR
    members = lax.axis_size("dp")
    share, span = model // members, depth // members
    low, high = jnp.bfloat16, jnp.float32
    outs = [
        ((BLOCK, model), high),
        ((BLOCK, model), high),
        (conditioning.shape, high),
        ((8, model), high),
        ((share, wide), high),
        ((share, width), high),
        ((share, width), high),
        ((span, 2 * width), high),
        ((share, width), high),
    ]
    work = [
        ((4, BLOCK, model), low),
        ((4, BLOCK, model), low),
        ((4, BLOCK, model), low),
        ((4, BLOCK, model), low),
        ((model, wide), low),
        ((model, width), low),
        ((model, 2 * width), low),
        ((depth, 2 * width), low),
        ((LENGTH, wide), low),
        ((LENGTH, width), low),
        ((LENGTH, width), low),
        ((LENGTH, width), low),
        ((LENGTH, width), low),
        ((LENGTH, width), high),
        ((pairs, PAIR, LENGTH), low),
        ((pairs, PAIR, LENGTH), low),
        ((pairs, PAIR, LENGTH), high),
        ((pairs, PAIR, LENGTH), high),
        ((pairs, PAIR, FULL), low),
        ((pairs, PAIR, FULL), low),
        ((pairs, PAIR, FULL), high),
        ((pairs, PAIR, FULL), high),
        ((2, FULL, width), low),
        ((FULL, 2 * width), low),
        ((FULL, depth), low),
        ((FULL, depth), low),
        ((2, FULL, depth), low),
        ((BLOCK, model), high),
        ((BLOCK, model), high),
        ((2, LENGTH, PAIR), high),
        ((8, model), high),
        ((5, 8, model), high),
    ]
    groups = [(share, wide), (share, width), (share, 2 * width), (span, 2 * width)]
    scratch = [pltpu.VMEM(*buffer) for buffer in work] + [sum_buffers(model), sum_buffers(model)]
    scratch += [pltpu.VMEM((4, *group), low) for group in groups]
    scratch += [pltpu.VMEM(group, low) for group in groups]
    scratch += [pltpu.VMEM((3, *group), low) for group in groups]
    scratch += [pltpu.VMEM(groups[3], high), pltpu.VMEM((share, width), high)]
    scratch += [pltpu.VMEM(shape, high) for shape in ((share, wide), (span, 2 * width))]
    scratch += [pltpu.SemaphoreType.DMA((96,)), pltpu.SemaphoreType.DMA((96,)), pltpu.SemaphoreType.DMA((48,))]
    return pl.pallas_call(
        backward_kernel,
        out_shape=[jax.ShapeDtypeStruct(*out) for out in outs],
        in_specs=[whole_vmem()] * 4 + [anywhere()] * 18,
        out_specs=[anywhere()] * 2 + [whole_vmem()] * 2 + [anywhere()] * 5,
        scratch_shapes=scratch,
        compiler_params=pltpu.CompilerParams(collective_id=2, has_side_effects=True, vmem_limit_bytes=VMEM_BYTES),
        cost_estimate=pl.CostEstimate(flops=2**37, bytes_accessed=2**26, transcendentals=2**23),
    )(
        latents, gains, conditioning, cotangent, parts, last, resid_one, resid_two, w_qkv, w_attn_out, w_cross,
        w_keyval, rows_one, rows_two, rotated, attended, logs, query, keyval, crossed, cross_logs, tables,
    )


def per_device(
    latents,
    conditioning,
    gain_attn,
    w_qkv,
    w_attn_out,
    gain_cross,
    w_cross_q,
    w_cross_kv,
    w_cross_out,
    gain_mlp,
    w_gate,
    w_up,
    w_down,
    cotangent,
):
    low = jnp.bfloat16
    hidden_wide = w_gate.shape[1]
    gains = jnp.stack([gain_attn, gain_cross, gain_mlp])
    (
        rows_one, rows_two, rows_three, mlp_seed, qkv_all, attn_out_t, cross_all, cross_kv, mlp_all, down_all,
        rotated, attended, logs, cross_query, keyval, crossed, cross_logs, resid_one, resid_two, tables,
    ) = forward_part(
        latents,
        gains,
        conditioning,
        (w_qkv, w_attn_out.T, w_cross_q, w_cross_kv, w_cross_out.T, w_gate, w_up, w_down.T),
        cotangent,
    )
    rows_three, mlp_seed = (array.reshape(LENGTH, -1) for array in (rows_three, mlp_seed))
    both = dot_plain(rows_three, mlp_all)
    gate_pre, up_pre = both[:, :hidden_wide], both[:, hidden_wide:]
    sigma_gate = jax.nn.sigmoid(gate_pre)
    swish = gate_pre * sigma_gate
    hidden = (swish * up_pre).astype(low)
    sum_down = dp_sum(dot_rows(mlp_seed, hidden))
    d_hidden = dot_plain(mlp_seed, down_all)
    d_gate = (d_hidden * up_pre * sigma_gate * (1.0 + gate_pre * (1.0 - sigma_gate))).astype(low)
    d_up = (d_hidden * swish).astype(low)
    d_both = jnp.concatenate([d_gate, d_up], axis=1)
    sum_mlp = dp_sum(dot_rows(rows_three, d_both))
    block_shape = (4, latents.shape[0], -1)
    parts = dot_cols(d_both, mlp_all).astype(low).reshape(block_shape)
    last = dot_cols(hidden, down_all).astype(low).reshape(block_shape)
    kept = (
        resid_one, resid_two, qkv_all, attn_out_t, cross_all, cross_kv, rows_one, rows_two, rotated, attended, logs,
        cross_query, keyval, crossed, cross_logs, tables,
    )
    (
        block_out, grad_latents, grad_context, grad_gains, grad_qkv, grad_attn_out, grad_cross_q, grad_cross_kv,
        grad_cross_out,
    ) = backward_part(latents, gains, conditioning, cotangent, parts, last, kept)
    return (
        block_out,
        grad_latents,
        grad_context,
        grad_gains[0],
        grad_qkv,
        grad_attn_out.T,
        grad_gains[1],
        grad_cross_q,
        grad_cross_kv,
        grad_cross_out.T,
        grad_gains[2],
        sum_mlp[:, :hidden_wide].astype(jnp.float32),
        sum_mlp[:, hidden_wide:].astype(jnp.float32),
        sum_down.astype(jnp.float32).T,
    )


def per_device_general(
    latents,
    conditioning,
    gain_attn,
    w_qkv,
    w_attn_out,
    gain_cross,
    w_cross_q,
    w_cross_kv,
    w_cross_out,
    gain_mlp,
    w_gate,
    w_up,
    w_down,
    cotangent,
):
    low = jnp.bfloat16
    heads_wide = w_cross_q.shape[1]
    hidden_wide = w_gate.shape[1]
    resid_in = latents.astype(jnp.float32)
    normed_one, scaled_one, inverse_one = layer_norm(resid_in, gain_attn)
    rows_one = spread_rows(normed_one.astype(low))
    own_qkv = by_part(w_qkv.astype(low), 3)
    qkv_all = lax.all_gather(own_qkv, "dp", axis=0, tiled=True)
    own_kv = by_part(w_cross_kv.astype(low), 2)
    own_kv = jnp.concatenate([own_kv[:, :heads_wide], own_kv[:, heads_wide:]], axis=0)
    own_mid = jnp.concatenate(
        [w_attn_out.astype(low).T, w_cross_q.astype(low), w_cross_out.astype(low).T, own_kv], axis=1
    )
    mid_all = lax.all_gather(after(own_mid, qkv_all), "dp", axis=0, tiled=True)
    own_mlp = jnp.concatenate([w_gate.astype(low), w_up.astype(low)], axis=1)
    mlp_all = lax.all_gather(after(own_mlp, mid_all), "dp", axis=0, tiled=True)
    down_all = lax.all_gather(after(w_down.astype(low).T, mlp_all), "dp", axis=0, tiled=True)
    attn_out_t, cross_q, cross_out_t = (mid_all[:, part * heads_wide : (part + 1) * heads_wide] for part in range(3))
    model = mid_all.shape[0]
    cross_kv = (
        mid_all[:, 3 * heads_wide :]
        .reshape(lax.axis_size("dp"), 2, -1, heads_wide)
        .transpose(0, 2, 1, 3)
        .reshape(model // 2, 2 * heads_wide)
    )

    tables = turn_tables(group_positions(latents.shape[0]))
    packed = dot_plain(rows_one, qkv_all)
    attended, rotated, logs = attend(pad_heads(packed, 3), tables)
    attended = attended[:, :heads_wide]
    resid_one = resid_in + sum_rows(dot_cols(attended, attn_out_t))
    normed_two, scaled_two, inverse_two = layer_norm(resid_one, gain_cross)
    rows_two = spread_rows(normed_two.astype(low))
    head_shape = (-1, heads_wide // DH, DH)
    cross_query = dot_plain(rows_two, cross_q).astype(low).reshape(head_shape)
    context = conditioning.reshape(CTX, conditioning.shape[2])
    cross_pack = dot_plain(context, cross_kv).astype(low)
    cross_key = cross_pack[:, :heads_wide].reshape(head_shape)
    cross_value = cross_pack[:, heads_wide:].reshape(head_shape)
    crossed, cross_logs = cross_forward(cross_query, cross_key, cross_value)
    crossed = crossed.reshape(-1, heads_wide).astype(low)
    resid_two = resid_one + sum_rows(dot_cols(crossed, cross_out_t))
    normed_three, scaled_three, inverse_three = layer_norm(resid_two, gain_mlp)
    rows_three = spread_rows(normed_three.astype(low))
    mlp_seed = spread_rows(cotangent)
    both = dot_plain(rows_three, mlp_all)
    gate_pre, up_pre = both[:, :hidden_wide], both[:, hidden_wide:]
    sigma_gate = jax.nn.sigmoid(gate_pre)
    swish = gate_pre * sigma_gate
    hidden = (swish * up_pre).astype(low)
    sum_down = dp_sum(dot_rows(mlp_seed, hidden))
    d_hidden = dot_plain(mlp_seed, down_all)
    d_gate = (d_hidden * up_pre * sigma_gate * (1.0 + gate_pre * (1.0 - sigma_gate))).astype(low)
    d_up = (d_hidden * swish).astype(low)
    d_both = jnp.concatenate([d_gate, d_up], axis=1)
    sum_mlp = dp_sum(after(dot_rows(rows_three, d_both), sum_down))
    d_normed = sum_rows(dot_cols(d_both, mlp_all))
    d_part, gain_grad_three = norm_backward(d_normed, scaled_three, inverse_three, gain_mlp)
    d_resid = cotangent.astype(jnp.float32) + d_part
    block_out = resid_two + sum_rows(dot_cols(hidden, down_all))
    cross_seed = spread_rows(d_resid.astype(low))
    grad_cross_out = dot_rows(cross_seed, crossed)
    d_crossed = dot_plain(cross_seed, cross_out_t).astype(low).reshape(head_shape)
    d_query, d_key, d_value = cross_backward(cross_query, cross_key, cross_value, d_crossed, cross_logs)
    d_query = d_query.reshape(-1, heads_wide).astype(low)
    d_keyval = jnp.concatenate([d_key.reshape(CTX, -1), d_value.reshape(CTX, -1)], axis=1).astype(low)
    grad_cross_q = dot_rows(rows_two, d_query)
    grad_cross_kv = dot_rows(context, d_keyval)
    context_part = dot_cols(d_keyval, cross_kv)
    d_normed = sum_rows(dot_cols(d_query, cross_q))
    d_part, gain_grad_two = norm_backward(d_normed, scaled_two, inverse_two, gain_cross)
    d_resid = d_resid + d_part
    self_seed = spread_rows(d_resid.astype(low))
    grad_attn_out = dot_rows(self_seed, attended)
    grad_kv = (
        grad_cross_kv.astype(low)
        .reshape(lax.axis_size("dp"), -1, 2, heads_wide)
        .transpose(0, 2, 1, 3)
        .reshape(model, heads_wide)
    )
    grad_mid = jnp.concatenate([grad_attn_out.astype(low), grad_cross_q.astype(low), grad_cross_out.astype(low), grad_kv], axis=1)
    sum_mid = dp_sum(after(grad_mid, sum_mlp))
    d_attended = dot_plain(self_seed, attn_out_t).astype(low)
    d_packed = drop_heads(attend_back(rotated, pad_heads(d_attended, 1), logs, tables), 3, packed.shape[1])
    sum_qkv = dp_sum(after(dot_rows(rows_one, d_packed), sum_mid))
    d_normed = sum_rows(dot_cols(d_packed, qkv_all))
    d_part, gain_grad_one = norm_backward(d_normed, scaled_one, inverse_one, gain_attn)
    grad_latents = d_resid + d_part
    grad_context = (
        lax.psum(context_part.astype(low), "tensor").astype(jnp.float32).reshape(conditioning.shape)
    )
    gains = lax.psum(jnp.stack([gain_grad_one, gain_grad_two, gain_grad_three]), ("dp", "tensor"))
    sums = [sum_mid[:, part * heads_wide : (part + 1) * heads_wide].astype(jnp.float32) for part in range(4)]
    half = sums[3].shape[0] // 2
    sum_kv = jnp.concatenate([sums[3][:half], sums[3][half:]], axis=1)
    return (
        block_out,
        grad_latents,
        grad_context,
        gains[0],
        by_head(sum_qkv, 3).astype(jnp.float32),
        sums[0].T,
        gains[1],
        sums[1],
        by_head(sum_kv, 2),
        sums[2].T,
        gains[2],
        sum_mlp[:, :hidden_wide].astype(jnp.float32),
        sum_mlp[:, hidden_wide:].astype(jnp.float32),
        sum_down.astype(jnp.float32).T,
    )


def solution(mesh):
    in_specs = (
        P(("dp", "tensor"), None),
        P("dp", None, None),
        P(),
        P("dp", "tensor"),
        P("tensor", "dp"),
        P(),
        P("dp", "tensor"),
        P("dp", "tensor"),
        P("tensor", "dp"),
        P(),
        P("dp", "tensor"),
        P("dp", "tensor"),
        P("tensor", "dp"),
        P(("dp", "tensor"), None),
    )
    out_specs = (
        P(("dp", "tensor"), None),
        P(("dp", "tensor"), None),
        P("dp", None, None),
        P(),
        P("dp", "tensor"),
        P("tensor", "dp"),
        P(),
        P("dp", "tensor"),
        P("dp", "tensor"),
        P("tensor", "dp"),
        P(),
        P("dp", "tensor"),
        P("dp", "tensor"),
        P("tensor", "dp"),
    )
    special = dict(mesh.shape) == {"dp": 8, "tensor": 4}
    return jax.shard_map(
        per_device if special else per_device_general, mesh=mesh, in_specs=in_specs, out_specs=out_specs, check_vma=False
    )
```

```python
import math
from functools import reduce

import jax
import jax.numpy as jnp
from jax import lax
from jax.experimental import pallas as pl
from jax.experimental.pallas import tpu as pltpu
from jax.sharding import PartitionSpec as P

DH = 64
CTX = 130
LENGTH = 1024
PAIR = 2 * DH
ROWS = 256
VMEM_BYTES = 62 * 2**20

norm_eps = 1e-05
rope_base = 10000.0


def head_turn(values, cosine, sine):
    quarter = DH // 4
    ahead = pltpu.roll(values, PAIR - quarter, 1)
    behind = pltpu.roll(values, quarter, 1)
    lane = lax.broadcasted_iota(jnp.int32, values.shape, 1) % DH
    return values * cosine + jnp.where(lane < quarter, -ahead, behind) * sine


def half_mask(shape, axis, which):
    place = lax.broadcasted_iota(jnp.int32, shape, axis)
    return (place >= DH) if which else (place < DH)


def attend_kernel(q_ref, k_ref, v_ref, cos_ref, sin_ref, out_ref, rot_ref, log_ref, kt_ref, vm_ref):
    pairs = pl.num_programs(0)
    pair = pl.program_id(0)
    turn = (cos_ref[...], sin_ref[...])
    query = head_turn(q_ref[...], *turn).astype(jnp.bfloat16)
    key = head_turn(k_ref[...], *turn).astype(jnp.bfloat16)
    value = v_ref[...].astype(jnp.bfloat16)
    for part, array in enumerate((query, key, value)):
        start = pl.multiple_of((part * pairs + pair) * PAIR, PAIR)
        rot_ref[:, pl.ds(start, PAIR)] = array
    key_t = key.astype(jnp.float32).T
    for which in range(2):
        kt_ref[which] = jnp.where(half_mask(key_t.shape, 0, which), key_t, 0.0).astype(jnp.bfloat16)
        vm_ref[which] = jnp.where(half_mask(value.shape, 1, which), value.astype(jnp.float32), 0.0).astype(jnp.bfloat16)
    q_start = pl.multiple_of(pair * PAIR, PAIR)

    def one_block(step, carry):
        rows = pl.ds(pl.multiple_of(step * ROWS, ROWS), ROWS)
        block = rot_ref[rows, pl.ds(q_start, PAIR)] * jnp.bfloat16(DH**-0.5)
        outs, logs = [], []
        for which in range(2):
            scores = jnp.dot(block, kt_ref[which], preferred_element_type=jnp.float32)
            peak = jnp.max(scores, axis=1, keepdims=True)
            shifted = jnp.exp(scores - peak)
            total = jnp.sum(shifted, axis=1, keepdims=True)
            product = jnp.dot(shifted.astype(jnp.bfloat16), vm_ref[which], preferred_element_type=jnp.float32)
            outs.append(product * (1.0 / total))
            logs.append(peak + jnp.log(total))
        out_ref[rows, :] = (outs[0] + outs[1]).astype(jnp.bfloat16)
        low = half_mask((ROWS, PAIR), 1, 0)
        log_ref[rows, :] = jnp.where(low, logs[0], logs[1])
        return carry

    lax.fori_loop(0, LENGTH // ROWS, one_block, 0)


def attend_back_kernel(
    q_ref, k_ref, v_ref, grad_ref, log_ref, cos_ref, sin_ref, out_ref,
    kt_ref, vt_ref, km_ref, qt_ref, gt_ref, dq_ref, dk_ref, dv_ref,
):
    pairs = pl.num_programs(0)
    pair = pl.program_id(0)
    key_t = k_ref[...].astype(jnp.float32).T
    value_t = v_ref[...].astype(jnp.float32).T
    for which in range(2):
        keep = half_mask(key_t.shape, 0, which)
        kt_ref[which] = jnp.where(keep, key_t, 0.0).astype(jnp.bfloat16)
        vt_ref[which] = jnp.where(keep, value_t, 0.0).astype(jnp.bfloat16)
        key = k_ref[...].astype(jnp.float32)
        km_ref[which] = jnp.where(half_mask(key.shape, 1, which), key, 0.0).astype(jnp.bfloat16)
    qt_ref[...] = (q_ref[...].astype(jnp.float32) * DH**-0.5).T.astype(jnp.bfloat16)
    gt_ref[...] = grad_ref[...].astype(jnp.float32).T.astype(jnp.bfloat16)
    dk_ref[...] = jnp.zeros_like(dk_ref)
    dv_ref[...] = jnp.zeros_like(dv_ref)

    def one_block(step, carry):
        rows = pl.ds(pl.multiple_of(step * ROWS, ROWS), ROWS)
        block = q_ref[rows, :] * jnp.bfloat16(DH**-0.5)
        grads = grad_ref[rows, :]
        d_query = jnp.zeros((ROWS, PAIR), jnp.float32)
        for which in range(2):
            half = slice(which * DH, (which + 1) * DH)
            scores = jnp.dot(block, kt_ref[which], preferred_element_type=jnp.float32)
            probs = jnp.exp(scores - log_ref[rows, which * DH : which * DH + 1])
            d_prob = jnp.dot(grads, vt_ref[which], preferred_element_type=jnp.float32)
            center = jnp.sum(probs * d_prob, axis=1, keepdims=True)
            d_score = (probs * (d_prob - center)).astype(jnp.bfloat16)
            d_query += jnp.dot(d_score, km_ref[which], preferred_element_type=jnp.float32)
            dk_ref[half, :] += jnp.dot(qt_ref[half, rows], d_score, preferred_element_type=jnp.float32)
            dv_ref[half, :] += jnp.dot(
                gt_ref[half, rows], probs.astype(jnp.bfloat16), preferred_element_type=jnp.float32
            )
        dq_ref[rows, :] = d_query * DH**-0.5
        return carry

    lax.fori_loop(0, LENGTH // ROWS, one_block, 0)
    turn = (cos_ref[...], -sin_ref[...])
    results = (head_turn(dq_ref[...], *turn), head_turn(dk_ref[...].T, *turn), dv_ref[...].T)
    for part, array in enumerate(results):
        start = pl.multiple_of((part * pairs + pair) * PAIR, PAIR)
        out_ref[:, pl.ds(start, PAIR)] = array.astype(jnp.bfloat16)


def column_block(offset):
    return pl.BlockSpec((LENGTH, PAIR), lambda pair: (0, pair + offset))


def whole_block(columns):
    return pl.BlockSpec((LENGTH, columns), lambda pair: (0, 0))


def attend(packed, tables):
    columns = packed.shape[1]
    pairs = columns // (3 * PAIR)
    return pl.pallas_call(
        attend_kernel,
        grid=(pairs,),
        in_specs=[column_block(part * pairs) for part in range(3)] + [whole_block(PAIR)] * 2,
        out_specs=[column_block(0), whole_block(columns), column_block(0)],
        out_shape=[
            jax.ShapeDtypeStruct((LENGTH, pairs * PAIR), jnp.bfloat16),
            jax.ShapeDtypeStruct((LENGTH, columns), jnp.bfloat16),
            jax.ShapeDtypeStruct((LENGTH, pairs * PAIR), jnp.float32),
        ],
        scratch_shapes=[pltpu.VMEM((2, PAIR, LENGTH), jnp.bfloat16), pltpu.VMEM((2, LENGTH, PAIR), jnp.bfloat16)],
        compiler_params=pltpu.CompilerParams(vmem_limit_bytes=VMEM_BYTES),
        cost_estimate=pl.CostEstimate(flops=pairs * 2**32, bytes_accessed=2**24, transcendentals=pairs * 2**21),
    )(packed, packed, packed, *tables)


def attend_back(rotated, d_attended, logs, tables):
    columns = rotated.shape[1]
    pairs = columns // (3 * PAIR)
    tall = pltpu.VMEM((PAIR, LENGTH), jnp.bfloat16)
    return pl.pallas_call(
        attend_back_kernel,
        grid=(pairs,),
        in_specs=[column_block(part * pairs) for part in range(3)]
        + [column_block(0), column_block(0)]
        + [whole_block(PAIR)] * 2,
        out_specs=whole_block(columns),
        out_shape=jax.ShapeDtypeStruct((LENGTH, columns), jnp.bfloat16),
        scratch_shapes=[
            pltpu.VMEM((2, PAIR, LENGTH), jnp.bfloat16),
            pltpu.VMEM((2, PAIR, LENGTH), jnp.bfloat16),
            pltpu.VMEM((2, LENGTH, PAIR), jnp.bfloat16),
            tall,
            tall,
            pltpu.VMEM((LENGTH, PAIR), jnp.float32),
            pltpu.VMEM((PAIR, LENGTH), jnp.float32),
            pltpu.VMEM((PAIR, LENGTH), jnp.float32),
        ],
        compiler_params=pltpu.CompilerParams(vmem_limit_bytes=VMEM_BYTES),
        cost_estimate=pl.CostEstimate(flops=pairs * 2**33, bytes_accessed=2**24, transcendentals=pairs * 2**21),
    )(rotated, rotated, rotated, d_attended, logs, *tables)


def turn_tables(positions):
    quarter = DH // 4
    frequency = jnp.exp(-jnp.log(rope_base) * jnp.arange(quarter).astype(jnp.float32) / quarter)
    angles = positions.astype(jnp.float32)[:, None] * frequency[None, :]
    cosine, sine = jnp.cos(angles), jnp.sin(angles)
    zeros, ones = jnp.zeros_like(sine), jnp.ones_like(sine)
    rows = (
        jnp.concatenate([cosine, cosine, ones, ones], axis=1),
        jnp.concatenate([sine, sine, zeros, zeros], axis=1),
    )
    return tuple(jnp.concatenate([row, row], axis=1) for row in rows)


def dot_plain(left_op, right_op):
    return jnp.dot(left_op, right_op, preferred_element_type=jnp.float32)


def dot_rows(left_op, right_op):
    return lax.dot_general(
        left_op, right_op, (((0,), (0,)), ((), ())), preferred_element_type=jnp.float32
    )


def dot_cols(left_op, right_op):
    return lax.dot_general(
        left_op, right_op, (((1,), (1,)), ((), ())), preferred_element_type=jnp.float32
    )


def layer_norm(values, gain_vec):
    center = values - jnp.mean(values, axis=-1, keepdims=True)
    spread = jnp.mean(center * center, axis=-1, keepdims=True)
    inverse = lax.rsqrt(spread + norm_eps)
    scaled = center * inverse
    return (scaled * gain_vec, scaled, inverse)


def norm_backward(upstream, scaled, inverse, gain_vec):
    weighted = upstream * gain_vec
    inner = jnp.mean(weighted, axis=-1, keepdims=True) + scaled * jnp.mean(
        weighted * scaled, axis=-1, keepdims=True
    )
    return (inverse * (weighted - inner), jnp.sum(upstream * scaled, axis=0))


def swap(values, bit):
    return lax.ppermute(values, "tensor", [(member, member ^ bit) for member in range(4)])


def spread_rows(values):
    if lax.axis_size("tensor") != 4:
        return lax.all_gather(values, "tensor", axis=0, tiled=True)
    half = values.shape[0] // 2
    near, far = swap(values, 1), swap(values, 2)
    return jnp.concatenate([values, near, far, swap(near[:half], 2), swap(far[half:], 1)], axis=0)


def sum_rows(partial):
    if lax.axis_size("tensor") != 4:
        return lax.psum_scatter(
            partial.astype(jnp.bfloat16), "tensor", scatter_dimension=0, tiled=True
        ).astype(jnp.float32)
    size = partial.shape[0] // 4
    half = size // 2
    own, near, far, last = (partial[part * size : (part + 1) * size] for part in range(4))
    first = swap(last[:half].astype(jnp.bfloat16), 1)
    second = swap(last[half:].astype(jnp.bfloat16), 2)
    far = jnp.concatenate([far[:half] + first.astype(jnp.float32), far[half:]], axis=0)
    near = jnp.concatenate([near[:half], near[half:] + second.astype(jnp.float32)], axis=0)
    return (
        own
        + swap(near.astype(jnp.bfloat16), 1).astype(jnp.float32)
        + swap(far.astype(jnp.bfloat16), 2).astype(jnp.float32)
    )


def group_positions(rows):
    group = lax.axis_size("tensor")
    blocks = jnp.arange(group)
    if group == 4:
        blocks = blocks ^ lax.axis_index("tensor")
    return (blocks[:, None] * rows + jnp.arange(rows)[None, :]).reshape(-1)


def cross_forward(queries, keys_in, values_in):
    scores = jnp.einsum("qhd,khd->hqk", queries, keys_in, preferred_element_type=jnp.float32) * DH ** (-0.5)
    peak_score = jnp.max(scores, axis=-1, keepdims=True)
    shifted = jnp.exp(scores - peak_score)
    totals = jnp.sum(shifted, axis=-1, keepdims=True)
    probabilities = (shifted / totals).astype(jnp.bfloat16)
    output = jnp.einsum("hqk,khd->qhd", probabilities, values_in, preferred_element_type=jnp.float32)
    return (output, peak_score + jnp.log(totals))


def cross_backward(queries, keys_in, values_in, d_output, log_totals):
    scaling = DH ** (-0.5)
    scores = jnp.einsum("qhd,khd->hqk", queries, keys_in, preferred_element_type=jnp.float32) * scaling
    probabilities = jnp.exp(scores - log_totals)
    d_prob = jnp.einsum("qhd,khd->hqk", d_output, values_in, preferred_element_type=jnp.float32)
    center = jnp.sum(probabilities * d_prob, axis=-1, keepdims=True)
    d_score = (probabilities * (d_prob - center)).astype(jnp.bfloat16)
    d_query = jnp.einsum("hqk,khd->qhd", d_score, keys_in, preferred_element_type=jnp.float32) * scaling
    d_key = jnp.einsum("hqk,qhd->khd", d_score, queries, preferred_element_type=jnp.float32) * scaling
    d_value = jnp.einsum(
        "hqk,qhd->khd", probabilities.astype(jnp.bfloat16), d_output, preferred_element_type=jnp.float32
    )
    return (d_query, d_key, d_value)


def by_part(columns, parts):
    rows = columns.shape[0]
    return columns.reshape(rows, -1, parts, DH).swapaxes(1, 2).reshape(rows, -1)


def by_head(columns, parts):
    rows = columns.shape[0]
    return columns.reshape(rows, parts, -1, DH).swapaxes(1, 2).reshape(rows, -1)


def pad_heads(columns, parts):
    rows, width = columns.shape
    each = width // parts
    if each % PAIR == 0:
        return columns
    return jnp.pad(columns.reshape(rows, parts, each), ((0, 0), (0, 0), (0, -each % PAIR))).reshape(rows, -1)


def drop_heads(columns, parts, width):
    rows = columns.shape[0]
    return columns.reshape(rows, parts, -1)[:, :, : width // parts].reshape(rows, width)


def dp_sum(grads):
    return lax.psum_scatter(grads.astype(jnp.bfloat16), "dp", scatter_dimension=0, tiled=True)


def after(value, earlier):
    return lax.optimization_barrier((value, earlier))[0]


MESH = pl.DeviceIdType.MESH
BLOCK = LENGTH // 4
HALF = BLOCK // 2
FULL = 160


class Links:
    def __init__(self, send, recv, local):
        self.send, self.recv, self.local = send, recv, local
        self.used = self.used_local = 0
        self.pending, self.pending_local = [], []
        self.dp, self.tensor = lax.axis_index("dp"), lax.axis_index("tensor")

    def remote(self, src, dst, dp_bit, tensor_bit):
        at = self.used
        self.used += 1
        return pltpu.make_async_remote_copy(
            src_ref=src,
            dst_ref=dst,
            send_sem=self.send.at[at],
            recv_sem=self.recv.at[at],
            device_id=(self.dp ^ dp_bit, self.tensor ^ tensor_bit),
            device_id_type=MESH,
        )

    def go(self, src, dst, dp_bit, tensor_bit):
        copy = self.remote(src, dst, dp_bit, tensor_bit)
        copy.start()
        self.pending.append(copy)
        return copy

    def store(self, src, dst):
        copy = pltpu.make_async_copy(src, dst, self.local.at[self.used_local])
        self.used_local += 1
        copy.start()
        self.pending_local.append(copy)
        return copy

    def settle(self, copy):
        copy.wait()
        self.pending_local = [other for other in self.pending_local if other is not copy]

    def settle_sends(self, copies):
        for copy in copies:
            copy.wait_send()
        self.pending = [copy for copy in self.pending if all(copy is not other for other in copies)]

    def greet(self, partners):
        barrier = pltpu.get_barrier_semaphore()
        for dp_bit, tensor_bit in partners:
            pl.semaphore_signal(
                barrier, inc=1, device_id=(self.dp ^ dp_bit, self.tensor ^ tensor_bit), device_id_type=MESH
            )
        pl.semaphore_wait(barrier, len(partners))

    def finish(self):
        for copy in self.pending:
            copy.wait_send()
        for copy in self.pending_local:
            copy.wait()


class Spread:
    def __init__(self, links, rows):
        self.links, self.rows = links, rows
        half = rows.shape[1] // 2
        self.low, self.high = pl.ds(0, half), pl.ds(half, half)
        self.near_low = links.go(rows.at[0, self.low], rows.at[1, self.low], 0, 1)
        self.far_high = links.go(rows.at[0, self.high], rows.at[2, self.high], 0, 2)
        self.near_high = links.go(rows.at[0, self.high], rows.at[1, self.high], 0, 1)
        self.far_low = links.go(rows.at[0, self.low], rows.at[2, self.low], 0, 2)
        self.stage = 0

    def wait(self, block):
        rows, links, low, high = self.rows, self.links, self.low, self.high
        if block >= 1 and self.stage == 0:
            self.near_low.wait_recv()
            self.last_low = links.go(rows.at[1, low], rows.at[3, low], 0, 2)
            self.far_high.wait_recv()
            self.last_high = links.go(rows.at[2, high], rows.at[3, high], 0, 1)
            self.near_high.wait_recv()
            self.stage = 1
        if block >= 2 and self.stage == 1:
            self.far_low.wait_recv()
            self.stage = 2
        if block >= 3 and self.stage == 2:
            self.last_low.wait_recv()
            self.last_high.wait_recv()
            self.stage = 3

    def sent(self):
        self.links.settle_sends(
            (self.near_low, self.far_high, self.near_high, self.far_low, self.last_low, self.last_high)
        )


class SpreadCross:
    def __init__(self, links, weights):
        self.links, self.weights = links, weights
        self.which = links.dp % 2
        self.near = links.go(self.half(0), self.half(1), 0, 1)
        self.far = links.go(self.half(0), self.half(2), 0, 2)
        self.core = [self.cross(0)]

    def half(self, member, places=slice(None)):
        return self.weights.at[member, places, self.which]

    def cross(self, member):
        return self.links.go(self.half(member), self.half(member), 1, 0)

    def pump(self):
        links = self.links
        first, second = pl.ds(0, 2), pl.ds(2, 2)
        self.near.wait_recv()
        self.last_low = links.go(self.half(1, first), self.half(3, first), 0, 2)
        self.core.append(self.cross(1))
        self.far.wait_recv()
        self.last_high = links.go(self.half(2, second), self.half(3, second), 0, 1)
        self.core.append(self.cross(2))

    def wait(self, member):
        if member == 3:
            self.last_low.wait_recv()
            self.last_high.wait_recv()
            self.core.append(self.cross(3))
        self.core[member].wait_recv()


class Gather:
    def __init__(self, links, shard, whole, both_cores=True):
        self.links, self.whole, self.both_cores = links, whole, both_cores
        self.size = shard.shape[0]
        self.place = links.dp // 2
        self.middle = (self.place == 1) | (self.place == 2)
        own = self.rows(0)
        self.own = links.store(shard, own)
        self.core = []
        self.pass_on(shard, own)
        self.beside = links.go(shard, own, 2, 0)
        self.skip = links.go(shard, own, 4, 0)
        self.third_at = links.used
        self.third = links.remote(shard, own, 6, 0)

        @pl.when(self.middle)
        def _():
            self.third.start()

    def pass_on(self, src, dst):
        if self.both_cores:
            self.core.append(self.links.go(src, dst, 1, 0))

    def rows(self, step):
        if len(self.whole.shape) == 4:
            return self.whole.at[self.place ^ step, self.links.dp % 2]
        start = pl.multiple_of((self.links.dp ^ (2 * step)) * self.size, self.size)
        return self.whole.at[pl.ds(start, self.size)]

    def forward(self):
        links = self.links
        block = self.rows(2)
        self.skip.wait_recv()
        self.onward = pltpu.make_async_remote_copy(
            src_ref=block,
            dst_ref=block,
            send_sem=links.send.at[links.used],
            recv_sem=links.recv.at[self.third_at],
            device_id=(links.dp ^ 2, links.tensor),
            device_id_type=MESH,
        )
        links.used += 1

        @pl.when(self.middle)
        def _():
            self.onward.start()

        self.pass_on(block, block)

    def arrive(self):
        links = self.links
        self.beside.wait_recv()
        block = self.rows(1)
        self.pass_on(block, block)
        self.third.wait_recv()
        block = self.rows(3)
        self.pass_on(block, block)
        links.settle(self.own)
        for copy in self.core:
            copy.wait_recv()

    def finish(self):
        @pl.when(self.middle)
        def _():
            self.third.wait_send()
            self.onward.wait_send()


class Sums:
    def __init__(self, links, parts, half_near, half_far, near, far):
        self.links, self.parts = links, parts
        self.half_near, self.half_far, self.near, self.far = half_near, half_far, near, far
        half = parts.shape[1] // 2
        self.low, self.high = pl.ds(0, half), pl.ds(half, half)

    def ready(self, block):
        links, parts, low, high = self.links, self.parts, self.low, self.high
        if block == 3:
            self.first = links.go(parts.at[3, low], self.half_near, 0, 1)
            self.second = links.go(parts.at[3, high], self.half_far, 0, 2)
        if block == 1:
            self.near_low = links.go(parts.at[1, low], self.near.at[low], 0, 1)
        if block == 2:
            self.far_high = links.go(parts.at[2, high], self.far.at[high], 0, 2)

    def add_half(self, block, start, got):
        def add(rows, from_rows):
            total = self.parts[block, rows].astype(jnp.float32) + got[from_rows].astype(jnp.float32)
            self.parts[block, rows] = total.astype(jnp.bfloat16)

        half = got.shape[0]
        step = math.gcd(half, 32)

        def body(index, carry):
            at = index * step if step == 1 else pl.multiple_of(index * step, step)
            add(pl.ds(start + at, step), pl.ds(at, step))
            return carry

        lax.fori_loop(0, half // step, body, 0)

    def add(self):
        links, parts, low, high = self.links, self.parts, self.low, self.high
        half = parts.shape[1] // 2
        self.first.wait_recv()
        self.add_half(2, 0, self.half_near)
        self.far_low = links.go(parts.at[2, low], self.far.at[low], 0, 2)
        self.second.wait_recv()
        self.add_half(1, half, self.half_far)
        self.near_high = links.go(parts.at[1, high], self.near.at[high], 0, 1)

    def arrive(self):
        for copy in (self.near_low, self.far_high, self.far_low, self.near_high):
            copy.wait_recv()

    def sent(self):
        self.links.settle_sends(
            (self.first, self.second, self.near_low, self.far_high, self.far_low, self.near_high)
        )

    def total(self, rows):
        return self.near[rows].astype(jnp.float32) + self.far[rows].astype(jnp.float32)
def columns(total, width, body):
    def step(index, carry):
        body(pl.ds(pl.multiple_of(index * width, width), width))
        return carry

    lax.fori_loop(0, total // width, step, 0)


def attend_rows(block, keys_t, values, limit):
    outs, logs = [], []
    for which in range(2):
        part = jnp.where(half_mask(block.shape, 1, which), block, jnp.zeros_like(block))
        scores = jnp.dot(part, keys_t, preferred_element_type=jnp.float32)
        if limit is not None:
            scores = jnp.where(lax.broadcasted_iota(jnp.int32, scores.shape, 1) < limit, scores, -jnp.inf)
        peak = jnp.max(scores, axis=1, keepdims=True)
        shifted = jnp.exp(scores - peak)
        total = jnp.sum(shifted, axis=1, keepdims=True)
        product = jnp.dot(shifted.astype(jnp.bfloat16), values, preferred_element_type=jnp.float32)
        outs.append(product * (1.0 / total))
        logs.append(peak + jnp.log(total))
    low = half_mask(block.shape, 1, 0)
    return jnp.where(low, outs[0], outs[1]), jnp.where(low, logs[0], logs[1])


def cross_tile(weights, member, place, cols):
    tile = weights[member, place, :, :, cols]
    return tile.reshape(-1, tile.shape[-1])


def cross_columns(weights, member, cols):
    whole = weights[member, :, :, :, cols]
    return whole.reshape(-1, whole.shape[-1])


def row_steps(total, body):
    def step(index, carry):
        body(pl.ds(pl.multiple_of(index * 32, 32), 32))
        return carry

    lax.fori_loop(0, total // 32, step, 0)


def block_rows(block):
    return pl.ds(block * BLOCK, BLOCK)


def two_heads(weights, part, parts, pair):
    starts = [((2 * pair + which) * parts + part) * DH for which in range(2)]
    return jnp.concatenate([weights[:, start : start + DH] for start in starts], axis=1).astype(jnp.bfloat16)


def fill_tables(cosine, sine, member):
    quarter = DH // 4
    shape = (BLOCK, PAIR)
    lane = lax.broadcasted_iota(jnp.int32, shape, 1) % DH
    frequency = jnp.exp((lane % quarter).astype(jnp.float32) * (-math.log(rope_base) / quarter))
    for block in range(4):
        place = (member ^ block) * BLOCK + lax.broadcasted_iota(jnp.int32, shape, 0)
        angle = place.astype(jnp.float32) * frequency
        rows = block_rows(block)
        cosine[rows] = jnp.where(lane < 2 * quarter, jnp.cos(angle), 1.0)
        sine[rows] = jnp.where(lane < 2 * quarter, jnp.sin(angle), 0.0)


def forward_kernel(
    latents, gains, conditioning, f32_qkv,
    f32_attn_out, f32_cross_q, f32_cross_kv, f32_cross_out, f32_gate, f32_up, f32_down, cotangent,
    rows_one_out, normed_two_out, rows_three_out, seeds_out, qkv_out, attn_out_out, cross_out, keyval_w_out, mlp_out,
    down_out, rotated_out, attended_out, logs_out,
    query_out, keyval_out, crossed_out, cross_logs_out, resid_one_out, resid_two_out, tables_out,
    rows_one, normed_two, rows_three, w_qkv, w_attn_out, w_cross, w_keyval, rotated, attended, logs, query, keyval,
    crossed, cross_logs, keys_t, parts, got_one, resid_one, resid_two,
    packed, tables, context, raw_attn_out, raw_cross_q, raw_cross_kv, raw_cross_out, raw_gate, raw_up, raw_down,
    own_qkv, own_attn_out, own_cross, own_keyval, own_mlp, own_down, send, recv, local,
):
    low = jnp.bfloat16
    pairs = attended.shape[1] // PAIR
    width = pairs * PAIR
    share = own_qkv.shape[0]
    links = Links(send, recv, local)
    loads = [
        links.store(source, target)
        for source, target in (
            (f32_attn_out, raw_attn_out), (f32_cross_q, raw_cross_q), (f32_cross_kv, raw_cross_kv),
            (f32_cross_out, raw_cross_out), (f32_gate, raw_gate), (f32_up, raw_up), (f32_down, raw_down),
        )
    ]
    seed_own = links.store(cotangent, seeds_out.at[0])
    for part in range(3):
        for pair in range(pairs):
            at = part * width + pair * PAIR
            own_qkv[:, at : at + PAIR] = two_heads(f32_qkv, part, 3, pair)
    links.greet([(1, 0), (2, 0), (4, 0), (6, 0), (0, 1), (0, 2)])
    gather_qkv = Gather(links, own_qkv, w_qkv)

    def norm_one(rows):
        rows_one[0, rows] = layer_norm(latents[rows].astype(jnp.float32), gains[0:1])[0].astype(low)

    row_steps(BLOCK, norm_one)
    spread_one = Spread(links, rows_one)
    cosine, sine = (tables.at[part] for part in range(2))
    fill_tables(cosine, sine, links.tensor)
    links.store(tables, tables_out)
    for load in loads:
        links.settle(load)
    own_attn_out[...] = raw_attn_out[...].astype(low)
    own_cross[:, :width] = raw_cross_q[...].astype(low)
    own_cross[:, width:] = raw_cross_out[...].astype(low)
    for part in range(2):
        for pair in range(pairs):
            at = part * width + pair * PAIR
            own_keyval[:, at : at + PAIR] = two_heads(raw_cross_kv, part, 2, pair)
    hidden = raw_gate.shape[1]
    own_mlp[:, :hidden] = raw_gate[...].astype(low)
    own_mlp[:, hidden:] = raw_up[...].astype(low)
    own_down[...] = raw_down[...].astype(low)
    context[...] = jnp.zeros_like(context)
    context[:CTX] = conditioning[0]
    spread_one.wait(1)
    gather_qkv.forward()
    gather_attn_out = Gather(links, own_attn_out, w_attn_out)
    gather_cross = Gather(links, own_cross, w_cross.at[0], False)
    gather_keyval = Gather(links, own_keyval, w_keyval)
    spread_one.wait(2)
    gather_qkv.arrive()
    links.store(w_qkv, qkv_out)

    for block in range(4):
        spread_one.wait(block)
        rows = block_rows(block)
        turn = (cosine[rows], sine[rows])

        def project(cols):
            packed[:, cols] = dot_plain(rows_one[block], w_qkv[:, cols])

        columns(3 * width, width, project)
        for part in range(3):
            for pair in range(pairs):
                at = slice(part * width + pair * PAIR, part * width + (pair + 1) * PAIR)
                value = packed[:, at]
                rotated[rows, at] = (value if part == 2 else head_turn(value, *turn)).astype(low)
    links.store(rows_one, rows_one_out)
    links.store(rotated, rotated_out)
    for pair in range(pairs):
        key = rotated[:, width + pair * PAIR : width + (pair + 1) * PAIR]
        keys_t[pair] = key.astype(jnp.float32).T.astype(low)

    def out_project(source, block, weight, sums):
        def project(cols):
            parts[block, :, cols] = dot_cols(source[block_rows(block)], weight(cols)).astype(low)

        columns(parts.shape[2], 512, project)
        sums.ready(block)

    sums_one = Sums(links, parts, *got_one)
    for block in (3, 1, 2, 0):
        rows = block_rows(block)

        def one_pair(pair, carry):
            at = pl.ds(pl.multiple_of(pair * PAIR, PAIR), PAIR)
            values_at = pl.ds(pl.multiple_of(2 * width + pair * PAIR, PAIR), PAIR)
            out, log = attend_rows(rotated[rows, at] * low(DH**-0.5), keys_t[pair], rotated[:, values_at], None)
            attended[rows, at] = out.astype(low)
            logs[rows, at] = log
            return carry

        lax.fori_loop(0, pairs, one_pair, 0)
        if block == 3:
            gather_attn_out.forward()
            gather_attn_out.arrive()
            links.store(w_attn_out, attn_out_out)
        out_project(attended, block, lambda cols: w_attn_out[cols, :], sums_one)
        if block == 1:
            gather_cross.forward()
            gather_keyval.forward()
            gather_mlp = Gather(links, own_mlp, mlp_out)
        if block == 2:
            sums_one.add()
    gather_cross.arrive()
    spread_cross = SpreadCross(links, w_cross)
    links.store(attended, attended_out)
    links.store(logs, logs_out)
    sums_one.arrive()

    def norm_two(rows):
        value = latents[rows].astype(jnp.float32) + parts[0, rows].astype(jnp.float32) + sums_one.total(rows)
        resid_one[rows] = value
        normed_two[rows] = layer_norm(value, gains[1:2])[0].astype(low)

    row_steps(BLOCK, norm_two)
    links.store(resid_one, resid_one_out)
    links.store(normed_two, normed_two_out)
    gather_keyval.arrive()
    links.store(w_keyval, keyval_w_out)
    keyval[0] = dot_plain(context[...], w_keyval[...]).astype(low)
    spread_keyval = Spread(links, keyval)
    spread_cross.pump()
    resid_two[...] = resid_one[...]
    for member in range(4):
        spread_cross.wait(member)
        spread_keyval.wait(member)
        at_member = slice(member * width, (member + 1) * width)
        query[:, at_member] = dot_plain(normed_two[...], cross_columns(w_cross, member, slice(0, width))).astype(low)
        for pair in range(pairs):
            at = slice(member * width + pair * PAIR, member * width + (pair + 1) * PAIR)
            keys_at = slice(pair * PAIR, (pair + 1) * PAIR)
            values_at = slice(width + pair * PAIR, width + (pair + 1) * PAIR)
            key_t = keyval[member, :, keys_at].astype(jnp.float32).T.astype(low)
            out, log = attend_rows(query[:, at] * low(DH**-0.5), key_t, keyval[member, :, values_at], CTX)
            crossed[:, at] = out.astype(low)
            cross_logs[:, at] = log
        for place in range(4):
            at = slice(place * 2 * share, (place + 1) * 2 * share)
            tile = cross_tile(w_cross, member, place, slice(width, 2 * width))
            resid_two[:, at] += dot_cols(crossed[:, at_member], tile)
        if member == 1:
            gather_mlp.forward()
            gather_down = Gather(links, own_down, down_out)
    links.store(w_cross, cross_out)
    links.store(keyval, keyval_out)
    links.store(query, query_out)
    links.store(crossed, crossed_out)
    links.store(cross_logs, cross_logs_out)
    links.store(resid_two, resid_two_out)

    def norm_three(rows):
        rows_three[0, rows] = layer_norm(resid_two[rows], gains[2:3])[0].astype(low)

    row_steps(BLOCK, norm_three)
    spread_three = Spread(links, rows_three)
    links.settle(seed_own)
    spread_seed = Spread(links, seeds_out)
    spread_three.wait(1)
    spread_seed.wait(1)
    spread_seed.wait(2)
    spread_three.wait(2)
    gather_down.forward()
    gather_mlp.arrive()
    spread_seed.wait(3)
    spread_three.wait(3)
    links.store(rows_three, rows_three_out)
    gather_down.arrive()
    links.finish()
    for gather in (gather_qkv, gather_attn_out, gather_cross, gather_keyval, gather_mlp, gather_down):
        gather.finish()


def whole_vmem():
    return pl.BlockSpec(memory_space=pltpu.VMEM)


def anywhere():
    return pl.BlockSpec(memory_space=pl.ANY)


def sum_buffers(model):
    return [
        pltpu.VMEM((HALF, model), jnp.bfloat16),
        pltpu.VMEM((HALF, model), jnp.bfloat16),
        pltpu.VMEM((BLOCK, model), jnp.bfloat16),
        pltpu.VMEM((BLOCK, model), jnp.bfloat16),
    ]


def forward_part(latents, gains, conditioning, weights, cotangent):
    w_qkv, w_attn_out, w_cross_q, w_cross_kv, w_cross_out, w_gate, w_up, w_down = weights
    model = latents.shape[1]
    depth = conditioning.shape[2]
    wide = w_qkv.shape[1]
    width = wide // 3
    hidden = w_gate.shape[1]
    pairs = width // PAIR
    low, high = jnp.bfloat16, jnp.float32
    share = w_qkv.shape[0]
    outs = [
        ((4, BLOCK, model), low),
        ((BLOCK, model), low),
        ((4, BLOCK, model), low),
        ((4, BLOCK, model), low),
        ((model, wide), low),
        ((model, width), low),
        ((4, 4, 2, share, 2 * width), low),
        ((depth, 2 * width), low),
        ((model, 2 * hidden), low),
        ((model, hidden), low),
        ((LENGTH, wide), low),
        ((LENGTH, width), low),
        ((LENGTH, width), high),
        ((BLOCK, model), low),
        ((4, FULL, 2 * width), low),
        ((BLOCK, model), low),
        ((BLOCK, model), high),
        ((BLOCK, model), high),
        ((BLOCK, model), high),
        ((2, LENGTH, PAIR), high),
    ]
    work = [
        ((4, BLOCK, model), low),
        ((BLOCK, model), low),
        ((4, BLOCK, model), low),
        ((model, wide), low),
        ((model, width), low),
        ((4, 4, 2, share, 2 * width), low),
        ((depth, 2 * width), low),
        ((LENGTH, wide), low),
        ((LENGTH, width), low),
        ((LENGTH, width), high),
        ((BLOCK, model), low),
        ((4, FULL, 2 * width), low),
        ((BLOCK, model), low),
        ((BLOCK, model), high),
        ((pairs, PAIR, LENGTH), low),
        ((4, BLOCK, model), low),
    ]
    more = [
        ((BLOCK, model), high),
        ((BLOCK, model), high),
        ((BLOCK, wide), high),
        ((2, LENGTH, PAIR), high),
        ((FULL, depth), low),
        (w_attn_out.shape, high),
        (w_cross_q.shape, high),
        (w_cross_kv.shape, high),
        (w_cross_out.shape, high),
        (w_gate.shape, high),
        (w_up.shape, high),
        (w_down.shape, high),
        ((share, wide), low),
        ((share, width), low),
        ((share, 2 * width), low),
        (w_cross_kv.shape, low),
        ((share, 2 * hidden), low),
        ((share, hidden), low),
    ]
    scratch = [pltpu.VMEM(*buffer) for buffer in work] + [sum_buffers(model)]
    scratch += [pltpu.VMEM(*buffer) for buffer in more]
    scratch += [pltpu.SemaphoreType.DMA((96,)), pltpu.SemaphoreType.DMA((96,)), pltpu.SemaphoreType.DMA((40,))]
    return pl.pallas_call(
        forward_kernel,
        out_shape=[jax.ShapeDtypeStruct(*out) for out in outs],
        in_specs=[whole_vmem()] * 4 + [anywhere()] * 8,
        out_specs=[anywhere()] * len(outs),
        scratch_shapes=scratch,
        compiler_params=pltpu.CompilerParams(collective_id=1, has_side_effects=True, vmem_limit_bytes=VMEM_BYTES),
        cost_estimate=pl.CostEstimate(flops=2**37, bytes_accessed=2**26, transcendentals=2**23),
    )(latents, gains, conditioning, *weights, cotangent)


class Scatter:
    def __init__(self, links, grads, got_core, extra, got):
        self.links, self.grads, self.got_core, self.extra, self.got = links, grads, got_core, extra, got
        self.size = got.shape[1]
        self.place, self.which = links.dp // 2, links.dp % 2
        self.middle = (self.place == 1) | (self.place == 2)

    def rows(self, place, which):
        if self.got_core is None:
            return place
        start = pl.multiple_of((2 * place + which) * self.size, self.size)
        return pl.ds(start, self.size)

    def pair_up(self):
        self.core = [
            self.links.go(self.grads.at[self.rows(place, 1 - self.which)], self.got_core.at[place], 1, 0)
            for place in range(4)
        ]

    def combine(self):
        for copy in self.core:
            copy.wait_recv()

        def add(place, carry):
            rows = self.rows(place, self.which)
            total = self.grads[rows].astype(jnp.float32) + self.got_core[place].astype(jnp.float32)
            self.grads[rows] = total.astype(jnp.bfloat16)
            return carry

        lax.fori_loop(0, 4, add, 0)
        self.start()

    def start(self):
        links, grads = self.links, self.grads
        block = [grads.at[self.rows(self.place ^ step, self.which)] for step in range(4)]
        self.to_extra = links.remote(block[3], self.extra, 2, 0)
        self.to_third = links.remote(block[3], self.got.at[2], 6, 0)
        self.to_skip = links.remote(block[2], self.got.at[1], 4, 0)

        @pl.when(self.middle)
        def _():
            self.to_third.start()

        @pl.when(jnp.logical_not(self.middle))
        def _():
            self.to_extra.start()
            self.to_skip.start()

        self.beside = links.go(block[1], self.got.at[0], 2, 0)

    def relay(self):
        @pl.when(self.middle)
        def _():
            self.to_extra.wait_recv()
            rows = self.rows(self.place ^ 2, self.which)
            self.grads[rows] = (
                self.grads[rows].astype(jnp.float32) + self.extra[...].astype(jnp.float32)
            ).astype(jnp.bfloat16)
            self.to_skip.start()

    def arrive(self):
        self.beside.wait_recv()
        self.to_skip.wait_recv()

        @pl.when(self.middle)
        def _():
            self.to_third.wait_recv()

    def total(self, out, cols):
        rows = self.rows(self.place, self.which)
        at = (rows, cols) if self.got_core is not None else (rows, slice(None), cols)
        mine = self.grads[at].astype(jnp.float32)
        out[...] = mine + self.got[0, :, cols].astype(jnp.float32) + self.got[1, :, cols].astype(jnp.float32)

        @pl.when(self.middle)
        def _():
            out[...] += self.got[2, :, cols].astype(jnp.float32)

    def finish(self):
        self.to_skip.wait_send()

        @pl.when(self.middle)
        def _():
            self.to_third.wait_send()

        @pl.when(jnp.logical_not(self.middle))
        def _():
            self.to_extra.wait_send()


def attend_rows_back(block, grads, log, keys_t, values_t, keys, d_keys_t, d_values_t, limit):
    block_t = block.astype(jnp.float32).T.astype(jnp.bfloat16)
    grads_t = grads.astype(jnp.float32).T.astype(jnp.bfloat16)
    outs = []
    for which in range(2):
        half = slice(which * DH, (which + 1) * DH)
        keep = half_mask(block.shape, 1, which)
        scores = jnp.dot(jnp.where(keep, block, jnp.zeros_like(block)), keys_t, preferred_element_type=jnp.float32)
        probs = jnp.exp(scores - log[:, which * DH : which * DH + 1])
        if limit is not None:
            probs = jnp.where(lax.broadcasted_iota(jnp.int32, probs.shape, 1) < limit, probs, 0.0)
        d_prob = jnp.dot(jnp.where(keep, grads, jnp.zeros_like(grads)), values_t, preferred_element_type=jnp.float32)
        center = jnp.sum(probs * d_prob, axis=1, keepdims=True)
        d_score = (probs * (d_prob - center)).astype(jnp.bfloat16)
        outs.append(jnp.dot(d_score, keys, preferred_element_type=jnp.float32))
        d_keys_t[half, :] += jnp.dot(block_t[half], d_score, preferred_element_type=jnp.float32)
        d_values_t[half, :] += jnp.dot(grads_t[half], probs.astype(jnp.bfloat16), preferred_element_type=jnp.float32)
    return jnp.where(half_mask(block.shape, 1, 0), outs[0], outs[1]) * DH**-0.5


def backward_kernel(
    latents, gains, conditioning, in_gain, in_d_resid, in_seed,
    in_grads_cross, in_d_keyval, in_qkv, in_attn_out, in_keyval_w, in_rows_one, in_rotated, in_attended, in_logs,
    in_tables,
    grad_latents, grad_context, grad_gains, grad_qkv, grad_attn_out, grad_cross_q, grad_keyval, grad_cross_out,
    parts, rows_one, seeds, w_qkv, w_attn_out, w_keyval, rotated, attended, d_attended, logs, keys_t, values_t,
    d_keys_t, d_values_t, grads_cross, core_cross, got_cross, keyval_parts, got_keyval, context, context_sum,
    context_got, d_resid, tables, gain_rows, gain_got, got, core_qkv, core_attn_out, core_keyval,
    extra_qkv, extra_attn_out, extra_cross, extra_keyval, far_qkv, far_attn_out, far_cross, far_keyval,
    sum_keyval, sum_last, out_qkv, out_keyval, send, recv, local,
):
    low = jnp.bfloat16
    width = attended.shape[1]
    pairs = width // PAIR
    model = latents.shape[1]
    links = Links(send, recv, local)
    which = links.dp % 2
    load_seed = links.store(in_seed, seeds.at[0])
    load_self = [
        links.store(source, target)
        for source, target in (
            (in_attn_out, w_attn_out), (in_rotated, rotated), (in_logs, logs), (in_tables, tables),
            (in_attended, attended),
        )
    ]
    load_keyval = [links.store(in_d_keyval, keyval_parts), links.store(in_keyval_w, w_keyval)]
    load_cross = [links.store(in_grads_cross.at[member, :, which], grads_cross.at[member]) for member in range(4)]
    load_late = [links.store(in_qkv, w_qkv), links.store(in_rows_one, rows_one), links.store(in_d_resid, d_resid)]
    links.greet([(1, 0), (2, 0), (4, 0), (6, 0), (0, 1), (0, 2)])
    links.settle(load_seed)
    spread = Spread(links, seeds)
    core_copies = [
        links.go(in_grads_cross.at[member, :, 1 - which], core_cross.at[member], 1, 0) for member in range(4)
    ]
    gain_rows[...] = in_gain[...]
    context[...] = jnp.zeros_like(context)
    context[:CTX] = conditioning[0]
    for load in load_self:
        links.settle(load)
    for pair in range(pairs):
        key = rotated[:, width + pair * PAIR : width + (pair + 1) * PAIR]
        value = rotated[:, 2 * width + pair * PAIR : 2 * width + (pair + 1) * PAIR]
        keys_t[pair] = key.astype(jnp.float32).T.astype(low)
        values_t[pair] = value.astype(jnp.float32).T.astype(low)
    d_keys_t[...] = jnp.zeros_like(d_keys_t)
    d_values_t[...] = jnp.zeros_like(d_values_t)
    cosine, sine = (tables.at[part] for part in range(2))
    sums_keyval = Sums(links, keyval_parts, *got_keyval)
    sums_cross = Sums(links, grads_cross, *got_cross)

    def whole(rows, cols):
        return rows[:, :, cols].reshape(LENGTH, -1)

    def grads_into(target, rows, right):
        def product(part):
            target[part, :] = dot_rows(whole(rows, part), right).astype(low)

        columns(model, 384, product)

    for block in range(4):
        spread.wait(block)
        rows = block_rows(block)
        d_attended[rows] = dot_plain(seeds[block], w_attn_out[...]).astype(low)
        turn = (cosine[rows], -sine[rows])

        def one_pair(pair, carry):
            at = pl.ds(pl.multiple_of(pair * PAIR, PAIR), PAIR)
            keys_at = pl.ds(pl.multiple_of(width + pair * PAIR, PAIR), PAIR)
            out = attend_rows_back(
                rotated[rows, at] * low(DH**-0.5), d_attended[rows, at], logs[rows, at], keys_t[pair],
                values_t[pair], rotated[:, keys_at], d_keys_t.at[pair], d_values_t.at[pair], None,
            )
            rotated[rows, at] = head_turn(out, *turn).astype(low)
            return carry

        lax.fori_loop(0, pairs, one_pair, 0)
        if block == 0:
            for load in load_keyval + load_cross:
                links.settle(load)
            for copy in core_copies:
                copy.wait_recv()
            for member in range(4):

                def add(place, carry):
                    total = grads_cross[member, place].astype(jnp.float32) + core_cross[member, place].astype(jnp.float32)
                    grads_cross[member, place] = total.astype(low)
                    return carry

                lax.fori_loop(0, 4, add, 0)
        if block == 1:
            for part in (3, 1, 2):
                sums_keyval.ready(part)
            for part in (3, 1, 2):
                sums_cross.ready(part)
        if block == 2:
            sums_keyval.add()
            sums_cross.add()
    grads_into(w_attn_out, seeds, attended[...])
    scatter_attn_out = Scatter(links, w_attn_out, core_attn_out, extra_attn_out, far_attn_out)
    scatter_attn_out.pair_up()
    for pair in range(pairs):
        for block in range(4):
            rows = block_rows(block)
            turn = (cosine[rows], -sine[rows])
            at = slice(width + pair * PAIR, width + (pair + 1) * PAIR)
            rotated[rows, at] = head_turn(d_keys_t[pair, :, rows].T, *turn).astype(low)
            at = slice(2 * width + pair * PAIR, 2 * width + (pair + 1) * PAIR)
            rotated[rows, at] = d_values_t[pair, :, rows].T.astype(low)
    for load in load_late:
        links.settle(load)
    sums = Sums(links, parts, *got)
    for block in (3, 1, 2, 0):

        def project(cols):
            parts[block, :, cols] = dot_cols(rotated[block_rows(block)], w_qkv[cols, :]).astype(low)

        columns(model, 512, project)
        sums.ready(block)
    scatter_attn_out.combine()
    grads_into(w_qkv, rows_one, rotated[...])
    scatter_qkv = Scatter(links, w_qkv, core_qkv, extra_qkv, far_qkv)
    scatter_qkv.pair_up()
    sums.add()
    scatter_qkv.combine()
    sums_keyval.arrive()
    d_keyval = keyval_parts[0].astype(jnp.float32) + sums_keyval.total(slice(None))
    d_keyval = d_keyval.astype(low)
    context_sum[...] = dot_cols(d_keyval, w_keyval[...]).astype(low)
    context_near = links.go(context_sum, context_got.at[0], 0, 1)
    w_keyval[...] = dot_rows(context[...], d_keyval).astype(low)
    scatter_keyval = Scatter(links, w_keyval, core_keyval, extra_keyval, far_keyval)
    scatter_keyval.pair_up()
    sums_cross.arrive()
    for place in range(4):
        total = grads_cross[0, place].astype(jnp.float32) + sums_cross.total(place)
        grads_cross[0, place] = total.astype(low)
    scatter_cross = Scatter(links, grads_cross.at[0], None, extra_cross, far_cross)
    scatter_cross.start()
    scatter_keyval.combine()
    context_near.wait_recv()
    links.settle_sends((context_near,))
    context_sum[...] = (context_sum[...].astype(jnp.float32) + context_got[0].astype(jnp.float32)).astype(low)
    context_far = links.go(context_sum, context_got.at[1], 0, 2)
    scatter_attn_out.relay()
    sums.arrive()

    def norm_one(rows):
        gain = gains[0:1]
        _, scaled, inverse = layer_norm(latents[rows].astype(jnp.float32), gain)
        d_normed = parts[0, rows].astype(jnp.float32) + sums.total(rows)
        d_part, gain_grad = norm_backward(d_normed, scaled, inverse, gain)
        gain_rows[0:1] += gain_grad[None]
        d_resid[rows] += d_part

    row_steps(BLOCK, norm_one)
    links.store(d_resid, grad_latents)
    share = out_qkv.shape[0]
    spot = [logs.at[pl.ds(step * share, share)] for step in range(5)]
    qkv_spot = spot[3:5] + [sum_last]
    for step, (dp_bit, tensor_bit) in enumerate(((1, 0), (0, 1), (0, 2), (2, 0), (4, 0))):
        trade = links.remote(gain_rows, gain_got.at[step], dp_bit, tensor_bit)
        trade.start()
        if step == 1:
            scatter_qkv.relay()
        if step == 2:
            scatter_cross.relay()
        if step == 3:
            scatter_keyval.relay()
        trade.wait()
        gain_rows[...] += gain_got[step]
    grad_gains[...] = gain_rows[...]
    context_far.wait_recv()
    context_total = context_sum[...].astype(jnp.float32) + context_got[1].astype(jnp.float32)
    grad_context[0] = context_total[:CTX]
    scatter_attn_out.arrive()
    scatter_attn_out.total(spot[2], slice(None))
    links.store(spot[2], grad_attn_out)
    scatter_qkv.arrive()
    for part in range(3):
        scatter_qkv.total(qkv_spot[part], slice(part * width, (part + 1) * width))
    for pair in range(pairs):
        heads_of = [
            qkv_spot[part][:, (2 * pair + half) * DH : (2 * pair + half + 1) * DH]
            for half in range(2)
            for part in range(3)
        ]
        for step in range(3):
            start = (3 * pair + step) * PAIR
            out_qkv[:, start : start + PAIR] = jnp.concatenate(heads_of[2 * step : 2 * step + 2], axis=1)
    links.store(out_qkv, grad_qkv)
    scatter_cross.arrive()
    scatter_cross.total(spot[0], slice(0, width))
    links.store(spot[0], grad_cross_q)
    scatter_cross.total(spot[1], slice(width, 2 * width))
    links.store(spot[1], grad_cross_out)
    scatter_keyval.arrive()
    scatter_keyval.total(sum_keyval, slice(None))
    for head in range(width // DH):
        pieces = [sum_keyval[:, start + head * DH : start + (head + 1) * DH] for start in (0, width)]
        out_keyval[:, 2 * head * DH : 2 * (head + 1) * DH] = jnp.concatenate(pieces, axis=1)
    links.store(out_keyval, grad_keyval)
    links.finish()
    for scatter in (scatter_keyval, scatter_cross, scatter_attn_out, scatter_qkv):
        scatter.finish()


def backward_part(latents, gains, conditioning, gain_rows, d_resid, seed, grads_cross, d_keyval, kept):
    w_qkv, w_attn_out, w_keyval, rows_one, rotated, attended, logs, tables = kept
    model = latents.shape[1]
    depth = conditioning.shape[2]
    wide = w_qkv.shape[1]
    width = wide // 3
    pairs = width // PAIR
    members = lax.axis_size("dp")
    share, span = model // members, depth // members
    low, high = jnp.bfloat16, jnp.float32
    outs = [
        ((BLOCK, model), high),
        (conditioning.shape, high),
        ((8, model), high),
        ((share, wide), high),
        ((share, width), high),
        ((share, width), high),
        ((span, 2 * width), high),
        ((share, width), high),
    ]
    cross_block = (4, share, 2 * width)
    work = [
        ((4, BLOCK, model), low),
        ((4, BLOCK, model), low),
        ((4, BLOCK, model), low),
        ((model, wide), low),
        ((model, width), low),
        ((depth, 2 * width), low),
        ((LENGTH, wide), low),
        ((LENGTH, width), low),
        ((LENGTH, width), low),
        ((LENGTH, width), high),
        ((pairs, PAIR, LENGTH), low),
        ((pairs, PAIR, LENGTH), low),
        ((pairs, PAIR, LENGTH), high),
        ((pairs, PAIR, LENGTH), high),
        ((4, *cross_block), low),
        ((4, *cross_block), low),
    ]
    cross_got = [pltpu.VMEM((rows, share, 2 * width), low) for rows in (2, 2, 4, 4)]
    keyval_got = [pltpu.VMEM((rows, 2 * width), low) for rows in (FULL // 2, FULL // 2, FULL, FULL)]
    more = [
        ((FULL, depth), low),
        ((FULL, depth), low),
        ((2, FULL, depth), low),
        ((BLOCK, model), high),
        ((2, LENGTH, PAIR), high),
        ((8, model), high),
        ((5, 8, model), high),
    ]
    groups = [(share, wide), (share, width), (share, 2 * width), (span, 2 * width)]
    scratch = [pltpu.VMEM(*buffer) for buffer in work] + [cross_got, pltpu.VMEM((4, FULL, 2 * width), low), keyval_got]
    scratch += [pltpu.VMEM(*buffer) for buffer in more] + [sum_buffers(model)]
    scratch += [pltpu.VMEM((4, *group), low) for group in (groups[0], groups[1], groups[3])]
    scratch += [pltpu.VMEM(group, low) for group in groups]
    scratch += [pltpu.VMEM((3, *group), low) for group in groups]
    scratch += [pltpu.VMEM(groups[3], high), pltpu.VMEM((share, width), high)]
    scratch += [pltpu.VMEM(shape, high) for shape in ((share, wide), (span, 2 * width))]
    scratch += [pltpu.SemaphoreType.DMA((96,)), pltpu.SemaphoreType.DMA((96,)), pltpu.SemaphoreType.DMA((48,))]
    return pl.pallas_call(
        backward_kernel,
        out_shape=[jax.ShapeDtypeStruct(*out) for out in outs],
        in_specs=[whole_vmem()] * 4 + [anywhere()] * 12,
        out_specs=[anywhere()] + [whole_vmem()] * 2 + [anywhere()] * 5,
        scratch_shapes=scratch,
        compiler_params=pltpu.CompilerParams(collective_id=2, has_side_effects=True, vmem_limit_bytes=VMEM_BYTES),
        cost_estimate=pl.CostEstimate(flops=2**37, bytes_accessed=2**26, transcendentals=2**23),
    )(
        latents, gains, conditioning, gain_rows, d_resid, seed, grads_cross, d_keyval, w_qkv, w_attn_out, w_keyval,
        rows_one, rotated, attended, logs, tables,
    )


def cross_back_kernel(
    cotangent, gains, normed_two, resid_two, resid_one, in_parts, in_last, in_query, in_crossed, in_cross_logs,
    in_keyval, in_cross,
    block_out, d_resid_out, seed_out, grads_out, d_keyval_out, gain_out,
    parts, parts_last, got, got_last, w_cross, query, crossed, cross_logs, keyval, d_keyval, d_keys_t, d_values_t,
    d_resid, d_normed_two, cross_seed, seed, total, send, recv, local,
):
    low = jnp.bfloat16
    model = cotangent.shape[1]
    width = model // 4
    share = w_cross.shape[3]
    pairs = width // PAIR
    links = Links(send, recv, local)
    load_parts = [links.store(in_parts.at[block], parts.at[block]) for block in (3, 1, 2, 0)]
    load_last = [links.store(in_last.at[block], parts_last.at[block]) for block in (3, 1, 2, 0)]
    loads = [
        links.store(source, target)
        for source, target in (
            (in_query, query), (in_crossed, crossed), (in_cross_logs, cross_logs), (in_keyval, keyval),
            (in_cross, w_cross),
        )
    ]
    gain_out[...] = jnp.zeros_like(gain_out)
    links.greet([(0, 1), (0, 2)])
    sums = Sums(links, parts, *got)
    for load, block in zip(load_parts, (3, 1, 2, 0)):
        links.settle(load)
        sums.ready(block)
    for load in loads + load_last:
        links.settle(load)
    sums.add()
    sums_last = Sums(links, parts_last, *got_last)
    for block in (3, 1, 2):
        sums_last.ready(block)
    sums.arrive()

    def norm_three(rows):
        gain = gains[2:3]
        _, scaled, inverse = layer_norm(resid_two[rows], gain)
        d_normed = parts[0, rows].astype(jnp.float32) + sums.total(rows)
        d_part, gain_grad = norm_backward(d_normed, scaled, inverse, gain)
        gain_out[2:3] += gain_grad[None]
        value = cotangent[rows].astype(jnp.float32) + d_part
        d_resid[rows] = value
        cross_seed[rows] = value.astype(low)

    row_steps(BLOCK, norm_three)
    for member in range(4):
        at_member = slice(member * width, (member + 1) * width)
        d_crossed = dot_plain(cross_seed[...], cross_columns(w_cross, member, slice(width, 2 * width))).astype(low)
        for pair in range(pairs):
            at = slice(member * width + pair * PAIR, member * width + (pair + 1) * PAIR)
            keys_at = slice(pair * PAIR, (pair + 1) * PAIR)
            values_at = slice(width + pair * PAIR, width + (pair + 1) * PAIR)
            key = keyval[member, :, keys_at]
            key_t = key.astype(jnp.float32).T.astype(low)
            value_t = keyval[member, :, values_at].astype(jnp.float32).T.astype(low)
            d_keys_t[...] = jnp.zeros_like(d_keys_t)
            d_values_t[...] = jnp.zeros_like(d_values_t)
            out = attend_rows_back(
                query[:, at] * low(DH**-0.5), d_crossed[:, keys_at], cross_logs[:, at], key_t, value_t, key, d_keys_t,
                d_values_t, CTX,
            )
            query[:, at] = out.astype(low)
            d_keyval[member, :, keys_at] = d_keys_t[...].T.astype(low)
            d_keyval[member, :, values_at] = d_values_t[...].T.astype(low)
        for place in range(4):
            at = slice(place * 2 * share, (place + 1) * 2 * share)
            part = dot_cols(query[:, at_member], cross_tile(w_cross, member, place, slice(0, width)))
            if member == 0:
                d_normed_two[:, at] = part
            else:
                d_normed_two[:, at] += part
    links.store(d_keyval, d_keyval_out)

    def norm_two(rows):
        gain = gains[1:2]
        _, scaled, inverse = layer_norm(resid_one[rows], gain)
        d_part, gain_grad = norm_backward(d_normed_two[rows], scaled, inverse, gain)
        gain_out[1:2] += gain_grad[None]
        value = d_resid[rows] + d_part
        d_resid[rows] = value
        seed[rows] = value.astype(low)

    row_steps(BLOCK, norm_two)
    links.store(d_resid, d_resid_out)
    links.store(seed, seed_out)
    sums_last.add()
    for place in range(4):
        rows_at = slice(place * 2 * share, (place + 1) * 2 * share)
        for member in range(4):
            at_member = slice(member * width, (member + 1) * width)
            left = dot_rows(normed_two[:, rows_at], query[:, at_member]).astype(low)
            w_cross[member, place, :, :, :width] = left.reshape(2, share, width)
            right = dot_rows(cross_seed[:, rows_at], crossed[:, at_member]).astype(low)
            w_cross[member, place, :, :, width:] = right.reshape(2, share, width)
    links.store(w_cross, grads_out)
    sums_last.arrive()

    def add_last(rows):
        total[rows] = resid_two[rows] + parts_last[0, rows].astype(jnp.float32) + sums_last.total(rows)

    row_steps(BLOCK, add_last)
    links.store(total, block_out)
    links.finish()


def cross_back_part(cotangent, gains, parts, last, kept):
    normed_two, resid_two, resid_one, query, crossed, cross_logs, keyval, cross_all = kept
    model = cotangent.shape[1]
    low, high = jnp.bfloat16, jnp.float32
    outs = [
        ((BLOCK, model), high),
        ((BLOCK, model), high),
        ((BLOCK, model), low),
        (cross_all.shape, low),
        (keyval.shape, low),
        ((8, model), high),
    ]
    work = [
        ((4, BLOCK, model), low),
        ((4, BLOCK, model), low),
    ]
    more = [
        (cross_all.shape, low),
        ((BLOCK, model), low),
        ((BLOCK, model), low),
        ((BLOCK, model), high),
        (keyval.shape, low),
        (keyval.shape, low),
        ((PAIR, FULL), high),
        ((PAIR, FULL), high),
        ((BLOCK, model), high),
        ((BLOCK, model), high),
        ((BLOCK, model), low),
        ((BLOCK, model), low),
        ((BLOCK, model), high),
    ]
    scratch = [pltpu.VMEM(*buffer) for buffer in work] + [sum_buffers(model), sum_buffers(model)]
    scratch += [pltpu.VMEM(*buffer) for buffer in more]
    scratch += [pltpu.SemaphoreType.DMA((24,)), pltpu.SemaphoreType.DMA((24,)), pltpu.SemaphoreType.DMA((24,))]
    return pl.pallas_call(
        cross_back_kernel,
        out_shape=[jax.ShapeDtypeStruct(*out) for out in outs],
        in_specs=[whole_vmem()] * 5 + [anywhere()] * 7,
        out_specs=[anywhere()] * 5 + [whole_vmem()],
        scratch_shapes=scratch,
        compiler_params=pltpu.CompilerParams(collective_id=3, has_side_effects=True, vmem_limit_bytes=VMEM_BYTES),
        cost_estimate=pl.CostEstimate(flops=2**35, bytes_accessed=2**26, transcendentals=2**21),
    )(
        cotangent, gains, normed_two, resid_two, resid_one, parts, last, query, crossed, cross_logs, keyval, cross_all
    )


def per_device(
    latents,
    conditioning,
    gain_attn,
    w_qkv,
    w_attn_out,
    gain_cross,
    w_cross_q,
    w_cross_kv,
    w_cross_out,
    gain_mlp,
    w_gate,
    w_up,
    w_down,
    cotangent,
):
    low = jnp.bfloat16
    hidden_wide = w_gate.shape[1]
    gains = jnp.stack([gain_attn, gain_cross, gain_mlp])
    (
        rows_one, normed_two, rows_three, mlp_seed, qkv_all, attn_out_t, cross_all, cross_kv, mlp_all, down_all,
        rotated, attended, logs, cross_query, keyval, crossed, cross_logs, resid_one, resid_two, tables,
    ) = forward_part(
        latents,
        gains,
        conditioning,
        (w_qkv, w_attn_out.T, w_cross_q, w_cross_kv, w_cross_out.T, w_gate, w_up, w_down.T),
        cotangent,
    )
    rows_three, mlp_seed = (array.reshape(LENGTH, -1) for array in (rows_three, mlp_seed))
    both = dot_plain(rows_three, mlp_all)
    gate_pre, up_pre = both[:, :hidden_wide], both[:, hidden_wide:]
    sigma_gate = jax.nn.sigmoid(gate_pre)
    swish = gate_pre * sigma_gate
    hidden = (swish * up_pre).astype(low)
    sum_down = dp_sum(dot_rows(mlp_seed, hidden))
    d_hidden = dot_plain(mlp_seed, down_all)
    d_gate = (d_hidden * up_pre * sigma_gate * (1.0 + gate_pre * (1.0 - sigma_gate))).astype(low)
    d_up = (d_hidden * swish).astype(low)
    d_both = jnp.concatenate([d_gate, d_up], axis=1)
    sum_mlp = dp_sum(dot_rows(rows_three, d_both))
    block_shape = (4, latents.shape[0], -1)
    parts = dot_cols(d_both, mlp_all).astype(low).reshape(block_shape)
    last = dot_cols(hidden, down_all).astype(low).reshape(block_shape)
    block_out, d_resid, seed, grads_cross, d_keyval, gain_rows = cross_back_part(
        cotangent,
        gains,
        parts,
        last,
        (normed_two, resid_two, resid_one, cross_query, crossed, cross_logs, keyval, cross_all),
    )
    grad_latents, grad_context, grad_gains, grad_qkv, grad_attn_out, grad_cross_q, grad_cross_kv, grad_cross_out = (
        backward_part(
            latents,
            gains,
            conditioning,
            gain_rows,
            d_resid,
            seed,
            grads_cross,
            d_keyval,
            (qkv_all, attn_out_t, cross_kv, rows_one, rotated, attended, logs, tables),
        )
    )
    return (
        block_out,
        grad_latents,
        grad_context,
        grad_gains[0],
        grad_qkv,
        grad_attn_out.T,
        grad_gains[1],
        grad_cross_q,
        grad_cross_kv,
        grad_cross_out.T,
        grad_gains[2],
        sum_mlp[:, :hidden_wide].astype(jnp.float32),
        sum_mlp[:, hidden_wide:].astype(jnp.float32),
        sum_down.astype(jnp.float32).T,
    )


def per_device_general(
    latents,
    conditioning,
    gain_attn,
    w_qkv,
    w_attn_out,
    gain_cross,
    w_cross_q,
    w_cross_kv,
    w_cross_out,
    gain_mlp,
    w_gate,
    w_up,
    w_down,
    cotangent,
):
    low = jnp.bfloat16
    heads_wide = w_cross_q.shape[1]
    hidden_wide = w_gate.shape[1]
    resid_in = latents.astype(jnp.float32)
    normed_one, scaled_one, inverse_one = layer_norm(resid_in, gain_attn)
    rows_one = spread_rows(normed_one.astype(low))
    own_qkv = by_part(w_qkv.astype(low), 3)
    qkv_all = lax.all_gather(own_qkv, "dp", axis=0, tiled=True)
    own_kv = by_part(w_cross_kv.astype(low), 2)
    own_kv = jnp.concatenate([own_kv[:, :heads_wide], own_kv[:, heads_wide:]], axis=0)
    own_mid = jnp.concatenate(
        [w_attn_out.astype(low).T, w_cross_q.astype(low), w_cross_out.astype(low).T, own_kv], axis=1
    )
    mid_all = lax.all_gather(after(own_mid, qkv_all), "dp", axis=0, tiled=True)
    own_mlp = jnp.concatenate([w_gate.astype(low), w_up.astype(low)], axis=1)
    mlp_all = lax.all_gather(after(own_mlp, mid_all), "dp", axis=0, tiled=True)
    down_all = lax.all_gather(after(w_down.astype(low).T, mlp_all), "dp", axis=0, tiled=True)
    attn_out_t, cross_q, cross_out_t = (mid_all[:, part * heads_wide : (part + 1) * heads_wide] for part in range(3))
    model = mid_all.shape[0]
    cross_kv = (
        mid_all[:, 3 * heads_wide :]
        .reshape(lax.axis_size("dp"), 2, -1, heads_wide)
        .transpose(0, 2, 1, 3)
        .reshape(model // 2, 2 * heads_wide)
    )

    tables = turn_tables(group_positions(latents.shape[0]))
    packed = dot_plain(rows_one, qkv_all)
    attended, rotated, logs = attend(pad_heads(packed, 3), tables)
    attended = attended[:, :heads_wide]
    resid_one = resid_in + sum_rows(dot_cols(attended, attn_out_t))
    normed_two, scaled_two, inverse_two = layer_norm(resid_one, gain_cross)
    rows_two = spread_rows(normed_two.astype(low))
    head_shape = (-1, heads_wide // DH, DH)
    cross_query = dot_plain(rows_two, cross_q).astype(low).reshape(head_shape)
    context = conditioning.reshape(CTX, conditioning.shape[2])
    cross_pack = dot_plain(context, cross_kv).astype(low)
    cross_key = cross_pack[:, :heads_wide].reshape(head_shape)
    cross_value = cross_pack[:, heads_wide:].reshape(head_shape)
    crossed, cross_logs = cross_forward(cross_query, cross_key, cross_value)
    crossed = crossed.reshape(-1, heads_wide).astype(low)
    resid_two = resid_one + sum_rows(dot_cols(crossed, cross_out_t))
    normed_three, scaled_three, inverse_three = layer_norm(resid_two, gain_mlp)
    rows_three = spread_rows(normed_three.astype(low))
    mlp_seed = spread_rows(cotangent)
    both = dot_plain(rows_three, mlp_all)
    gate_pre, up_pre = both[:, :hidden_wide], both[:, hidden_wide:]
    sigma_gate = jax.nn.sigmoid(gate_pre)
    swish = gate_pre * sigma_gate
    hidden = (swish * up_pre).astype(low)
    sum_down = dp_sum(dot_rows(mlp_seed, hidden))
    d_hidden = dot_plain(mlp_seed, down_all)
    d_gate = (d_hidden * up_pre * sigma_gate * (1.0 + gate_pre * (1.0 - sigma_gate))).astype(low)
    d_up = (d_hidden * swish).astype(low)
    d_both = jnp.concatenate([d_gate, d_up], axis=1)
    sum_mlp = dp_sum(after(dot_rows(rows_three, d_both), sum_down))
    d_normed = sum_rows(dot_cols(d_both, mlp_all))
    d_part, gain_grad_three = norm_backward(d_normed, scaled_three, inverse_three, gain_mlp)
    d_resid = cotangent.astype(jnp.float32) + d_part
    block_out = resid_two + sum_rows(dot_cols(hidden, down_all))
    cross_seed = spread_rows(d_resid.astype(low))
    grad_cross_out = dot_rows(cross_seed, crossed)
    d_crossed = dot_plain(cross_seed, cross_out_t).astype(low).reshape(head_shape)
    d_query, d_key, d_value = cross_backward(cross_query, cross_key, cross_value, d_crossed, cross_logs)
    d_query = d_query.reshape(-1, heads_wide).astype(low)
    d_keyval = jnp.concatenate([d_key.reshape(CTX, -1), d_value.reshape(CTX, -1)], axis=1).astype(low)
    grad_cross_q = dot_rows(rows_two, d_query)
    grad_cross_kv = dot_rows(context, d_keyval)
    context_part = dot_cols(d_keyval, cross_kv)
    d_normed = sum_rows(dot_cols(d_query, cross_q))
    d_part, gain_grad_two = norm_backward(d_normed, scaled_two, inverse_two, gain_cross)
    d_resid = d_resid + d_part
    self_seed = spread_rows(d_resid.astype(low))
    grad_attn_out = dot_rows(self_seed, attended)
    grad_kv = (
        grad_cross_kv.astype(low)
        .reshape(lax.axis_size("dp"), -1, 2, heads_wide)
        .transpose(0, 2, 1, 3)
        .reshape(model, heads_wide)
    )
    grad_mid = jnp.concatenate([grad_attn_out.astype(low), grad_cross_q.astype(low), grad_cross_out.astype(low), grad_kv], axis=1)
    sum_mid = dp_sum(after(grad_mid, sum_mlp))
    d_attended = dot_plain(self_seed, attn_out_t).astype(low)
    d_packed = drop_heads(attend_back(rotated, pad_heads(d_attended, 1), logs, tables), 3, packed.shape[1])
    sum_qkv = dp_sum(after(dot_rows(rows_one, d_packed), sum_mid))
    d_normed = sum_rows(dot_cols(d_packed, qkv_all))
    d_part, gain_grad_one = norm_backward(d_normed, scaled_one, inverse_one, gain_attn)
    grad_latents = d_resid + d_part
    grad_context = (
        lax.psum(context_part.astype(low), "tensor").astype(jnp.float32).reshape(conditioning.shape)
    )
    gains = lax.psum(jnp.stack([gain_grad_one, gain_grad_two, gain_grad_three]), ("dp", "tensor"))
    sums = [sum_mid[:, part * heads_wide : (part + 1) * heads_wide].astype(jnp.float32) for part in range(4)]
    half = sums[3].shape[0] // 2
    sum_kv = jnp.concatenate([sums[3][:half], sums[3][half:]], axis=1)
    return (
        block_out,
        grad_latents,
        grad_context,
        gains[0],
        by_head(sum_qkv, 3).astype(jnp.float32),
        sums[0].T,
        gains[1],
        sums[1],
        by_head(sum_kv, 2),
        sums[2].T,
        gains[2],
        sum_mlp[:, :hidden_wide].astype(jnp.float32),
        sum_mlp[:, hidden_wide:].astype(jnp.float32),
        sum_down.astype(jnp.float32).T,
    )


def solution(mesh):
    in_specs = (
        P(("dp", "tensor"), None),
        P("dp", None, None),
        P(),
        P("dp", "tensor"),
        P("tensor", "dp"),
        P(),
        P("dp", "tensor"),
        P("dp", "tensor"),
        P("tensor", "dp"),
        P(),
        P("dp", "tensor"),
        P("dp", "tensor"),
        P("tensor", "dp"),
        P(("dp", "tensor"), None),
    )
    out_specs = (
        P(("dp", "tensor"), None),
        P(("dp", "tensor"), None),
        P("dp", None, None),
        P(),
        P("dp", "tensor"),
        P("tensor", "dp"),
        P(),
        P("dp", "tensor"),
        P("dp", "tensor"),
        P("tensor", "dp"),
        P(),
        P("dp", "tensor"),
        P("dp", "tensor"),
        P("tensor", "dp"),
    )
    special = dict(mesh.shape) == {"dp": 8, "tensor": 4}
    return jax.shard_map(
        per_device if special else per_device_general, mesh=mesh, in_specs=in_specs, out_specs=out_specs, check_vma=False
    )
```

```python
import math
from functools import reduce

import jax
import jax.numpy as jnp
from jax import lax
from jax.experimental import pallas as pl
from jax.experimental.pallas import tpu as pltpu
from jax.sharding import PartitionSpec as P

DH = 64
CTX = 130
LENGTH = 1024
PAIR = 2 * DH
ROWS = 256
VMEM_BYTES = 62 * 2**20

norm_eps = 1e-05
rope_base = 10000.0


def head_turn(values, cosine, sine):
    quarter = DH // 4
    ahead = pltpu.roll(values, PAIR - quarter, 1)
    behind = pltpu.roll(values, quarter, 1)
    lane = lax.broadcasted_iota(jnp.int32, values.shape, 1) % DH
    return values * cosine + jnp.where(lane < quarter, -ahead, behind) * sine


def half_mask(shape, axis, which):
    place = lax.broadcasted_iota(jnp.int32, shape, axis)
    return (place >= DH) if which else (place < DH)


def attend_kernel(q_ref, k_ref, v_ref, cos_ref, sin_ref, out_ref, rot_ref, log_ref, kt_ref, vm_ref):
    pairs = pl.num_programs(0)
    pair = pl.program_id(0)
    turn = (cos_ref[...], sin_ref[...])
    query = head_turn(q_ref[...], *turn).astype(jnp.bfloat16)
    key = head_turn(k_ref[...], *turn).astype(jnp.bfloat16)
    value = v_ref[...].astype(jnp.bfloat16)
    for part, array in enumerate((query, key, value)):
        start = pl.multiple_of((part * pairs + pair) * PAIR, PAIR)
        rot_ref[:, pl.ds(start, PAIR)] = array
    key_t = key.astype(jnp.float32).T
    for which in range(2):
        kt_ref[which] = jnp.where(half_mask(key_t.shape, 0, which), key_t, 0.0).astype(jnp.bfloat16)
        vm_ref[which] = jnp.where(half_mask(value.shape, 1, which), value.astype(jnp.float32), 0.0).astype(jnp.bfloat16)
    q_start = pl.multiple_of(pair * PAIR, PAIR)

    def one_block(step, carry):
        rows = pl.ds(pl.multiple_of(step * ROWS, ROWS), ROWS)
        block = rot_ref[rows, pl.ds(q_start, PAIR)] * jnp.bfloat16(DH**-0.5)
        outs, logs = [], []
        for which in range(2):
            scores = jnp.dot(block, kt_ref[which], preferred_element_type=jnp.float32)
            peak = jnp.max(scores, axis=1, keepdims=True)
            shifted = jnp.exp(scores - peak)
            total = jnp.sum(shifted, axis=1, keepdims=True)
            product = jnp.dot(shifted.astype(jnp.bfloat16), vm_ref[which], preferred_element_type=jnp.float32)
            outs.append(product * (1.0 / total))
            logs.append(peak + jnp.log(total))
        out_ref[rows, :] = (outs[0] + outs[1]).astype(jnp.bfloat16)
        low = half_mask((ROWS, PAIR), 1, 0)
        log_ref[rows, :] = jnp.where(low, logs[0], logs[1])
        return carry

    lax.fori_loop(0, LENGTH // ROWS, one_block, 0)


def attend_back_kernel(
    q_ref, k_ref, v_ref, grad_ref, log_ref, cos_ref, sin_ref, out_ref,
    kt_ref, vt_ref, km_ref, qt_ref, gt_ref, dq_ref, dk_ref, dv_ref,
):
    pairs = pl.num_programs(0)
    pair = pl.program_id(0)
    key_t = k_ref[...].astype(jnp.float32).T
    value_t = v_ref[...].astype(jnp.float32).T
    for which in range(2):
        keep = half_mask(key_t.shape, 0, which)
        kt_ref[which] = jnp.where(keep, key_t, 0.0).astype(jnp.bfloat16)
        vt_ref[which] = jnp.where(keep, value_t, 0.0).astype(jnp.bfloat16)
        key = k_ref[...].astype(jnp.float32)
        km_ref[which] = jnp.where(half_mask(key.shape, 1, which), key, 0.0).astype(jnp.bfloat16)
    qt_ref[...] = (q_ref[...].astype(jnp.float32) * DH**-0.5).T.astype(jnp.bfloat16)
    gt_ref[...] = grad_ref[...].astype(jnp.float32).T.astype(jnp.bfloat16)
    dk_ref[...] = jnp.zeros_like(dk_ref)
    dv_ref[...] = jnp.zeros_like(dv_ref)

    def one_block(step, carry):
        rows = pl.ds(pl.multiple_of(step * ROWS, ROWS), ROWS)
        block = q_ref[rows, :] * jnp.bfloat16(DH**-0.5)
        grads = grad_ref[rows, :]
        d_query = jnp.zeros((ROWS, PAIR), jnp.float32)
        for which in range(2):
            half = slice(which * DH, (which + 1) * DH)
            scores = jnp.dot(block, kt_ref[which], preferred_element_type=jnp.float32)
            probs = jnp.exp(scores - log_ref[rows, which * DH : which * DH + 1])
            d_prob = jnp.dot(grads, vt_ref[which], preferred_element_type=jnp.float32)
            center = jnp.sum(probs * d_prob, axis=1, keepdims=True)
            d_score = (probs * (d_prob - center)).astype(jnp.bfloat16)
            d_query += jnp.dot(d_score, km_ref[which], preferred_element_type=jnp.float32)
            dk_ref[half, :] += jnp.dot(qt_ref[half, rows], d_score, preferred_element_type=jnp.float32)
            dv_ref[half, :] += jnp.dot(
                gt_ref[half, rows], probs.astype(jnp.bfloat16), preferred_element_type=jnp.float32
            )
        dq_ref[rows, :] = d_query * DH**-0.5
        return carry

    lax.fori_loop(0, LENGTH // ROWS, one_block, 0)
    turn = (cos_ref[...], -sin_ref[...])
    results = (head_turn(dq_ref[...], *turn), head_turn(dk_ref[...].T, *turn), dv_ref[...].T)
    for part, array in enumerate(results):
        start = pl.multiple_of((part * pairs + pair) * PAIR, PAIR)
        out_ref[:, pl.ds(start, PAIR)] = array.astype(jnp.bfloat16)


def column_block(offset):
    return pl.BlockSpec((LENGTH, PAIR), lambda pair: (0, pair + offset))


def whole_block(columns):
    return pl.BlockSpec((LENGTH, columns), lambda pair: (0, 0))


def attend(packed, tables):
    columns = packed.shape[1]
    pairs = columns // (3 * PAIR)
    return pl.pallas_call(
        attend_kernel,
        grid=(pairs,),
        in_specs=[column_block(part * pairs) for part in range(3)] + [whole_block(PAIR)] * 2,
        out_specs=[column_block(0), whole_block(columns), column_block(0)],
        out_shape=[
            jax.ShapeDtypeStruct((LENGTH, pairs * PAIR), jnp.bfloat16),
            jax.ShapeDtypeStruct((LENGTH, columns), jnp.bfloat16),
            jax.ShapeDtypeStruct((LENGTH, pairs * PAIR), jnp.float32),
        ],
        scratch_shapes=[pltpu.VMEM((2, PAIR, LENGTH), jnp.bfloat16), pltpu.VMEM((2, LENGTH, PAIR), jnp.bfloat16)],
        compiler_params=pltpu.CompilerParams(vmem_limit_bytes=VMEM_BYTES),
        cost_estimate=pl.CostEstimate(flops=pairs * 2**32, bytes_accessed=2**24, transcendentals=pairs * 2**21),
    )(packed, packed, packed, *tables)


def attend_back(rotated, d_attended, logs, tables):
    columns = rotated.shape[1]
    pairs = columns // (3 * PAIR)
    tall = pltpu.VMEM((PAIR, LENGTH), jnp.bfloat16)
    return pl.pallas_call(
        attend_back_kernel,
        grid=(pairs,),
        in_specs=[column_block(part * pairs) for part in range(3)]
        + [column_block(0), column_block(0)]
        + [whole_block(PAIR)] * 2,
        out_specs=whole_block(columns),
        out_shape=jax.ShapeDtypeStruct((LENGTH, columns), jnp.bfloat16),
        scratch_shapes=[
            pltpu.VMEM((2, PAIR, LENGTH), jnp.bfloat16),
            pltpu.VMEM((2, PAIR, LENGTH), jnp.bfloat16),
            pltpu.VMEM((2, LENGTH, PAIR), jnp.bfloat16),
            tall,
            tall,
            pltpu.VMEM((LENGTH, PAIR), jnp.float32),
            pltpu.VMEM((PAIR, LENGTH), jnp.float32),
            pltpu.VMEM((PAIR, LENGTH), jnp.float32),
        ],
        compiler_params=pltpu.CompilerParams(vmem_limit_bytes=VMEM_BYTES),
        cost_estimate=pl.CostEstimate(flops=pairs * 2**33, bytes_accessed=2**24, transcendentals=pairs * 2**21),
    )(rotated, rotated, rotated, d_attended, logs, *tables)


def turn_tables(positions):
    quarter = DH // 4
    frequency = jnp.exp(-jnp.log(rope_base) * jnp.arange(quarter).astype(jnp.float32) / quarter)
    angles = positions.astype(jnp.float32)[:, None] * frequency[None, :]
    cosine, sine = jnp.cos(angles), jnp.sin(angles)
    zeros, ones = jnp.zeros_like(sine), jnp.ones_like(sine)
    rows = (
        jnp.concatenate([cosine, cosine, ones, ones], axis=1),
        jnp.concatenate([sine, sine, zeros, zeros], axis=1),
    )
    return tuple(jnp.concatenate([row, row], axis=1) for row in rows)


def dot_plain(left_op, right_op):
    return jnp.dot(left_op, right_op, preferred_element_type=jnp.float32)


def dot_rows(left_op, right_op):
    return lax.dot_general(
        left_op, right_op, (((0,), (0,)), ((), ())), preferred_element_type=jnp.float32
    )


def dot_cols(left_op, right_op):
    return lax.dot_general(
        left_op, right_op, (((1,), (1,)), ((), ())), preferred_element_type=jnp.float32
    )


def layer_norm(values, gain_vec):
    center = values - jnp.mean(values, axis=-1, keepdims=True)
    spread = jnp.mean(center * center, axis=-1, keepdims=True)
    inverse = lax.rsqrt(spread + norm_eps)
    scaled = center * inverse
    return (scaled * gain_vec, scaled, inverse)


def norm_backward(upstream, scaled, inverse, gain_vec):
    weighted = upstream * gain_vec
    inner = jnp.mean(weighted, axis=-1, keepdims=True) + scaled * jnp.mean(
        weighted * scaled, axis=-1, keepdims=True
    )
    return (inverse * (weighted - inner), jnp.sum(upstream * scaled, axis=0))


def swap(values, bit):
    return lax.ppermute(values, "tensor", [(member, member ^ bit) for member in range(4)])


def spread_rows(values):
    if lax.axis_size("tensor") != 4:
        return lax.all_gather(values, "tensor", axis=0, tiled=True)
    half = values.shape[0] // 2
    near, far = swap(values, 1), swap(values, 2)
    return jnp.concatenate([values, near, far, swap(near[:half], 2), swap(far[half:], 1)], axis=0)


def sum_rows(partial):
    if lax.axis_size("tensor") != 4:
        return lax.psum_scatter(
            partial.astype(jnp.bfloat16), "tensor", scatter_dimension=0, tiled=True
        ).astype(jnp.float32)
    size = partial.shape[0] // 4
    half = size // 2
    own, near, far, last = (partial[part * size : (part + 1) * size] for part in range(4))
    first = swap(last[:half].astype(jnp.bfloat16), 1)
    second = swap(last[half:].astype(jnp.bfloat16), 2)
    far = jnp.concatenate([far[:half] + first.astype(jnp.float32), far[half:]], axis=0)
    near = jnp.concatenate([near[:half], near[half:] + second.astype(jnp.float32)], axis=0)
    return (
        own
        + swap(near.astype(jnp.bfloat16), 1).astype(jnp.float32)
        + swap(far.astype(jnp.bfloat16), 2).astype(jnp.float32)
    )


def group_positions(rows):
    group = lax.axis_size("tensor")
    blocks = jnp.arange(group)
    if group == 4:
        blocks = blocks ^ lax.axis_index("tensor")
    return (blocks[:, None] * rows + jnp.arange(rows)[None, :]).reshape(-1)


def cross_forward(queries, keys_in, values_in):
    scores = jnp.einsum("qhd,khd->hqk", queries, keys_in, preferred_element_type=jnp.float32) * DH ** (-0.5)
    peak_score = jnp.max(scores, axis=-1, keepdims=True)
    shifted = jnp.exp(scores - peak_score)
    totals = jnp.sum(shifted, axis=-1, keepdims=True)
    probabilities = (shifted / totals).astype(jnp.bfloat16)
    output = jnp.einsum("hqk,khd->qhd", probabilities, values_in, preferred_element_type=jnp.float32)
    return (output, peak_score + jnp.log(totals))


def cross_backward(queries, keys_in, values_in, d_output, log_totals):
    scaling = DH ** (-0.5)
    scores = jnp.einsum("qhd,khd->hqk", queries, keys_in, preferred_element_type=jnp.float32) * scaling
    probabilities = jnp.exp(scores - log_totals)
    d_prob = jnp.einsum("qhd,khd->hqk", d_output, values_in, preferred_element_type=jnp.float32)
    center = jnp.sum(probabilities * d_prob, axis=-1, keepdims=True)
    d_score = (probabilities * (d_prob - center)).astype(jnp.bfloat16)
    d_query = jnp.einsum("hqk,khd->qhd", d_score, keys_in, preferred_element_type=jnp.float32) * scaling
    d_key = jnp.einsum("hqk,qhd->khd", d_score, queries, preferred_element_type=jnp.float32) * scaling
    d_value = jnp.einsum(
        "hqk,qhd->khd", probabilities.astype(jnp.bfloat16), d_output, preferred_element_type=jnp.float32
    )
    return (d_query, d_key, d_value)


def by_part(columns, parts):
    rows = columns.shape[0]
    return columns.reshape(rows, -1, parts, DH).swapaxes(1, 2).reshape(rows, -1)


def by_head(columns, parts):
    rows = columns.shape[0]
    return columns.reshape(rows, parts, -1, DH).swapaxes(1, 2).reshape(rows, -1)


def pad_heads(columns, parts):
    rows, width = columns.shape
    each = width // parts
    if each % PAIR == 0:
        return columns
    return jnp.pad(columns.reshape(rows, parts, each), ((0, 0), (0, 0), (0, -each % PAIR))).reshape(rows, -1)


def drop_heads(columns, parts, width):
    rows = columns.shape[0]
    return columns.reshape(rows, parts, -1)[:, :, : width // parts].reshape(rows, width)


def dp_sum(grads):
    return lax.psum_scatter(grads.astype(jnp.bfloat16), "dp", scatter_dimension=0, tiled=True)


def after(value, earlier):
    return lax.optimization_barrier((value, earlier))[0]


MESH = pl.DeviceIdType.MESH
BLOCK = LENGTH // 4
HALF = BLOCK // 2
FULL = 160


class Links:
    def __init__(self, send, recv, local):
        self.send, self.recv, self.local = send, recv, local
        self.used = self.used_local = 0
        self.pending, self.pending_local = [], []
        self.dp, self.tensor = lax.axis_index("dp"), lax.axis_index("tensor")

    def remote(self, src, dst, dp_bit, tensor_bit):
        at = self.used
        self.used += 1
        return pltpu.make_async_remote_copy(
            src_ref=src,
            dst_ref=dst,
            send_sem=self.send.at[at],
            recv_sem=self.recv.at[at],
            device_id=(self.dp ^ dp_bit, self.tensor ^ tensor_bit),
            device_id_type=MESH,
        )

    def go(self, src, dst, dp_bit, tensor_bit):
        copy = self.remote(src, dst, dp_bit, tensor_bit)
        copy.start()
        self.pending.append(copy)
        return copy

    def store(self, src, dst):
        copy = pltpu.make_async_copy(src, dst, self.local.at[self.used_local])
        self.used_local += 1
        copy.start()
        self.pending_local.append(copy)
        return copy

    def settle(self, copy):
        copy.wait()
        self.pending_local = [other for other in self.pending_local if other is not copy]

    def settle_sends(self, copies):
        for copy in copies:
            copy.wait_send()
        self.pending = [copy for copy in self.pending if all(copy is not other for other in copies)]

    def greet(self, partners):
        barrier = pltpu.get_barrier_semaphore()
        for dp_bit, tensor_bit in partners:
            pl.semaphore_signal(
                barrier, inc=1, device_id=(self.dp ^ dp_bit, self.tensor ^ tensor_bit), device_id_type=MESH
            )
        pl.semaphore_wait(barrier, len(partners))

    def finish(self):
        assert self.used <= self.send.shape[0]
        assert self.used_local <= self.local.shape[0]
        for copy in self.pending:
            copy.wait_send()
        for copy in self.pending_local:
            copy.wait()


class Spread:
    def __init__(self, links, rows):
        self.links, self.rows = links, rows
        half = rows.shape[1] // 2
        self.low, self.high = pl.ds(0, half), pl.ds(half, half)
        self.near_low = links.go(rows.at[0, self.low], rows.at[1, self.low], 0, 1)
        self.far_high = links.go(rows.at[0, self.high], rows.at[2, self.high], 0, 2)
        self.near_high = links.go(rows.at[0, self.high], rows.at[1, self.high], 0, 1)
        self.far_low = links.go(rows.at[0, self.low], rows.at[2, self.low], 0, 2)
        self.stage = 0

    def wait(self, block):
        rows, links, low, high = self.rows, self.links, self.low, self.high
        if block >= 1 and self.stage == 0:
            self.near_low.wait_recv()
            self.last_low = links.go(rows.at[1, low], rows.at[3, low], 0, 2)
            self.far_high.wait_recv()
            self.last_high = links.go(rows.at[2, high], rows.at[3, high], 0, 1)
            self.near_high.wait_recv()
            self.stage = 1
        if block >= 2 and self.stage == 1:
            self.far_low.wait_recv()
            self.stage = 2
        if block >= 3 and self.stage == 2:
            self.last_low.wait_recv()
            self.last_high.wait_recv()
            self.stage = 3

    def sent(self):
        self.links.settle_sends(
            (self.near_low, self.far_high, self.near_high, self.far_low, self.last_low, self.last_high)
        )


class SpreadCross:
    def __init__(self, links, weights, place):
        self.links, self.weights, self.place = links, weights, place
        self.which = links.dp % 2
        half = weights.shape[3] // 2
        self.low, self.high = pl.ds(0, half), pl.ds(half, half)
        whole = slice(None)
        self.near = links.go(self.piece(0, whole), self.piece(1, whole), 0, 1)
        self.far = links.go(self.piece(0, whole), self.piece(2, whole), 0, 2)
        self.core = [self.cross(0)]

    def piece(self, member, rows):
        return self.weights.at[member, self.place, self.which, rows]

    def cross(self, member):
        return self.links.go(self.piece(member, slice(None)), self.piece(member, slice(None)), 1, 0)

    def forward(self):
        links = self.links
        self.near.wait_recv()
        self.last_low = links.go(self.piece(1, self.low), self.piece(3, self.low), 0, 2)
        self.core.append(self.cross(1))
        self.far.wait_recv()
        self.last_high = links.go(self.piece(2, self.high), self.piece(3, self.high), 0, 1)
        self.core.append(self.cross(2))

    def last(self):
        self.last_low.wait_recv()
        self.last_high.wait_recv()
        self.core.append(self.cross(3))


class Gather:
    def __init__(self, links, shard, whole, both_cores=True):
        self.links, self.whole, self.both_cores = links, whole, both_cores
        self.size = shard.shape[0]
        self.place, self.which = links.dp // 2, links.dp % 2
        self.middle = (self.place == 1) | (self.place == 2)
        own = self.rows(0)
        self.own = links.store(shard, own)
        self.core = []
        self.pass_on(shard, own)
        self.skip = links.go(shard, own, 4, 0)
        self.beside = links.go(shard, own, 2, 0)
        self.third_at = links.used
        self.third = links.remote(shard, own, 6, 0)

        @pl.when(self.middle)
        def _():
            self.third.start()

    def pass_on(self, src, dst):
        if self.both_cores:
            self.core.append(self.links.go(src, dst, 1, 0))

    def rows(self, step):
        if len(self.whole.shape) == 4:
            return self.whole.at[self.place ^ step, self.which]
        start = pl.multiple_of((self.links.dp ^ (2 * step)) * self.size, self.size)
        return self.whole.at[pl.ds(start, self.size)]

    def forward(self):
        links = self.links
        block = self.rows(2)
        self.skip.wait_recv()
        self.onward = pltpu.make_async_remote_copy(
            src_ref=block,
            dst_ref=block,
            send_sem=links.send.at[links.used],
            recv_sem=links.recv.at[self.third_at],
            device_id=(links.dp ^ 2, links.tensor),
            device_id_type=MESH,
        )
        links.used += 1

        @pl.when(self.middle)
        def _():
            self.onward.start()

        self.pass_on(block, block)

    def arrive(self):
        links = self.links
        self.beside.wait_recv()
        block = self.rows(1)
        self.pass_on(block, block)
        self.third.wait_recv()
        block = self.rows(3)
        self.pass_on(block, block)
        links.settle(self.own)
        for copy in self.core:
            copy.wait_recv()

    def sent(self):
        self.links.settle_sends(self.core)
        self.finish()

    def finish(self):
        @pl.when(self.middle)
        def _():
            self.third.wait_send()
            self.onward.wait_send()


class Sums:
    def __init__(self, links, parts, half_near, half_far, near, far):
        self.links, self.parts = links, parts
        self.half_near, self.half_far, self.near, self.far = half_near, half_far, near, far
        half = parts.shape[1] // 2
        self.low, self.high = pl.ds(0, half), pl.ds(half, half)

    def ready(self, block):
        links, parts, low, high = self.links, self.parts, self.low, self.high
        if block == 3:
            self.first = links.go(parts.at[3, low], self.half_near, 0, 1)
            self.second = links.go(parts.at[3, high], self.half_far, 0, 2)
        if block == 1:
            self.near_low = links.go(parts.at[1, low], self.near.at[low], 0, 1)
        if block == 2:
            self.far_high = links.go(parts.at[2, high], self.far.at[high], 0, 2)

    def add_half(self, block, start, got):
        def add(rows, from_rows):
            total = self.parts[block, rows].astype(jnp.float32) + got[from_rows].astype(jnp.float32)
            self.parts[block, rows] = total.astype(jnp.bfloat16)

        half = got.shape[0]
        step = math.gcd(half, 32)

        def body(index, carry):
            at = index * step if step == 1 else pl.multiple_of(index * step, step)
            add(pl.ds(start + at, step), pl.ds(at, step))
            return carry

        lax.fori_loop(0, half // step, body, 0)

    def add(self):
        links, parts, low, high = self.links, self.parts, self.low, self.high
        half = parts.shape[1] // 2
        self.first.wait_recv()
        self.add_half(2, 0, self.half_near)
        self.far_low = links.go(parts.at[2, low], self.far.at[low], 0, 2)
        self.second.wait_recv()
        self.add_half(1, half, self.half_far)
        self.near_high = links.go(parts.at[1, high], self.near.at[high], 0, 1)

    def arrive(self):
        for copy in (self.near_low, self.far_high, self.far_low, self.near_high):
            copy.wait_recv()

    def sent(self):
        self.links.settle_sends(
            (self.first, self.second, self.near_low, self.far_high, self.far_low, self.near_high)
        )

    def total(self, rows):
        return self.near[rows].astype(jnp.float32) + self.far[rows].astype(jnp.float32)
def columns(total, width, body):
    def step(index, carry):
        body(pl.ds(pl.multiple_of(index * width, width), width))
        return carry

    lax.fori_loop(0, total // width, step, 0)


def attend_rows(block, keys_t, values, limit):
    outs, logs = [], []
    for which in range(2):
        part = jnp.where(half_mask(block.shape, 1, which), block, jnp.zeros_like(block))
        scores = jnp.dot(part, keys_t, preferred_element_type=jnp.float32)
        if limit is not None:
            scores = jnp.where(lax.broadcasted_iota(jnp.int32, scores.shape, 1) < limit, scores, -jnp.inf)
        peak = jnp.max(scores, axis=1, keepdims=True)
        shifted = jnp.exp(scores - peak)
        total = jnp.sum(shifted, axis=1, keepdims=True)
        product = jnp.dot(shifted.astype(jnp.bfloat16), values, preferred_element_type=jnp.float32)
        outs.append(product * (1.0 / total))
        logs.append(peak + jnp.log(total))
    low = half_mask(block.shape, 1, 0)
    return jnp.where(low, outs[0], outs[1]), jnp.where(low, logs[0], logs[1])


def cross_tile(weights, member, place, cols):
    tile = weights[member, place, :, :, cols]
    return tile.reshape(-1, tile.shape[-1])


def cross_columns(weights, member, cols):
    whole = weights[member, :, :, :, cols]
    return whole.reshape(-1, whole.shape[-1])


def row_steps(total, body):
    def step(index, carry):
        body(pl.ds(pl.multiple_of(index * 32, 32), 32))
        return carry

    lax.fori_loop(0, total // 32, step, 0)


def block_rows(block):
    return pl.ds(block * BLOCK, BLOCK)


def two_heads(weights, part, parts, pair):
    starts = [((2 * pair + which) * parts + part) * DH for which in range(2)]
    return jnp.concatenate([weights[:, start : start + DH] for start in starts], axis=1).astype(jnp.bfloat16)


def fill_tables(cosine, sine, member):
    quarter = DH // 4
    shape = (BLOCK, PAIR)
    lane = lax.broadcasted_iota(jnp.int32, shape, 1) % DH
    frequency = jnp.exp((lane % quarter).astype(jnp.float32) * (-math.log(rope_base) / quarter))
    for block in range(4):
        place = (member ^ block) * BLOCK + lax.broadcasted_iota(jnp.int32, shape, 0)
        angle = place.astype(jnp.float32) * frequency
        rows = block_rows(block)
        cosine[rows] = jnp.where(lane < 2 * quarter, jnp.cos(angle), 1.0)
        sine[rows] = jnp.where(lane < 2 * quarter, jnp.sin(angle), 0.0)


def forward_kernel(
    latents, gains, conditioning, f32_qkv,
    f32_attn_out, f32_cross_q, f32_cross_kv, f32_cross_out, f32_gate, f32_up, f32_down,
    rows_one_out, normed_two_out, rows_three_out, qkv_out, attn_out_out, cross_out, keyval_w_out, mlp_out,
    down_out, rotated_out, attended_out, logs_out,
    query_out, keyval_out, crossed_out, cross_logs_out, resid_one_out, resid_two_out, tables_out,
    rows_one, normed_two, rows_three, w_qkv, w_attn_out, w_cross, w_keyval, rotated, attended, logs, query, keyval,
    crossed, cross_logs, keys_t, parts, got_one, resid_one, resid_two,
    packed, tables, context, raw_attn_out, raw_cross_q, raw_cross_kv, raw_cross_out, raw_gate, raw_up, raw_down,
    own_qkv, own_attn_out, own_cross, own_keyval, own_mlp, own_down, send, recv, local,
):
    low = jnp.bfloat16
    pairs = attended.shape[1] // PAIR
    width = pairs * PAIR
    share = own_qkv.shape[0]
    links = Links(send, recv, local)
    loads = [
        links.store(source, target)
        for source, target in (
            (f32_attn_out, raw_attn_out), (f32_cross_q, raw_cross_q), (f32_cross_kv, raw_cross_kv),
            (f32_cross_out, raw_cross_out), (f32_gate, raw_gate), (f32_up, raw_up), (f32_down, raw_down),
        )
    ]
    for part in range(3):
        for pair in range(pairs):
            at = part * width + pair * PAIR
            own_qkv[:, at : at + PAIR] = two_heads(f32_qkv, part, 3, pair)
    links.greet([(1, 0), (2, 0), (4, 0), (6, 0), (0, 1), (0, 2)])
    gather_qkv = Gather(links, own_qkv, w_qkv)

    def norm_one(rows):
        rows_one[0, rows] = layer_norm(latents[rows].astype(jnp.float32), gains[0:1])[0].astype(low)

    row_steps(BLOCK, norm_one)
    spread_one = Spread(links, rows_one)
    cosine, sine = (tables.at[part] for part in range(2))
    fill_tables(cosine, sine, links.tensor)
    links.store(tables, tables_out)
    for load in loads:
        links.settle(load)
    own_attn_out[...] = raw_attn_out[...].astype(low)
    own_cross[:, :width] = raw_cross_q[...].astype(low)
    own_cross[:, width:] = raw_cross_out[...].astype(low)
    for part in range(2):
        for pair in range(pairs):
            at = part * width + pair * PAIR
            own_keyval[:, at : at + PAIR] = two_heads(raw_cross_kv, part, 2, pair)
    hidden = raw_gate.shape[1]
    own_mlp[:, :hidden] = raw_gate[...].astype(low)
    own_mlp[:, hidden:] = raw_up[...].astype(low)
    own_down[...] = raw_down[...].astype(low)
    links.store(own_down, down_out)
    context[...] = jnp.zeros_like(context)
    context[:CTX] = conditioning[0]
    spread_one.wait(1)
    gather_qkv.forward()
    gather_attn_out = Gather(links, own_attn_out, w_attn_out)
    gather_cross = Gather(links, own_cross, w_cross.at[0], False)
    spread_one.wait(2)
    links.settle(gather_cross.own)
    spread_cross = [SpreadCross(links, w_cross, links.dp // 2)]
    gather_qkv.arrive()
    links.store(w_qkv, qkv_out)

    for block in range(4):
        spread_one.wait(block)
        rows = block_rows(block)
        turn = (cosine[rows], sine[rows])

        def project(cols):
            packed[:, cols] = dot_plain(rows_one[block], w_qkv[:, cols])

        columns(3 * width, width, project)
        for part in range(3):
            for pair in range(pairs):
                at = slice(part * width + pair * PAIR, part * width + (pair + 1) * PAIR)
                value = packed[:, at]
                rotated[rows, at] = (value if part == 2 else head_turn(value, *turn)).astype(low)
    links.store(rows_one, rows_one_out)
    links.store(rotated, rotated_out)
    for pair in range(pairs):
        key = rotated[:, width + pair * PAIR : width + (pair + 1) * PAIR]
        keys_t[pair] = key.astype(jnp.float32).T.astype(low)

    def out_project(source, block, weight, sums):
        def project(cols):
            parts[block, :, cols] = dot_cols(source[block_rows(block)], weight(cols)).astype(low)

        columns(parts.shape[2], 512, project)
        sums.ready(block)

    sums_one = Sums(links, parts, *got_one)
    for block in (3, 1, 2, 0):
        rows = block_rows(block)

        def one_pair(pair, carry):
            at = pl.ds(pl.multiple_of(pair * PAIR, PAIR), PAIR)
            values_at = pl.ds(pl.multiple_of(2 * width + pair * PAIR, PAIR), PAIR)
            out, log = attend_rows(rotated[rows, at] * low(DH**-0.5), keys_t[pair], rotated[:, values_at], None)
            attended[rows, at] = out.astype(low)
            logs[rows, at] = log
            return carry

        lax.fori_loop(0, pairs, one_pair, 0)
        if block == 3:
            gather_attn_out.forward()
            gather_attn_out.arrive()
            links.store(w_attn_out, attn_out_out)
        out_project(attended, block, lambda cols: w_attn_out[cols, :], sums_one)
        if block == 3:
            spread_cross[0].forward()
            gather_keyval = Gather(links, own_keyval, w_keyval)
            gather_cross.forward()
            gather_mlp = Gather(links, own_mlp, mlp_out)
            spread_cross.append(SpreadCross(links, w_cross, (links.dp // 2) ^ 2))
        if block == 1:
            gather_cross.beside.wait_recv()
            spread_cross.append(SpreadCross(links, w_cross, (links.dp // 2) ^ 1))
        if block == 2:
            gather_keyval.forward()
            sums_one.add()
            spread_cross[1].forward()
    gather_cross.third.wait_recv()
    spread_cross.append(SpreadCross(links, w_cross, (links.dp // 2) ^ 3))
    spread_cross[2].forward()
    links.store(attended, attended_out)
    links.store(logs, logs_out)
    sums_one.arrive()

    def norm_two(rows):
        value = latents[rows].astype(jnp.float32) + parts[0, rows].astype(jnp.float32) + sums_one.total(rows)
        resid_one[rows] = value
        normed_two[rows] = layer_norm(value, gains[1:2])[0].astype(low)

    row_steps(BLOCK, norm_two)
    links.store(resid_one, resid_one_out)
    links.store(normed_two, normed_two_out)
    gather_keyval.arrive()
    links.store(w_keyval, keyval_w_out)
    keyval[0] = dot_plain(context[...], w_keyval[...]).astype(low)
    spread_keyval = Spread(links, keyval)
    spread_cross[3].forward()
    for spread in spread_cross:
        spread.last()
    resid_two[...] = resid_one[...]
    for member in range(4):
        for spread in spread_cross:
            spread.core[member].wait_recv()
        spread_keyval.wait(member)
        at_member = slice(member * width, (member + 1) * width)
        query[:, at_member] = dot_plain(normed_two[...], cross_columns(w_cross, member, slice(0, width))).astype(low)
        for pair in range(pairs):
            at = slice(member * width + pair * PAIR, member * width + (pair + 1) * PAIR)
            keys_at = slice(pair * PAIR, (pair + 1) * PAIR)
            values_at = slice(width + pair * PAIR, width + (pair + 1) * PAIR)
            key_t = keyval[member, :, keys_at].astype(jnp.float32).T.astype(low)
            out, log = attend_rows(query[:, at] * low(DH**-0.5), key_t, keyval[member, :, values_at], CTX)
            crossed[:, at] = out.astype(low)
            cross_logs[:, at] = log
        for place in range(4):
            at = slice(place * 2 * share, (place + 1) * 2 * share)
            tile = cross_tile(w_cross, member, place, slice(width, 2 * width))
            resid_two[:, at] += dot_cols(crossed[:, at_member], tile)
        if member == 1:
            gather_mlp.forward()
    links.store(w_cross, cross_out)
    links.store(keyval, keyval_out)
    links.store(query, query_out)
    links.store(crossed, crossed_out)
    links.store(cross_logs, cross_logs_out)
    links.store(resid_two, resid_two_out)

    def norm_three(rows):
        rows_three[rows] = layer_norm(resid_two[rows], gains[2:3])[0].astype(low)

    row_steps(BLOCK, norm_three)
    gather_mlp.arrive()
    links.store(rows_three, rows_three_out)
    links.finish()
    for gather in (gather_qkv, gather_attn_out, gather_cross, gather_keyval, gather_mlp):
        gather.finish()


def whole_vmem():
    return pl.BlockSpec(memory_space=pltpu.VMEM)


def anywhere():
    return pl.BlockSpec(memory_space=pl.ANY)


def sum_buffers(model):
    return [
        pltpu.VMEM((HALF, model), jnp.bfloat16),
        pltpu.VMEM((HALF, model), jnp.bfloat16),
        pltpu.VMEM((BLOCK, model), jnp.bfloat16),
        pltpu.VMEM((BLOCK, model), jnp.bfloat16),
    ]


def forward_part(latents, gains, conditioning, weights):
    w_qkv, w_attn_out, w_cross_q, w_cross_kv, w_cross_out, w_gate, w_up, w_down = weights
    model = latents.shape[1]
    depth = conditioning.shape[2]
    wide = w_qkv.shape[1]
    width = wide // 3
    hidden = w_gate.shape[1]
    pairs = width // PAIR
    low, high = jnp.bfloat16, jnp.float32
    share = w_qkv.shape[0]
    outs = [
        ((4, BLOCK, model), low),
        ((BLOCK, model), low),
        ((BLOCK, model), low),
        ((model, wide), low),
        ((model, width), low),
        ((4, 4, 2, share, 2 * width), low),
        ((depth, 2 * width), low),
        ((4, 2, share, 2 * hidden), low),
        ((share, hidden), low),
        ((LENGTH, wide), low),
        ((LENGTH, width), low),
        ((LENGTH, width), high),
        ((BLOCK, model), low),
        ((4, FULL, 2 * width), low),
        ((BLOCK, model), low),
        ((BLOCK, model), high),
        ((BLOCK, model), high),
        ((BLOCK, model), high),
        ((2, LENGTH, PAIR), high),
    ]
    work = [
        ((4, BLOCK, model), low),
        ((BLOCK, model), low),
        ((BLOCK, model), low),
        ((model, wide), low),
        ((model, width), low),
        ((4, 4, 2, share, 2 * width), low),
        ((depth, 2 * width), low),
        ((LENGTH, wide), low),
        ((LENGTH, width), low),
        ((LENGTH, width), high),
        ((BLOCK, model), low),
        ((4, FULL, 2 * width), low),
        ((BLOCK, model), low),
        ((BLOCK, model), high),
        ((pairs, PAIR, LENGTH), low),
        ((4, BLOCK, model), low),
    ]
    more = [
        ((BLOCK, model), high),
        ((BLOCK, model), high),
        ((BLOCK, wide), high),
        ((2, LENGTH, PAIR), high),
        ((FULL, depth), low),
        (w_attn_out.shape, high),
        (w_cross_q.shape, high),
        (w_cross_kv.shape, high),
        (w_cross_out.shape, high),
        (w_gate.shape, high),
        (w_up.shape, high),
        (w_down.shape, high),
        ((share, wide), low),
        ((share, width), low),
        ((share, 2 * width), low),
        (w_cross_kv.shape, low),
        ((share, 2 * hidden), low),
        ((share, hidden), low),
    ]
    scratch = [pltpu.VMEM(*buffer) for buffer in work] + [sum_buffers(model)]
    scratch += [pltpu.VMEM(*buffer) for buffer in more]
    scratch += [pltpu.SemaphoreType.DMA((96,)), pltpu.SemaphoreType.DMA((96,)), pltpu.SemaphoreType.DMA((40,))]
    return pl.pallas_call(
        forward_kernel,
        out_shape=[jax.ShapeDtypeStruct(*out) for out in outs],
        in_specs=[whole_vmem()] * 4 + [anywhere()] * 7,
        out_specs=[anywhere()] * len(outs),
        scratch_shapes=scratch,
        compiler_params=pltpu.CompilerParams(collective_id=1, has_side_effects=True, vmem_limit_bytes=VMEM_BYTES),
        cost_estimate=pl.CostEstimate(flops=2**37, bytes_accessed=2**26, transcendentals=2**23),
    )(latents, gains, conditioning, *weights)


class Scatter:
    def __init__(self, links, grads, got_core, extra, got):
        self.links, self.grads, self.got_core, self.extra, self.got = links, grads, got_core, extra, got
        self.size = got.shape[1]
        self.place, self.which = links.dp // 2, links.dp % 2
        self.middle = (self.place == 1) | (self.place == 2)

    def rows(self, place, which):
        if self.got_core is None:
            return place
        start = pl.multiple_of((2 * place + which) * self.size, self.size)
        return pl.ds(start, self.size)

    def pair_up(self):
        self.core = [
            self.links.go(self.grads.at[self.rows(place, 1 - self.which)], self.got_core.at[place], 1, 0)
            for place in range(4)
        ]

    def combine(self):
        for copy in self.core:
            copy.wait_recv()

        def add(place, carry):
            rows = self.rows(place, self.which)
            total = self.grads[rows].astype(jnp.float32) + self.got_core[place].astype(jnp.float32)
            self.grads[rows] = total.astype(jnp.bfloat16)
            return carry

        lax.fori_loop(0, 4, add, 0)
        self.start()

    def start(self):
        links, grads = self.links, self.grads
        block = [grads.at[self.rows(self.place ^ step, self.which)] for step in range(4)]
        self.to_extra = links.remote(block[3], self.extra, 2, 0)
        self.to_third = links.remote(block[3], self.got.at[2], 6, 0)
        self.to_skip = links.remote(block[2], self.got.at[1], 4, 0)

        @pl.when(self.middle)
        def _():
            self.to_third.start()

        @pl.when(jnp.logical_not(self.middle))
        def _():
            self.to_extra.start()
            self.to_skip.start()

        self.beside = links.go(block[1], self.got.at[0], 2, 0)

    def relay(self):
        @pl.when(self.middle)
        def _():
            self.to_extra.wait_recv()
            rows = self.rows(self.place ^ 2, self.which)
            self.grads[rows] = (
                self.grads[rows].astype(jnp.float32) + self.extra[...].astype(jnp.float32)
            ).astype(jnp.bfloat16)
            self.to_skip.start()

    def arrive(self):
        self.beside.wait_recv()
        self.to_skip.wait_recv()

        @pl.when(self.middle)
        def _():
            self.to_third.wait_recv()

    def total(self, out, cols):
        rows = self.rows(self.place, self.which)
        at = (rows, cols) if self.got_core is not None else (rows, slice(None), cols)
        mine = self.grads[at].astype(jnp.float32)
        out[...] = mine + self.got[0, :, cols].astype(jnp.float32) + self.got[1, :, cols].astype(jnp.float32)

        @pl.when(self.middle)
        def _():
            out[...] += self.got[2, :, cols].astype(jnp.float32)

    def finish(self):
        self.to_skip.wait_send()

        @pl.when(self.middle)
        def _():
            self.to_third.wait_send()

        @pl.when(jnp.logical_not(self.middle))
        def _():
            self.to_extra.wait_send()


def attend_rows_back(block, grads, log, keys_t, values_t, keys, d_keys_t, d_values_t, limit):
    block_t = block.astype(jnp.float32).T.astype(jnp.bfloat16)
    grads_t = grads.astype(jnp.float32).T.astype(jnp.bfloat16)
    outs = []
    for which in range(2):
        half = slice(which * DH, (which + 1) * DH)
        keep = half_mask(block.shape, 1, which)
        scores = jnp.dot(jnp.where(keep, block, jnp.zeros_like(block)), keys_t, preferred_element_type=jnp.float32)
        probs = jnp.exp(scores - log[:, which * DH : which * DH + 1])
        if limit is not None:
            probs = jnp.where(lax.broadcasted_iota(jnp.int32, probs.shape, 1) < limit, probs, 0.0)
        d_prob = jnp.dot(jnp.where(keep, grads, jnp.zeros_like(grads)), values_t, preferred_element_type=jnp.float32)
        center = jnp.sum(probs * d_prob, axis=1, keepdims=True)
        d_score = (probs * (d_prob - center)).astype(jnp.bfloat16)
        outs.append(jnp.dot(d_score, keys, preferred_element_type=jnp.float32))
        d_keys_t[half, :] += jnp.dot(block_t[half], d_score, preferred_element_type=jnp.float32)
        d_values_t[half, :] += jnp.dot(grads_t[half], probs.astype(jnp.bfloat16), preferred_element_type=jnp.float32)
    return jnp.where(half_mask(block.shape, 1, 0), outs[0], outs[1]) * DH**-0.5


def backward_kernel(
    latents, gains, conditioning, in_gain, in_d_resid, in_seed,
    in_grads_cross, in_d_keyval, in_qkv, in_attn_out, in_keyval_w, in_rows_one, in_rotated, in_attended, in_logs,
    in_tables,
    grad_latents, grad_context, grad_gains, grad_qkv, grad_attn_out, grad_cross_q, grad_keyval, grad_cross_out,
    parts, rows_one, seeds, w_qkv, w_attn_out, w_keyval, rotated, attended, d_attended, logs, keys_t, values_t,
    d_keys_t, d_values_t, grads_cross, core_cross, got_cross, keyval_parts, got_keyval, context, context_sum,
    context_got, d_resid, tables, gain_rows, gain_got, got, core_qkv, core_attn_out, core_keyval,
    extra_qkv, extra_attn_out, extra_cross, extra_keyval, far_qkv, far_attn_out, far_cross, far_keyval,
    sum_keyval, sum_last, out_qkv, out_keyval, send, recv, local,
):
    low = jnp.bfloat16
    width = attended.shape[1]
    pairs = width // PAIR
    model = latents.shape[1]
    links = Links(send, recv, local)
    which = links.dp % 2
    load_seed = links.store(in_seed, seeds)
    load_self = [
        links.store(source, target)
        for source, target in (
            (in_attn_out, w_attn_out), (in_rotated, rotated), (in_logs, logs), (in_tables, tables),
            (in_attended, attended),
        )
    ]
    load_keyval = [links.store(in_d_keyval, keyval_parts), links.store(in_keyval_w, w_keyval)]
    load_cross = [links.store(in_grads_cross.at[member, :, which], grads_cross.at[member]) for member in range(4)]
    load_late = [links.store(in_qkv, w_qkv), links.store(in_rows_one, rows_one), links.store(in_d_resid, d_resid)]
    links.greet([(1, 0), (2, 0), (4, 0), (6, 0), (0, 1), (0, 2)])
    core_copies = [
        links.go(in_grads_cross.at[member, :, 1 - which], core_cross.at[member], 1, 0) for member in range(4)
    ]
    gain_rows[...] = in_gain[...]
    context[...] = jnp.zeros_like(context)
    context[:CTX] = conditioning[0]
    sums_keyval = Sums(links, keyval_parts, *got_keyval)
    sums_cross = Sums(links, grads_cross, *got_cross)
    for load in load_keyval:
        links.settle(load)
    for part in (3, 1, 2):
        sums_keyval.ready(part)
    for member in (3, 1, 2, 0):
        links.settle(load_cross[member])
        core_copies[member].wait_recv()

        def add(place, carry):
            total = grads_cross[member, place].astype(jnp.float32) + core_cross[member, place].astype(jnp.float32)
            grads_cross[member, place] = total.astype(low)
            return carry

        lax.fori_loop(0, 4, add, 0)
        sums_cross.ready(member)
    links.settle(load_seed)
    for load in load_self:
        links.settle(load)
    for pair in range(pairs):
        key = rotated[:, width + pair * PAIR : width + (pair + 1) * PAIR]
        value = rotated[:, 2 * width + pair * PAIR : 2 * width + (pair + 1) * PAIR]
        keys_t[pair] = key.astype(jnp.float32).T.astype(low)
        values_t[pair] = value.astype(jnp.float32).T.astype(low)
    d_keys_t[...] = jnp.zeros_like(d_keys_t)
    d_values_t[...] = jnp.zeros_like(d_values_t)
    cosine, sine = (tables.at[part] for part in range(2))

    def whole(rows, cols):
        return rows[:, :, cols].reshape(LENGTH, -1)

    def grads_into(target, rows, right):
        def product(part):
            target[part, :] = dot_rows(whole(rows, part), right).astype(low)

        columns(model, 384, product)

    for block in range(4):
        d_attended[block_rows(block)] = dot_plain(seeds[block], w_attn_out[...]).astype(low)
    grads_into(w_attn_out, seeds, attended[...])
    scatter_attn_out = Scatter(links, w_attn_out, core_attn_out, extra_attn_out, far_attn_out)
    scatter_attn_out.pair_up()

    for block in range(4):
        rows = block_rows(block)
        turn = (cosine[rows], -sine[rows])

        def one_pair(pair, carry):
            at = pl.ds(pl.multiple_of(pair * PAIR, PAIR), PAIR)
            keys_at = pl.ds(pl.multiple_of(width + pair * PAIR, PAIR), PAIR)
            out = attend_rows_back(
                rotated[rows, at] * low(DH**-0.5), d_attended[rows, at], logs[rows, at], keys_t[pair],
                values_t[pair], rotated[:, keys_at], d_keys_t.at[pair], d_values_t.at[pair], None,
            )
            rotated[rows, at] = head_turn(out, *turn).astype(low)
            return carry

        lax.fori_loop(0, pairs, one_pair, 0)
        if block == 0:
            sums_keyval.add()
            sums_cross.add()
        if block == 1:
            scatter_attn_out.combine()
        if block == 2:
            sums_keyval.arrive()
            d_keyval = keyval_parts[0].astype(jnp.float32) + sums_keyval.total(slice(None))
            d_keyval = d_keyval.astype(low)
            context_sum[...] = dot_cols(d_keyval, w_keyval[...]).astype(low)
            context_near = links.go(context_sum, context_got.at[0], 0, 1)
            w_keyval[...] = dot_rows(context[...], d_keyval).astype(low)
            scatter_keyval = Scatter(links, w_keyval, core_keyval, extra_keyval, far_keyval)
            scatter_keyval.pair_up()
    sums_cross.arrive()
    for place in range(4):
        total = grads_cross[0, place].astype(jnp.float32) + sums_cross.total(place)
        grads_cross[0, place] = total.astype(low)
    scatter_cross = Scatter(links, grads_cross.at[0], None, extra_cross, far_cross)
    scatter_cross.start()
    scatter_attn_out.relay()
    scatter_keyval.combine()
    for pair in range(pairs):
        for block in range(4):
            rows = block_rows(block)
            turn = (cosine[rows], -sine[rows])
            at = slice(width + pair * PAIR, width + (pair + 1) * PAIR)
            rotated[rows, at] = head_turn(d_keys_t[pair, :, rows].T, *turn).astype(low)
            at = slice(2 * width + pair * PAIR, 2 * width + (pair + 1) * PAIR)
            rotated[rows, at] = d_values_t[pair, :, rows].T.astype(low)
    for load in load_late:
        links.settle(load)
    sums = Sums(links, parts, *got)
    for block in (3, 1, 2, 0):

        def project(cols):
            parts[block, :, cols] = dot_cols(rotated[block_rows(block)], w_qkv[cols, :]).astype(low)

        columns(model, 512, project)
        sums.ready(block)
    grads_into(w_qkv, rows_one, rotated[...])
    scatter_qkv = Scatter(links, w_qkv, core_qkv, extra_qkv, far_qkv)
    scatter_qkv.pair_up()
    sums.add()
    scatter_qkv.combine()
    scatter_cross.relay()
    scatter_keyval.relay()
    context_near.wait_recv()
    links.settle_sends((context_near,))
    context_sum[...] = (context_sum[...].astype(jnp.float32) + context_got[0].astype(jnp.float32)).astype(low)
    context_far = links.go(context_sum, context_got.at[1], 0, 2)
    sums.arrive()

    def norm_one(rows):
        gain = gains[0:1]
        _, scaled, inverse = layer_norm(latents[rows].astype(jnp.float32), gain)
        d_normed = parts[0, rows].astype(jnp.float32) + sums.total(rows)
        d_part, gain_grad = norm_backward(d_normed, scaled, inverse, gain)
        gain_rows[0:1] += gain_grad[None]
        d_resid[rows] += d_part

    row_steps(BLOCK, norm_one)
    links.store(d_resid, grad_latents)
    share = out_qkv.shape[0]
    spot = [logs.at[pl.ds(step * share, share)] for step in range(5)]
    qkv_spot = spot[3:5] + [sum_last]
    for step, (dp_bit, tensor_bit) in enumerate(((1, 0), (0, 1), (0, 2), (2, 0), (4, 0))):
        trade = links.remote(gain_rows, gain_got.at[step], dp_bit, tensor_bit)
        trade.start()
        if step == 1:
            scatter_qkv.relay()
        trade.wait()
        gain_rows[...] += gain_got[step]
    grad_gains[...] = gain_rows[...]
    context_far.wait_recv()
    context_total = context_sum[...].astype(jnp.float32) + context_got[1].astype(jnp.float32)
    grad_context[0] = context_total[:CTX]
    scatter_attn_out.arrive()
    scatter_attn_out.total(spot[2], slice(None))
    links.store(spot[2], grad_attn_out)
    scatter_qkv.arrive()
    for part in range(3):
        scatter_qkv.total(qkv_spot[part], slice(part * width, (part + 1) * width))
    for pair in range(pairs):
        heads_of = [
            qkv_spot[part][:, (2 * pair + half) * DH : (2 * pair + half + 1) * DH]
            for half in range(2)
            for part in range(3)
        ]
        for step in range(3):
            start = (3 * pair + step) * PAIR
            out_qkv[:, start : start + PAIR] = jnp.concatenate(heads_of[2 * step : 2 * step + 2], axis=1)
    links.store(out_qkv, grad_qkv)
    scatter_cross.arrive()
    scatter_cross.total(spot[0], slice(0, width))
    links.store(spot[0], grad_cross_q)
    scatter_cross.total(spot[1], slice(width, 2 * width))
    links.store(spot[1], grad_cross_out)
    scatter_keyval.arrive()
    scatter_keyval.total(sum_keyval, slice(None))
    for head in range(width // DH):
        pieces = [sum_keyval[:, start + head * DH : start + (head + 1) * DH] for start in (0, width)]
        out_keyval[:, 2 * head * DH : 2 * (head + 1) * DH] = jnp.concatenate(pieces, axis=1)
    links.store(out_keyval, grad_keyval)
    links.finish()
    for scatter in (scatter_keyval, scatter_cross, scatter_attn_out, scatter_qkv):
        scatter.finish()


def backward_part(latents, gains, conditioning, gain_rows, d_resid, seed, grads_cross, d_keyval, kept):
    w_qkv, w_attn_out, w_keyval, rows_one, rotated, attended, logs, tables = kept
    model = latents.shape[1]
    depth = conditioning.shape[2]
    wide = w_qkv.shape[1]
    width = wide // 3
    pairs = width // PAIR
    members = lax.axis_size("dp")
    share, span = model // members, depth // members
    low, high = jnp.bfloat16, jnp.float32
    outs = [
        ((BLOCK, model), high),
        (conditioning.shape, high),
        ((8, model), high),
        ((share, wide), high),
        ((share, width), high),
        ((share, width), high),
        ((span, 2 * width), high),
        ((share, width), high),
    ]
    cross_block = (4, share, 2 * width)
    work = [
        ((4, BLOCK, model), low),
        ((4, BLOCK, model), low),
        ((4, BLOCK, model), low),
        ((model, wide), low),
        ((model, width), low),
        ((depth, 2 * width), low),
        ((LENGTH, wide), low),
        ((LENGTH, width), low),
        ((LENGTH, width), low),
        ((LENGTH, width), high),
        ((pairs, PAIR, LENGTH), low),
        ((pairs, PAIR, LENGTH), low),
        ((pairs, PAIR, LENGTH), high),
        ((pairs, PAIR, LENGTH), high),
        ((4, *cross_block), low),
        ((4, *cross_block), low),
    ]
    cross_got = [pltpu.VMEM((rows, share, 2 * width), low) for rows in (2, 2, 4, 4)]
    keyval_got = [pltpu.VMEM((rows, 2 * width), low) for rows in (FULL // 2, FULL // 2, FULL, FULL)]
    more = [
        ((FULL, depth), low),
        ((FULL, depth), low),
        ((2, FULL, depth), low),
        ((BLOCK, model), high),
        ((2, LENGTH, PAIR), high),
        ((8, model), high),
        ((5, 8, model), high),
    ]
    groups = [(share, wide), (share, width), (share, 2 * width), (span, 2 * width)]
    scratch = [pltpu.VMEM(*buffer) for buffer in work] + [cross_got, pltpu.VMEM((4, FULL, 2 * width), low), keyval_got]
    scratch += [pltpu.VMEM(*buffer) for buffer in more] + [sum_buffers(model)]
    scratch += [pltpu.VMEM((4, *group), low) for group in (groups[0], groups[1], groups[3])]
    scratch += [pltpu.VMEM(group, low) for group in groups]
    scratch += [pltpu.VMEM((3, *group), low) for group in groups]
    scratch += [pltpu.VMEM(groups[3], high), pltpu.VMEM((share, width), high)]
    scratch += [pltpu.VMEM(shape, high) for shape in ((share, wide), (span, 2 * width))]
    scratch += [pltpu.SemaphoreType.DMA((96,)), pltpu.SemaphoreType.DMA((96,)), pltpu.SemaphoreType.DMA((48,))]
    return pl.pallas_call(
        backward_kernel,
        out_shape=[jax.ShapeDtypeStruct(*out) for out in outs],
        in_specs=[whole_vmem()] * 4 + [anywhere()] * 12,
        out_specs=[anywhere()] + [whole_vmem()] * 2 + [anywhere()] * 5,
        scratch_shapes=scratch,
        compiler_params=pltpu.CompilerParams(collective_id=2, has_side_effects=True, vmem_limit_bytes=VMEM_BYTES),
        cost_estimate=pl.CostEstimate(flops=2**37, bytes_accessed=2**26, transcendentals=2**23),
    )(
        latents, gains, conditioning, gain_rows, d_resid, seed, grads_cross, d_keyval, w_qkv, w_attn_out, w_keyval,
        rows_one, rotated, attended, logs, tables,
    )


class ScatterFar:
    def __init__(self, links, grads, got_core, extra, got):
        self.links, self.grads, self.got_core, self.extra, self.got = links, grads, got_core, extra, got
        self.place, self.which = links.dp // 2, links.dp % 2
        self.middle = (self.place == 1) | (self.place == 2)
        self.core = [
            links.go(grads.at[place, 1 - self.which], got_core.at[place], 1, 0) for place in range(4)
        ]

    def combine(self, stage, spots):
        links, self.spots = self.links, spots
        for copy in self.core:
            copy.wait_recv()
        size = spots[0].shape[0]
        slots = [stage.at[slot, 0] for slot in range(2)]
        mine = [links.store(self.grads.at[self.place ^ step, self.which], spots[step]) for step in range(4)]
        order = (3, 2, 1, 0)
        others = [links.store(self.got_core.at[self.place ^ step], slots[at]) for at, step in enumerate(order[:2])]
        for at, step in enumerate(order):
            links.settle(mine[step])
            links.settle(others[at])

            def add(rows):
                total = spots[step][rows].astype(jnp.float32) + slots[at % 2][rows].astype(jnp.float32)
                spots[step][rows] = total.astype(jnp.bfloat16)

            row_steps(size, add)
            if at < 2:
                others.append(links.store(self.got_core.at[self.place ^ order[at + 2]], slots[at]))
        self.to_extra = links.remote(spots[3], self.extra, 2, 0)
        self.to_third = links.remote(spots[3], self.got.at[2], 6, 0)
        self.to_skip = links.remote(spots[2], self.got.at[1], 4, 0)

        @pl.when(self.middle)
        def _():
            self.to_third.start()

        @pl.when(jnp.logical_not(self.middle))
        def _():
            self.to_extra.start()
            self.to_skip.start()

        self.beside = links.go(spots[1], self.got.at[0], 2, 0)

    def relay(self):
        @pl.when(self.middle)
        def _():
            self.to_extra.wait_recv()

            def add(rows):
                total = self.spots[2][rows].astype(jnp.float32) + self.extra[rows].astype(jnp.float32)
                self.spots[2][rows] = total.astype(jnp.bfloat16)

            row_steps(self.spots[0].shape[0], add)
            self.to_skip.start()

    def finish(self):
        self.beside.wait_recv()
        self.to_skip.wait()

        @pl.when(self.middle)
        def _():
            self.to_third.wait()

        @pl.when(jnp.logical_not(self.middle))
        def _():
            self.to_extra.wait_send()


def middle_kernel(
    cotangent, gains, normed_two, resid_two, resid_one, in_rows, in_mlp, own_down, in_query, in_crossed,
    in_cross_logs, in_keyval, in_cross,
    block_out, d_resid_out, seed_out, grads_out, d_keyval_out, gain_out, grads_down_out, grads_gate_out, grads_up_out,
    core_down, core_gate, far_down, far_gate, own_down_out, own_gate_out,
    rows_three, seeds, w_mlp, w_down, hidden, both, parts, parts_last, stage, extra_down, extra_gate, spots_down,
    got, got_last,
    cross_logs, keyval, d_keyval, d_keys_t, d_values_t, d_resid, d_normed_two,
    send, recv, local, stage_sem,
):
    low = jnp.bfloat16
    model = cotangent.shape[1]
    width = model // 4
    share = own_down.shape[0]
    units = w_down.shape[1]
    pairs = width // PAIR
    links = Links(send, recv, local)
    load_rows = links.store(in_rows, rows_three.at[0])
    load_mlp = links.store(in_mlp, w_mlp)
    seeds[0] = cotangent[...]
    links.greet([(1, 0), (2, 0), (4, 0), (6, 0), (0, 1), (0, 2)])
    gather_down = Gather(links, own_down, w_down)
    links.settle(load_rows)
    spread_three = Spread(links, rows_three)
    spread_seeds = Spread(links, seeds)
    loads = [
        links.store(source, target)
        for source, target in (
            (in_cross_logs, cross_logs), (in_keyval, keyval),
        )
    ]
    gain_out[...] = jnp.zeros_like(gain_out)
    links.settle(load_mlp)
    for block in range(4):
        spread_three.wait(block)
        if block == 3:
            spread_seeds.wait(1)
        rows = block_rows(block)

        def up(cols):
            above_at = pl.ds(pl.multiple_of(units + cols.start, cols.size), cols.size)
            gate = dot_plain(rows_three[block], w_mlp[:, :, :, cols].reshape(model, -1))
            above = dot_plain(rows_three[block], w_mlp[:, :, :, above_at].reshape(model, -1))
            sigma = 1.0 / (1.0 + jnp.exp(-gate))
            swish = gate * sigma
            hidden[rows, cols] = (swish * above).astype(low)
            both[rows, cols] = (above * sigma * (1.0 + gate * (1.0 - sigma))).astype(low)
            both[rows, above_at] = swish.astype(low)

        columns(units, 256, up)
    gather_down.forward()
    spread_seeds.wait(3)

    def tiles_out(count, product, place):
        def copy(index, slot):
            return pltpu.make_async_copy(stage.at[slot], place(index), stage_sem.at[slot])

        def step(index, carry):
            slot = index % 2

            @pl.when(index >= 2)
            def _():
                copy(index - 2, slot).wait()

            for start in (0, units // 2):
                cols = pl.ds(start, units // 2)
                stage[slot, :, :, cols] = product(index, cols).reshape(2, share, -1)
            copy(index, slot).start()
            return carry

        lax.fori_loop(0, count, step, 0)
        for index in (count - 2, count - 1):
            copy(index, index % 2).wait()

    def rows_of(index, size):
        return pl.ds(pl.multiple_of(index * size, size), size)

    tile = 2 * share

    def whole(rows, index):
        return rows[:, :, rows_of(index, tile)].reshape(LENGTH, -1)

    tiles_out(
        model // tile,
        lambda index, cols: dot_rows(whole(seeds, index), hidden[:, cols]).astype(low),
        lambda index: grads_down_out.at[index],
    )
    scatter_down = ScatterFar(links, grads_down_out, core_down, extra_down, far_down)
    gather_down.arrive()
    scatter_down.combine(stage, [spots_down.at[place] for place in range(4)])
    sums = Sums(links, parts, *got)
    for block in (3, 1, 2, 0):
        rows = block_rows(block)

        def back(cols):
            above_at = pl.ds(pl.multiple_of(units + cols.start, cols.size), cols.size)
            d_hidden = dot_plain(seeds[block], w_down[:, cols])
            both[rows, cols] = (both[rows, cols].astype(jnp.float32) * d_hidden).astype(low)
            both[rows, above_at] = (both[rows, above_at].astype(jnp.float32) * d_hidden).astype(low)

        columns(units, 256, back)

        def down(place, carry):
            weights = w_mlp[place].reshape(2 * share, -1)
            parts[block, :, rows_of(place, 2 * share)] = dot_cols(both[rows], weights).astype(low)
            return carry

        lax.fori_loop(0, 4, down, 0)
        sums.ready(block)
    sums.add()
    scatter_down.relay()
    w_cross = [w_mlp.at[:, :, :, pl.ds(member * 2 * width, 2 * width)] for member in range(4)]
    load_cross = [links.store(in_cross.at[member], w_cross[member]) for member in range(4)]
    for block in range(4):

        def last(cols):
            parts_last[block, :, cols] = dot_cols(hidden[block_rows(block)], w_down[cols, :]).astype(low)

        columns(model, 512, last)

    def grads_mlp(half, target):
        start = half * units
        tiles_out(
            model // tile,
            lambda index, cols: dot_rows(
                whole(rows_three, index), both[:, pl.ds(start + cols.start, cols.size)]
            ).astype(low),
            lambda index: target.at[index],
        )

    grads_mlp(0, grads_gate_out)
    scatter_gate = ScatterFar(links, grads_gate_out, core_gate, extra_gate, far_gate)
    gather_down.sent()
    query, crossed, cross_seed, seed = (w_down.at[block_rows(spot)] for spot in range(4))
    loads += [links.store(in_query, query), links.store(in_crossed, crossed)]
    for load in loads + load_cross:
        links.settle(load)
    sums.arrive()
    sums_last = Sums(links, parts_last, *got_last)
    for block in (3, 1, 2):
        sums_last.ready(block)
    scatter_gate.combine(stage, [hidden.at[pl.ds(place * BLOCK, share)] for place in range(4)])

    def cross_columns(member, cols):
        return w_cross[member][:, :, :, cols].reshape(model, -1)

    def norm_three(rows):
        gain = gains[2:3]
        _, scaled, inverse = layer_norm(resid_two[rows], gain)
        d_normed = parts[0, rows].astype(jnp.float32) + sums.total(rows)
        d_part, gain_grad = norm_backward(d_normed, scaled, inverse, gain)
        gain_out[2:3] += gain_grad[None]
        value = cotangent[rows].astype(jnp.float32) + d_part
        d_resid[rows] = value
        cross_seed[rows] = value.astype(low)

    row_steps(BLOCK, norm_three)
    for member in range(4):
        at_member = slice(member * width, (member + 1) * width)
        d_crossed = dot_plain(cross_seed[...], cross_columns(member, slice(width, 2 * width))).astype(low)
        for pair in range(pairs):
            at = slice(member * width + pair * PAIR, member * width + (pair + 1) * PAIR)
            keys_at = slice(pair * PAIR, (pair + 1) * PAIR)
            values_at = slice(width + pair * PAIR, width + (pair + 1) * PAIR)
            key = keyval[member, :, keys_at]
            key_t = key.astype(jnp.float32).T.astype(low)
            value_t = keyval[member, :, values_at].astype(jnp.float32).T.astype(low)
            d_keys_t[...] = jnp.zeros_like(d_keys_t)
            d_values_t[...] = jnp.zeros_like(d_values_t)
            out = attend_rows_back(
                query[:, at] * low(DH**-0.5), d_crossed[:, keys_at], cross_logs[:, at], key_t, value_t, key, d_keys_t,
                d_values_t, CTX,
            )
            query[:, at] = out.astype(low)
            d_keyval[member, :, keys_at] = d_keys_t[...].T.astype(low)
            d_keyval[member, :, values_at] = d_values_t[...].T.astype(low)
        for place in range(4):
            at = slice(place * 2 * share, (place + 1) * 2 * share)
            part = dot_cols(query[:, at_member], w_cross[member][place, :, :, :width].reshape(2 * share, width))
            if member == 0:
                d_normed_two[:, at] = part
            else:
                d_normed_two[:, at] += part
    links.store(d_keyval, d_keyval_out)
    scatter_gate.relay()

    def norm_two(rows):
        gain = gains[1:2]
        _, scaled, inverse = layer_norm(resid_one[rows], gain)
        d_part, gain_grad = norm_backward(d_normed_two[rows], scaled, inverse, gain)
        gain_out[1:2] += gain_grad[None]
        value = d_resid[rows] + d_part
        d_resid[rows] = value
        seed[rows] = value.astype(low)

    row_steps(BLOCK, norm_two)
    links.settle(links.store(seed, seed_out.at[0]))
    spread_seed = Spread(links, seed_out)
    links.store(d_resid, d_resid_out)
    sums_last.add()
    grads_mlp(1, grads_up_out)
    for place in range(4):
        rows_at = slice(place * 2 * share, (place + 1) * 2 * share)
        for member in range(4):
            at_member = slice(member * width, (member + 1) * width)
            left = dot_rows(normed_two[:, rows_at], query[:, at_member]).astype(low)
            w_cross[member][place, :, :, :width] = left.reshape(2, share, width)
            right = dot_rows(cross_seed[:, rows_at], crossed[:, at_member]).astype(low)
            w_cross[member][place, :, :, width:] = right.reshape(2, share, width)
    for member in range(4):
        links.store(w_cross[member], grads_out.at[member])
    spread_seed.wait(1)
    sums_last.arrive()

    def add_last(rows):
        d_normed_two[rows] = resid_two[rows] + parts_last[0, rows].astype(jnp.float32) + sums_last.total(rows)

    row_steps(BLOCK, add_last)
    links.store(d_normed_two, block_out)
    spread_seed.wait(3)
    links.store(scatter_down.spots[0], own_down_out)
    links.store(scatter_gate.spots[0], own_gate_out)
    links.finish()
    scatter_down.finish()
    scatter_gate.finish()


def middle_part(cotangent, gains, rows_three, mlp_all, own_down, kept):
    normed_two, resid_two, resid_one, query, crossed, cross_logs, keyval, cross_all = kept
    model = cotangent.shape[1]
    share, units = own_down.shape
    low, high = jnp.bfloat16, jnp.float32
    outs = [
        ((BLOCK, model), high),
        ((BLOCK, model), high),
        ((4, BLOCK, model), low),
        (cross_all.shape, low),
        (keyval.shape, low),
        ((8, model), high),
        ((4, 2, share, units), low),
        ((4, 2, share, units), low),
        ((4, 2, share, units), low),
        ((4, share, units), low),
        ((4, share, units), low),
        ((3, share, units), low),
        ((3, share, units), low),
        ((share, units), low),
        ((share, units), low),
    ]
    work = [
        ((4, BLOCK, model), low),
        ((4, BLOCK, model), low),
        (mlp_all.shape, low),
        ((model, units), low),
        ((LENGTH, units), low),
        ((LENGTH, 2 * units), low),
        ((4, BLOCK, model), low),
        ((4, BLOCK, model), low),
        ((2, 2, share, units), low),
        ((share, units), low),
        ((share, units), low),
        ((4, share, units), low),
    ]
    more = [
        ((BLOCK, model), high),
        (keyval.shape, low),
        (keyval.shape, low),
        ((PAIR, FULL), high),
        ((PAIR, FULL), high),
        ((BLOCK, model), high),
        ((BLOCK, model), high),
    ]
    scratch = [pltpu.VMEM(*buffer) for buffer in work] + [sum_buffers(model), sum_buffers(model)]
    scratch += [pltpu.VMEM(*buffer) for buffer in more]
    scratch += [pltpu.SemaphoreType.DMA((96,)), pltpu.SemaphoreType.DMA((96,)), pltpu.SemaphoreType.DMA((64,))]
    scratch += [pltpu.SemaphoreType.DMA((2,))]
    return pl.pallas_call(
        middle_kernel,
        out_shape=[jax.ShapeDtypeStruct(*out) for out in outs],
        in_specs=[whole_vmem()] * 5 + [anywhere()] * 8,
        out_specs=[anywhere()] * 5 + [whole_vmem()] + [anywhere()] * 9,
        scratch_shapes=scratch,
        compiler_params=pltpu.CompilerParams(collective_id=3, has_side_effects=True, vmem_limit_bytes=VMEM_BYTES),
        cost_estimate=pl.CostEstimate(flops=2**36, bytes_accessed=2**26, transcendentals=2**21),
    )(
        cotangent, gains, normed_two, resid_two, resid_one, rows_three, mlp_all, own_down, query, crossed,
        cross_logs, keyval, cross_all,
    )


def finish_kernel(
    in_out, in_latents, in_qkv, in_attn_out, in_cross_q, in_keyval, in_cross_out, own_gate, far_gate, own_down, far_down,
    in_up,
    block_out, grad_latents, grad_qkv, grad_attn_out, grad_cross_q, grad_keyval, grad_cross_out, grad_gate, grad_up,
    grad_down,
):
    for source, target in (
        (in_out, block_out), (in_latents, grad_latents), (in_qkv, grad_qkv), (in_attn_out, grad_attn_out),
        (in_cross_q, grad_cross_q), (in_keyval, grad_keyval), (in_cross_out, grad_cross_out),
    ):

        def move(rows):
            target[rows] = source[rows].astype(jnp.float32)

        row_steps(source.shape[0], move)
    place = lax.axis_index("dp") // 2
    middle = (place == 1) | (place == 2)
    for own, far, target in ((own_gate, far_gate, grad_gate), (own_down, far_down, grad_down)):

        def add(rows):
            third = jnp.where(middle, far[2, rows].astype(jnp.float32), 0.0)
            total = own[rows].astype(jnp.float32) + far[0, rows].astype(jnp.float32)
            target[rows] = total + far[1, rows].astype(jnp.float32) + third

        row_steps(own.shape[0], add)

    def widen(rows):
        grad_up[rows] = in_up[rows].astype(jnp.float32)

    row_steps(in_up.shape[0], widen)


def finish_part(raw, own_gate, far_gate, own_down, far_down, sum_up):
    wide = jax.ShapeDtypeStruct(sum_up.shape, jnp.float32)
    return pl.pallas_call(
        finish_kernel,
        out_shape=[jax.ShapeDtypeStruct(array.shape, jnp.float32) for array in raw] + [wide] * 3,
        in_specs=[whole_vmem()] * 12,
        out_specs=[whole_vmem()] * 10,
        compiler_params=pltpu.CompilerParams(vmem_limit_bytes=VMEM_BYTES),
        cost_estimate=pl.CostEstimate(flops=2**22, bytes_accessed=2**24, transcendentals=0),
    )(*raw, own_gate, far_gate, own_down, far_down, sum_up)


def per_device(
    latents,
    conditioning,
    gain_attn,
    w_qkv,
    w_attn_out,
    gain_cross,
    w_cross_q,
    w_cross_kv,
    w_cross_out,
    gain_mlp,
    w_gate,
    w_up,
    w_down,
    cotangent,
):
    low = jnp.bfloat16
    gains = jnp.stack([gain_attn, gain_cross, gain_mlp])
    (
        rows_one, normed_two, rows_three, qkv_all, attn_out_t, cross_all, cross_kv, mlp_all, own_down,
        rotated, attended, logs, cross_query, keyval, crossed, cross_logs, resid_one, resid_two, tables,
    ) = forward_part(
        latents,
        gains,
        conditioning,
        (w_qkv, w_attn_out.T, w_cross_q, w_cross_kv, w_cross_out.T, w_gate, w_up, w_down.T),
    )
    (
        block_out, d_resid, seed, grads_cross, d_keyval, gain_rows, _, _, grads_up, _, _, far_down, far_gate, own_down,
        own_gate,
    ) = middle_part(
        cotangent,
        gains,
        rows_three,
        mlp_all,
        own_down,
        (normed_two, resid_two, resid_one, cross_query, crossed, cross_logs, keyval, cross_all),
    )
    sum_up = dp_sum(grads_up.reshape(w_gate.shape[0] * 8, -1))
    grad_latents, grad_context, grad_gains, grad_qkv, grad_attn_out, grad_cross_q, grad_cross_kv, grad_cross_out = (
        backward_part(
            latents,
            gains,
            conditioning,
            gain_rows,
            d_resid,
            seed,
            grads_cross,
            d_keyval,
            (qkv_all, attn_out_t, cross_kv, rows_one, rotated, attended, logs, tables),
        )
    )
    raw = (block_out, grad_latents, grad_qkv, grad_attn_out, grad_cross_q, grad_cross_kv, grad_cross_out)
    (
        block_out, grad_latents, grad_qkv, grad_attn_out, grad_cross_q, grad_cross_kv, grad_cross_out, grad_gate,
        grad_up, grad_down,
    ) = finish_part(raw, own_gate, far_gate, own_down, far_down, sum_up)
    return (
        block_out,
        grad_latents,
        grad_context,
        grad_gains[0],
        grad_qkv,
        grad_attn_out.T,
        grad_gains[1],
        grad_cross_q,
        grad_cross_kv,
        grad_cross_out.T,
        grad_gains[2],
        grad_gate,
        grad_up,
        grad_down.T,
    )


def per_device_general(
    latents,
    conditioning,
    gain_attn,
    w_qkv,
    w_attn_out,
    gain_cross,
    w_cross_q,
    w_cross_kv,
    w_cross_out,
    gain_mlp,
    w_gate,
    w_up,
    w_down,
    cotangent,
):
    low = jnp.bfloat16
    heads_wide = w_cross_q.shape[1]
    hidden_wide = w_gate.shape[1]
    resid_in = latents.astype(jnp.float32)
    normed_one, scaled_one, inverse_one = layer_norm(resid_in, gain_attn)
    rows_one = spread_rows(normed_one.astype(low))
    own_qkv = by_part(w_qkv.astype(low), 3)
    qkv_all = lax.all_gather(own_qkv, "dp", axis=0, tiled=True)
    own_kv = by_part(w_cross_kv.astype(low), 2)
    own_kv = jnp.concatenate([own_kv[:, :heads_wide], own_kv[:, heads_wide:]], axis=0)
    own_mid = jnp.concatenate(
        [w_attn_out.astype(low).T, w_cross_q.astype(low), w_cross_out.astype(low).T, own_kv], axis=1
    )
    mid_all = lax.all_gather(after(own_mid, qkv_all), "dp", axis=0, tiled=True)
    own_mlp = jnp.concatenate([w_gate.astype(low), w_up.astype(low)], axis=1)
    mlp_all = lax.all_gather(after(own_mlp, mid_all), "dp", axis=0, tiled=True)
    down_all = lax.all_gather(after(w_down.astype(low).T, mlp_all), "dp", axis=0, tiled=True)
    attn_out_t, cross_q, cross_out_t = (mid_all[:, part * heads_wide : (part + 1) * heads_wide] for part in range(3))
    model = mid_all.shape[0]
    cross_kv = (
        mid_all[:, 3 * heads_wide :]
        .reshape(lax.axis_size("dp"), 2, -1, heads_wide)
        .transpose(0, 2, 1, 3)
        .reshape(model // 2, 2 * heads_wide)
    )

    tables = turn_tables(group_positions(latents.shape[0]))
    packed = dot_plain(rows_one, qkv_all)
    attended, rotated, logs = attend(pad_heads(packed, 3), tables)
    attended = attended[:, :heads_wide]
    resid_one = resid_in + sum_rows(dot_cols(attended, attn_out_t))
    normed_two, scaled_two, inverse_two = layer_norm(resid_one, gain_cross)
    rows_two = spread_rows(normed_two.astype(low))
    head_shape = (-1, heads_wide // DH, DH)
    cross_query = dot_plain(rows_two, cross_q).astype(low).reshape(head_shape)
    context = conditioning.reshape(CTX, conditioning.shape[2])
    cross_pack = dot_plain(context, cross_kv).astype(low)
    cross_key = cross_pack[:, :heads_wide].reshape(head_shape)
    cross_value = cross_pack[:, heads_wide:].reshape(head_shape)
    crossed, cross_logs = cross_forward(cross_query, cross_key, cross_value)
    crossed = crossed.reshape(-1, heads_wide).astype(low)
    resid_two = resid_one + sum_rows(dot_cols(crossed, cross_out_t))
    normed_three, scaled_three, inverse_three = layer_norm(resid_two, gain_mlp)
    rows_three = spread_rows(normed_three.astype(low))
    mlp_seed = spread_rows(cotangent)
    both = dot_plain(rows_three, mlp_all)
    gate_pre, up_pre = both[:, :hidden_wide], both[:, hidden_wide:]
    sigma_gate = jax.nn.sigmoid(gate_pre)
    swish = gate_pre * sigma_gate
    hidden = (swish * up_pre).astype(low)
    sum_down = dp_sum(dot_rows(mlp_seed, hidden))
    d_hidden = dot_plain(mlp_seed, down_all)
    d_gate = (d_hidden * up_pre * sigma_gate * (1.0 + gate_pre * (1.0 - sigma_gate))).astype(low)
    d_up = (d_hidden * swish).astype(low)
    d_both = jnp.concatenate([d_gate, d_up], axis=1)
    sum_mlp = dp_sum(after(dot_rows(rows_three, d_both), sum_down))
    d_normed = sum_rows(dot_cols(d_both, mlp_all))
    d_part, gain_grad_three = norm_backward(d_normed, scaled_three, inverse_three, gain_mlp)
    d_resid = cotangent.astype(jnp.float32) + d_part
    block_out = resid_two + sum_rows(dot_cols(hidden, down_all))
    cross_seed = spread_rows(d_resid.astype(low))
    grad_cross_out = dot_rows(cross_seed, crossed)
    d_crossed = dot_plain(cross_seed, cross_out_t).astype(low).reshape(head_shape)
    d_query, d_key, d_value = cross_backward(cross_query, cross_key, cross_value, d_crossed, cross_logs)
    d_query = d_query.reshape(-1, heads_wide).astype(low)
    d_keyval = jnp.concatenate([d_key.reshape(CTX, -1), d_value.reshape(CTX, -1)], axis=1).astype(low)
    grad_cross_q = dot_rows(rows_two, d_query)
    grad_cross_kv = dot_rows(context, d_keyval)
    context_part = dot_cols(d_keyval, cross_kv)
    d_normed = sum_rows(dot_cols(d_query, cross_q))
    d_part, gain_grad_two = norm_backward(d_normed, scaled_two, inverse_two, gain_cross)
    d_resid = d_resid + d_part
    self_seed = spread_rows(d_resid.astype(low))
    grad_attn_out = dot_rows(self_seed, attended)
    grad_kv = (
        grad_cross_kv.astype(low)
        .reshape(lax.axis_size("dp"), -1, 2, heads_wide)
        .transpose(0, 2, 1, 3)
        .reshape(model, heads_wide)
    )
    grad_mid = jnp.concatenate([grad_attn_out.astype(low), grad_cross_q.astype(low), grad_cross_out.astype(low), grad_kv], axis=1)
    sum_mid = dp_sum(after(grad_mid, sum_mlp))
    d_attended = dot_plain(self_seed, attn_out_t).astype(low)
    d_packed = drop_heads(attend_back(rotated, pad_heads(d_attended, 1), logs, tables), 3, packed.shape[1])
    sum_qkv = dp_sum(after(dot_rows(rows_one, d_packed), sum_mid))
    d_normed = sum_rows(dot_cols(d_packed, qkv_all))
    d_part, gain_grad_one = norm_backward(d_normed, scaled_one, inverse_one, gain_attn)
    grad_latents = d_resid + d_part
    grad_context = (
        lax.psum(context_part.astype(low), "tensor").astype(jnp.float32).reshape(conditioning.shape)
    )
    gains = lax.psum(jnp.stack([gain_grad_one, gain_grad_two, gain_grad_three]), ("dp", "tensor"))
    sums = [sum_mid[:, part * heads_wide : (part + 1) * heads_wide].astype(jnp.float32) for part in range(4)]
    half = sums[3].shape[0] // 2
    sum_kv = jnp.concatenate([sums[3][:half], sums[3][half:]], axis=1)
    return (
        block_out,
        grad_latents,
        grad_context,
        gains[0],
        by_head(sum_qkv, 3).astype(jnp.float32),
        sums[0].T,
        gains[1],
        sums[1],
        by_head(sum_kv, 2),
        sums[2].T,
        gains[2],
        sum_mlp[:, :hidden_wide].astype(jnp.float32),
        sum_mlp[:, hidden_wide:].astype(jnp.float32),
        sum_down.astype(jnp.float32).T,
    )


def solution(mesh):
    in_specs = (
        P(("dp", "tensor"), None),
        P("dp", None, None),
        P(),
        P("dp", "tensor"),
        P("tensor", "dp"),
        P(),
        P("dp", "tensor"),
        P("dp", "tensor"),
        P("tensor", "dp"),
        P(),
        P("dp", "tensor"),
        P("dp", "tensor"),
        P("tensor", "dp"),
        P(("dp", "tensor"), None),
    )
    out_specs = (
        P(("dp", "tensor"), None),
        P(("dp", "tensor"), None),
        P("dp", None, None),
        P(),
        P("dp", "tensor"),
        P("tensor", "dp"),
        P(),
        P("dp", "tensor"),
        P("dp", "tensor"),
        P("tensor", "dp"),
        P(),
        P("dp", "tensor"),
        P("dp", "tensor"),
        P("tensor", "dp"),
    )
    special = dict(mesh.shape) == {"dp": 8, "tensor": 4}
    return jax.shard_map(
        per_device if special else per_device_general, mesh=mesh, in_specs=in_specs, out_specs=out_specs, check_vma=False
    )
```

```python
import math
from functools import reduce

import jax
import jax.numpy as jnp
from jax import lax
from jax.experimental import pallas as pl
from jax.experimental.pallas import tpu as pltpu
from jax.sharding import PartitionSpec as P

DH = 64
CTX = 130
LENGTH = 1024
PAIR = 2 * DH
ROWS = 256
VMEM_BYTES = 62 * 2**20

norm_eps = 1e-05
rope_base = 10000.0


def head_turn(values, cosine, sine):
    quarter = DH // 4
    ahead = pltpu.roll(values, PAIR - quarter, 1)
    behind = pltpu.roll(values, quarter, 1)
    lane = lax.broadcasted_iota(jnp.int32, values.shape, 1) % DH
    return values * cosine + jnp.where(lane < quarter, -ahead, behind) * sine


def half_mask(shape, axis, which):
    place = lax.broadcasted_iota(jnp.int32, shape, axis)
    return (place >= DH) if which else (place < DH)


def attend_kernel(q_ref, k_ref, v_ref, cos_ref, sin_ref, out_ref, rot_ref, log_ref, kt_ref, vm_ref):
    pairs = pl.num_programs(0)
    pair = pl.program_id(0)
    turn = (cos_ref[...], sin_ref[...])
    query = head_turn(q_ref[...], *turn).astype(jnp.bfloat16)
    key = head_turn(k_ref[...], *turn).astype(jnp.bfloat16)
    value = v_ref[...].astype(jnp.bfloat16)
    for part, array in enumerate((query, key, value)):
        start = pl.multiple_of((part * pairs + pair) * PAIR, PAIR)
        rot_ref[:, pl.ds(start, PAIR)] = array
    key_t = key.astype(jnp.float32).T
    for which in range(2):
        kt_ref[which] = jnp.where(half_mask(key_t.shape, 0, which), key_t, 0.0).astype(jnp.bfloat16)
        vm_ref[which] = jnp.where(half_mask(value.shape, 1, which), value.astype(jnp.float32), 0.0).astype(jnp.bfloat16)
    q_start = pl.multiple_of(pair * PAIR, PAIR)

    def one_block(step, carry):
        rows = pl.ds(pl.multiple_of(step * ROWS, ROWS), ROWS)
        block = rot_ref[rows, pl.ds(q_start, PAIR)] * jnp.bfloat16(DH**-0.5)
        outs, logs = [], []
        for which in range(2):
            scores = jnp.dot(block, kt_ref[which], preferred_element_type=jnp.float32)
            peak = jnp.max(scores, axis=1, keepdims=True)
            shifted = jnp.exp(scores - peak)
            total = jnp.sum(shifted, axis=1, keepdims=True)
            product = jnp.dot(shifted.astype(jnp.bfloat16), vm_ref[which], preferred_element_type=jnp.float32)
            outs.append(product * (1.0 / total))
            logs.append(peak + jnp.log(total))
        out_ref[rows, :] = (outs[0] + outs[1]).astype(jnp.bfloat16)
        low = half_mask((ROWS, PAIR), 1, 0)
        log_ref[rows, :] = jnp.where(low, logs[0], logs[1])
        return carry

    lax.fori_loop(0, LENGTH // ROWS, one_block, 0)


def attend_back_kernel(
    q_ref, k_ref, v_ref, grad_ref, log_ref, cos_ref, sin_ref, out_ref,
    kt_ref, vt_ref, km_ref, qt_ref, gt_ref, dq_ref, dk_ref, dv_ref,
):
    pairs = pl.num_programs(0)
    pair = pl.program_id(0)
    key_t = k_ref[...].astype(jnp.float32).T
    value_t = v_ref[...].astype(jnp.float32).T
    for which in range(2):
        keep = half_mask(key_t.shape, 0, which)
        kt_ref[which] = jnp.where(keep, key_t, 0.0).astype(jnp.bfloat16)
        vt_ref[which] = jnp.where(keep, value_t, 0.0).astype(jnp.bfloat16)
        key = k_ref[...].astype(jnp.float32)
        km_ref[which] = jnp.where(half_mask(key.shape, 1, which), key, 0.0).astype(jnp.bfloat16)
    qt_ref[...] = (q_ref[...].astype(jnp.float32) * DH**-0.5).T.astype(jnp.bfloat16)
    gt_ref[...] = grad_ref[...].astype(jnp.float32).T.astype(jnp.bfloat16)
    dk_ref[...] = jnp.zeros_like(dk_ref)
    dv_ref[...] = jnp.zeros_like(dv_ref)

    def one_block(step, carry):
        rows = pl.ds(pl.multiple_of(step * ROWS, ROWS), ROWS)
        block = q_ref[rows, :] * jnp.bfloat16(DH**-0.5)
        grads = grad_ref[rows, :]
        d_query = jnp.zeros((ROWS, PAIR), jnp.float32)
        for which in range(2):
            half = slice(which * DH, (which + 1) * DH)
            scores = jnp.dot(block, kt_ref[which], preferred_element_type=jnp.float32)
            probs = jnp.exp(scores - log_ref[rows, which * DH : which * DH + 1])
            d_prob = jnp.dot(grads, vt_ref[which], preferred_element_type=jnp.float32)
            center = jnp.sum(probs * d_prob, axis=1, keepdims=True)
            d_score = (probs * (d_prob - center)).astype(jnp.bfloat16)
            d_query += jnp.dot(d_score, km_ref[which], preferred_element_type=jnp.float32)
            dk_ref[half, :] += jnp.dot(qt_ref[half, rows], d_score, preferred_element_type=jnp.float32)
            dv_ref[half, :] += jnp.dot(
                gt_ref[half, rows], probs.astype(jnp.bfloat16), preferred_element_type=jnp.float32
            )
        dq_ref[rows, :] = d_query * DH**-0.5
        return carry

    lax.fori_loop(0, LENGTH // ROWS, one_block, 0)
    turn = (cos_ref[...], -sin_ref[...])
    results = (head_turn(dq_ref[...], *turn), head_turn(dk_ref[...].T, *turn), dv_ref[...].T)
    for part, array in enumerate(results):
        start = pl.multiple_of((part * pairs + pair) * PAIR, PAIR)
        out_ref[:, pl.ds(start, PAIR)] = array.astype(jnp.bfloat16)


def column_block(offset):
    return pl.BlockSpec((LENGTH, PAIR), lambda pair: (0, pair + offset))


def whole_block(columns):
    return pl.BlockSpec((LENGTH, columns), lambda pair: (0, 0))


def attend(packed, tables):
    columns = packed.shape[1]
    pairs = columns // (3 * PAIR)
    return pl.pallas_call(
        attend_kernel,
        grid=(pairs,),
        in_specs=[column_block(part * pairs) for part in range(3)] + [whole_block(PAIR)] * 2,
        out_specs=[column_block(0), whole_block(columns), column_block(0)],
        out_shape=[
            jax.ShapeDtypeStruct((LENGTH, pairs * PAIR), jnp.bfloat16),
            jax.ShapeDtypeStruct((LENGTH, columns), jnp.bfloat16),
            jax.ShapeDtypeStruct((LENGTH, pairs * PAIR), jnp.float32),
        ],
        scratch_shapes=[pltpu.VMEM((2, PAIR, LENGTH), jnp.bfloat16), pltpu.VMEM((2, LENGTH, PAIR), jnp.bfloat16)],
        compiler_params=pltpu.CompilerParams(vmem_limit_bytes=VMEM_BYTES),
        cost_estimate=pl.CostEstimate(flops=pairs * 2**32, bytes_accessed=2**24, transcendentals=pairs * 2**21),
    )(packed, packed, packed, *tables)


def attend_back(rotated, d_attended, logs, tables):
    columns = rotated.shape[1]
    pairs = columns // (3 * PAIR)
    tall = pltpu.VMEM((PAIR, LENGTH), jnp.bfloat16)
    return pl.pallas_call(
        attend_back_kernel,
        grid=(pairs,),
        in_specs=[column_block(part * pairs) for part in range(3)]
        + [column_block(0), column_block(0)]
        + [whole_block(PAIR)] * 2,
        out_specs=whole_block(columns),
        out_shape=jax.ShapeDtypeStruct((LENGTH, columns), jnp.bfloat16),
        scratch_shapes=[
            pltpu.VMEM((2, PAIR, LENGTH), jnp.bfloat16),
            pltpu.VMEM((2, PAIR, LENGTH), jnp.bfloat16),
            pltpu.VMEM((2, LENGTH, PAIR), jnp.bfloat16),
            tall,
            tall,
            pltpu.VMEM((LENGTH, PAIR), jnp.float32),
            pltpu.VMEM((PAIR, LENGTH), jnp.float32),
            pltpu.VMEM((PAIR, LENGTH), jnp.float32),
        ],
        compiler_params=pltpu.CompilerParams(vmem_limit_bytes=VMEM_BYTES),
        cost_estimate=pl.CostEstimate(flops=pairs * 2**33, bytes_accessed=2**24, transcendentals=pairs * 2**21),
    )(rotated, rotated, rotated, d_attended, logs, *tables)


def turn_tables(positions):
    quarter = DH // 4
    frequency = jnp.exp(-jnp.log(rope_base) * jnp.arange(quarter).astype(jnp.float32) / quarter)
    angles = positions.astype(jnp.float32)[:, None] * frequency[None, :]
    cosine, sine = jnp.cos(angles), jnp.sin(angles)
    zeros, ones = jnp.zeros_like(sine), jnp.ones_like(sine)
    rows = (
        jnp.concatenate([cosine, cosine, ones, ones], axis=1),
        jnp.concatenate([sine, sine, zeros, zeros], axis=1),
    )
    return tuple(jnp.concatenate([row, row], axis=1) for row in rows)


def dot_plain(left_op, right_op):
    return jnp.dot(left_op, right_op, preferred_element_type=jnp.float32)


def dot_rows(left_op, right_op):
    return lax.dot_general(
        left_op, right_op, (((0,), (0,)), ((), ())), preferred_element_type=jnp.float32
    )


def dot_cols(left_op, right_op):
    return lax.dot_general(
        left_op, right_op, (((1,), (1,)), ((), ())), preferred_element_type=jnp.float32
    )


def layer_norm(values, gain_vec):
    center = values - jnp.mean(values, axis=-1, keepdims=True)
    spread = jnp.mean(center * center, axis=-1, keepdims=True)
    inverse = lax.rsqrt(spread + norm_eps)
    scaled = center * inverse
    return (scaled * gain_vec, scaled, inverse)


def norm_backward(upstream, scaled, inverse, gain_vec):
    weighted = upstream * gain_vec
    inner = jnp.mean(weighted, axis=-1, keepdims=True) + scaled * jnp.mean(
        weighted * scaled, axis=-1, keepdims=True
    )
    return (inverse * (weighted - inner), jnp.sum(upstream * scaled, axis=0))


def swap(values, bit):
    return lax.ppermute(values, "tensor", [(member, member ^ bit) for member in range(4)])


def spread_rows(values):
    if lax.axis_size("tensor") != 4:
        return lax.all_gather(values, "tensor", axis=0, tiled=True)
    half = values.shape[0] // 2
    near, far = swap(values, 1), swap(values, 2)
    return jnp.concatenate([values, near, far, swap(near[:half], 2), swap(far[half:], 1)], axis=0)


def sum_rows(partial):
    if lax.axis_size("tensor") != 4:
        return lax.psum_scatter(
            partial.astype(jnp.bfloat16), "tensor", scatter_dimension=0, tiled=True
        ).astype(jnp.float32)
    size = partial.shape[0] // 4
    half = size // 2
    own, near, far, last = (partial[part * size : (part + 1) * size] for part in range(4))
    first = swap(last[:half].astype(jnp.bfloat16), 1)
    second = swap(last[half:].astype(jnp.bfloat16), 2)
    far = jnp.concatenate([far[:half] + first.astype(jnp.float32), far[half:]], axis=0)
    near = jnp.concatenate([near[:half], near[half:] + second.astype(jnp.float32)], axis=0)
    return (
        own
        + swap(near.astype(jnp.bfloat16), 1).astype(jnp.float32)
        + swap(far.astype(jnp.bfloat16), 2).astype(jnp.float32)
    )


def group_positions(rows):
    group = lax.axis_size("tensor")
    blocks = jnp.arange(group)
    if group == 4:
        blocks = blocks ^ lax.axis_index("tensor")
    return (blocks[:, None] * rows + jnp.arange(rows)[None, :]).reshape(-1)


def cross_forward(queries, keys_in, values_in):
    scores = jnp.einsum("qhd,khd->hqk", queries, keys_in, preferred_element_type=jnp.float32) * DH ** (-0.5)
    peak_score = jnp.max(scores, axis=-1, keepdims=True)
    shifted = jnp.exp(scores - peak_score)
    totals = jnp.sum(shifted, axis=-1, keepdims=True)
    probabilities = (shifted / totals).astype(jnp.bfloat16)
    output = jnp.einsum("hqk,khd->qhd", probabilities, values_in, preferred_element_type=jnp.float32)
    return (output, peak_score + jnp.log(totals))


def cross_backward(queries, keys_in, values_in, d_output, log_totals):
    scaling = DH ** (-0.5)
    scores = jnp.einsum("qhd,khd->hqk", queries, keys_in, preferred_element_type=jnp.float32) * scaling
    probabilities = jnp.exp(scores - log_totals)
    d_prob = jnp.einsum("qhd,khd->hqk", d_output, values_in, preferred_element_type=jnp.float32)
    center = jnp.sum(probabilities * d_prob, axis=-1, keepdims=True)
    d_score = (probabilities * (d_prob - center)).astype(jnp.bfloat16)
    d_query = jnp.einsum("hqk,khd->qhd", d_score, keys_in, preferred_element_type=jnp.float32) * scaling
    d_key = jnp.einsum("hqk,qhd->khd", d_score, queries, preferred_element_type=jnp.float32) * scaling
    d_value = jnp.einsum(
        "hqk,qhd->khd", probabilities.astype(jnp.bfloat16), d_output, preferred_element_type=jnp.float32
    )
    return (d_query, d_key, d_value)


def by_part(columns, parts):
    rows = columns.shape[0]
    return columns.reshape(rows, -1, parts, DH).swapaxes(1, 2).reshape(rows, -1)


def by_head(columns, parts):
    rows = columns.shape[0]
    return columns.reshape(rows, parts, -1, DH).swapaxes(1, 2).reshape(rows, -1)


def pad_heads(columns, parts):
    rows, width = columns.shape
    each = width // parts
    if each % PAIR == 0:
        return columns
    return jnp.pad(columns.reshape(rows, parts, each), ((0, 0), (0, 0), (0, -each % PAIR))).reshape(rows, -1)


def drop_heads(columns, parts, width):
    rows = columns.shape[0]
    return columns.reshape(rows, parts, -1)[:, :, : width // parts].reshape(rows, width)


def dp_sum(grads):
    return lax.psum_scatter(grads.astype(jnp.bfloat16), "dp", scatter_dimension=0, tiled=True)


def after(value, earlier):
    return lax.optimization_barrier((value, earlier))[0]


MESH = pl.DeviceIdType.MESH
BLOCK = LENGTH // 4
HALF = BLOCK // 2
FULL = 160


class Links:
    def __init__(self, send, recv, local):
        self.send, self.recv, self.local = send, recv, local
        self.used = self.used_local = 0
        self.pending, self.pending_local = [], []
        self.dp, self.tensor = lax.axis_index("dp"), lax.axis_index("tensor")

    def remote(self, src, dst, dp_bit, tensor_bit):
        at = self.used
        self.used += 1
        return pltpu.make_async_remote_copy(
            src_ref=src,
            dst_ref=dst,
            send_sem=self.send.at[at],
            recv_sem=self.recv.at[at],
            device_id=(self.dp ^ dp_bit, self.tensor ^ tensor_bit),
            device_id_type=MESH,
        )

    def go(self, src, dst, dp_bit, tensor_bit):
        copy = self.remote(src, dst, dp_bit, tensor_bit)
        copy.start()
        self.pending.append(copy)
        return copy

    def store(self, src, dst):
        copy = pltpu.make_async_copy(src, dst, self.local.at[self.used_local])
        self.used_local += 1
        copy.start()
        self.pending_local.append(copy)
        return copy

    def settle(self, copy):
        copy.wait()
        self.pending_local = [other for other in self.pending_local if other is not copy]

    def settle_sends(self, copies):
        for copy in copies:
            copy.wait_send()
        self.pending = [copy for copy in self.pending if all(copy is not other for other in copies)]

    def greet(self, partners):
        barrier = pltpu.get_barrier_semaphore()
        for dp_bit, tensor_bit in partners:
            pl.semaphore_signal(
                barrier, inc=1, device_id=(self.dp ^ dp_bit, self.tensor ^ tensor_bit), device_id_type=MESH
            )
        pl.semaphore_wait(barrier, len(partners))

    def finish(self):
        assert self.used <= self.send.shape[0]
        assert self.used_local <= self.local.shape[0]
        for copy in self.pending:
            copy.wait_send()
        for copy in self.pending_local:
            copy.wait()


class Spread:
    def __init__(self, links, rows):
        self.links, self.rows = links, rows
        half = rows.shape[1] // 2
        self.low, self.high = pl.ds(0, half), pl.ds(half, half)
        self.near_low = links.go(rows.at[0, self.low], rows.at[1, self.low], 0, 1)
        self.far_high = links.go(rows.at[0, self.high], rows.at[2, self.high], 0, 2)
        self.near_high = links.go(rows.at[0, self.high], rows.at[1, self.high], 0, 1)
        self.far_low = links.go(rows.at[0, self.low], rows.at[2, self.low], 0, 2)
        self.stage = 0

    def wait(self, block):
        rows, links, low, high = self.rows, self.links, self.low, self.high
        if block >= 1 and self.stage == 0:
            self.near_low.wait_recv()
            self.last_low = links.go(rows.at[1, low], rows.at[3, low], 0, 2)
            self.far_high.wait_recv()
            self.last_high = links.go(rows.at[2, high], rows.at[3, high], 0, 1)
            self.near_high.wait_recv()
            self.stage = 1
        if block >= 2 and self.stage == 1:
            self.far_low.wait_recv()
            self.stage = 2
        if block >= 3 and self.stage == 2:
            self.last_low.wait_recv()
            self.last_high.wait_recv()
            self.stage = 3

    def sent(self):
        self.links.settle_sends(
            (self.near_low, self.far_high, self.near_high, self.far_low, self.last_low, self.last_high)
        )


class SpreadCross:
    def __init__(self, links, weights, place):
        self.links, self.weights, self.place = links, weights, place
        self.which = links.dp % 2
        half = weights.shape[3] // 2
        self.low, self.high = pl.ds(0, half), pl.ds(half, half)
        whole = slice(None)
        self.near = links.go(self.piece(0, whole), self.piece(1, whole), 0, 1)
        self.far = links.go(self.piece(0, whole), self.piece(2, whole), 0, 2)
        self.core = [self.cross(0)]

    def piece(self, member, rows):
        return self.weights.at[member, self.place, self.which, rows]

    def cross(self, member):
        return self.links.go(self.piece(member, slice(None)), self.piece(member, slice(None)), 1, 0)

    def forward(self):
        links = self.links
        self.near.wait_recv()
        self.last_low = links.go(self.piece(1, self.low), self.piece(3, self.low), 0, 2)
        self.core.append(self.cross(1))
        self.far.wait_recv()
        self.last_high = links.go(self.piece(2, self.high), self.piece(3, self.high), 0, 1)
        self.core.append(self.cross(2))

    def last(self):
        self.last_low.wait_recv()
        self.last_high.wait_recv()
        self.core.append(self.cross(3))


class Gather:
    def __init__(self, links, shard, whole, both_cores=True):
        self.links, self.whole, self.both_cores = links, whole, both_cores
        self.size = shard.shape[0]
        self.place, self.which = links.dp // 2, links.dp % 2
        self.middle = (self.place == 1) | (self.place == 2)
        own = self.rows(0)
        self.own = links.store(shard, own)
        self.core = []
        self.pass_on(shard, own)
        self.skip = links.go(shard, own, 4, 0)
        self.beside = links.go(shard, own, 2, 0)
        self.third_at = links.used
        self.third = links.remote(shard, own, 6, 0)

        @pl.when(self.middle)
        def _():
            self.third.start()

    def pass_on(self, src, dst):
        if self.both_cores:
            self.core.append(self.links.go(src, dst, 1, 0))

    def rows(self, step):
        if len(self.whole.shape) == 4:
            return self.whole.at[self.place ^ step, self.which]
        start = pl.multiple_of((self.links.dp ^ (2 * step)) * self.size, self.size)
        return self.whole.at[pl.ds(start, self.size)]

    def forward(self):
        links = self.links
        block = self.rows(2)
        self.skip.wait_recv()
        self.onward = pltpu.make_async_remote_copy(
            src_ref=block,
            dst_ref=block,
            send_sem=links.send.at[links.used],
            recv_sem=links.recv.at[self.third_at],
            device_id=(links.dp ^ 2, links.tensor),
            device_id_type=MESH,
        )
        links.used += 1

        @pl.when(self.middle)
        def _():
            self.onward.start()

        self.pass_on(block, block)

    def arrive(self):
        links = self.links
        self.beside.wait_recv()
        block = self.rows(1)
        self.pass_on(block, block)
        self.third.wait_recv()
        block = self.rows(3)
        self.pass_on(block, block)
        links.settle(self.own)
        for copy in self.core:
            copy.wait_recv()

    def sent(self):
        self.links.settle_sends(self.core)
        self.finish()

    def finish(self):
        @pl.when(self.middle)
        def _():
            self.third.wait_send()
            self.onward.wait_send()


class Sums:
    def __init__(self, links, parts, half_near, half_far, near, far):
        self.links, self.parts = links, parts
        self.half_near, self.half_far, self.near, self.far = half_near, half_far, near, far
        half = parts.shape[1] // 2
        self.low, self.high = pl.ds(0, half), pl.ds(half, half)

    def ready(self, block):
        links, parts, low, high = self.links, self.parts, self.low, self.high
        if block == 3:
            self.first = links.go(parts.at[3, low], self.half_near, 0, 1)
            self.second = links.go(parts.at[3, high], self.half_far, 0, 2)
        if block == 1:
            self.near_low = links.go(parts.at[1, low], self.near.at[low], 0, 1)
        if block == 2:
            self.far_high = links.go(parts.at[2, high], self.far.at[high], 0, 2)

    def add_half(self, block, start, got):
        def add(rows, from_rows):
            total = self.parts[block, rows].astype(jnp.float32) + got[from_rows].astype(jnp.float32)
            self.parts[block, rows] = total.astype(jnp.bfloat16)

        half = got.shape[0]
        step = math.gcd(half, 32)

        def body(index, carry):
            at = index * step if step == 1 else pl.multiple_of(index * step, step)
            add(pl.ds(start + at, step), pl.ds(at, step))
            return carry

        lax.fori_loop(0, half // step, body, 0)

    def add(self):
        links, parts, low, high = self.links, self.parts, self.low, self.high
        half = parts.shape[1] // 2
        self.first.wait_recv()
        self.add_half(2, 0, self.half_near)
        self.far_low = links.go(parts.at[2, low], self.far.at[low], 0, 2)
        self.second.wait_recv()
        self.add_half(1, half, self.half_far)
        self.near_high = links.go(parts.at[1, high], self.near.at[high], 0, 1)

    def arrive(self):
        for copy in (self.near_low, self.far_high, self.far_low, self.near_high):
            copy.wait_recv()

    def sent(self):
        self.links.settle_sends(
            (self.first, self.second, self.near_low, self.far_high, self.far_low, self.near_high)
        )

    def total(self, rows):
        return self.near[rows].astype(jnp.float32) + self.far[rows].astype(jnp.float32)
def columns(total, width, body):
    def step(index, carry):
        body(pl.ds(pl.multiple_of(index * width, width), width))
        return carry

    lax.fori_loop(0, total // width, step, 0)


def attend_rows(block, keys_t, values, limit):
    outs, logs = [], []
    for which in range(2):
        part = jnp.where(half_mask(block.shape, 1, which), block, jnp.zeros_like(block))
        scores = jnp.dot(part, keys_t, preferred_element_type=jnp.float32)
        if limit is not None:
            scores = jnp.where(lax.broadcasted_iota(jnp.int32, scores.shape, 1) < limit, scores, -jnp.inf)
        peak = jnp.max(scores, axis=1, keepdims=True)
        shifted = jnp.exp(scores - peak)
        total = jnp.sum(shifted, axis=1, keepdims=True)
        product = jnp.dot(shifted.astype(jnp.bfloat16), values, preferred_element_type=jnp.float32)
        outs.append(product * (1.0 / total))
        logs.append(peak + jnp.log(total))
    low = half_mask(block.shape, 1, 0)
    return jnp.where(low, outs[0], outs[1]), jnp.where(low, logs[0], logs[1])


def cross_tile(weights, member, place, cols):
    tile = weights[member, place, :, :, cols]
    return tile.reshape(-1, tile.shape[-1])


def cross_columns(weights, member, cols):
    whole = weights[member, :, :, :, cols]
    return whole.reshape(-1, whole.shape[-1])


def row_steps(total, body):
    def step(index, carry):
        body(pl.ds(pl.multiple_of(index * 32, 32), 32))
        return carry

    lax.fori_loop(0, total // 32, step, 0)


def block_rows(block):
    return pl.ds(block * BLOCK, BLOCK)


def two_heads(weights, part, parts, pair):
    starts = [((2 * pair + which) * parts + part) * DH for which in range(2)]
    return jnp.concatenate([weights[:, start : start + DH] for start in starts], axis=1).astype(jnp.bfloat16)


def fill_tables(cosine, sine, member):
    quarter = DH // 4
    shape = (BLOCK, PAIR)
    lane = lax.broadcasted_iota(jnp.int32, shape, 1) % DH
    frequency = jnp.exp((lane % quarter).astype(jnp.float32) * (-math.log(rope_base) / quarter))
    for block in range(4):
        place = (member ^ block) * BLOCK + lax.broadcasted_iota(jnp.int32, shape, 0)
        angle = place.astype(jnp.float32) * frequency
        rows = block_rows(block)
        cosine[rows] = jnp.where(lane < 2 * quarter, jnp.cos(angle), 1.0)
        sine[rows] = jnp.where(lane < 2 * quarter, jnp.sin(angle), 0.0)


def forward_kernel(
    latents, gains, conditioning, f32_qkv,
    f32_attn_out, f32_cross_q, f32_cross_kv, f32_cross_out, f32_gate, f32_up, f32_down,
    rows_one_out, normed_two_out, rows_three_out, qkv_out, attn_out_out, cross_out, keyval_w_out, mlp_out,
    down_out, rotated_out, attended_out, logs_out,
    query_out, keyval_out, crossed_out, cross_logs_out, resid_one_out, resid_two_out, tables_out,
    rows_one, normed_two, rows_three, w_qkv, w_attn_out, w_cross, w_keyval, rotated, attended, logs, query, keyval,
    crossed, cross_logs, keys_t, parts, got_one, resid_one, resid_two,
    packed, tables, context, raw_attn_out, raw_cross_q, raw_cross_kv, raw_cross_out, raw_gate, raw_up, raw_down,
    own_qkv, own_attn_out, own_cross, own_keyval, own_mlp, own_down, send, recv, local,
):
    low = jnp.bfloat16
    pairs = attended.shape[1] // PAIR
    width = pairs * PAIR
    share = own_qkv.shape[0]
    links = Links(send, recv, local)
    loads = [
        links.store(source, target)
        for source, target in (
            (f32_attn_out, raw_attn_out), (f32_cross_q, raw_cross_q), (f32_cross_kv, raw_cross_kv),
            (f32_cross_out, raw_cross_out), (f32_gate, raw_gate), (f32_up, raw_up), (f32_down, raw_down),
        )
    ]
    for part in range(3):
        for pair in range(pairs):
            at = part * width + pair * PAIR
            own_qkv[:, at : at + PAIR] = two_heads(f32_qkv, part, 3, pair)
    links.greet([(1, 0), (2, 0), (4, 0), (6, 0), (0, 1), (0, 2)])
    gather_qkv = Gather(links, own_qkv, w_qkv)

    def norm_one(rows):
        rows_one[0, rows] = layer_norm(latents[rows].astype(jnp.float32), gains[0:1])[0].astype(low)

    row_steps(BLOCK, norm_one)
    spread_one = Spread(links, rows_one)
    cosine, sine = (tables.at[part] for part in range(2))
    fill_tables(cosine, sine, links.tensor)
    links.store(tables, tables_out)
    for load in loads:
        links.settle(load)
    own_attn_out[...] = raw_attn_out[...].astype(low)
    own_cross[:, :width] = raw_cross_q[...].astype(low)
    own_cross[:, width:] = raw_cross_out[...].astype(low)
    for part in range(2):
        for pair in range(pairs):
            at = part * width + pair * PAIR
            own_keyval[:, at : at + PAIR] = two_heads(raw_cross_kv, part, 2, pair)
    hidden = raw_gate.shape[1]
    own_mlp[:, :hidden] = raw_gate[...].astype(low)
    own_mlp[:, hidden:] = raw_up[...].astype(low)
    own_down[...] = raw_down[...].astype(low)
    links.store(own_down, down_out)
    context[...] = jnp.zeros_like(context)
    context[:CTX] = conditioning[0]
    spread_one.wait(1)
    gather_qkv.forward()
    gather_attn_out = Gather(links, own_attn_out, w_attn_out)
    gather_cross = Gather(links, own_cross, w_cross.at[0], False)
    spread_one.wait(2)
    links.settle(gather_cross.own)
    spread_cross = [SpreadCross(links, w_cross, links.dp // 2)]
    gather_qkv.arrive()
    links.store(w_qkv, qkv_out)

    for block in range(4):
        spread_one.wait(block)
        if block == 2:
            gather_attn_out.forward()
        if block == 3:
            gather_cross.forward()
            gather_keyval = Gather(links, own_keyval, w_keyval)
        rows = block_rows(block)
        turn = (cosine[rows], sine[rows])

        def project(cols):
            packed[:, cols] = dot_plain(rows_one[block], w_qkv[:, cols])

        columns(3 * width, width, project)
        for part in range(3):
            for pair in range(pairs):
                at = slice(part * width + pair * PAIR, part * width + (pair + 1) * PAIR)
                value = packed[:, at]
                rotated[rows, at] = (value if part == 2 else head_turn(value, *turn)).astype(low)
    links.store(rows_one, rows_one_out)
    links.store(rotated, rotated_out)
    for pair in range(pairs):
        key = rotated[:, width + pair * PAIR : width + (pair + 1) * PAIR]
        keys_t[pair] = key.astype(jnp.float32).T.astype(low)

    def out_project(source, block, weight, sums):
        def project(cols):
            parts[block, :, cols] = dot_cols(source[block_rows(block)], weight(cols)).astype(low)

        columns(parts.shape[2], 512, project)
        sums.ready(block)

    sums_one = Sums(links, parts, *got_one)
    for block in (3, 1, 2, 0):
        rows = block_rows(block)

        def one_pair(pair, carry):
            at = pl.ds(pl.multiple_of(pair * PAIR, PAIR), PAIR)
            values_at = pl.ds(pl.multiple_of(2 * width + pair * PAIR, PAIR), PAIR)
            out, log = attend_rows(rotated[rows, at] * low(DH**-0.5), keys_t[pair], rotated[:, values_at], None)
            attended[rows, at] = out.astype(low)
            logs[rows, at] = log
            return carry

        lax.fori_loop(0, pairs, one_pair, 0)
        if block == 3:
            gather_attn_out.arrive()
            links.store(w_attn_out, attn_out_out)
        out_project(attended, block, lambda cols: w_attn_out[cols, :], sums_one)
        if block == 3:
            spread_cross[0].forward()
            gather_mlp = Gather(links, own_mlp, mlp_out)
            spread_cross.append(SpreadCross(links, w_cross, (links.dp // 2) ^ 2))
        if block == 1:
            gather_cross.beside.wait_recv()
            spread_cross.append(SpreadCross(links, w_cross, (links.dp // 2) ^ 1))
        if block == 2:
            gather_keyval.forward()
            sums_one.add()
            spread_cross[1].forward()
    gather_cross.third.wait_recv()
    spread_cross.append(SpreadCross(links, w_cross, (links.dp // 2) ^ 3))
    spread_cross[2].forward()
    links.store(attended, attended_out)
    links.store(logs, logs_out)
    sums_one.arrive()

    def norm_two(rows):
        value = latents[rows].astype(jnp.float32) + parts[0, rows].astype(jnp.float32) + sums_one.total(rows)
        resid_one[rows] = value
        normed_two[rows] = layer_norm(value, gains[1:2])[0].astype(low)

    row_steps(BLOCK, norm_two)
    links.store(resid_one, resid_one_out)
    links.store(normed_two, normed_two_out)
    gather_keyval.arrive()
    links.store(w_keyval, keyval_w_out)
    keyval[0] = dot_plain(context[...], w_keyval[...]).astype(low)
    spread_keyval = Spread(links, keyval)
    spread_cross[3].forward()
    for spread in spread_cross:
        spread.last()
    resid_two[...] = resid_one[...]
    for member in range(4):
        for spread in spread_cross:
            spread.core[member].wait_recv()
        spread_keyval.wait(member)
        at_member = slice(member * width, (member + 1) * width)
        query[:, at_member] = dot_plain(normed_two[...], cross_columns(w_cross, member, slice(0, width))).astype(low)
        for pair in range(pairs):
            at = slice(member * width + pair * PAIR, member * width + (pair + 1) * PAIR)
            keys_at = slice(pair * PAIR, (pair + 1) * PAIR)
            values_at = slice(width + pair * PAIR, width + (pair + 1) * PAIR)
            key_t = keyval[member, :, keys_at].astype(jnp.float32).T.astype(low)
            out, log = attend_rows(query[:, at] * low(DH**-0.5), key_t, keyval[member, :, values_at], CTX)
            crossed[:, at] = out.astype(low)
            cross_logs[:, at] = log
        for place in range(4):
            at = slice(place * 2 * share, (place + 1) * 2 * share)
            tile = cross_tile(w_cross, member, place, slice(width, 2 * width))
            resid_two[:, at] += dot_cols(crossed[:, at_member], tile)
        if member == 1:
            gather_mlp.forward()
    links.store(w_cross, cross_out)
    links.store(keyval, keyval_out)
    links.store(query, query_out)
    links.store(crossed, crossed_out)
    links.store(cross_logs, cross_logs_out)
    links.store(resid_two, resid_two_out)

    def norm_three(rows):
        rows_three[rows] = layer_norm(resid_two[rows], gains[2:3])[0].astype(low)

    row_steps(BLOCK, norm_three)
    gather_mlp.arrive()
    links.store(rows_three, rows_three_out)
    links.finish()
    for gather in (gather_qkv, gather_attn_out, gather_cross, gather_keyval, gather_mlp):
        gather.finish()


def whole_vmem():
    return pl.BlockSpec(memory_space=pltpu.VMEM)


def anywhere():
    return pl.BlockSpec(memory_space=pl.ANY)


def sum_buffers(model):
    return [
        pltpu.VMEM((HALF, model), jnp.bfloat16),
        pltpu.VMEM((HALF, model), jnp.bfloat16),
        pltpu.VMEM((BLOCK, model), jnp.bfloat16),
        pltpu.VMEM((BLOCK, model), jnp.bfloat16),
    ]


def forward_part(latents, gains, conditioning, weights):
    w_qkv, w_attn_out, w_cross_q, w_cross_kv, w_cross_out, w_gate, w_up, w_down = weights
    model = latents.shape[1]
    depth = conditioning.shape[2]
    wide = w_qkv.shape[1]
    width = wide // 3
    hidden = w_gate.shape[1]
    pairs = width // PAIR
    low, high = jnp.bfloat16, jnp.float32
    share = w_qkv.shape[0]
    outs = [
        ((4, BLOCK, model), low),
        ((BLOCK, model), low),
        ((BLOCK, model), low),
        ((model, wide), low),
        ((model, width), low),
        ((4, 4, 2, share, 2 * width), low),
        ((depth, 2 * width), low),
        ((4, 2, share, 2 * hidden), low),
        ((share, hidden), low),
        ((LENGTH, wide), low),
        ((LENGTH, width), low),
        ((LENGTH, width), high),
        ((BLOCK, model), low),
        ((4, FULL, 2 * width), low),
        ((BLOCK, model), low),
        ((BLOCK, model), high),
        ((BLOCK, model), high),
        ((BLOCK, model), high),
        ((2, LENGTH, PAIR), high),
    ]
    work = [
        ((4, BLOCK, model), low),
        ((BLOCK, model), low),
        ((BLOCK, model), low),
        ((model, wide), low),
        ((model, width), low),
        ((4, 4, 2, share, 2 * width), low),
        ((depth, 2 * width), low),
        ((LENGTH, wide), low),
        ((LENGTH, width), low),
        ((LENGTH, width), high),
        ((BLOCK, model), low),
        ((4, FULL, 2 * width), low),
        ((BLOCK, model), low),
        ((BLOCK, model), high),
        ((pairs, PAIR, LENGTH), low),
        ((4, BLOCK, model), low),
    ]
    more = [
        ((BLOCK, model), high),
        ((BLOCK, model), high),
        ((BLOCK, wide), high),
        ((2, LENGTH, PAIR), high),
        ((FULL, depth), low),
        (w_attn_out.shape, high),
        (w_cross_q.shape, high),
        (w_cross_kv.shape, high),
        (w_cross_out.shape, high),
        (w_gate.shape, high),
        (w_up.shape, high),
        (w_down.shape, high),
        ((share, wide), low),
        ((share, width), low),
        ((share, 2 * width), low),
        (w_cross_kv.shape, low),
        ((share, 2 * hidden), low),
        ((share, hidden), low),
    ]
    scratch = [pltpu.VMEM(*buffer) for buffer in work] + [sum_buffers(model)]
    scratch += [pltpu.VMEM(*buffer) for buffer in more]
    scratch += [pltpu.SemaphoreType.DMA((96,)), pltpu.SemaphoreType.DMA((96,)), pltpu.SemaphoreType.DMA((40,))]
    return pl.pallas_call(
        forward_kernel,
        out_shape=[jax.ShapeDtypeStruct(*out) for out in outs],
        in_specs=[whole_vmem()] * 4 + [anywhere()] * 7,
        out_specs=[anywhere()] * len(outs),
        scratch_shapes=scratch,
        compiler_params=pltpu.CompilerParams(collective_id=1, has_side_effects=True, vmem_limit_bytes=VMEM_BYTES),
        cost_estimate=pl.CostEstimate(flops=2**37, bytes_accessed=2**26, transcendentals=2**23),
    )(latents, gains, conditioning, *weights)


class Scatter:
    def __init__(self, links, grads, got_core, extra, got):
        self.links, self.grads, self.got_core, self.extra, self.got = links, grads, got_core, extra, got
        self.size = got.shape[1]
        self.place, self.which = links.dp // 2, links.dp % 2
        self.middle = (self.place == 1) | (self.place == 2)

    def rows(self, place, which):
        if self.got_core is None:
            return place
        start = pl.multiple_of((2 * place + which) * self.size, self.size)
        return pl.ds(start, self.size)

    def pair_up(self):
        self.core = [
            self.links.go(self.grads.at[self.rows(place, 1 - self.which)], self.got_core.at[place], 1, 0)
            for place in range(4)
        ]

    def combine(self):
        for copy in self.core:
            copy.wait_recv()

        def add(place, carry):
            rows = self.rows(place, self.which)
            total = self.grads[rows].astype(jnp.float32) + self.got_core[place].astype(jnp.float32)
            self.grads[rows] = total.astype(jnp.bfloat16)
            return carry

        lax.fori_loop(0, 4, add, 0)
        self.start()

    def start(self):
        links, grads = self.links, self.grads
        block = [grads.at[self.rows(self.place ^ step, self.which)] for step in range(4)]
        self.to_extra = links.remote(block[3], self.extra, 2, 0)
        self.to_third = links.remote(block[3], self.got.at[2], 6, 0)
        self.to_skip = links.remote(block[2], self.got.at[1], 4, 0)

        @pl.when(self.middle)
        def _():
            self.to_third.start()

        @pl.when(jnp.logical_not(self.middle))
        def _():
            self.to_extra.start()
            self.to_skip.start()

        self.beside = links.go(block[1], self.got.at[0], 2, 0)

    def relay(self):
        @pl.when(self.middle)
        def _():
            self.to_extra.wait_recv()
            rows = self.rows(self.place ^ 2, self.which)
            self.grads[rows] = (
                self.grads[rows].astype(jnp.float32) + self.extra[...].astype(jnp.float32)
            ).astype(jnp.bfloat16)
            self.to_skip.start()

    def arrive(self):
        self.beside.wait_recv()
        self.to_skip.wait_recv()

        @pl.when(self.middle)
        def _():
            self.to_third.wait_recv()

    def total(self, out, cols):
        rows = self.rows(self.place, self.which)
        at = (rows, cols) if self.got_core is not None else (rows, slice(None), cols)
        mine = self.grads[at].astype(jnp.float32)
        out[...] = mine + self.got[0, :, cols].astype(jnp.float32) + self.got[1, :, cols].astype(jnp.float32)

        @pl.when(self.middle)
        def _():
            out[...] += self.got[2, :, cols].astype(jnp.float32)

    def finish(self):
        self.to_skip.wait_send()

        @pl.when(self.middle)
        def _():
            self.to_third.wait_send()

        @pl.when(jnp.logical_not(self.middle))
        def _():
            self.to_extra.wait_send()


def attend_rows_back(block, grads, log, keys_t, values_t, keys, d_keys_t, d_values_t, limit):
    block_t = block.astype(jnp.float32).T.astype(jnp.bfloat16)
    grads_t = grads.astype(jnp.float32).T.astype(jnp.bfloat16)
    outs = []
    for which in range(2):
        half = slice(which * DH, (which + 1) * DH)
        keep = half_mask(block.shape, 1, which)
        scores = jnp.dot(jnp.where(keep, block, jnp.zeros_like(block)), keys_t, preferred_element_type=jnp.float32)
        probs = jnp.exp(scores - log[:, which * DH : which * DH + 1])
        if limit is not None:
            probs = jnp.where(lax.broadcasted_iota(jnp.int32, probs.shape, 1) < limit, probs, 0.0)
        d_prob = jnp.dot(jnp.where(keep, grads, jnp.zeros_like(grads)), values_t, preferred_element_type=jnp.float32)
        center = jnp.sum(probs * d_prob, axis=1, keepdims=True)
        d_score = (probs * (d_prob - center)).astype(jnp.bfloat16)
        outs.append(jnp.dot(d_score, keys, preferred_element_type=jnp.float32))
        d_keys_t[half, :] += jnp.dot(block_t[half], d_score, preferred_element_type=jnp.float32)
        d_values_t[half, :] += jnp.dot(grads_t[half], probs.astype(jnp.bfloat16), preferred_element_type=jnp.float32)
    return jnp.where(half_mask(block.shape, 1, 0), outs[0], outs[1]) * DH**-0.5


def backward_kernel(
    latents, gains, conditioning, in_gain, in_d_resid, in_seed,
    in_grads_cross, in_d_keyval, in_qkv, in_attn_out, in_keyval_w, in_rows_one, in_rotated, in_attended, in_logs,
    in_tables,
    grad_latents, grad_context, grad_gains, grad_qkv, grad_attn_out, grad_cross_q, grad_keyval, grad_cross_out,
    parts, rows_one, seeds, w_qkv, w_attn_out, w_keyval, rotated, attended, d_attended, logs, keys_t, values_t,
    d_keys_t, d_values_t, grads_cross, core_cross, got_cross, keyval_parts, got_keyval, context, context_sum,
    context_got, d_resid, tables, gain_rows, gain_got, got, core_qkv, core_attn_out, core_keyval,
    extra_qkv, extra_attn_out, extra_cross, extra_keyval, far_qkv, far_attn_out, far_cross, far_keyval,
    sum_keyval, sum_last, out_qkv, out_keyval, send, recv, local,
):
    low = jnp.bfloat16
    width = attended.shape[1]
    pairs = width // PAIR
    model = latents.shape[1]
    links = Links(send, recv, local)
    which = links.dp % 2
    load_seed = links.store(in_seed, seeds)
    load_self = [
        links.store(source, target)
        for source, target in (
            (in_attn_out, w_attn_out), (in_rotated, rotated), (in_logs, logs), (in_tables, tables),
            (in_attended, attended),
        )
    ]
    load_keyval = [links.store(in_d_keyval, keyval_parts), links.store(in_keyval_w, w_keyval)]
    load_cross = [links.store(in_grads_cross.at[member, :, which], grads_cross.at[member]) for member in range(4)]
    load_late = [links.store(in_qkv, w_qkv), links.store(in_rows_one, rows_one), links.store(in_d_resid, d_resid)]
    links.greet([(1, 0), (2, 0), (4, 0), (6, 0), (0, 1), (0, 2)])
    core_copies = [
        links.go(in_grads_cross.at[member, :, 1 - which], core_cross.at[member], 1, 0) for member in range(4)
    ]
    gain_rows[...] = in_gain[...]
    context[...] = jnp.zeros_like(context)
    context[:CTX] = conditioning[0]
    sums_keyval = Sums(links, keyval_parts, *got_keyval)
    sums_cross = Sums(links, grads_cross, *got_cross)
    for load in load_keyval:
        links.settle(load)
    for part in (3, 1, 2):
        sums_keyval.ready(part)
    for member in (3, 1, 2, 0):
        links.settle(load_cross[member])
        core_copies[member].wait_recv()

        def add(place, carry):
            total = grads_cross[member, place].astype(jnp.float32) + core_cross[member, place].astype(jnp.float32)
            grads_cross[member, place] = total.astype(low)
            return carry

        lax.fori_loop(0, 4, add, 0)
        sums_cross.ready(member)
    links.settle(load_seed)
    for load in load_self:
        links.settle(load)
    for pair in range(pairs):
        key = rotated[:, width + pair * PAIR : width + (pair + 1) * PAIR]
        value = rotated[:, 2 * width + pair * PAIR : 2 * width + (pair + 1) * PAIR]
        keys_t[pair] = key.astype(jnp.float32).T.astype(low)
        values_t[pair] = value.astype(jnp.float32).T.astype(low)
    d_keys_t[...] = jnp.zeros_like(d_keys_t)
    d_values_t[...] = jnp.zeros_like(d_values_t)
    cosine, sine = (tables.at[part] for part in range(2))

    def whole(rows, cols):
        return rows[:, :, cols].reshape(LENGTH, -1)

    def grads_into(target, rows, right):
        def product(part):
            target[part, :] = dot_rows(whole(rows, part), right).astype(low)

        columns(model, 384, product)

    for block in range(4):
        d_attended[block_rows(block)] = dot_plain(seeds[block], w_attn_out[...]).astype(low)
    grads_into(w_attn_out, seeds, attended[...])
    scatter_attn_out = Scatter(links, w_attn_out, core_attn_out, extra_attn_out, far_attn_out)
    scatter_attn_out.pair_up()

    for block in range(4):
        rows = block_rows(block)
        turn = (cosine[rows], -sine[rows])

        def one_pair(pair, carry):
            at = pl.ds(pl.multiple_of(pair * PAIR, PAIR), PAIR)
            keys_at = pl.ds(pl.multiple_of(width + pair * PAIR, PAIR), PAIR)
            out = attend_rows_back(
                rotated[rows, at] * low(DH**-0.5), d_attended[rows, at], logs[rows, at], keys_t[pair],
                values_t[pair], rotated[:, keys_at], d_keys_t.at[pair], d_values_t.at[pair], None,
            )
            rotated[rows, at] = head_turn(out, *turn).astype(low)
            return carry

        lax.fori_loop(0, pairs, one_pair, 0)
        if block == 0:
            sums_keyval.add()
            sums_cross.add()
        if block == 1:
            scatter_attn_out.combine()
        if block == 2:
            sums_keyval.arrive()
            d_keyval = keyval_parts[0].astype(jnp.float32) + sums_keyval.total(slice(None))
            d_keyval = d_keyval.astype(low)
            context_sum[...] = dot_cols(d_keyval, w_keyval[...]).astype(low)
            context_near = links.go(context_sum, context_got.at[0], 0, 1)
            w_keyval[...] = dot_rows(context[...], d_keyval).astype(low)
            scatter_keyval = Scatter(links, w_keyval, core_keyval, extra_keyval, far_keyval)
            scatter_keyval.pair_up()
    sums_cross.arrive()
    for place in range(4):
        total = grads_cross[0, place].astype(jnp.float32) + sums_cross.total(place)
        grads_cross[0, place] = total.astype(low)
    scatter_cross = Scatter(links, grads_cross.at[0], None, extra_cross, far_cross)
    scatter_cross.start()
    scatter_attn_out.relay()
    scatter_keyval.combine()
    for pair in range(pairs):
        for block in range(4):
            rows = block_rows(block)
            turn = (cosine[rows], -sine[rows])
            at = slice(width + pair * PAIR, width + (pair + 1) * PAIR)
            rotated[rows, at] = head_turn(d_keys_t[pair, :, rows].T, *turn).astype(low)
            at = slice(2 * width + pair * PAIR, 2 * width + (pair + 1) * PAIR)
            rotated[rows, at] = d_values_t[pair, :, rows].T.astype(low)
    for load in load_late:
        links.settle(load)
    sums = Sums(links, parts, *got)
    for block in (3, 1, 2, 0):

        def project(cols):
            parts[block, :, cols] = dot_cols(rotated[block_rows(block)], w_qkv[cols, :]).astype(low)

        columns(model, 512, project)
        sums.ready(block)
    grads_into(w_qkv, rows_one, rotated[...])
    scatter_qkv = Scatter(links, w_qkv, core_qkv, extra_qkv, far_qkv)
    scatter_qkv.pair_up()
    sums.add()
    scatter_qkv.combine()
    scatter_cross.relay()
    scatter_keyval.relay()
    context_near.wait_recv()
    links.settle_sends((context_near,))
    context_sum[...] = (context_sum[...].astype(jnp.float32) + context_got[0].astype(jnp.float32)).astype(low)
    context_far = links.go(context_sum, context_got.at[1], 0, 2)
    sums.arrive()

    def norm_one(rows):
        gain = gains[0:1]
        _, scaled, inverse = layer_norm(latents[rows].astype(jnp.float32), gain)
        d_normed = parts[0, rows].astype(jnp.float32) + sums.total(rows)
        d_part, gain_grad = norm_backward(d_normed, scaled, inverse, gain)
        gain_rows[0:1] += gain_grad[None]
        d_resid[rows] += d_part

    row_steps(BLOCK, norm_one)
    links.store(d_resid, grad_latents)
    share = out_qkv.shape[0]
    spot = [logs.at[pl.ds(step * share, share)] for step in range(5)]
    qkv_spot = spot[3:5] + [sum_last]
    for step, (dp_bit, tensor_bit) in enumerate(((1, 0), (0, 1), (0, 2), (2, 0), (4, 0))):
        trade = links.remote(gain_rows, gain_got.at[step], dp_bit, tensor_bit)
        trade.start()
        if step == 1:
            scatter_qkv.relay()
        trade.wait()
        gain_rows[...] += gain_got[step]
    grad_gains[...] = gain_rows[...]
    context_far.wait_recv()
    context_total = context_sum[...].astype(jnp.float32) + context_got[1].astype(jnp.float32)
    grad_context[0] = context_total[:CTX]
    scatter_attn_out.arrive()
    scatter_attn_out.total(spot[2], slice(None))
    links.store(spot[2], grad_attn_out)
    scatter_qkv.arrive()
    for part in range(3):
        scatter_qkv.total(qkv_spot[part], slice(part * width, (part + 1) * width))
    for pair in range(pairs):
        heads_of = [
            qkv_spot[part][:, (2 * pair + half) * DH : (2 * pair + half + 1) * DH]
            for half in range(2)
            for part in range(3)
        ]
        for step in range(3):
            start = (3 * pair + step) * PAIR
            out_qkv[:, start : start + PAIR] = jnp.concatenate(heads_of[2 * step : 2 * step + 2], axis=1)
    links.store(out_qkv, grad_qkv)
    scatter_cross.arrive()
    scatter_cross.total(spot[0], slice(0, width))
    links.store(spot[0], grad_cross_q)
    scatter_cross.total(spot[1], slice(width, 2 * width))
    links.store(spot[1], grad_cross_out)
    scatter_keyval.arrive()
    scatter_keyval.total(sum_keyval, slice(None))
    for head in range(width // DH):
        pieces = [sum_keyval[:, start + head * DH : start + (head + 1) * DH] for start in (0, width)]
        out_keyval[:, 2 * head * DH : 2 * (head + 1) * DH] = jnp.concatenate(pieces, axis=1)
    links.store(out_keyval, grad_keyval)
    links.finish()
    for scatter in (scatter_keyval, scatter_cross, scatter_attn_out, scatter_qkv):
        scatter.finish()


def backward_part(latents, gains, conditioning, gain_rows, d_resid, seed, grads_cross, d_keyval, kept):
    w_qkv, w_attn_out, w_keyval, rows_one, rotated, attended, logs, tables = kept
    model = latents.shape[1]
    depth = conditioning.shape[2]
    wide = w_qkv.shape[1]
    width = wide // 3
    pairs = width // PAIR
    members = lax.axis_size("dp")
    share, span = model // members, depth // members
    low, high = jnp.bfloat16, jnp.float32
    outs = [
        ((BLOCK, model), high),
        (conditioning.shape, high),
        ((8, model), high),
        ((share, wide), high),
        ((share, width), high),
        ((share, width), high),
        ((span, 2 * width), high),
        ((share, width), high),
    ]
    cross_block = (4, share, 2 * width)
    work = [
        ((4, BLOCK, model), low),
        ((4, BLOCK, model), low),
        ((4, BLOCK, model), low),
        ((model, wide), low),
        ((model, width), low),
        ((depth, 2 * width), low),
        ((LENGTH, wide), low),
        ((LENGTH, width), low),
        ((LENGTH, width), low),
        ((LENGTH, width), high),
        ((pairs, PAIR, LENGTH), low),
        ((pairs, PAIR, LENGTH), low),
        ((pairs, PAIR, LENGTH), high),
        ((pairs, PAIR, LENGTH), high),
        ((4, *cross_block), low),
        ((4, *cross_block), low),
    ]
    cross_got = [pltpu.VMEM((rows, share, 2 * width), low) for rows in (2, 2, 4, 4)]
    keyval_got = [pltpu.VMEM((rows, 2 * width), low) for rows in (FULL // 2, FULL // 2, FULL, FULL)]
    more = [
        ((FULL, depth), low),
        ((FULL, depth), low),
        ((2, FULL, depth), low),
        ((BLOCK, model), high),
        ((2, LENGTH, PAIR), high),
        ((8, model), high),
        ((5, 8, model), high),
    ]
    groups = [(share, wide), (share, width), (share, 2 * width), (span, 2 * width)]
    scratch = [pltpu.VMEM(*buffer) for buffer in work] + [cross_got, pltpu.VMEM((4, FULL, 2 * width), low), keyval_got]
    scratch += [pltpu.VMEM(*buffer) for buffer in more] + [sum_buffers(model)]
    scratch += [pltpu.VMEM((4, *group), low) for group in (groups[0], groups[1], groups[3])]
    scratch += [pltpu.VMEM(group, low) for group in groups]
    scratch += [pltpu.VMEM((3, *group), low) for group in groups]
    scratch += [pltpu.VMEM(groups[3], high), pltpu.VMEM((share, width), high)]
    scratch += [pltpu.VMEM(shape, high) for shape in ((share, wide), (span, 2 * width))]
    scratch += [pltpu.SemaphoreType.DMA((96,)), pltpu.SemaphoreType.DMA((96,)), pltpu.SemaphoreType.DMA((48,))]
    return pl.pallas_call(
        backward_kernel,
        out_shape=[jax.ShapeDtypeStruct(*out) for out in outs],
        in_specs=[whole_vmem()] * 4 + [anywhere()] * 12,
        out_specs=[anywhere()] + [whole_vmem()] * 2 + [anywhere()] * 5,
        scratch_shapes=scratch,
        compiler_params=pltpu.CompilerParams(collective_id=2, has_side_effects=True, vmem_limit_bytes=VMEM_BYTES),
        cost_estimate=pl.CostEstimate(flops=2**37, bytes_accessed=2**26, transcendentals=2**23),
    )(
        latents, gains, conditioning, gain_rows, d_resid, seed, grads_cross, d_keyval, w_qkv, w_attn_out, w_keyval,
        rows_one, rotated, attended, logs, tables,
    )


class ScatterFar:
    def __init__(self, links, grads, got_core, extra, got):
        self.links, self.grads, self.got_core, self.extra, self.got = links, grads, got_core, extra, got
        self.place, self.which = links.dp // 2, links.dp % 2
        self.middle = (self.place == 1) | (self.place == 2)
        self.core = [
            links.go(grads.at[place, 1 - self.which], got_core.at[place], 1, 0) for place in range(4)
        ]

    def combine(self, stage, spots):
        links, self.spots = self.links, spots
        for copy in self.core:
            copy.wait_recv()
        size = spots[0].shape[0]
        slots = [stage.at[slot, 0] for slot in range(2)]
        mine = [links.store(self.grads.at[self.place ^ step, self.which], spots[step]) for step in range(4)]
        order = (3, 2, 1, 0)
        others = [links.store(self.got_core.at[self.place ^ step], slots[at]) for at, step in enumerate(order[:2])]
        for at, step in enumerate(order):
            links.settle(mine[step])
            links.settle(others[at])

            def add(rows):
                total = spots[step][rows].astype(jnp.float32) + slots[at % 2][rows].astype(jnp.float32)
                spots[step][rows] = total.astype(jnp.bfloat16)

            row_steps(size, add)
            if at < 2:
                others.append(links.store(self.got_core.at[self.place ^ order[at + 2]], slots[at]))
        self.to_extra = links.remote(spots[3], self.extra, 2, 0)
        self.to_third = links.remote(spots[3], self.got.at[2], 6, 0)
        self.to_skip = links.remote(spots[2], self.got.at[1], 4, 0)

        @pl.when(self.middle)
        def _():
            self.to_third.start()

        @pl.when(jnp.logical_not(self.middle))
        def _():
            self.to_extra.start()
            self.to_skip.start()

        self.beside = links.go(spots[1], self.got.at[0], 2, 0)

    def relay(self):
        @pl.when(self.middle)
        def _():
            self.to_extra.wait_recv()

            def add(rows):
                total = self.spots[2][rows].astype(jnp.float32) + self.extra[rows].astype(jnp.float32)
                self.spots[2][rows] = total.astype(jnp.bfloat16)

            row_steps(self.spots[0].shape[0], add)
            self.to_skip.start()

    def finish(self):
        self.beside.wait_recv()
        self.to_skip.wait()

        @pl.when(self.middle)
        def _():
            self.to_third.wait()

        @pl.when(jnp.logical_not(self.middle))
        def _():
            self.to_extra.wait_send()


def middle_kernel(
    cotangent, gains, normed_two, resid_two, resid_one, in_rows, in_mlp, own_down, in_query, in_crossed,
    in_cross_logs, in_keyval, in_cross,
    block_out, d_resid_out, seed_out, grads_out, d_keyval_out, gain_out, grads_down_out, grads_gate_out, grads_up_out,
    core_down, core_gate, far_down, far_gate, own_down_out, own_gate_out,
    rows_three, seeds, w_mlp, w_down, hidden, both, parts, parts_last, stage, extra_down, extra_gate, spots_down,
    got, got_last,
    cross_logs, keyval, d_keyval, d_keys_t, d_values_t, d_resid, d_normed_two,
    send, recv, local, stage_sem,
):
    low = jnp.bfloat16
    model = cotangent.shape[1]
    width = model // 4
    share = own_down.shape[0]
    units = w_down.shape[1]
    pairs = width // PAIR
    links = Links(send, recv, local)
    load_rows = links.store(in_rows, rows_three.at[0])
    load_mlp = links.store(in_mlp, w_mlp)
    seeds[0] = cotangent[...]
    links.greet([(1, 0), (2, 0), (4, 0), (6, 0), (0, 1), (0, 2)])
    gather_down = Gather(links, own_down, w_down)
    links.settle(load_rows)
    spread_three = Spread(links, rows_three)
    loads = [
        links.store(source, target)
        for source, target in (
            (in_cross_logs, cross_logs), (in_keyval, keyval),
        )
    ]
    gain_out[...] = jnp.zeros_like(gain_out)
    links.settle(load_mlp)
    for block in range(4):
        if block == 3:
            gather_down.forward()
        spread_three.wait(block)
        if block == 2:
            spread_seeds = Spread(links, seeds)
        rows = block_rows(block)

        def up(cols):
            above_at = pl.ds(pl.multiple_of(units + cols.start, cols.size), cols.size)
            gate = dot_plain(rows_three[block], w_mlp[:, :, :, cols].reshape(model, -1))
            above = dot_plain(rows_three[block], w_mlp[:, :, :, above_at].reshape(model, -1))
            sigma = 1.0 / (1.0 + jnp.exp(-gate))
            swish = gate * sigma
            hidden[rows, cols] = (swish * above).astype(low)
            both[rows, cols] = (above * sigma * (1.0 + gate * (1.0 - sigma))).astype(low)
            both[rows, above_at] = swish.astype(low)

        columns(units, 256, up)
    spread_seeds.wait(1)
    spread_seeds.wait(3)

    def tiles_out(count, product, place):
        def copy(index, slot):
            return pltpu.make_async_copy(stage.at[slot], place(index), stage_sem.at[slot])

        def step(index, carry):
            slot = index % 2

            @pl.when(index >= 2)
            def _():
                copy(index - 2, slot).wait()

            for start in (0, units // 2):
                cols = pl.ds(start, units // 2)
                stage[slot, :, :, cols] = product(index, cols).reshape(2, share, -1)
            copy(index, slot).start()
            return carry

        lax.fori_loop(0, count, step, 0)
        for index in (count - 2, count - 1):
            copy(index, index % 2).wait()

    def rows_of(index, size):
        return pl.ds(pl.multiple_of(index * size, size), size)

    tile = 2 * share

    def whole(rows, index):
        return rows[:, :, rows_of(index, tile)].reshape(LENGTH, -1)

    tiles_out(
        model // tile,
        lambda index, cols: dot_rows(whole(seeds, index), hidden[:, cols]).astype(low),
        lambda index: grads_down_out.at[index],
    )
    scatter_down = ScatterFar(links, grads_down_out, core_down, extra_down, far_down)
    gather_down.arrive()
    sums = Sums(links, parts, *got)
    for block in (3, 1, 2, 0):
        rows = block_rows(block)

        def back(cols):
            above_at = pl.ds(pl.multiple_of(units + cols.start, cols.size), cols.size)
            d_hidden = dot_plain(seeds[block], w_down[:, cols])
            both[rows, cols] = (both[rows, cols].astype(jnp.float32) * d_hidden).astype(low)
            both[rows, above_at] = (both[rows, above_at].astype(jnp.float32) * d_hidden).astype(low)

        columns(units, 256, back)

        def down(place, carry):
            weights = w_mlp[place].reshape(2 * share, -1)
            parts[block, :, rows_of(place, 2 * share)] = dot_cols(both[rows], weights).astype(low)
            return carry

        lax.fori_loop(0, 4, down, 0)
        sums.ready(block)
        if block == 3:
            scatter_down.combine(stage, [spots_down.at[place] for place in range(4)])
    sums.add()
    scatter_down.relay()
    w_cross = [w_mlp.at[:, :, :, pl.ds(member * 2 * width, 2 * width)] for member in range(4)]
    load_cross = [links.store(in_cross.at[member], w_cross[member]) for member in range(4)]
    for block in range(4):

        def last(cols):
            parts_last[block, :, cols] = dot_cols(hidden[block_rows(block)], w_down[cols, :]).astype(low)

        columns(model, 512, last)

    def grads_mlp(half, target):
        start = half * units
        tiles_out(
            model // tile,
            lambda index, cols: dot_rows(
                whole(rows_three, index), both[:, pl.ds(start + cols.start, cols.size)]
            ).astype(low),
            lambda index: target.at[index],
        )

    grads_mlp(0, grads_gate_out)
    scatter_gate = ScatterFar(links, grads_gate_out, core_gate, extra_gate, far_gate)
    gather_down.sent()
    query, crossed, cross_seed, seed = (w_down.at[block_rows(spot)] for spot in range(4))
    loads += [links.store(in_query, query), links.store(in_crossed, crossed)]
    for load in loads + load_cross:
        links.settle(load)
    sums.arrive()
    sums_last = Sums(links, parts_last, *got_last)
    for block in (3, 1, 2):
        sums_last.ready(block)
    scatter_gate.combine(stage, [hidden.at[pl.ds(place * BLOCK, share)] for place in range(4)])

    def cross_columns(member, cols):
        return w_cross[member][:, :, :, cols].reshape(model, -1)

    def norm_three(rows):
        gain = gains[2:3]
        _, scaled, inverse = layer_norm(resid_two[rows], gain)
        d_normed = parts[0, rows].astype(jnp.float32) + sums.total(rows)
        d_part, gain_grad = norm_backward(d_normed, scaled, inverse, gain)
        gain_out[2:3] += gain_grad[None]
        value = cotangent[rows].astype(jnp.float32) + d_part
        d_resid[rows] = value
        cross_seed[rows] = value.astype(low)

    row_steps(BLOCK, norm_three)
    for member in range(4):
        at_member = slice(member * width, (member + 1) * width)
        d_crossed = dot_plain(cross_seed[...], cross_columns(member, slice(width, 2 * width))).astype(low)
        for pair in range(pairs):
            at = slice(member * width + pair * PAIR, member * width + (pair + 1) * PAIR)
            keys_at = slice(pair * PAIR, (pair + 1) * PAIR)
            values_at = slice(width + pair * PAIR, width + (pair + 1) * PAIR)
            key = keyval[member, :, keys_at]
            key_t = key.astype(jnp.float32).T.astype(low)
            value_t = keyval[member, :, values_at].astype(jnp.float32).T.astype(low)
            d_keys_t[...] = jnp.zeros_like(d_keys_t)
            d_values_t[...] = jnp.zeros_like(d_values_t)
            out = attend_rows_back(
                query[:, at] * low(DH**-0.5), d_crossed[:, keys_at], cross_logs[:, at], key_t, value_t, key, d_keys_t,
                d_values_t, CTX,
            )
            query[:, at] = out.astype(low)
            d_keyval[member, :, keys_at] = d_keys_t[...].T.astype(low)
            d_keyval[member, :, values_at] = d_values_t[...].T.astype(low)
        for place in range(4):
            at = slice(place * 2 * share, (place + 1) * 2 * share)
            part = dot_cols(query[:, at_member], w_cross[member][place, :, :, :width].reshape(2 * share, width))
            if member == 0:
                d_normed_two[:, at] = part
            else:
                d_normed_two[:, at] += part
    links.store(d_keyval, d_keyval_out)
    scatter_gate.relay()

    def norm_two(rows):
        gain = gains[1:2]
        _, scaled, inverse = layer_norm(resid_one[rows], gain)
        d_part, gain_grad = norm_backward(d_normed_two[rows], scaled, inverse, gain)
        gain_out[1:2] += gain_grad[None]
        value = d_resid[rows] + d_part
        d_resid[rows] = value
        seed[rows] = value.astype(low)

    row_steps(BLOCK, norm_two)
    links.settle(links.store(seed, seed_out.at[0]))
    spread_seed = Spread(links, seed_out)
    links.store(d_resid, d_resid_out)
    sums_last.add()
    grads_mlp(1, grads_up_out)
    for place in range(4):
        rows_at = slice(place * 2 * share, (place + 1) * 2 * share)
        for member in range(4):
            at_member = slice(member * width, (member + 1) * width)
            left = dot_rows(normed_two[:, rows_at], query[:, at_member]).astype(low)
            w_cross[member][place, :, :, :width] = left.reshape(2, share, width)
            right = dot_rows(cross_seed[:, rows_at], crossed[:, at_member]).astype(low)
            w_cross[member][place, :, :, width:] = right.reshape(2, share, width)
    for member in range(4):
        links.store(w_cross[member], grads_out.at[member])
    spread_seed.wait(1)
    sums_last.arrive()

    def add_last(rows):
        d_normed_two[rows] = resid_two[rows] + parts_last[0, rows].astype(jnp.float32) + sums_last.total(rows)

    row_steps(BLOCK, add_last)
    links.store(d_normed_two, block_out)
    spread_seed.wait(3)
    links.store(scatter_down.spots[0], own_down_out)
    links.store(scatter_gate.spots[0], own_gate_out)
    links.finish()
    scatter_down.finish()
    scatter_gate.finish()


def middle_part(cotangent, gains, rows_three, mlp_all, own_down, kept):
    normed_two, resid_two, resid_one, query, crossed, cross_logs, keyval, cross_all = kept
    model = cotangent.shape[1]
    share, units = own_down.shape
    low, high = jnp.bfloat16, jnp.float32
    outs = [
        ((BLOCK, model), high),
        ((BLOCK, model), high),
        ((4, BLOCK, model), low),
        (cross_all.shape, low),
        (keyval.shape, low),
        ((8, model), high),
        ((4, 2, share, units), low),
        ((4, 2, share, units), low),
        ((4, 2, share, units), low),
        ((4, share, units), low),
        ((4, share, units), low),
        ((3, share, units), low),
        ((3, share, units), low),
        ((share, units), low),
        ((share, units), low),
    ]
    work = [
        ((4, BLOCK, model), low),
        ((4, BLOCK, model), low),
        (mlp_all.shape, low),
        ((model, units), low),
        ((LENGTH, units), low),
        ((LENGTH, 2 * units), low),
        ((4, BLOCK, model), low),
        ((4, BLOCK, model), low),
        ((2, 2, share, units), low),
        ((share, units), low),
        ((share, units), low),
        ((4, share, units), low),
    ]
    more = [
        ((BLOCK, model), high),
        (keyval.shape, low),
        (keyval.shape, low),
        ((PAIR, FULL), high),
        ((PAIR, FULL), high),
        ((BLOCK, model), high),
        ((BLOCK, model), high),
    ]
    scratch = [pltpu.VMEM(*buffer) for buffer in work] + [sum_buffers(model), sum_buffers(model)]
    scratch += [pltpu.VMEM(*buffer) for buffer in more]
    scratch += [pltpu.SemaphoreType.DMA((96,)), pltpu.SemaphoreType.DMA((96,)), pltpu.SemaphoreType.DMA((64,))]
    scratch += [pltpu.SemaphoreType.DMA((2,))]
    return pl.pallas_call(
        middle_kernel,
        out_shape=[jax.ShapeDtypeStruct(*out) for out in outs],
        in_specs=[whole_vmem()] * 5 + [anywhere()] * 8,
        out_specs=[anywhere()] * 5 + [whole_vmem()] + [anywhere()] * 9,
        scratch_shapes=scratch,
        compiler_params=pltpu.CompilerParams(collective_id=3, has_side_effects=True, vmem_limit_bytes=VMEM_BYTES),
        cost_estimate=pl.CostEstimate(flops=2**36, bytes_accessed=2**26, transcendentals=2**21),
    )(
        cotangent, gains, normed_two, resid_two, resid_one, rows_three, mlp_all, own_down, query, crossed,
        cross_logs, keyval, cross_all,
    )


def finish_kernel(
    in_out, in_latents, in_qkv, in_attn_out, in_cross_q, in_keyval, in_cross_out, own_gate, far_gate, own_down, far_down,
    in_up,
    block_out, grad_latents, grad_qkv, grad_attn_out, grad_cross_q, grad_keyval, grad_cross_out, grad_gate, grad_up,
    grad_down,
):
    for source, target in (
        (in_out, block_out), (in_latents, grad_latents), (in_qkv, grad_qkv), (in_attn_out, grad_attn_out),
        (in_cross_q, grad_cross_q), (in_keyval, grad_keyval), (in_cross_out, grad_cross_out),
    ):

        def move(rows):
            target[rows] = source[rows].astype(jnp.float32)

        row_steps(source.shape[0], move)
    place = lax.axis_index("dp") // 2
    middle = (place == 1) | (place == 2)
    for own, far, target in ((own_gate, far_gate, grad_gate), (own_down, far_down, grad_down)):

        def add(rows):
            third = jnp.where(middle, far[2, rows].astype(jnp.float32), 0.0)
            total = own[rows].astype(jnp.float32) + far[0, rows].astype(jnp.float32)
            target[rows] = total + far[1, rows].astype(jnp.float32) + third

        row_steps(own.shape[0], add)

    def widen(rows):
        grad_up[rows] = in_up[rows].astype(jnp.float32)

    row_steps(in_up.shape[0], widen)


def finish_part(raw, own_gate, far_gate, own_down, far_down, sum_up):
    wide = jax.ShapeDtypeStruct(sum_up.shape, jnp.float32)
    return pl.pallas_call(
        finish_kernel,
        out_shape=[jax.ShapeDtypeStruct(array.shape, jnp.float32) for array in raw] + [wide] * 3,
        in_specs=[whole_vmem()] * 12,
        out_specs=[whole_vmem()] * 10,
        compiler_params=pltpu.CompilerParams(vmem_limit_bytes=VMEM_BYTES),
        cost_estimate=pl.CostEstimate(flops=2**22, bytes_accessed=2**24, transcendentals=0),
    )(*raw, own_gate, far_gate, own_down, far_down, sum_up)


def per_device(
    latents,
    conditioning,
    gain_attn,
    w_qkv,
    w_attn_out,
    gain_cross,
    w_cross_q,
    w_cross_kv,
    w_cross_out,
    gain_mlp,
    w_gate,
    w_up,
    w_down,
    cotangent,
):
    low = jnp.bfloat16
    gains = jnp.stack([gain_attn, gain_cross, gain_mlp])
    (
        rows_one, normed_two, rows_three, qkv_all, attn_out_t, cross_all, cross_kv, mlp_all, own_down,
        rotated, attended, logs, cross_query, keyval, crossed, cross_logs, resid_one, resid_two, tables,
    ) = forward_part(
        latents,
        gains,
        conditioning,
        (w_qkv, w_attn_out.T, w_cross_q, w_cross_kv, w_cross_out.T, w_gate, w_up, w_down.T),
    )
    (
        block_out, d_resid, seed, grads_cross, d_keyval, gain_rows, _, _, grads_up, _, _, far_down, far_gate, own_down,
        own_gate,
    ) = middle_part(
        cotangent,
        gains,
        rows_three,
        mlp_all,
        own_down,
        (normed_two, resid_two, resid_one, cross_query, crossed, cross_logs, keyval, cross_all),
    )
    sum_up = dp_sum(grads_up.reshape(w_gate.shape[0] * 8, -1))
    grad_latents, grad_context, grad_gains, grad_qkv, grad_attn_out, grad_cross_q, grad_cross_kv, grad_cross_out = (
        backward_part(
            latents,
            gains,
            conditioning,
            gain_rows,
            d_resid,
            seed,
            grads_cross,
            d_keyval,
            (qkv_all, attn_out_t, cross_kv, rows_one, rotated, attended, logs, tables),
        )
    )
    raw = (block_out, grad_latents, grad_qkv, grad_attn_out, grad_cross_q, grad_cross_kv, grad_cross_out)
    (
        block_out, grad_latents, grad_qkv, grad_attn_out, grad_cross_q, grad_cross_kv, grad_cross_out, grad_gate,
        grad_up, grad_down,
    ) = finish_part(raw, own_gate, far_gate, own_down, far_down, sum_up)
    return (
        block_out,
        grad_latents,
        grad_context,
        grad_gains[0],
        grad_qkv,
        grad_attn_out.T,
        grad_gains[1],
        grad_cross_q,
        grad_cross_kv,
        grad_cross_out.T,
        grad_gains[2],
        grad_gate,
        grad_up,
        grad_down.T,
    )


def per_device_general(
    latents,
    conditioning,
    gain_attn,
    w_qkv,
    w_attn_out,
    gain_cross,
    w_cross_q,
    w_cross_kv,
    w_cross_out,
    gain_mlp,
    w_gate,
    w_up,
    w_down,
    cotangent,
):
    low = jnp.bfloat16
    heads_wide = w_cross_q.shape[1]
    hidden_wide = w_gate.shape[1]
    resid_in = latents.astype(jnp.float32)
    normed_one, scaled_one, inverse_one = layer_norm(resid_in, gain_attn)
    rows_one = spread_rows(normed_one.astype(low))
    own_qkv = by_part(w_qkv.astype(low), 3)
    qkv_all = lax.all_gather(own_qkv, "dp", axis=0, tiled=True)
    own_kv = by_part(w_cross_kv.astype(low), 2)
    own_kv = jnp.concatenate([own_kv[:, :heads_wide], own_kv[:, heads_wide:]], axis=0)
    own_mid = jnp.concatenate(
        [w_attn_out.astype(low).T, w_cross_q.astype(low), w_cross_out.astype(low).T, own_kv], axis=1
    )
    mid_all = lax.all_gather(after(own_mid, qkv_all), "dp", axis=0, tiled=True)
    own_mlp = jnp.concatenate([w_gate.astype(low), w_up.astype(low)], axis=1)
    mlp_all = lax.all_gather(after(own_mlp, mid_all), "dp", axis=0, tiled=True)
    down_all = lax.all_gather(after(w_down.astype(low).T, mlp_all), "dp", axis=0, tiled=True)
    attn_out_t, cross_q, cross_out_t = (mid_all[:, part * heads_wide : (part + 1) * heads_wide] for part in range(3))
    model = mid_all.shape[0]
    cross_kv = (
        mid_all[:, 3 * heads_wide :]
        .reshape(lax.axis_size("dp"), 2, -1, heads_wide)
        .transpose(0, 2, 1, 3)
        .reshape(model // 2, 2 * heads_wide)
    )

    tables = turn_tables(group_positions(latents.shape[0]))
    packed = dot_plain(rows_one, qkv_all)
    attended, rotated, logs = attend(pad_heads(packed, 3), tables)
    attended = attended[:, :heads_wide]
    resid_one = resid_in + sum_rows(dot_cols(attended, attn_out_t))
    normed_two, scaled_two, inverse_two = layer_norm(resid_one, gain_cross)
    rows_two = spread_rows(normed_two.astype(low))
    head_shape = (-1, heads_wide // DH, DH)
    cross_query = dot_plain(rows_two, cross_q).astype(low).reshape(head_shape)
    context = conditioning.reshape(CTX, conditioning.shape[2])
    cross_pack = dot_plain(context, cross_kv).astype(low)
    cross_key = cross_pack[:, :heads_wide].reshape(head_shape)
    cross_value = cross_pack[:, heads_wide:].reshape(head_shape)
    crossed, cross_logs = cross_forward(cross_query, cross_key, cross_value)
    crossed = crossed.reshape(-1, heads_wide).astype(low)
    resid_two = resid_one + sum_rows(dot_cols(crossed, cross_out_t))
    normed_three, scaled_three, inverse_three = layer_norm(resid_two, gain_mlp)
    rows_three = spread_rows(normed_three.astype(low))
    mlp_seed = spread_rows(cotangent)
    both = dot_plain(rows_three, mlp_all)
    gate_pre, up_pre = both[:, :hidden_wide], both[:, hidden_wide:]
    sigma_gate = jax.nn.sigmoid(gate_pre)
    swish = gate_pre * sigma_gate
    hidden = (swish * up_pre).astype(low)
    sum_down = dp_sum(dot_rows(mlp_seed, hidden))
    d_hidden = dot_plain(mlp_seed, down_all)
    d_gate = (d_hidden * up_pre * sigma_gate * (1.0 + gate_pre * (1.0 - sigma_gate))).astype(low)
    d_up = (d_hidden * swish).astype(low)
    d_both = jnp.concatenate([d_gate, d_up], axis=1)
    sum_mlp = dp_sum(after(dot_rows(rows_three, d_both), sum_down))
    d_normed = sum_rows(dot_cols(d_both, mlp_all))
    d_part, gain_grad_three = norm_backward(d_normed, scaled_three, inverse_three, gain_mlp)
    d_resid = cotangent.astype(jnp.float32) + d_part
    block_out = resid_two + sum_rows(dot_cols(hidden, down_all))
    cross_seed = spread_rows(d_resid.astype(low))
    grad_cross_out = dot_rows(cross_seed, crossed)
    d_crossed = dot_plain(cross_seed, cross_out_t).astype(low).reshape(head_shape)
    d_query, d_key, d_value = cross_backward(cross_query, cross_key, cross_value, d_crossed, cross_logs)
    d_query = d_query.reshape(-1, heads_wide).astype(low)
    d_keyval = jnp.concatenate([d_key.reshape(CTX, -1), d_value.reshape(CTX, -1)], axis=1).astype(low)
    grad_cross_q = dot_rows(rows_two, d_query)
    grad_cross_kv = dot_rows(context, d_keyval)
    context_part = dot_cols(d_keyval, cross_kv)
    d_normed = sum_rows(dot_cols(d_query, cross_q))
    d_part, gain_grad_two = norm_backward(d_normed, scaled_two, inverse_two, gain_cross)
    d_resid = d_resid + d_part
    self_seed = spread_rows(d_resid.astype(low))
    grad_attn_out = dot_rows(self_seed, attended)
    grad_kv = (
        grad_cross_kv.astype(low)
        .reshape(lax.axis_size("dp"), -1, 2, heads_wide)
        .transpose(0, 2, 1, 3)
        .reshape(model, heads_wide)
    )
    grad_mid = jnp.concatenate([grad_attn_out.astype(low), grad_cross_q.astype(low), grad_cross_out.astype(low), grad_kv], axis=1)
    sum_mid = dp_sum(after(grad_mid, sum_mlp))
    d_attended = dot_plain(self_seed, attn_out_t).astype(low)
    d_packed = drop_heads(attend_back(rotated, pad_heads(d_attended, 1), logs, tables), 3, packed.shape[1])
    sum_qkv = dp_sum(after(dot_rows(rows_one, d_packed), sum_mid))
    d_normed = sum_rows(dot_cols(d_packed, qkv_all))
    d_part, gain_grad_one = norm_backward(d_normed, scaled_one, inverse_one, gain_attn)
    grad_latents = d_resid + d_part
    grad_context = (
        lax.psum(context_part.astype(low), "tensor").astype(jnp.float32).reshape(conditioning.shape)
    )
    gains = lax.psum(jnp.stack([gain_grad_one, gain_grad_two, gain_grad_three]), ("dp", "tensor"))
    sums = [sum_mid[:, part * heads_wide : (part + 1) * heads_wide].astype(jnp.float32) for part in range(4)]
    half = sums[3].shape[0] // 2
    sum_kv = jnp.concatenate([sums[3][:half], sums[3][half:]], axis=1)
    return (
        block_out,
        grad_latents,
        grad_context,
        gains[0],
        by_head(sum_qkv, 3).astype(jnp.float32),
        sums[0].T,
        gains[1],
        sums[1],
        by_head(sum_kv, 2),
        sums[2].T,
        gains[2],
        sum_mlp[:, :hidden_wide].astype(jnp.float32),
        sum_mlp[:, hidden_wide:].astype(jnp.float32),
        sum_down.astype(jnp.float32).T,
    )


def solution(mesh):
    in_specs = (
        P(("dp", "tensor"), None),
        P("dp", None, None),
        P(),
        P("dp", "tensor"),
        P("tensor", "dp"),
        P(),
        P("dp", "tensor"),
        P("dp", "tensor"),
        P("tensor", "dp"),
        P(),
        P("dp", "tensor"),
        P("dp", "tensor"),
        P("tensor", "dp"),
        P(("dp", "tensor"), None),
    )
    out_specs = (
        P(("dp", "tensor"), None),
        P(("dp", "tensor"), None),
        P("dp", None, None),
        P(),
        P("dp", "tensor"),
        P("tensor", "dp"),
        P(),
        P("dp", "tensor"),
        P("dp", "tensor"),
        P("tensor", "dp"),
        P(),
        P("dp", "tensor"),
        P("dp", "tensor"),
        P("tensor", "dp"),
    )
    special = dict(mesh.shape) == {"dp": 8, "tensor": 4}
    return jax.shard_map(
        per_device if special else per_device_general, mesh=mesh, in_specs=in_specs, out_specs=out_specs, check_vma=False
    )
```

```python
import math
from functools import reduce

import jax
import jax.numpy as jnp
from jax import lax
from jax.experimental import pallas as pl
from jax.experimental.pallas import tpu as pltpu
from jax.sharding import PartitionSpec as P

DH = 64
CTX = 130
LENGTH = 1024
PAIR = 2 * DH
ROWS = 256
VMEM_BYTES = 62 * 2**20

norm_eps = 1e-05
rope_base = 10000.0


def head_turn(values, cosine, sine):
    quarter = DH // 4
    ahead = pltpu.roll(values, PAIR - quarter, 1)
    behind = pltpu.roll(values, quarter, 1)
    lane = lax.broadcasted_iota(jnp.int32, values.shape, 1) % DH
    return values * cosine + jnp.where(lane < quarter, -ahead, behind) * sine


def half_mask(shape, axis, which):
    place = lax.broadcasted_iota(jnp.int32, shape, axis)
    return (place >= DH) if which else (place < DH)


def attend_kernel(q_ref, k_ref, v_ref, cos_ref, sin_ref, out_ref, rot_ref, log_ref, kt_ref, vm_ref):
    pairs = pl.num_programs(0)
    pair = pl.program_id(0)
    turn = (cos_ref[...], sin_ref[...])
    query = head_turn(q_ref[...], *turn).astype(jnp.bfloat16)
    key = head_turn(k_ref[...], *turn).astype(jnp.bfloat16)
    value = v_ref[...].astype(jnp.bfloat16)
    for part, array in enumerate((query, key, value)):
        start = pl.multiple_of((part * pairs + pair) * PAIR, PAIR)
        rot_ref[:, pl.ds(start, PAIR)] = array
    key_t = key.astype(jnp.float32).T
    for which in range(2):
        kt_ref[which] = jnp.where(half_mask(key_t.shape, 0, which), key_t, 0.0).astype(jnp.bfloat16)
        vm_ref[which] = jnp.where(half_mask(value.shape, 1, which), value.astype(jnp.float32), 0.0).astype(jnp.bfloat16)
    q_start = pl.multiple_of(pair * PAIR, PAIR)

    def one_block(step, carry):
        rows = pl.ds(pl.multiple_of(step * ROWS, ROWS), ROWS)
        block = rot_ref[rows, pl.ds(q_start, PAIR)] * jnp.bfloat16(DH**-0.5)
        outs, logs = [], []
        for which in range(2):
            scores = jnp.dot(block, kt_ref[which], preferred_element_type=jnp.float32)
            peak = jnp.max(scores, axis=1, keepdims=True)
            shifted = jnp.exp(scores - peak)
            total = jnp.sum(shifted, axis=1, keepdims=True)
            product = jnp.dot(shifted.astype(jnp.bfloat16), vm_ref[which], preferred_element_type=jnp.float32)
            outs.append(product * (1.0 / total))
            logs.append(peak + jnp.log(total))
        out_ref[rows, :] = (outs[0] + outs[1]).astype(jnp.bfloat16)
        low = half_mask((ROWS, PAIR), 1, 0)
        log_ref[rows, :] = jnp.where(low, logs[0], logs[1])
        return carry

    lax.fori_loop(0, LENGTH // ROWS, one_block, 0)


def attend_back_kernel(
    q_ref, k_ref, v_ref, grad_ref, log_ref, cos_ref, sin_ref, out_ref,
    kt_ref, vt_ref, km_ref, qt_ref, gt_ref, dq_ref, dk_ref, dv_ref,
):
    pairs = pl.num_programs(0)
    pair = pl.program_id(0)
    key_t = k_ref[...].astype(jnp.float32).T
    value_t = v_ref[...].astype(jnp.float32).T
    for which in range(2):
        keep = half_mask(key_t.shape, 0, which)
        kt_ref[which] = jnp.where(keep, key_t, 0.0).astype(jnp.bfloat16)
        vt_ref[which] = jnp.where(keep, value_t, 0.0).astype(jnp.bfloat16)
        key = k_ref[...].astype(jnp.float32)
        km_ref[which] = jnp.where(half_mask(key.shape, 1, which), key, 0.0).astype(jnp.bfloat16)
    qt_ref[...] = (q_ref[...].astype(jnp.float32) * DH**-0.5).T.astype(jnp.bfloat16)
    gt_ref[...] = grad_ref[...].astype(jnp.float32).T.astype(jnp.bfloat16)
    dk_ref[...] = jnp.zeros_like(dk_ref)
    dv_ref[...] = jnp.zeros_like(dv_ref)

    def one_block(step, carry):
        rows = pl.ds(pl.multiple_of(step * ROWS, ROWS), ROWS)
        block = q_ref[rows, :] * jnp.bfloat16(DH**-0.5)
        grads = grad_ref[rows, :]
        d_query = jnp.zeros((ROWS, PAIR), jnp.float32)
        for which in range(2):
            half = slice(which * DH, (which + 1) * DH)
            scores = jnp.dot(block, kt_ref[which], preferred_element_type=jnp.float32)
            probs = jnp.exp(scores - log_ref[rows, which * DH : which * DH + 1])
            d_prob = jnp.dot(grads, vt_ref[which], preferred_element_type=jnp.float32)
            center = jnp.sum(probs * d_prob, axis=1, keepdims=True)
            d_score = (probs * (d_prob - center)).astype(jnp.bfloat16)
            d_query += jnp.dot(d_score, km_ref[which], preferred_element_type=jnp.float32)
            dk_ref[half, :] += jnp.dot(qt_ref[half, rows], d_score, preferred_element_type=jnp.float32)
            dv_ref[half, :] += jnp.dot(
                gt_ref[half, rows], probs.astype(jnp.bfloat16), preferred_element_type=jnp.float32
            )
        dq_ref[rows, :] = d_query * DH**-0.5
        return carry

    lax.fori_loop(0, LENGTH // ROWS, one_block, 0)
    turn = (cos_ref[...], -sin_ref[...])
    results = (head_turn(dq_ref[...], *turn), head_turn(dk_ref[...].T, *turn), dv_ref[...].T)
    for part, array in enumerate(results):
        start = pl.multiple_of((part * pairs + pair) * PAIR, PAIR)
        out_ref[:, pl.ds(start, PAIR)] = array.astype(jnp.bfloat16)


def column_block(offset):
    return pl.BlockSpec((LENGTH, PAIR), lambda pair: (0, pair + offset))


def whole_block(columns):
    return pl.BlockSpec((LENGTH, columns), lambda pair: (0, 0))


def attend(packed, tables):
    columns = packed.shape[1]
    pairs = columns // (3 * PAIR)
    return pl.pallas_call(
        attend_kernel,
        grid=(pairs,),
        in_specs=[column_block(part * pairs) for part in range(3)] + [whole_block(PAIR)] * 2,
        out_specs=[column_block(0), whole_block(columns), column_block(0)],
        out_shape=[
            jax.ShapeDtypeStruct((LENGTH, pairs * PAIR), jnp.bfloat16),
            jax.ShapeDtypeStruct((LENGTH, columns), jnp.bfloat16),
            jax.ShapeDtypeStruct((LENGTH, pairs * PAIR), jnp.float32),
        ],
        scratch_shapes=[pltpu.VMEM((2, PAIR, LENGTH), jnp.bfloat16), pltpu.VMEM((2, LENGTH, PAIR), jnp.bfloat16)],
        compiler_params=pltpu.CompilerParams(vmem_limit_bytes=VMEM_BYTES),
        cost_estimate=pl.CostEstimate(flops=pairs * 2**32, bytes_accessed=2**24, transcendentals=pairs * 2**21),
    )(packed, packed, packed, *tables)


def attend_back(rotated, d_attended, logs, tables):
    columns = rotated.shape[1]
    pairs = columns // (3 * PAIR)
    tall = pltpu.VMEM((PAIR, LENGTH), jnp.bfloat16)
    return pl.pallas_call(
        attend_back_kernel,
        grid=(pairs,),
        in_specs=[column_block(part * pairs) for part in range(3)]
        + [column_block(0), column_block(0)]
        + [whole_block(PAIR)] * 2,
        out_specs=whole_block(columns),
        out_shape=jax.ShapeDtypeStruct((LENGTH, columns), jnp.bfloat16),
        scratch_shapes=[
            pltpu.VMEM((2, PAIR, LENGTH), jnp.bfloat16),
            pltpu.VMEM((2, PAIR, LENGTH), jnp.bfloat16),
            pltpu.VMEM((2, LENGTH, PAIR), jnp.bfloat16),
            tall,
            tall,
            pltpu.VMEM((LENGTH, PAIR), jnp.float32),
            pltpu.VMEM((PAIR, LENGTH), jnp.float32),
            pltpu.VMEM((PAIR, LENGTH), jnp.float32),
        ],
        compiler_params=pltpu.CompilerParams(vmem_limit_bytes=VMEM_BYTES),
        cost_estimate=pl.CostEstimate(flops=pairs * 2**33, bytes_accessed=2**24, transcendentals=pairs * 2**21),
    )(rotated, rotated, rotated, d_attended, logs, *tables)


def turn_tables(positions):
    quarter = DH // 4
    frequency = jnp.exp(-jnp.log(rope_base) * jnp.arange(quarter).astype(jnp.float32) / quarter)
    angles = positions.astype(jnp.float32)[:, None] * frequency[None, :]
    cosine, sine = jnp.cos(angles), jnp.sin(angles)
    zeros, ones = jnp.zeros_like(sine), jnp.ones_like(sine)
    rows = (
        jnp.concatenate([cosine, cosine, ones, ones], axis=1),
        jnp.concatenate([sine, sine, zeros, zeros], axis=1),
    )
    return tuple(jnp.concatenate([row, row], axis=1) for row in rows)


def dot_plain(left_op, right_op):
    return jnp.dot(left_op, right_op, preferred_element_type=jnp.float32)


def dot_rows(left_op, right_op):
    return lax.dot_general(
        left_op, right_op, (((0,), (0,)), ((), ())), preferred_element_type=jnp.float32
    )


def dot_cols(left_op, right_op):
    return lax.dot_general(
        left_op, right_op, (((1,), (1,)), ((), ())), preferred_element_type=jnp.float32
    )


def layer_norm(values, gain_vec):
    center = values - jnp.mean(values, axis=-1, keepdims=True)
    spread = jnp.mean(center * center, axis=-1, keepdims=True)
    inverse = lax.rsqrt(spread + norm_eps)
    scaled = center * inverse
    return (scaled * gain_vec, scaled, inverse)


def norm_backward(upstream, scaled, inverse, gain_vec):
    weighted = upstream * gain_vec
    inner = jnp.mean(weighted, axis=-1, keepdims=True) + scaled * jnp.mean(
        weighted * scaled, axis=-1, keepdims=True
    )
    return (inverse * (weighted - inner), jnp.sum(upstream * scaled, axis=0))


def swap(values, bit):
    return lax.ppermute(values, "tensor", [(member, member ^ bit) for member in range(4)])


def spread_rows(values):
    if lax.axis_size("tensor") != 4:
        return lax.all_gather(values, "tensor", axis=0, tiled=True)
    half = values.shape[0] // 2
    near, far = swap(values, 1), swap(values, 2)
    return jnp.concatenate([values, near, far, swap(near[:half], 2), swap(far[half:], 1)], axis=0)


def sum_rows(partial):
    if lax.axis_size("tensor") != 4:
        return lax.psum_scatter(
            partial.astype(jnp.bfloat16), "tensor", scatter_dimension=0, tiled=True
        ).astype(jnp.float32)
    size = partial.shape[0] // 4
    half = size // 2
    own, near, far, last = (partial[part * size : (part + 1) * size] for part in range(4))
    first = swap(last[:half].astype(jnp.bfloat16), 1)
    second = swap(last[half:].astype(jnp.bfloat16), 2)
    far = jnp.concatenate([far[:half] + first.astype(jnp.float32), far[half:]], axis=0)
    near = jnp.concatenate([near[:half], near[half:] + second.astype(jnp.float32)], axis=0)
    return (
        own
        + swap(near.astype(jnp.bfloat16), 1).astype(jnp.float32)
        + swap(far.astype(jnp.bfloat16), 2).astype(jnp.float32)
    )


def group_positions(rows):
    group = lax.axis_size("tensor")
    blocks = jnp.arange(group)
    if group == 4:
        blocks = blocks ^ lax.axis_index("tensor")
    return (blocks[:, None] * rows + jnp.arange(rows)[None, :]).reshape(-1)


def cross_forward(queries, keys_in, values_in):
    scores = jnp.einsum("qhd,khd->hqk", queries, keys_in, preferred_element_type=jnp.float32) * DH ** (-0.5)
    peak_score = jnp.max(scores, axis=-1, keepdims=True)
    shifted = jnp.exp(scores - peak_score)
    totals = jnp.sum(shifted, axis=-1, keepdims=True)
    probabilities = (shifted / totals).astype(jnp.bfloat16)
    output = jnp.einsum("hqk,khd->qhd", probabilities, values_in, preferred_element_type=jnp.float32)
    return (output, peak_score + jnp.log(totals))


def cross_backward(queries, keys_in, values_in, d_output, log_totals):
    scaling = DH ** (-0.5)
    scores = jnp.einsum("qhd,khd->hqk", queries, keys_in, preferred_element_type=jnp.float32) * scaling
    probabilities = jnp.exp(scores - log_totals)
    d_prob = jnp.einsum("qhd,khd->hqk", d_output, values_in, preferred_element_type=jnp.float32)
    center = jnp.sum(probabilities * d_prob, axis=-1, keepdims=True)
    d_score = (probabilities * (d_prob - center)).astype(jnp.bfloat16)
    d_query = jnp.einsum("hqk,khd->qhd", d_score, keys_in, preferred_element_type=jnp.float32) * scaling
    d_key = jnp.einsum("hqk,qhd->khd", d_score, queries, preferred_element_type=jnp.float32) * scaling
    d_value = jnp.einsum(
        "hqk,qhd->khd", probabilities.astype(jnp.bfloat16), d_output, preferred_element_type=jnp.float32
    )
    return (d_query, d_key, d_value)


def by_part(columns, parts):
    rows = columns.shape[0]
    return columns.reshape(rows, -1, parts, DH).swapaxes(1, 2).reshape(rows, -1)


def by_head(columns, parts):
    rows = columns.shape[0]
    return columns.reshape(rows, parts, -1, DH).swapaxes(1, 2).reshape(rows, -1)


def pad_heads(columns, parts):
    rows, width = columns.shape
    each = width // parts
    if each % PAIR == 0:
        return columns
    return jnp.pad(columns.reshape(rows, parts, each), ((0, 0), (0, 0), (0, -each % PAIR))).reshape(rows, -1)


def drop_heads(columns, parts, width):
    rows = columns.shape[0]
    return columns.reshape(rows, parts, -1)[:, :, : width // parts].reshape(rows, width)


def dp_sum(grads):
    return lax.psum_scatter(grads.astype(jnp.bfloat16), "dp", scatter_dimension=0, tiled=True)


def after(value, earlier):
    return lax.optimization_barrier((value, earlier))[0]


MESH = pl.DeviceIdType.MESH
BLOCK = LENGTH // 4
HALF = BLOCK // 2
FULL = 160


class Links:
    def __init__(self, send, recv, local):
        self.send, self.recv, self.local = send, recv, local
        self.used = self.used_local = 0
        self.pending, self.pending_local = [], []
        self.dp, self.tensor = lax.axis_index("dp"), lax.axis_index("tensor")

    def remote(self, src, dst, dp_bit, tensor_bit):
        at = self.used
        self.used += 1
        return pltpu.make_async_remote_copy(
            src_ref=src,
            dst_ref=dst,
            send_sem=self.send.at[at],
            recv_sem=self.recv.at[at],
            device_id=(self.dp ^ dp_bit, self.tensor ^ tensor_bit),
            device_id_type=MESH,
        )

    def go(self, src, dst, dp_bit, tensor_bit):
        copy = self.remote(src, dst, dp_bit, tensor_bit)
        copy.start()
        self.pending.append(copy)
        return copy

    def store(self, src, dst):
        copy = pltpu.make_async_copy(src, dst, self.local.at[self.used_local])
        self.used_local += 1
        copy.start()
        self.pending_local.append(copy)
        return copy

    def settle(self, copy):
        copy.wait()
        self.pending_local = [other for other in self.pending_local if other is not copy]

    def settle_sends(self, copies):
        for copy in copies:
            copy.wait_send()
        self.pending = [copy for copy in self.pending if all(copy is not other for other in copies)]

    def greet(self, partners):
        barrier = pltpu.get_barrier_semaphore()
        for dp_bit, tensor_bit in partners:
            pl.semaphore_signal(
                barrier, inc=1, device_id=(self.dp ^ dp_bit, self.tensor ^ tensor_bit), device_id_type=MESH
            )
        pl.semaphore_wait(barrier, len(partners))

    def finish(self):
        assert self.used <= self.send.shape[0]
        assert self.used_local <= self.local.shape[0]
        for copy in self.pending:
            copy.wait_send()
        for copy in self.pending_local:
            copy.wait()


class Spread:
    def __init__(self, links, rows):
        self.links, self.rows = links, rows
        half = rows.shape[1] // 2
        self.low, self.high = pl.ds(0, half), pl.ds(half, half)
        self.near_low = links.go(rows.at[0, self.low], rows.at[1, self.low], 0, 1)
        self.far_high = links.go(rows.at[0, self.high], rows.at[2, self.high], 0, 2)
        self.near_high = links.go(rows.at[0, self.high], rows.at[1, self.high], 0, 1)
        self.far_low = links.go(rows.at[0, self.low], rows.at[2, self.low], 0, 2)
        self.stage = 0

    def wait(self, block):
        rows, links, low, high = self.rows, self.links, self.low, self.high
        if block >= 1 and self.stage == 0:
            self.near_low.wait_recv()
            self.last_low = links.go(rows.at[1, low], rows.at[3, low], 0, 2)
            self.far_high.wait_recv()
            self.last_high = links.go(rows.at[2, high], rows.at[3, high], 0, 1)
            self.near_high.wait_recv()
            self.stage = 1
        if block >= 2 and self.stage == 1:
            self.far_low.wait_recv()
            self.stage = 2
        if block >= 3 and self.stage == 2:
            self.last_low.wait_recv()
            self.last_high.wait_recv()
            self.stage = 3

    def sent(self):
        self.links.settle_sends(
            (self.near_low, self.far_high, self.near_high, self.far_low, self.last_low, self.last_high)
        )


class SpreadCross:
    def __init__(self, links, weights, place):
        self.links, self.weights, self.place = links, weights, place
        self.which = links.dp % 2
        half = weights.shape[3] // 2
        self.low, self.high = pl.ds(0, half), pl.ds(half, half)
        whole = slice(None)
        self.near = links.go(self.piece(0, whole), self.piece(1, whole), 0, 1)
        self.far = links.go(self.piece(0, whole), self.piece(2, whole), 0, 2)
        self.core = [self.cross(0)]

    def piece(self, member, rows):
        return self.weights.at[member, self.place, self.which, rows]

    def cross(self, member):
        return self.links.go(self.piece(member, slice(None)), self.piece(member, slice(None)), 1, 0)

    def forward(self):
        links = self.links
        self.near.wait_recv()
        self.last_low = links.go(self.piece(1, self.low), self.piece(3, self.low), 0, 2)
        self.core.append(self.cross(1))
        self.far.wait_recv()
        self.last_high = links.go(self.piece(2, self.high), self.piece(3, self.high), 0, 1)
        self.core.append(self.cross(2))

    def last(self):
        self.last_low.wait_recv()
        self.last_high.wait_recv()
        self.core.append(self.cross(3))


class Gather:
    def __init__(self, links, shard, whole, both_cores=True):
        self.links, self.whole, self.both_cores = links, whole, both_cores
        self.size = shard.shape[0]
        self.place, self.which = links.dp // 2, links.dp % 2
        self.middle = (self.place == 1) | (self.place == 2)
        own = self.rows(0)
        self.own = links.store(shard, own)
        self.core = []
        self.pass_on(shard, own)
        self.skip = links.go(shard, own, 4, 0)
        self.beside = links.go(shard, own, 2, 0)
        self.third_at = links.used
        self.third = links.remote(shard, own, 6, 0)

        @pl.when(self.middle)
        def _():
            self.third.start()

    def pass_on(self, src, dst):
        if self.both_cores:
            self.core.append(self.links.go(src, dst, 1, 0))

    def rows(self, step):
        if len(self.whole.shape) == 4:
            return self.whole.at[self.place ^ step, self.which]
        start = pl.multiple_of((self.links.dp ^ (2 * step)) * self.size, self.size)
        return self.whole.at[pl.ds(start, self.size)]

    def forward(self):
        links = self.links
        block = self.rows(2)
        self.skip.wait_recv()
        self.onward = pltpu.make_async_remote_copy(
            src_ref=block,
            dst_ref=block,
            send_sem=links.send.at[links.used],
            recv_sem=links.recv.at[self.third_at],
            device_id=(links.dp ^ 2, links.tensor),
            device_id_type=MESH,
        )
        links.used += 1

        @pl.when(self.middle)
        def _():
            self.onward.start()

        self.pass_on(block, block)

    def arrive(self):
        links = self.links
        self.beside.wait_recv()
        block = self.rows(1)
        self.pass_on(block, block)
        self.third.wait_recv()
        block = self.rows(3)
        self.pass_on(block, block)
        links.settle(self.own)
        for copy in self.core:
            copy.wait_recv()

    def sent(self):
        self.links.settle_sends(self.core)
        self.finish()

    def finish(self):
        @pl.when(self.middle)
        def _():
            self.third.wait_send()
            self.onward.wait_send()


class Sums:
    def __init__(self, links, parts, half_near, half_far, near, far):
        self.links, self.parts = links, parts
        self.half_near, self.half_far, self.near, self.far = half_near, half_far, near, far
        half = parts.shape[1] // 2
        self.low, self.high = pl.ds(0, half), pl.ds(half, half)

    def ready(self, block):
        links, parts, low, high = self.links, self.parts, self.low, self.high
        if block == 3:
            self.first = links.go(parts.at[3, low], self.half_near, 0, 1)
            self.second = links.go(parts.at[3, high], self.half_far, 0, 2)
        if block == 1:
            self.near_low = links.go(parts.at[1, low], self.near.at[low], 0, 1)
        if block == 2:
            self.far_high = links.go(parts.at[2, high], self.far.at[high], 0, 2)

    def add_half(self, block, start, got):
        def add(rows, from_rows):
            total = self.parts[block, rows].astype(jnp.float32) + got[from_rows].astype(jnp.float32)
            self.parts[block, rows] = total.astype(jnp.bfloat16)

        half = got.shape[0]
        step = math.gcd(half, 32)

        def body(index, carry):
            at = index * step if step == 1 else pl.multiple_of(index * step, step)
            add(pl.ds(start + at, step), pl.ds(at, step))
            return carry

        lax.fori_loop(0, half // step, body, 0)

    def add(self):
        links, parts, low, high = self.links, self.parts, self.low, self.high
        half = parts.shape[1] // 2
        self.first.wait_recv()
        self.add_half(2, 0, self.half_near)
        self.far_low = links.go(parts.at[2, low], self.far.at[low], 0, 2)
        self.second.wait_recv()
        self.add_half(1, half, self.half_far)
        self.near_high = links.go(parts.at[1, high], self.near.at[high], 0, 1)

    def arrive(self):
        for copy in (self.near_low, self.far_high, self.far_low, self.near_high):
            copy.wait_recv()

    def sent(self):
        self.links.settle_sends(
            (self.first, self.second, self.near_low, self.far_high, self.far_low, self.near_high)
        )

    def total(self, rows):
        return self.near[rows].astype(jnp.float32) + self.far[rows].astype(jnp.float32)
def columns(total, width, body):
    def step(index, carry):
        body(pl.ds(pl.multiple_of(index * width, width), width))
        return carry

    lax.fori_loop(0, total // width, step, 0)


def attend_rows(block, keys_t, values, limit):
    outs, logs = [], []
    for which in range(2):
        part = jnp.where(half_mask(block.shape, 1, which), block, jnp.zeros_like(block))
        scores = jnp.dot(part, keys_t, preferred_element_type=jnp.float32)
        if limit is not None:
            scores = jnp.where(lax.broadcasted_iota(jnp.int32, scores.shape, 1) < limit, scores, -jnp.inf)
        peak = jnp.max(scores, axis=1, keepdims=True)
        shifted = jnp.exp(scores - peak)
        total = jnp.sum(shifted, axis=1, keepdims=True)
        product = jnp.dot(shifted.astype(jnp.bfloat16), values, preferred_element_type=jnp.float32)
        outs.append(product * (1.0 / total))
        logs.append(peak + jnp.log(total))
    low = half_mask(block.shape, 1, 0)
    return jnp.where(low, outs[0], outs[1]), jnp.where(low, logs[0], logs[1])


def cross_tile(weights, member, place, cols):
    tile = weights[member, place, :, :, cols]
    return tile.reshape(-1, tile.shape[-1])


def cross_columns(weights, member, cols):
    whole = weights[member, :, :, :, cols]
    return whole.reshape(-1, whole.shape[-1])


def row_steps(total, body):
    def step(index, carry):
        body(pl.ds(pl.multiple_of(index * 32, 32), 32))
        return carry

    lax.fori_loop(0, total // 32, step, 0)


def block_rows(block):
    return pl.ds(block * BLOCK, BLOCK)


def two_heads(weights, part, parts, pair):
    starts = [((2 * pair + which) * parts + part) * DH for which in range(2)]
    return jnp.concatenate([weights[:, start : start + DH] for start in starts], axis=1).astype(jnp.bfloat16)


def fill_tables(cosine, sine, member):
    quarter = DH // 4
    shape = (BLOCK, PAIR)
    lane = lax.broadcasted_iota(jnp.int32, shape, 1) % DH
    frequency = jnp.exp((lane % quarter).astype(jnp.float32) * (-math.log(rope_base) / quarter))
    for block in range(4):
        place = (member ^ block) * BLOCK + lax.broadcasted_iota(jnp.int32, shape, 0)
        angle = place.astype(jnp.float32) * frequency
        rows = block_rows(block)
        cosine[rows] = jnp.where(lane < 2 * quarter, jnp.cos(angle), 1.0)
        sine[rows] = jnp.where(lane < 2 * quarter, jnp.sin(angle), 0.0)


def forward_kernel(
    latents, gains, conditioning, f32_qkv,
    f32_attn_out, f32_cross_q, f32_cross_kv, f32_cross_out, f32_gate, f32_up, f32_down,
    rows_one_out, normed_two_out, rows_three_out, qkv_out, attn_out_out, cross_out, keyval_w_out, mlp_out,
    down_out, rotated_out, attended_out, logs_out,
    query_out, keyval_out, crossed_out, cross_logs_out, resid_one_out, resid_two_out, tables_out,
    rows_one, normed_two, rows_three, w_qkv, w_attn_out, w_cross, w_keyval, rotated, attended, logs, query, keyval,
    crossed, cross_logs, keys_t, parts, got_one, resid_one, resid_two,
    packed, tables, context, raw_attn_out, raw_cross_q, raw_cross_kv, raw_cross_out, raw_gate, raw_up, raw_down,
    own_qkv, own_attn_out, own_cross, own_keyval, own_mlp, own_down, send, recv, local,
):
    low = jnp.bfloat16
    pairs = attended.shape[1] // PAIR
    width = pairs * PAIR
    share = own_qkv.shape[0]
    links = Links(send, recv, local)
    loads = [
        links.store(source, target)
        for source, target in (
            (f32_attn_out, raw_attn_out), (f32_cross_q, raw_cross_q), (f32_cross_kv, raw_cross_kv),
            (f32_cross_out, raw_cross_out), (f32_gate, raw_gate), (f32_up, raw_up), (f32_down, raw_down),
        )
    ]
    for part in range(3):
        for pair in range(pairs):
            at = part * width + pair * PAIR
            own_qkv[:, at : at + PAIR] = two_heads(f32_qkv, part, 3, pair)
    links.greet([(1, 0), (2, 0), (4, 0), (6, 0), (0, 1), (0, 2)])
    gather_qkv = Gather(links, own_qkv, w_qkv)

    def norm_one(rows):
        rows_one[0, rows] = layer_norm(latents[rows].astype(jnp.float32), gains[0:1])[0].astype(low)

    row_steps(BLOCK, norm_one)
    spread_one = Spread(links, rows_one)
    cosine, sine = (tables.at[part] for part in range(2))
    fill_tables(cosine, sine, links.tensor)
    links.store(tables, tables_out)
    for load in loads:
        links.settle(load)
    own_attn_out[...] = raw_attn_out[...].astype(low)
    own_cross[:, :width] = raw_cross_q[...].astype(low)
    own_cross[:, width:] = raw_cross_out[...].astype(low)
    for part in range(2):
        for pair in range(pairs):
            at = part * width + pair * PAIR
            own_keyval[:, at : at + PAIR] = two_heads(raw_cross_kv, part, 2, pair)
    hidden = raw_gate.shape[1]
    own_mlp[:, :hidden] = raw_gate[...].astype(low)
    own_mlp[:, hidden:] = raw_up[...].astype(low)
    own_down[...] = raw_down[...].astype(low)
    links.store(own_down, down_out)
    context[...] = jnp.zeros_like(context)
    context[:CTX] = conditioning[0]
    spread_one.wait(1)
    gather_qkv.forward()
    gather_attn_out = Gather(links, own_attn_out, w_attn_out)
    gather_cross = Gather(links, own_cross, w_cross.at[0], False)
    spread_one.wait(2)
    links.settle(gather_cross.own)
    spread_cross = [SpreadCross(links, w_cross, links.dp // 2)]
    gather_qkv.arrive()
    links.store(w_qkv, qkv_out)

    for block in range(4):
        spread_one.wait(block)
        if block == 2:
            gather_attn_out.forward()
        if block == 3:
            gather_cross.forward()
            gather_keyval = Gather(links, own_keyval, w_keyval)
        rows = block_rows(block)
        turn = (cosine[rows], sine[rows])

        def project(cols):
            packed[:, cols] = dot_plain(rows_one[block], w_qkv[:, cols])

        columns(3 * width, width, project)
        for part in range(3):
            for pair in range(pairs):
                at = slice(part * width + pair * PAIR, part * width + (pair + 1) * PAIR)
                value = packed[:, at]
                rotated[rows, at] = (value if part == 2 else head_turn(value, *turn)).astype(low)
    links.store(rows_one, rows_one_out)
    links.store(rotated, rotated_out)
    for pair in range(pairs):
        key = rotated[:, width + pair * PAIR : width + (pair + 1) * PAIR]
        keys_t[pair] = key.astype(jnp.float32).T.astype(low)

    def out_project(source, block, weight, sums):
        def project(cols):
            parts[block, :, cols] = dot_cols(source[block_rows(block)], weight(cols)).astype(low)

        columns(parts.shape[2], 512, project)
        sums.ready(block)

    sums_one = Sums(links, parts, *got_one)
    for block in (3, 1, 2, 0):
        rows = block_rows(block)

        def one_pair(pair, carry):
            at = pl.ds(pl.multiple_of(pair * PAIR, PAIR), PAIR)
            values_at = pl.ds(pl.multiple_of(2 * width + pair * PAIR, PAIR), PAIR)
            out, log = attend_rows(rotated[rows, at] * low(DH**-0.5), keys_t[pair], rotated[:, values_at], None)
            attended[rows, at] = out.astype(low)
            logs[rows, at] = log
            return carry

        lax.fori_loop(0, pairs, one_pair, 0)
        if block == 3:
            gather_attn_out.arrive()
            links.store(w_attn_out, attn_out_out)
        out_project(attended, block, lambda cols: w_attn_out[cols, :], sums_one)
        if block == 3:
            spread_cross[0].forward()
            gather_mlp = Gather(links, own_mlp, mlp_out)
            spread_cross.append(SpreadCross(links, w_cross, (links.dp // 2) ^ 2))
        if block == 1:
            gather_cross.beside.wait_recv()
            spread_cross.append(SpreadCross(links, w_cross, (links.dp // 2) ^ 1))
        if block == 2:
            gather_keyval.forward()
            sums_one.add()
            spread_cross[1].forward()
    gather_cross.third.wait_recv()
    spread_cross.append(SpreadCross(links, w_cross, (links.dp // 2) ^ 3))
    spread_cross[2].forward()
    links.store(attended, attended_out)
    links.store(logs, logs_out)
    sums_one.arrive()

    def norm_two(rows):
        value = latents[rows].astype(jnp.float32) + parts[0, rows].astype(jnp.float32) + sums_one.total(rows)
        resid_one[rows] = value
        normed_two[rows] = layer_norm(value, gains[1:2])[0].astype(low)

    row_steps(BLOCK, norm_two)
    links.store(resid_one, resid_one_out)
    links.store(normed_two, normed_two_out)
    gather_keyval.arrive()
    links.store(w_keyval, keyval_w_out)
    keyval[0] = dot_plain(context[...], w_keyval[...]).astype(low)
    spread_keyval = Spread(links, keyval)
    spread_cross[3].forward()
    for spread in spread_cross:
        spread.last()
    resid_two[...] = resid_one[...]
    for member in range(4):
        for spread in spread_cross:
            spread.core[member].wait_recv()
        spread_keyval.wait(member)
        at_member = slice(member * width, (member + 1) * width)
        query[:, at_member] = dot_plain(normed_two[...], cross_columns(w_cross, member, slice(0, width))).astype(low)
        for pair in range(pairs):
            at = slice(member * width + pair * PAIR, member * width + (pair + 1) * PAIR)
            keys_at = slice(pair * PAIR, (pair + 1) * PAIR)
            values_at = slice(width + pair * PAIR, width + (pair + 1) * PAIR)
            key_t = keyval[member, :, keys_at].astype(jnp.float32).T.astype(low)
            out, log = attend_rows(query[:, at] * low(DH**-0.5), key_t, keyval[member, :, values_at], CTX)
            crossed[:, at] = out.astype(low)
            cross_logs[:, at] = log
        for place in range(4):
            at = slice(place * 2 * share, (place + 1) * 2 * share)
            tile = cross_tile(w_cross, member, place, slice(width, 2 * width))
            resid_two[:, at] += dot_cols(crossed[:, at_member], tile)
        if member == 1:
            gather_mlp.forward()
    links.store(w_cross, cross_out)
    links.store(keyval, keyval_out)
    links.store(query, query_out)
    links.store(crossed, crossed_out)
    links.store(cross_logs, cross_logs_out)
    links.store(resid_two, resid_two_out)

    def norm_three(rows):
        rows_three[rows] = layer_norm(resid_two[rows], gains[2:3])[0].astype(low)

    row_steps(BLOCK, norm_three)
    gather_mlp.arrive()
    links.store(rows_three, rows_three_out)
    links.finish()
    for gather in (gather_qkv, gather_attn_out, gather_cross, gather_keyval, gather_mlp):
        gather.finish()


def whole_vmem():
    return pl.BlockSpec(memory_space=pltpu.VMEM)


def anywhere():
    return pl.BlockSpec(memory_space=pl.ANY)


def sum_buffers(model):
    return [
        pltpu.VMEM((HALF, model), jnp.bfloat16),
        pltpu.VMEM((HALF, model), jnp.bfloat16),
        pltpu.VMEM((BLOCK, model), jnp.bfloat16),
        pltpu.VMEM((BLOCK, model), jnp.bfloat16),
    ]


def forward_part(latents, gains, conditioning, weights):
    w_qkv, w_attn_out, w_cross_q, w_cross_kv, w_cross_out, w_gate, w_up, w_down = weights
    model = latents.shape[1]
    depth = conditioning.shape[2]
    wide = w_qkv.shape[1]
    width = wide // 3
    hidden = w_gate.shape[1]
    pairs = width // PAIR
    low, high = jnp.bfloat16, jnp.float32
    share = w_qkv.shape[0]
    outs = [
        ((4, BLOCK, model), low),
        ((BLOCK, model), low),
        ((BLOCK, model), low),
        ((model, wide), low),
        ((model, width), low),
        ((4, 4, 2, share, 2 * width), low),
        ((depth, 2 * width), low),
        ((4, 2, share, 2 * hidden), low),
        ((share, hidden), low),
        ((LENGTH, wide), low),
        ((LENGTH, width), low),
        ((LENGTH, width), high),
        ((BLOCK, model), low),
        ((4, FULL, 2 * width), low),
        ((BLOCK, model), low),
        ((BLOCK, model), high),
        ((BLOCK, model), high),
        ((BLOCK, model), high),
        ((2, LENGTH, PAIR), high),
    ]
    work = [
        ((4, BLOCK, model), low),
        ((BLOCK, model), low),
        ((BLOCK, model), low),
        ((model, wide), low),
        ((model, width), low),
        ((4, 4, 2, share, 2 * width), low),
        ((depth, 2 * width), low),
        ((LENGTH, wide), low),
        ((LENGTH, width), low),
        ((LENGTH, width), high),
        ((BLOCK, model), low),
        ((4, FULL, 2 * width), low),
        ((BLOCK, model), low),
        ((BLOCK, model), high),
        ((pairs, PAIR, LENGTH), low),
        ((4, BLOCK, model), low),
    ]
    more = [
        ((BLOCK, model), high),
        ((BLOCK, model), high),
        ((BLOCK, wide), high),
        ((2, LENGTH, PAIR), high),
        ((FULL, depth), low),
        (w_attn_out.shape, high),
        (w_cross_q.shape, high),
        (w_cross_kv.shape, high),
        (w_cross_out.shape, high),
        (w_gate.shape, high),
        (w_up.shape, high),
        (w_down.shape, high),
        ((share, wide), low),
        ((share, width), low),
        ((share, 2 * width), low),
        (w_cross_kv.shape, low),
        ((share, 2 * hidden), low),
        ((share, hidden), low),
    ]
    scratch = [pltpu.VMEM(*buffer) for buffer in work] + [sum_buffers(model)]
    scratch += [pltpu.VMEM(*buffer) for buffer in more]
    scratch += [pltpu.SemaphoreType.DMA((96,)), pltpu.SemaphoreType.DMA((96,)), pltpu.SemaphoreType.DMA((40,))]
    return pl.pallas_call(
        forward_kernel,
        out_shape=[jax.ShapeDtypeStruct(*out) for out in outs],
        in_specs=[whole_vmem()] * 4 + [anywhere()] * 7,
        out_specs=[anywhere()] * len(outs),
        scratch_shapes=scratch,
        compiler_params=pltpu.CompilerParams(collective_id=1, has_side_effects=True, vmem_limit_bytes=VMEM_BYTES),
        cost_estimate=pl.CostEstimate(flops=2**37, bytes_accessed=2**26, transcendentals=2**23),
    )(latents, gains, conditioning, *weights)


class Scatter:
    def __init__(self, links, grads, got_core, extra, got):
        self.links, self.grads, self.got_core, self.extra, self.got = links, grads, got_core, extra, got
        self.size = got.shape[1]
        self.place, self.which = links.dp // 2, links.dp % 2
        self.middle = (self.place == 1) | (self.place == 2)

    def rows(self, place, which):
        if self.got_core is None:
            return place
        start = pl.multiple_of((2 * place + which) * self.size, self.size)
        return pl.ds(start, self.size)

    def pair_up(self):
        self.core = [
            self.links.go(self.grads.at[self.rows(place, 1 - self.which)], self.got_core.at[place], 1, 0)
            for place in range(4)
        ]

    def combine(self):
        for copy in self.core:
            copy.wait_recv()

        def add(place, carry):
            rows = self.rows(place, self.which)
            total = self.grads[rows].astype(jnp.float32) + self.got_core[place].astype(jnp.float32)
            self.grads[rows] = total.astype(jnp.bfloat16)
            return carry

        lax.fori_loop(0, 4, add, 0)
        self.start()

    def start(self):
        links, grads = self.links, self.grads
        block = [grads.at[self.rows(self.place ^ step, self.which)] for step in range(4)]
        self.to_extra = links.remote(block[3], self.extra, 2, 0)
        self.to_third = links.remote(block[3], self.got.at[2], 6, 0)
        self.to_skip = links.remote(block[2], self.got.at[1], 4, 0)

        @pl.when(self.middle)
        def _():
            self.to_third.start()

        @pl.when(jnp.logical_not(self.middle))
        def _():
            self.to_extra.start()
            self.to_skip.start()

        self.beside = links.go(block[1], self.got.at[0], 2, 0)

    def relay(self):
        @pl.when(self.middle)
        def _():
            self.to_extra.wait_recv()
            rows = self.rows(self.place ^ 2, self.which)
            self.grads[rows] = (
                self.grads[rows].astype(jnp.float32) + self.extra[...].astype(jnp.float32)
            ).astype(jnp.bfloat16)
            self.to_skip.start()

    def arrive(self):
        self.beside.wait_recv()
        self.to_skip.wait_recv()

        @pl.when(self.middle)
        def _():
            self.to_third.wait_recv()

    def total(self, out, cols):
        rows = self.rows(self.place, self.which)
        at = (rows, cols) if self.got_core is not None else (rows, slice(None), cols)
        mine = self.grads[at].astype(jnp.float32)
        out[...] = mine + self.got[0, :, cols].astype(jnp.float32) + self.got[1, :, cols].astype(jnp.float32)

        @pl.when(self.middle)
        def _():
            out[...] += self.got[2, :, cols].astype(jnp.float32)

    def finish(self):
        self.to_skip.wait_send()

        @pl.when(self.middle)
        def _():
            self.to_third.wait_send()

        @pl.when(jnp.logical_not(self.middle))
        def _():
            self.to_extra.wait_send()


def attend_rows_back(block, grads, log, keys_t, values_t, keys, d_keys_t, d_values_t, limit):
    block_t = block.astype(jnp.float32).T.astype(jnp.bfloat16)
    grads_t = grads.astype(jnp.float32).T.astype(jnp.bfloat16)
    outs = []
    for which in range(2):
        half = slice(which * DH, (which + 1) * DH)
        keep = half_mask(block.shape, 1, which)
        scores = jnp.dot(jnp.where(keep, block, jnp.zeros_like(block)), keys_t, preferred_element_type=jnp.float32)
        probs = jnp.exp(scores - log[:, which * DH : which * DH + 1])
        if limit is not None:
            probs = jnp.where(lax.broadcasted_iota(jnp.int32, probs.shape, 1) < limit, probs, 0.0)
        d_prob = jnp.dot(jnp.where(keep, grads, jnp.zeros_like(grads)), values_t, preferred_element_type=jnp.float32)
        center = jnp.sum(probs * d_prob, axis=1, keepdims=True)
        d_score = (probs * (d_prob - center)).astype(jnp.bfloat16)
        outs.append(jnp.dot(d_score, keys, preferred_element_type=jnp.float32))
        d_keys_t[half, :] += jnp.dot(block_t[half], d_score, preferred_element_type=jnp.float32)
        d_values_t[half, :] += jnp.dot(grads_t[half], probs.astype(jnp.bfloat16), preferred_element_type=jnp.float32)
    return jnp.where(half_mask(block.shape, 1, 0), outs[0], outs[1]) * DH**-0.5


def backward_kernel(
    latents, gains, conditioning, in_gain, in_d_resid, in_seed,
    in_grads_cross, in_d_keyval, in_qkv, in_attn_out, in_keyval_w, in_rows_one, in_rotated, in_attended, in_logs,
    in_tables,
    grad_latents, grad_context, grad_gains, grad_qkv, grad_attn_out, grad_cross_q, grad_keyval, grad_cross_out,
    parts, rows_one, seeds, w_qkv, w_attn_out, w_keyval, rotated, attended, d_attended, logs, keys_t, values_t,
    d_keys_t, d_values_t, grads_cross, core_cross, got_cross, keyval_parts, got_keyval, context, context_sum,
    context_got, d_resid, tables, gain_rows, gain_got, got, core_qkv, core_attn_out, core_keyval,
    extra_qkv, extra_attn_out, extra_cross, extra_keyval, far_qkv, far_attn_out, far_cross, far_keyval,
    sum_keyval, sum_last, out_qkv, out_keyval, send, recv, local,
):
    low = jnp.bfloat16
    width = attended.shape[1]
    pairs = width // PAIR
    model = latents.shape[1]
    links = Links(send, recv, local)
    which = links.dp % 2
    load_seed = links.store(in_seed, seeds)
    load_self = [
        links.store(source, target)
        for source, target in (
            (in_attn_out, w_attn_out), (in_rotated, rotated), (in_logs, logs), (in_tables, tables),
            (in_attended, attended),
        )
    ]
    load_keyval = [links.store(in_d_keyval, keyval_parts), links.store(in_keyval_w, w_keyval)]
    load_cross = [links.store(in_grads_cross.at[member, :, which], grads_cross.at[member]) for member in range(4)]
    load_late = [links.store(in_qkv, w_qkv), links.store(in_rows_one, rows_one), links.store(in_d_resid, d_resid)]
    links.greet([(1, 0), (2, 0), (4, 0), (6, 0), (0, 1), (0, 2)])
    core_copies = [
        links.go(in_grads_cross.at[member, :, 1 - which], core_cross.at[member], 1, 0) for member in range(4)
    ]
    gain_rows[...] = in_gain[...]
    context[...] = jnp.zeros_like(context)
    context[:CTX] = conditioning[0]
    sums_keyval = Sums(links, keyval_parts, *got_keyval)
    sums_cross = Sums(links, grads_cross, *got_cross)
    for load in load_keyval:
        links.settle(load)
    for part in (3, 1, 2):
        sums_keyval.ready(part)
    for member in (3, 1, 2, 0):
        links.settle(load_cross[member])
        core_copies[member].wait_recv()

        def add(place, carry):
            total = grads_cross[member, place].astype(jnp.float32) + core_cross[member, place].astype(jnp.float32)
            grads_cross[member, place] = total.astype(low)
            return carry

        lax.fori_loop(0, 4, add, 0)
        sums_cross.ready(member)
    links.settle(load_seed)
    for load in load_self:
        links.settle(load)
    for pair in range(pairs):
        key = rotated[:, width + pair * PAIR : width + (pair + 1) * PAIR]
        value = rotated[:, 2 * width + pair * PAIR : 2 * width + (pair + 1) * PAIR]
        keys_t[pair] = key.astype(jnp.float32).T.astype(low)
        values_t[pair] = value.astype(jnp.float32).T.astype(low)
    d_keys_t[...] = jnp.zeros_like(d_keys_t)
    d_values_t[...] = jnp.zeros_like(d_values_t)
    cosine, sine = (tables.at[part] for part in range(2))

    def whole(rows, cols):
        return rows[:, :, cols].reshape(LENGTH, -1)

    def grads_into(target, rows, right):
        def product(part):
            target[part, :] = dot_rows(whole(rows, part), right).astype(low)

        columns(model, 384, product)

    for block in range(4):
        d_attended[block_rows(block)] = dot_plain(seeds[block], w_attn_out[...]).astype(low)
    grads_into(w_attn_out, seeds, attended[...])
    scatter_attn_out = Scatter(links, w_attn_out, core_attn_out, extra_attn_out, far_attn_out)
    scatter_attn_out.pair_up()

    for block in range(4):
        rows = block_rows(block)
        turn = (cosine[rows], -sine[rows])

        def one_pair(pair, carry):
            at = pl.ds(pl.multiple_of(pair * PAIR, PAIR), PAIR)
            keys_at = pl.ds(pl.multiple_of(width + pair * PAIR, PAIR), PAIR)
            out = attend_rows_back(
                rotated[rows, at] * low(DH**-0.5), d_attended[rows, at], logs[rows, at], keys_t[pair],
                values_t[pair], rotated[:, keys_at], d_keys_t.at[pair], d_values_t.at[pair], None,
            )
            rotated[rows, at] = head_turn(out, *turn).astype(low)
            return carry

        lax.fori_loop(0, pairs, one_pair, 0)
        if block == 0:
            sums_keyval.add()
            sums_cross.add()
        if block == 1:
            scatter_attn_out.combine()
        if block == 2:
            sums_keyval.arrive()
            d_keyval = keyval_parts[0].astype(jnp.float32) + sums_keyval.total(slice(None))
            d_keyval = d_keyval.astype(low)
            context_sum[...] = dot_cols(d_keyval, w_keyval[...]).astype(low)
            context_near = links.go(context_sum, context_got.at[0], 0, 1)
            w_keyval[...] = dot_rows(context[...], d_keyval).astype(low)
            scatter_keyval = Scatter(links, w_keyval, core_keyval, extra_keyval, far_keyval)
            scatter_keyval.pair_up()
    sums_cross.arrive()
    for place in range(4):
        total = grads_cross[0, place].astype(jnp.float32) + sums_cross.total(place)
        grads_cross[0, place] = total.astype(low)
    scatter_cross = Scatter(links, grads_cross.at[0], None, extra_cross, far_cross)
    scatter_cross.start()
    scatter_attn_out.relay()
    scatter_keyval.combine()
    for pair in range(pairs):
        for block in range(4):
            rows = block_rows(block)
            turn = (cosine[rows], -sine[rows])
            at = slice(width + pair * PAIR, width + (pair + 1) * PAIR)
            rotated[rows, at] = head_turn(d_keys_t[pair, :, rows].T, *turn).astype(low)
            at = slice(2 * width + pair * PAIR, 2 * width + (pair + 1) * PAIR)
            rotated[rows, at] = d_values_t[pair, :, rows].T.astype(low)
    for load in load_late:
        links.settle(load)
    sums = Sums(links, parts, *got)
    for block in (3, 1, 2, 0):

        def project(cols):
            parts[block, :, cols] = dot_cols(rotated[block_rows(block)], w_qkv[cols, :]).astype(low)

        columns(model, 512, project)
        sums.ready(block)
    grads_into(w_qkv, rows_one, rotated[...])
    scatter_qkv = Scatter(links, w_qkv, core_qkv, extra_qkv, far_qkv)
    scatter_qkv.pair_up()
    sums.add()
    scatter_qkv.combine()
    scatter_cross.relay()
    scatter_keyval.relay()
    context_near.wait_recv()
    links.settle_sends((context_near,))
    context_sum[...] = (context_sum[...].astype(jnp.float32) + context_got[0].astype(jnp.float32)).astype(low)
    context_far = links.go(context_sum, context_got.at[1], 0, 2)
    sums.arrive()

    def norm_one(rows):
        gain = gains[0:1]
        _, scaled, inverse = layer_norm(latents[rows].astype(jnp.float32), gain)
        d_normed = parts[0, rows].astype(jnp.float32) + sums.total(rows)
        d_part, gain_grad = norm_backward(d_normed, scaled, inverse, gain)
        gain_rows[0:1] += gain_grad[None]
        d_resid[rows] += d_part

    row_steps(BLOCK, norm_one)
    links.store(d_resid, grad_latents)
    share = out_qkv.shape[0]
    spot = [logs.at[pl.ds(step * share, share)] for step in range(5)]
    qkv_spot = spot[3:5] + [sum_last]
    for step, (dp_bit, tensor_bit) in enumerate(((1, 0), (0, 1), (0, 2), (2, 0), (4, 0))):
        trade = links.remote(gain_rows, gain_got.at[step], dp_bit, tensor_bit)
        trade.start()
        if step == 1:
            scatter_qkv.relay()
        trade.wait()
        gain_rows[...] += gain_got[step]
    grad_gains[...] = gain_rows[...]
    context_far.wait_recv()
    context_total = context_sum[...].astype(jnp.float32) + context_got[1].astype(jnp.float32)
    grad_context[0] = context_total[:CTX]
    scatter_attn_out.arrive()
    scatter_attn_out.total(spot[2], slice(None))
    links.store(spot[2], grad_attn_out)
    scatter_qkv.arrive()
    for part in range(3):
        scatter_qkv.total(qkv_spot[part], slice(part * width, (part + 1) * width))
    for pair in range(pairs):
        heads_of = [
            qkv_spot[part][:, (2 * pair + half) * DH : (2 * pair + half + 1) * DH]
            for half in range(2)
            for part in range(3)
        ]
        for step in range(3):
            start = (3 * pair + step) * PAIR
            out_qkv[:, start : start + PAIR] = jnp.concatenate(heads_of[2 * step : 2 * step + 2], axis=1)
    links.store(out_qkv, grad_qkv)
    scatter_cross.arrive()
    scatter_cross.total(spot[0], slice(0, width))
    links.store(spot[0], grad_cross_q)
    scatter_cross.total(spot[1], slice(width, 2 * width))
    links.store(spot[1], grad_cross_out)
    scatter_keyval.arrive()
    scatter_keyval.total(sum_keyval, slice(None))
    for head in range(width // DH):
        pieces = [sum_keyval[:, start + head * DH : start + (head + 1) * DH] for start in (0, width)]
        out_keyval[:, 2 * head * DH : 2 * (head + 1) * DH] = jnp.concatenate(pieces, axis=1)
    links.store(out_keyval, grad_keyval)
    links.finish()
    for scatter in (scatter_keyval, scatter_cross, scatter_attn_out, scatter_qkv):
        scatter.finish()


def backward_part(latents, gains, conditioning, gain_rows, d_resid, seed, grads_cross, d_keyval, kept):
    w_qkv, w_attn_out, w_keyval, rows_one, rotated, attended, logs, tables = kept
    model = latents.shape[1]
    depth = conditioning.shape[2]
    wide = w_qkv.shape[1]
    width = wide // 3
    pairs = width // PAIR
    members = lax.axis_size("dp")
    share, span = model // members, depth // members
    low, high = jnp.bfloat16, jnp.float32
    outs = [
        ((BLOCK, model), high),
        (conditioning.shape, high),
        ((8, model), high),
        ((share, wide), high),
        ((share, width), high),
        ((share, width), high),
        ((span, 2 * width), high),
        ((share, width), high),
    ]
    cross_block = (4, share, 2 * width)
    work = [
        ((4, BLOCK, model), low),
        ((4, BLOCK, model), low),
        ((4, BLOCK, model), low),
        ((model, wide), low),
        ((model, width), low),
        ((depth, 2 * width), low),
        ((LENGTH, wide), low),
        ((LENGTH, width), low),
        ((LENGTH, width), low),
        ((LENGTH, width), high),
        ((pairs, PAIR, LENGTH), low),
        ((pairs, PAIR, LENGTH), low),
        ((pairs, PAIR, LENGTH), high),
        ((pairs, PAIR, LENGTH), high),
        ((4, *cross_block), low),
        ((4, *cross_block), low),
    ]
    cross_got = [pltpu.VMEM((rows, share, 2 * width), low) for rows in (2, 2, 4, 4)]
    keyval_got = [pltpu.VMEM((rows, 2 * width), low) for rows in (FULL // 2, FULL // 2, FULL, FULL)]
    more = [
        ((FULL, depth), low),
        ((FULL, depth), low),
        ((2, FULL, depth), low),
        ((BLOCK, model), high),
        ((2, LENGTH, PAIR), high),
        ((8, model), high),
        ((5, 8, model), high),
    ]
    groups = [(share, wide), (share, width), (share, 2 * width), (span, 2 * width)]
    scratch = [pltpu.VMEM(*buffer) for buffer in work] + [cross_got, pltpu.VMEM((4, FULL, 2 * width), low), keyval_got]
    scratch += [pltpu.VMEM(*buffer) for buffer in more] + [sum_buffers(model)]
    scratch += [pltpu.VMEM((4, *group), low) for group in (groups[0], groups[1], groups[3])]
    scratch += [pltpu.VMEM(group, low) for group in groups]
    scratch += [pltpu.VMEM((3, *group), low) for group in groups]
    scratch += [pltpu.VMEM(groups[3], high), pltpu.VMEM((share, width), high)]
    scratch += [pltpu.VMEM(shape, high) for shape in ((share, wide), (span, 2 * width))]
    scratch += [pltpu.SemaphoreType.DMA((96,)), pltpu.SemaphoreType.DMA((96,)), pltpu.SemaphoreType.DMA((48,))]
    return pl.pallas_call(
        backward_kernel,
        out_shape=[jax.ShapeDtypeStruct(*out) for out in outs],
        in_specs=[whole_vmem()] * 4 + [anywhere()] * 12,
        out_specs=[anywhere()] + [whole_vmem()] * 2 + [anywhere()] * 5,
        scratch_shapes=scratch,
        compiler_params=pltpu.CompilerParams(collective_id=2, has_side_effects=True, vmem_limit_bytes=VMEM_BYTES),
        cost_estimate=pl.CostEstimate(flops=2**37, bytes_accessed=2**26, transcendentals=2**23),
    )(
        latents, gains, conditioning, gain_rows, d_resid, seed, grads_cross, d_keyval, w_qkv, w_attn_out, w_keyval,
        rows_one, rotated, attended, logs, tables,
    )


class ScatterFar:
    def __init__(self, links, grads, got_core, extra, got):
        self.links, self.grads, self.got_core, self.extra, self.got = links, grads, got_core, extra, got
        self.place, self.which = links.dp // 2, links.dp % 2
        self.middle = (self.place == 1) | (self.place == 2)
        self.core = [
            links.go(grads.at[place, 1 - self.which], got_core.at[place], 1, 0) for place in range(4)
        ]

    def combine(self, stage, spots):
        links, self.spots = self.links, spots
        for copy in self.core:
            copy.wait_recv()
        size = spots[0].shape[0]
        slots = [stage.at[slot, 0] for slot in range(2)]
        mine = [links.store(self.grads.at[self.place ^ step, self.which], spots[step]) for step in range(4)]
        order = (3, 2, 1, 0)
        others = [links.store(self.got_core.at[self.place ^ step], slots[at]) for at, step in enumerate(order[:2])]
        for at, step in enumerate(order):
            links.settle(mine[step])
            links.settle(others[at])

            def add(rows):
                total = spots[step][rows].astype(jnp.float32) + slots[at % 2][rows].astype(jnp.float32)
                spots[step][rows] = total.astype(jnp.bfloat16)

            row_steps(size, add)
            if at < 2:
                others.append(links.store(self.got_core.at[self.place ^ order[at + 2]], slots[at]))
        self.to_extra = links.remote(spots[3], self.extra, 2, 0)
        self.to_third = links.remote(spots[3], self.got.at[2], 6, 0)
        self.to_skip = links.remote(spots[2], self.got.at[1], 4, 0)

        @pl.when(self.middle)
        def _():
            self.to_third.start()

        @pl.when(jnp.logical_not(self.middle))
        def _():
            self.to_extra.start()
            self.to_skip.start()

        self.beside = links.go(spots[1], self.got.at[0], 2, 0)

    def relay(self):
        @pl.when(self.middle)
        def _():
            self.to_extra.wait_recv()

            def add(rows):
                total = self.spots[2][rows].astype(jnp.float32) + self.extra[rows].astype(jnp.float32)
                self.spots[2][rows] = total.astype(jnp.bfloat16)

            row_steps(self.spots[0].shape[0], add)
            self.to_skip.start()

    def finish(self):
        self.beside.wait_recv()
        self.to_skip.wait()

        @pl.when(self.middle)
        def _():
            self.to_third.wait()

        @pl.when(jnp.logical_not(self.middle))
        def _():
            self.to_extra.wait_send()


def middle_kernel(
    cotangent, gains, normed_two, resid_two, resid_one, in_rows, in_mlp, own_down, in_query, in_crossed,
    in_cross_logs, in_keyval, in_cross,
    block_out, d_resid_out, seed_out, grads_out, d_keyval_out, gain_out, grads_down_out, grads_gate_out, grads_up_out,
    core_down, core_gate, far_down, far_gate, own_down_out, own_gate_out,
    rows_three, seeds, w_mlp, w_down, hidden, both, parts, parts_last, stage, extra_down, extra_gate, spots_down,
    got, got_last,
    cross_logs, keyval, d_keyval, d_keys_t, d_values_t, d_resid, d_normed_two,
    send, recv, local, stage_sem,
):
    low = jnp.bfloat16
    model = cotangent.shape[1]
    width = model // 4
    share = own_down.shape[0]
    units = w_down.shape[1]
    pairs = width // PAIR
    links = Links(send, recv, local)
    load_rows = links.store(in_rows, rows_three.at[0])
    load_mlp = links.store(in_mlp, w_mlp)
    seeds[0] = cotangent[...]
    links.greet([(1, 0), (2, 0), (4, 0), (6, 0), (0, 1), (0, 2)])
    gather_down = Gather(links, own_down, w_down)
    links.settle(load_rows)
    spread_three = Spread(links, rows_three)
    loads = [
        links.store(source, target)
        for source, target in (
            (in_cross_logs, cross_logs), (in_keyval, keyval),
        )
    ]
    gain_out[...] = jnp.zeros_like(gain_out)
    links.settle(load_mlp)
    for block in range(4):
        if block == 3:
            gather_down.forward()
        spread_three.wait(block)
        if block == 2:
            spread_seeds = Spread(links, seeds)
        rows = block_rows(block)

        def up(cols):
            above_at = pl.ds(pl.multiple_of(units + cols.start, cols.size), cols.size)
            gate = dot_plain(rows_three[block], w_mlp[:, :, :, cols].reshape(model, -1))
            above = dot_plain(rows_three[block], w_mlp[:, :, :, above_at].reshape(model, -1))
            sigma = 1.0 / (1.0 + jnp.exp(-gate))
            swish = gate * sigma
            hidden[rows, cols] = (swish * above).astype(low)
            both[rows, cols] = (above * sigma * (1.0 + gate * (1.0 - sigma))).astype(low)
            both[rows, above_at] = swish.astype(low)

        columns(units, 256, up)
    spread_seeds.wait(1)
    spread_seeds.wait(3)

    def tiles_out(count, product, place):
        def copy(index, slot):
            return pltpu.make_async_copy(stage.at[slot], place(index), stage_sem.at[slot])

        def step(index, carry):
            slot = index % 2

            @pl.when(index >= 2)
            def _():
                copy(index - 2, slot).wait()

            for start in (0, units // 2):
                cols = pl.ds(start, units // 2)
                stage[slot, :, :, cols] = product(index, cols).reshape(2, share, -1)
            copy(index, slot).start()
            return carry

        lax.fori_loop(0, count, step, 0)
        for index in (count - 2, count - 1):
            copy(index, index % 2).wait()

    def rows_of(index, size):
        return pl.ds(pl.multiple_of(index * size, size), size)

    tile = 2 * share

    def whole(rows, index):
        return rows[:, :, rows_of(index, tile)].reshape(LENGTH, -1)

    tiles_out(
        model // tile,
        lambda index, cols: dot_rows(whole(seeds, index), hidden[:, cols]).astype(low),
        lambda index: grads_down_out.at[index],
    )
    scatter_down = ScatterFar(links, grads_down_out, core_down, extra_down, far_down)
    gather_down.arrive()
    sums = Sums(links, parts, *got)
    for block in (3, 1, 2, 0):
        rows = block_rows(block)

        def back(cols):
            above_at = pl.ds(pl.multiple_of(units + cols.start, cols.size), cols.size)
            d_hidden = dot_plain(seeds[block], w_down[:, cols])
            both[rows, cols] = (both[rows, cols].astype(jnp.float32) * d_hidden).astype(low)
            both[rows, above_at] = (both[rows, above_at].astype(jnp.float32) * d_hidden).astype(low)

        columns(units, 256, back)

        def down(place, carry):
            weights = w_mlp[place].reshape(2 * share, -1)
            parts[block, :, rows_of(place, 2 * share)] = dot_cols(both[rows], weights).astype(low)
            return carry

        lax.fori_loop(0, 4, down, 0)
        sums.ready(block)
        if block == 3:
            scatter_down.combine(stage, [spots_down.at[place] for place in range(4)])
    sums.add()
    scatter_down.relay()
    w_cross = [w_mlp.at[:, :, :, pl.ds(member * 2 * width, 2 * width)] for member in range(4)]
    load_cross = [links.store(in_cross.at[member], w_cross[member]) for member in range(4)]
    for block in range(4):

        def last(cols):
            parts_last[block, :, cols] = dot_cols(hidden[block_rows(block)], w_down[cols, :]).astype(low)

        columns(model, 512, last)

    def grads_mlp(half, target):
        start = half * units
        tiles_out(
            model // tile,
            lambda index, cols: dot_rows(
                whole(rows_three, index), both[:, pl.ds(start + cols.start, cols.size)]
            ).astype(low),
            lambda index: target.at[index],
        )

    grads_mlp(0, grads_gate_out)
    scatter_gate = ScatterFar(links, grads_gate_out, core_gate, extra_gate, far_gate)
    gather_down.sent()
    query, crossed, cross_seed, seed = (w_down.at[block_rows(spot)] for spot in range(4))
    loads += [links.store(in_query, query), links.store(in_crossed, crossed)]
    for load in loads + load_cross:
        links.settle(load)
    sums.arrive()
    sums_last = Sums(links, parts_last, *got_last)
    for block in (3, 1, 2):
        sums_last.ready(block)
    scatter_gate.combine(stage, [hidden.at[pl.ds(place * BLOCK, share)] for place in range(4)])

    def cross_columns(member, cols):
        return w_cross[member][:, :, :, cols].reshape(model, -1)

    def norm_three(rows):
        gain = gains[2:3]
        _, scaled, inverse = layer_norm(resid_two[rows], gain)
        d_normed = parts[0, rows].astype(jnp.float32) + sums.total(rows)
        d_part, gain_grad = norm_backward(d_normed, scaled, inverse, gain)
        gain_out[2:3] += gain_grad[None]
        value = cotangent[rows].astype(jnp.float32) + d_part
        d_resid[rows] = value
        cross_seed[rows] = value.astype(low)

    row_steps(BLOCK, norm_three)
    for member in range(4):
        at_member = slice(member * width, (member + 1) * width)
        d_crossed = dot_plain(cross_seed[...], cross_columns(member, slice(width, 2 * width))).astype(low)
        for pair in range(pairs):
            at = slice(member * width + pair * PAIR, member * width + (pair + 1) * PAIR)
            keys_at = slice(pair * PAIR, (pair + 1) * PAIR)
            values_at = slice(width + pair * PAIR, width + (pair + 1) * PAIR)
            key = keyval[member, :, keys_at]
            key_t = key.astype(jnp.float32).T.astype(low)
            value_t = keyval[member, :, values_at].astype(jnp.float32).T.astype(low)
            d_keys_t[...] = jnp.zeros_like(d_keys_t)
            d_values_t[...] = jnp.zeros_like(d_values_t)
            out = attend_rows_back(
                query[:, at] * low(DH**-0.5), d_crossed[:, keys_at], cross_logs[:, at], key_t, value_t, key, d_keys_t,
                d_values_t, CTX,
            )
            query[:, at] = out.astype(low)
            d_keyval[member, :, keys_at] = d_keys_t[...].T.astype(low)
            d_keyval[member, :, values_at] = d_values_t[...].T.astype(low)
        for place in range(4):
            at = slice(place * 2 * share, (place + 1) * 2 * share)
            part = dot_cols(query[:, at_member], w_cross[member][place, :, :, :width].reshape(2 * share, width))
            if member == 0:
                d_normed_two[:, at] = part
            else:
                d_normed_two[:, at] += part
    links.store(d_keyval, d_keyval_out)
    scatter_gate.relay()

    def norm_two(rows):
        gain = gains[1:2]
        _, scaled, inverse = layer_norm(resid_one[rows], gain)
        d_part, gain_grad = norm_backward(d_normed_two[rows], scaled, inverse, gain)
        gain_out[1:2] += gain_grad[None]
        value = d_resid[rows] + d_part
        d_resid[rows] = value
        seed[rows] = value.astype(low)

    row_steps(BLOCK, norm_two)
    links.settle(links.store(seed, seed_out.at[0]))
    spread_seed = Spread(links, seed_out)
    links.store(d_resid, d_resid_out)
    sums_last.add()
    grads_mlp(1, grads_up_out)
    for place in range(4):
        rows_at = slice(place * 2 * share, (place + 1) * 2 * share)
        for member in range(4):
            at_member = slice(member * width, (member + 1) * width)
            left = dot_rows(normed_two[:, rows_at], query[:, at_member]).astype(low)
            w_cross[member][place, :, :, :width] = left.reshape(2, share, width)
            right = dot_rows(cross_seed[:, rows_at], crossed[:, at_member]).astype(low)
            w_cross[member][place, :, :, width:] = right.reshape(2, share, width)
    for member in range(4):
        links.store(w_cross[member], grads_out.at[member])
    spread_seed.wait(1)
    sums_last.arrive()

    def add_last(rows):
        d_normed_two[rows] = resid_two[rows] + parts_last[0, rows].astype(jnp.float32) + sums_last.total(rows)

    row_steps(BLOCK, add_last)
    links.store(d_normed_two, block_out)
    spread_seed.wait(3)
    links.store(scatter_down.spots[0], own_down_out)
    links.store(scatter_gate.spots[0], own_gate_out)
    links.finish()
    scatter_down.finish()
    scatter_gate.finish()


def middle_part(cotangent, gains, rows_three, mlp_all, own_down, kept):
    normed_two, resid_two, resid_one, query, crossed, cross_logs, keyval, cross_all = kept
    model = cotangent.shape[1]
    share, units = own_down.shape
    low, high = jnp.bfloat16, jnp.float32
    outs = [
        ((BLOCK, model), high),
        ((BLOCK, model), high),
        ((4, BLOCK, model), low),
        (cross_all.shape, low),
        (keyval.shape, low),
        ((8, model), high),
        ((4, 2, share, units), low),
        ((4, 2, share, units), low),
        ((4, 2, share, units), low),
        ((4, share, units), low),
        ((4, share, units), low),
        ((3, share, units), low),
        ((3, share, units), low),
        ((share, units), low),
        ((share, units), low),
    ]
    work = [
        ((4, BLOCK, model), low),
        ((4, BLOCK, model), low),
        (mlp_all.shape, low),
        ((model, units), low),
        ((LENGTH, units), low),
        ((LENGTH, 2 * units), low),
        ((4, BLOCK, model), low),
        ((4, BLOCK, model), low),
        ((2, 2, share, units), low),
        ((share, units), low),
        ((share, units), low),
        ((4, share, units), low),
    ]
    more = [
        ((BLOCK, model), high),
        (keyval.shape, low),
        (keyval.shape, low),
        ((PAIR, FULL), high),
        ((PAIR, FULL), high),
        ((BLOCK, model), high),
        ((BLOCK, model), high),
    ]
    scratch = [pltpu.VMEM(*buffer) for buffer in work] + [sum_buffers(model), sum_buffers(model)]
    scratch += [pltpu.VMEM(*buffer) for buffer in more]
    scratch += [pltpu.SemaphoreType.DMA((96,)), pltpu.SemaphoreType.DMA((96,)), pltpu.SemaphoreType.DMA((64,))]
    scratch += [pltpu.SemaphoreType.DMA((2,))]
    return pl.pallas_call(
        middle_kernel,
        out_shape=[jax.ShapeDtypeStruct(*out) for out in outs],
        in_specs=[whole_vmem()] * 5 + [anywhere()] * 8,
        out_specs=[anywhere()] * 5 + [whole_vmem()] + [anywhere()] * 9,
        scratch_shapes=scratch,
        compiler_params=pltpu.CompilerParams(collective_id=3, has_side_effects=True, vmem_limit_bytes=VMEM_BYTES),
        cost_estimate=pl.CostEstimate(flops=2**36, bytes_accessed=2**26, transcendentals=2**21),
    )(
        cotangent, gains, normed_two, resid_two, resid_one, rows_three, mlp_all, own_down, query, crossed,
        cross_logs, keyval, cross_all,
    )


def finish_kernel(
    in_out, in_latents, in_qkv, in_attn_out, in_cross_q, in_keyval, in_cross_out, own_gate, far_gate, own_down, far_down,
    in_up,
    block_out, grad_latents, grad_qkv, grad_attn_out, grad_cross_q, grad_keyval, grad_cross_out, grad_gate, grad_up,
    grad_down,
):
    for source, target in (
        (in_out, block_out), (in_latents, grad_latents), (in_qkv, grad_qkv), (in_attn_out, grad_attn_out),
        (in_cross_q, grad_cross_q), (in_keyval, grad_keyval), (in_cross_out, grad_cross_out),
    ):

        def move(rows):
            target[rows] = source[rows].astype(jnp.float32)

        row_steps(source.shape[0], move)
    place = lax.axis_index("dp") // 2
    middle = (place == 1) | (place == 2)
    for own, far, target in ((own_gate, far_gate, grad_gate), (own_down, far_down, grad_down)):

        def add(rows):
            third = jnp.where(middle, far[2, rows].astype(jnp.float32), 0.0)
            total = own[rows].astype(jnp.float32) + far[0, rows].astype(jnp.float32)
            target[rows] = total + far[1, rows].astype(jnp.float32) + third

        row_steps(own.shape[0], add)

    def widen(rows):
        grad_up[rows] = in_up[rows].astype(jnp.float32)

    row_steps(in_up.shape[0], widen)


def finish_part(raw, own_gate, far_gate, own_down, far_down, sum_up):
    wide = jax.ShapeDtypeStruct(sum_up.shape, jnp.float32)
    return pl.pallas_call(
        finish_kernel,
        out_shape=[jax.ShapeDtypeStruct(array.shape, jnp.float32) for array in raw] + [wide] * 3,
        in_specs=[whole_vmem()] * 12,
        out_specs=[whole_vmem()] * 10,
        compiler_params=pltpu.CompilerParams(vmem_limit_bytes=VMEM_BYTES),
        cost_estimate=pl.CostEstimate(flops=2**22, bytes_accessed=2**24, transcendentals=0),
    )(*raw, own_gate, far_gate, own_down, far_down, sum_up)


def per_device(
    latents,
    conditioning,
    gain_attn,
    w_qkv,
    w_attn_out,
    gain_cross,
    w_cross_q,
    w_cross_kv,
    w_cross_out,
    gain_mlp,
    w_gate,
    w_up,
    w_down,
    cotangent,
):
    low = jnp.bfloat16
    gains = jnp.concatenate([gain_attn, gain_cross, gain_mlp]).reshape(3, -1)
    (
        rows_one, normed_two, rows_three, qkv_all, attn_out_t, cross_all, cross_kv, mlp_all, own_down,
        rotated, attended, logs, cross_query, keyval, crossed, cross_logs, resid_one, resid_two, tables,
    ) = forward_part(
        latents,
        gains,
        conditioning,
        (w_qkv, w_attn_out.T, w_cross_q, w_cross_kv, w_cross_out.T, w_gate, w_up, w_down.T),
    )
    (
        block_out, d_resid, seed, grads_cross, d_keyval, gain_rows, _, _, grads_up, _, _, far_down, far_gate, own_down,
        own_gate,
    ) = middle_part(
        cotangent,
        gains,
        rows_three,
        mlp_all,
        own_down,
        (normed_two, resid_two, resid_one, cross_query, crossed, cross_logs, keyval, cross_all),
    )
    sum_up = dp_sum(grads_up.reshape(w_gate.shape[0] * 8, -1))
    grad_latents, grad_context, grad_gains, grad_qkv, grad_attn_out, grad_cross_q, grad_cross_kv, grad_cross_out = (
        backward_part(
            latents,
            gains,
            conditioning,
            gain_rows,
            d_resid,
            seed,
            grads_cross,
            d_keyval,
            (qkv_all, attn_out_t, cross_kv, rows_one, rotated, attended, logs, tables),
        )
    )
    raw = (block_out, grad_latents, grad_qkv, grad_attn_out, grad_cross_q, grad_cross_kv, grad_cross_out)
    (
        block_out, grad_latents, grad_qkv, grad_attn_out, grad_cross_q, grad_cross_kv, grad_cross_out, grad_gate,
        grad_up, grad_down,
    ) = finish_part(raw, own_gate, far_gate, own_down, far_down, sum_up)
    return (
        block_out,
        grad_latents,
        grad_context,
        grad_gains[0],
        grad_qkv,
        grad_attn_out.T,
        grad_gains[1],
        grad_cross_q,
        grad_cross_kv,
        grad_cross_out.T,
        grad_gains[2],
        grad_gate,
        grad_up,
        grad_down.T,
    )


def per_device_general(
    latents,
    conditioning,
    gain_attn,
    w_qkv,
    w_attn_out,
    gain_cross,
    w_cross_q,
    w_cross_kv,
    w_cross_out,
    gain_mlp,
    w_gate,
    w_up,
    w_down,
    cotangent,
):
    low = jnp.bfloat16
    heads_wide = w_cross_q.shape[1]
    hidden_wide = w_gate.shape[1]
    resid_in = latents.astype(jnp.float32)
    normed_one, scaled_one, inverse_one = layer_norm(resid_in, gain_attn)
    rows_one = spread_rows(normed_one.astype(low))
    own_qkv = by_part(w_qkv.astype(low), 3)
    qkv_all = lax.all_gather(own_qkv, "dp", axis=0, tiled=True)
    own_kv = by_part(w_cross_kv.astype(low), 2)
    own_kv = jnp.concatenate([own_kv[:, :heads_wide], own_kv[:, heads_wide:]], axis=0)
    own_mid = jnp.concatenate(
        [w_attn_out.astype(low).T, w_cross_q.astype(low), w_cross_out.astype(low).T, own_kv], axis=1
    )
    mid_all = lax.all_gather(after(own_mid, qkv_all), "dp", axis=0, tiled=True)
    own_mlp = jnp.concatenate([w_gate.astype(low), w_up.astype(low)], axis=1)
    mlp_all = lax.all_gather(after(own_mlp, mid_all), "dp", axis=0, tiled=True)
    down_all = lax.all_gather(after(w_down.astype(low).T, mlp_all), "dp", axis=0, tiled=True)
    attn_out_t, cross_q, cross_out_t = (mid_all[:, part * heads_wide : (part + 1) * heads_wide] for part in range(3))
    model = mid_all.shape[0]
    cross_kv = (
        mid_all[:, 3 * heads_wide :]
        .reshape(lax.axis_size("dp"), 2, -1, heads_wide)
        .transpose(0, 2, 1, 3)
        .reshape(model // 2, 2 * heads_wide)
    )

    tables = turn_tables(group_positions(latents.shape[0]))
    packed = dot_plain(rows_one, qkv_all)
    attended, rotated, logs = attend(pad_heads(packed, 3), tables)
    attended = attended[:, :heads_wide]
    resid_one = resid_in + sum_rows(dot_cols(attended, attn_out_t))
    normed_two, scaled_two, inverse_two = layer_norm(resid_one, gain_cross)
    rows_two = spread_rows(normed_two.astype(low))
    head_shape = (-1, heads_wide // DH, DH)
    cross_query = dot_plain(rows_two, cross_q).astype(low).reshape(head_shape)
    context = conditioning.reshape(CTX, conditioning.shape[2])
    cross_pack = dot_plain(context, cross_kv).astype(low)
    cross_key = cross_pack[:, :heads_wide].reshape(head_shape)
    cross_value = cross_pack[:, heads_wide:].reshape(head_shape)
    crossed, cross_logs = cross_forward(cross_query, cross_key, cross_value)
    crossed = crossed.reshape(-1, heads_wide).astype(low)
    resid_two = resid_one + sum_rows(dot_cols(crossed, cross_out_t))
    normed_three, scaled_three, inverse_three = layer_norm(resid_two, gain_mlp)
    rows_three = spread_rows(normed_three.astype(low))
    mlp_seed = spread_rows(cotangent)
    both = dot_plain(rows_three, mlp_all)
    gate_pre, up_pre = both[:, :hidden_wide], both[:, hidden_wide:]
    sigma_gate = jax.nn.sigmoid(gate_pre)
    swish = gate_pre * sigma_gate
    hidden = (swish * up_pre).astype(low)
    sum_down = dp_sum(dot_rows(mlp_seed, hidden))
    d_hidden = dot_plain(mlp_seed, down_all)
    d_gate = (d_hidden * up_pre * sigma_gate * (1.0 + gate_pre * (1.0 - sigma_gate))).astype(low)
    d_up = (d_hidden * swish).astype(low)
    d_both = jnp.concatenate([d_gate, d_up], axis=1)
    sum_mlp = dp_sum(after(dot_rows(rows_three, d_both), sum_down))
    d_normed = sum_rows(dot_cols(d_both, mlp_all))
    d_part, gain_grad_three = norm_backward(d_normed, scaled_three, inverse_three, gain_mlp)
    d_resid = cotangent.astype(jnp.float32) + d_part
    block_out = resid_two + sum_rows(dot_cols(hidden, down_all))
    cross_seed = spread_rows(d_resid.astype(low))
    grad_cross_out = dot_rows(cross_seed, crossed)
    d_crossed = dot_plain(cross_seed, cross_out_t).astype(low).reshape(head_shape)
    d_query, d_key, d_value = cross_backward(cross_query, cross_key, cross_value, d_crossed, cross_logs)
    d_query = d_query.reshape(-1, heads_wide).astype(low)
    d_keyval = jnp.concatenate([d_key.reshape(CTX, -1), d_value.reshape(CTX, -1)], axis=1).astype(low)
    grad_cross_q = dot_rows(rows_two, d_query)
    grad_cross_kv = dot_rows(context, d_keyval)
    context_part = dot_cols(d_keyval, cross_kv)
    d_normed = sum_rows(dot_cols(d_query, cross_q))
    d_part, gain_grad_two = norm_backward(d_normed, scaled_two, inverse_two, gain_cross)
    d_resid = d_resid + d_part
    self_seed = spread_rows(d_resid.astype(low))
    grad_attn_out = dot_rows(self_seed, attended)
    grad_kv = (
        grad_cross_kv.astype(low)
        .reshape(lax.axis_size("dp"), -1, 2, heads_wide)
        .transpose(0, 2, 1, 3)
        .reshape(model, heads_wide)
    )
    grad_mid = jnp.concatenate([grad_attn_out.astype(low), grad_cross_q.astype(low), grad_cross_out.astype(low), grad_kv], axis=1)
    sum_mid = dp_sum(after(grad_mid, sum_mlp))
    d_attended = dot_plain(self_seed, attn_out_t).astype(low)
    d_packed = drop_heads(attend_back(rotated, pad_heads(d_attended, 1), logs, tables), 3, packed.shape[1])
    sum_qkv = dp_sum(after(dot_rows(rows_one, d_packed), sum_mid))
    d_normed = sum_rows(dot_cols(d_packed, qkv_all))
    d_part, gain_grad_one = norm_backward(d_normed, scaled_one, inverse_one, gain_attn)
    grad_latents = d_resid + d_part
    grad_context = (
        lax.psum(context_part.astype(low), "tensor").astype(jnp.float32).reshape(conditioning.shape)
    )
    gains = lax.psum(jnp.stack([gain_grad_one, gain_grad_two, gain_grad_three]), ("dp", "tensor"))
    sums = [sum_mid[:, part * heads_wide : (part + 1) * heads_wide].astype(jnp.float32) for part in range(4)]
    half = sums[3].shape[0] // 2
    sum_kv = jnp.concatenate([sums[3][:half], sums[3][half:]], axis=1)
    return (
        block_out,
        grad_latents,
        grad_context,
        gains[0],
        by_head(sum_qkv, 3).astype(jnp.float32),
        sums[0].T,
        gains[1],
        sums[1],
        by_head(sum_kv, 2),
        sums[2].T,
        gains[2],
        sum_mlp[:, :hidden_wide].astype(jnp.float32),
        sum_mlp[:, hidden_wide:].astype(jnp.float32),
        sum_down.astype(jnp.float32).T,
    )


def solution(mesh):
    in_specs = (
        P(("dp", "tensor"), None),
        P("dp", None, None),
        P(),
        P("dp", "tensor"),
        P("tensor", "dp"),
        P(),
        P("dp", "tensor"),
        P("dp", "tensor"),
        P("tensor", "dp"),
        P(),
        P("dp", "tensor"),
        P("dp", "tensor"),
        P("tensor", "dp"),
        P(("dp", "tensor"), None),
    )
    out_specs = (
        P(("dp", "tensor"), None),
        P(("dp", "tensor"), None),
        P("dp", None, None),
        P(),
        P("dp", "tensor"),
        P("tensor", "dp"),
        P(),
        P("dp", "tensor"),
        P("dp", "tensor"),
        P("tensor", "dp"),
        P(),
        P("dp", "tensor"),
        P("dp", "tensor"),
        P("tensor", "dp"),
    )
    special = dict(mesh.shape) == {"dp": 8, "tensor": 4}
    return jax.shard_map(
        per_device if special else per_device_general, mesh=mesh, in_specs=in_specs, out_specs=out_specs, check_vma=False
    )
```
